32 devices in a mesh: dp: 8 (over z, x), proj: 4 (over y, core).
Axes of the slice: x: 2, y: 2, z: 4, core: 2. Of those that a mesh axis runs over, the one named last changes fastest.
Arguments:
- inputs: bfloat16 [8192, 1024], P('dp'), may hold values from -6 to 6
- targets: int32 [8192], P('dp'), may hold values from 0 to 50303
- lengths: int32 [8], replicated, may hold values from 1 to 1024, as said below
- norm_gain_vectors: float32 [3, 1024], replicated, may hold values from 0.5 to 1.5
- query_key_value_weight: bfloat16 [1024, 3, 1024], P(None, None, 'proj')
- attention_output_weight: bfloat16 [1024, 1024], P('proj'), may hold values from -2 to 2
- feedforward_input_weight: bfloat16 [1024, 4096], P(None, 'proj'), may hold values from -0.1875 to 0.1875
- feedforward_output_weight: bfloat16 [4096, 1024], P('proj'), may hold values from -0.09375 to 0.09375
- unembed: bfloat16 [1024, 50304], P(None, 'proj')
- adapter_down_maps: float32 [4, 1024, 128], P(None, 'proj', 'dp'), may hold values from -0.1875 to 0.1875
- adapter_up_maps: float32 [4, 128, 1024], P(None, 'dp', 'proj'), may hold values from -0.5 to 0.5
- down_first_moment: float32 [4, 1024, 128], P(None, 'proj', 'dp'), may hold values from -3.0517578e-05 to 3.0517578e-05
- up_first_moment: float32 [4, 128, 1024], P(None, 'dp', 'proj'), may hold values from -3.0517578e-05 to 3.0517578e-05
- down_second_moment: float32 [4, 1024, 128], P(None, 'proj', 'dp'), may hold values from 2.4080276e-11 to 9.6321104e-11
- up_second_moment: float32 [4, 128, 1024], P(None, 'dp', 'proj'), may hold values from 2.4080276e-11 to 9.6321104e-11
- target_gradient_sketches: float32 [4, 8, 32, 32], P(None, None, 'proj'), may hold values from -6 to 6
- seeds: int32 [8], replicated, may hold values from 0 to 99999
Outputs:
- loss_parts: float32 [2], replicated
- grad_norm: float32 [1], replicated
- influence: float32 [8], P('dp')
- down_maps_updated: float32 [4, 1024, 128], P(None, 'proj', 'dp')
- up_maps_updated: float32 [4, 128, 1024], P(None, 'dp', 'proj')
- down_first_updated: float32 [4, 1024, 128], P(None, 'proj', 'dp')
- up_first_updated: float32 [4, 128, 1024], P(None, 'dp', 'proj')
- down_second_updated: float32 [4, 1024, 128], P(None, 'proj', 'dp')
- up_second_updated: float32 [4, 128, 1024], P(None, 'dp', 'proj')
The draws below stay inside these ranges and needn't reach their ends.
Inputs may be any that keep to these rules, and one draw needn't show every extreme that they name: lengths[s] is the number of counted tokens of sequence s; the largest is 1024.
All inputs are finite; a program needn't handle non-finite values.
Results may differ from the reference program's by a relative error of at most 0.019.
Values may be sent and summed in bfloat16 or wider, within the bound.
No kernel may reach another device: no remote copies, remote signals or barrier semaphores. Data moves between devices by JAX's collectives and lax.ppermute only.
A program may use at most 192 MiB of HBM per device.

```python
import math
import jax
import jax.numpy as jnp
import numpy as np
from jax import lax

MODEL_DIM = 1024
HEAD = 64
ROT = 16
FF = 4096
VOCAB = 50304
ADAPTER_RANKS = 128
SK = 32
CKPTS = 4
STEP = 10
LEN = 1024
SEQS = 8
TOKENS = 8192


def draw_lengths(key, part):
    key = jax.random.fold_in(key, 11)
    seq_index = jnp.arange(SEQS, dtype=jnp.int32)
    floor_len = LEN // 3
    base_len = floor_len + (LEN - floor_len) * seq_index // max(SEQS - 1, 1)
    jitter = jax.random.randint(key, (SEQS,), 0, LEN // 8 + 1, dtype=jnp.int32)
    drawn = jnp.maximum(base_len - jitter, 1)
    return jnp.where(seq_index == SEQS - 1, LEN, drawn).astype(jnp.int32)


def draw_query_key_value_weight(key, part):
    key = jax.random.fold_in(key, 12)
    noise = jax.random.normal(key, (MODEL_DIM, 3, MODEL_DIM), jnp.float32)
    ramp = 0.6 + 1.2 * jnp.arange(MODEL_DIM, dtype=jnp.float32) / MODEL_DIM
    column_scale = jnp.stack([jnp.ones((MODEL_DIM,), jnp.float32), jnp.ones((MODEL_DIM,), jnp.float32), ramp])
    return (noise * column_scale[None] / MODEL_DIM ** 0.5).astype(jnp.bfloat16)


def draw_unembed(key, part):
    key = jax.random.fold_in(key, 13)
    column_place = jnp.arange(VOCAB, dtype=jnp.float32) / (VOCAB - 1)
    noise = jax.random.normal(key, (MODEL_DIM, VOCAB), jnp.float32)
    ramp = 1.0 + 2.0 * column_place
    return (noise * ramp[None, :] / MODEL_DIM ** 0.5).astype(jnp.bfloat16)


def touch_ends(entries, key, least, top_value):
    dims = entries.shape
    spot = [jax.random.randint(jax.random.fold_in(key, axis), (), 0, dims[axis]) for axis in range(len(dims))]
    entries = entries.at[tuple(spot)].set(least)
    longest = dims.index(max(dims))
    spot[longest] = (spot[longest] + 1) % dims[longest]
    return entries.at[tuple(spot)].set(top_value)


def level_of(own_key, dims, split, least, high):
    gain = 1.0
    for axis_at, blocks in split:
        heights = jax.random.uniform(jax.random.fold_in(jax.random.fold_in(own_key, 6), axis_at), (blocks,), jnp.float32, least / len(split), high / len(split))
        gain = gain * jnp.repeat(jnp.exp(heights), dims[axis_at] // blocks).reshape((-1,) + (1,) * (len(dims) - 1 - axis_at))
    return gain


def rank_table(amount, slope):
    weights = [(1 << 20) // math.isqrt(rank ** slope) + 1 for rank in range(1, amount + 1)]
    scale = 1 + sum(weights) // (1 << 30)
    return np.cumsum(np.array([max(1, weight // scale) for weight in weights]))


def ranked_ids(stream_key, extent, number_of, skew):
    grid = rank_table(number_of, skew)
    lot = jax.random.randint(jax.random.fold_in(stream_key, 1), extent, 0, int(grid[number_of - 1]))
    rank = jnp.searchsorted(jnp.asarray(grid, jnp.int32), lot, side="right")
    return jax.random.permutation(jax.random.fold_in(stream_key, 2), number_of)[rank].astype(jnp.int32)


def gaussian(own_key, dims, width, limit, split=(), held_as=jnp.bfloat16):
    values = jax.random.normal(own_key, dims, jnp.float32) * width
    if len(split) > 0:
        values = level_of(own_key, dims, split, -0.22, 0.18) * values
    return jnp.clip(values, min=-limit, max=limit).astype(held_as)


def setup_inputs(seed: int = 0) -> dict:
    key_of = jax.random.split(jax.random.key(seed), 18)
    inputs = gaussian(key_of[0], (TOKENS, MODEL_DIM), 1.0, 6.0, ((0, 8),))
    targets = touch_ends(ranked_ids(key_of[1], (TOKENS,), VOCAB, 2), jax.random.fold_in(key_of[1], 3), 0, VOCAB - 1).astype(jnp.int32)
    lengths = draw_lengths(jax.random.fold_in(key_of[17], 71), 0)
    norm_gain_vectors = jnp.clip(1.0 + 0.1 * jax.random.normal(key_of[3], (3, MODEL_DIM), jnp.float32), 0.5, 1.5)
    query_key_value_weight = draw_query_key_value_weight(jax.random.fold_in(key_of[17], 71), 0)
    attention_output_weight = gaussian(key_of[5], (MODEL_DIM, MODEL_DIM), 8 ** -0.5, 2.0, ((0, 4),))
    feedforward_input_weight = gaussian(key_of[6], (MODEL_DIM, FF), MODEL_DIM ** -0.5, 0.1875, ((1, 4),))
    feedforward_output_weight = gaussian(key_of[7], (FF, MODEL_DIM), FF ** -0.5, 0.09375, ((0, 4),))
    unembed = draw_unembed(jax.random.fold_in(key_of[17], 71), 0)
    adapter_down_maps = gaussian(key_of[9], (4, MODEL_DIM, ADAPTER_RANKS), MODEL_DIM ** -0.5, 0.1875, ((1, 4), (2, 8)), jnp.float32)
    adapter_up_maps = gaussian(key_of[10], (4, ADAPTER_RANKS, MODEL_DIM), ADAPTER_RANKS ** -0.5, 0.5, ((1, 8), (2, 4)), jnp.float32)
    down_first_moment = gaussian(key_of[11], (4, MODEL_DIM, ADAPTER_RANKS), (0.11 * 0.05 / (8 * MODEL_DIM * ADAPTER_RANKS) ** 0.5), 3.0517578125e-05, ((1, 4), (2, 8)), jnp.float32)
    up_first_moment = gaussian(key_of[12], (4, ADAPTER_RANKS, MODEL_DIM), (0.11 * 0.05 / (8 * MODEL_DIM * ADAPTER_RANKS) ** 0.5), 3.0517578125e-05, ((1, 8), (2, 4)), jnp.float32)
    down_second_moment = jnp.clip(jnp.exp(math.log(9.632110387070014e-11) - 1.3862944 * jax.random.uniform(key_of[13], (4, MODEL_DIM, ADAPTER_RANKS), jnp.float32) ** level_of(key_of[13], (4, MODEL_DIM, ADAPTER_RANKS), ((1, 4), (2, 8)), -0.2, 0.2)), 2.4080275967675036e-11, 9.632110387070014e-11)
    up_second_moment = jnp.clip(jnp.exp(math.log(9.632110387070014e-11) - 1.3862944 * jax.random.uniform(key_of[14], (4, ADAPTER_RANKS, MODEL_DIM), jnp.float32) ** level_of(key_of[14], (4, ADAPTER_RANKS, MODEL_DIM), ((1, 8), (2, 4)), -0.2, 0.2)), 2.4080275967675036e-11, 9.632110387070014e-11)
    target_gradient_sketches = gaussian(key_of[15], (CKPTS, 8, SK, SK), 1.0, 6.0, ((2, 4),), jnp.float32)
    seeds = touch_ends(jax.random.randint(key_of[16], (8,), 0, 100000), jax.random.fold_in(key_of[16], 1), 0, 99999).astype(jnp.int32)
    return dict(inputs=inputs, targets=targets, lengths=lengths, norm_gain_vectors=norm_gain_vectors, query_key_value_weight=query_key_value_weight, attention_output_weight=attention_output_weight, feedforward_input_weight=feedforward_input_weight, feedforward_output_weight=feedforward_output_weight, unembed=unembed, adapter_down_maps=adapter_down_maps, adapter_up_maps=adapter_up_maps, down_first_moment=down_first_moment, up_first_moment=up_first_moment, down_second_moment=down_second_moment, up_second_moment=up_second_moment, target_gradient_sketches=target_gradient_sketches, seeds=seeds)


@jax.custom_vjp
def reduced_precision(v):
    return lax.optimization_barrier(v.astype(jnp.bfloat16)).astype(jnp.float32)

@jax.custom_vjp
def reduced_backward(v):
    return v

def low_keep(v):
    return (reduced_precision(v), None)

def low_pass(kept, grad):
    return (grad,)

def back_keep(v):
    return (v, None)

def back_low(kept, grad):
    return (reduced_precision(grad),)
reduced_precision.defvjp(low_keep, low_pass)
reduced_backward.defvjp(back_keep, back_low)
EPS_NORM = 1e-05
ADAPTER_SCALE = 0.25
CLIP_NORM = 0.05
LEARN_RATE = 0.05
BETA_ONE = 0.9
BETA_TWO = 0.99
ADAM_EPS = 1e-08
WEIGHT_DECAY = 0.01
highest_precision = lax.Precision.HIGHEST

def layer_norm(in_value, in_gain):
    center = in_value - lax.optimization_barrier(jnp.mean(in_value, axis=-1, keepdims=True))
    spread = lax.optimization_barrier(jnp.mean(center * center, axis=-1, keepdims=True))
    return center * lax.rsqrt(spread + EPS_NORM) * in_gain

def rotary_tables(row_count, rot_width):
    half_rot = rot_width // 2
    positions = jnp.arange(row_count, dtype=jnp.float32)
    inv_freq = jnp.exp(jnp.arange(half_rot, dtype=jnp.float32) * (-2.0 * math.log(10000.0) / rot_width))
    angles = positions[:, None] * inv_freq[None, :]
    return (jnp.cos(angles), jnp.sin(angles))

def rotary(in_value, cosine, sine_tab):
    half_rot = cosine.shape[-1]
    first_half = in_value[..., :half_rot]
    second_half = in_value[..., half_rot:2 * half_rot]
    cos_rows = cosine[:, None, :]
    sin_rows = sine_tab[:, None, :]
    return jnp.concatenate([first_half * cos_rows - second_half * sin_rows, second_half * cos_rows + first_half * sin_rows, in_value[..., 2 * half_rot:]], axis=-1)

def sign_table(row_start, row_count, col_start, col_count, seed_value):
    row_ids = (jnp.arange(row_count, dtype=jnp.int32) + row_start)[:, None]
    col_ids = (jnp.arange(col_count, dtype=jnp.int32) + col_start)[None, :]
    hashed = row_ids * 1640531527 + col_ids * 747796405 + seed_value * 277803737
    hashed = hashed ^ hashed >> 15 & 131071
    hashed = hashed * 2024237689
    hashed = hashed ^ hashed >> 13 & 524287
    bit_value = hashed >> 17 & 1
    return 1.0 - 2.0 * bit_value.astype(jnp.float32)

def project(matrix, seed_value, col_start, col_count, sketch_width):
    left_table = sign_table(0, matrix.shape[0], col_start, col_count, 2 * seed_value)
    right_table = sign_table(0, matrix.shape[1], 0, sketch_width, 2 * seed_value + 1)
    inner = jnp.dot(left_table.T, matrix, precision=highest_precision)
    return jnp.dot(inner, right_table, precision=highest_precision)

def sequence_loss(adapter_params, frozen, data):
    adapter_down_maps, adapter_up_maps = adapter_params
    norm_gain_vectors, query_key_value_weight, attention_output_weight, feedforward_input_weight, feedforward_output_weight, unembed = frozen
    residual_stream, targets, length, token_total = data
    head_count = MODEL_DIM // HEAD
    down_reduced = reduced_precision(adapter_down_maps)
    up_reduced = reduced_precision(adapter_up_maps)
    h_attn = reduced_precision(layer_norm(residual_stream, norm_gain_vectors[0]))
    h_mlp = reduced_precision(layer_norm(residual_stream, norm_gain_vectors[1]))
    frozen_projection = jnp.dot(h_attn, query_key_value_weight.reshape(MODEL_DIM, 3 * MODEL_DIM), precision=highest_precision).reshape(LEN, 3, MODEL_DIM)
    rank_input = reduced_backward(reduced_precision(jnp.einsum('nd,kdr->nkr', h_attn, down_reduced[:3], precision=highest_precision)))
    before_rotation = reduced_backward(frozen_projection + ADAPTER_SCALE * jnp.einsum('yau,auq->yaq', rank_input, up_reduced[:3], precision=highest_precision))
    cosine, sine_tab = rotary_tables(LEN, ROT)
    queries = reduced_precision(rotary(before_rotation[:, 0].reshape(LEN, head_count, HEAD), cosine, sine_tab))
    key_rows = reduced_precision(rotary(before_rotation[:, 1].reshape(LEN, head_count, HEAD), cosine, sine_tab))
    values = reduced_precision(before_rotation[:, 2].reshape(LEN, head_count, HEAD))
    scores = reduced_backward(jnp.einsum('qhd,khd->hqk', queries, key_rows, precision=highest_precision) * HEAD ** (-0.5))
    causal = jnp.arange(LEN)[:, None] >= jnp.arange(LEN)[None, :]
    weights = reduced_precision(jax.nn.softmax(jnp.where(causal[None], scores, -1e+30), axis=-1))
    attention_output = reduced_backward(reduced_precision(jnp.einsum('hqk,khd->qhd', weights, values, precision=highest_precision).reshape(LEN, MODEL_DIM)))
    rank_output = reduced_backward(reduced_precision(jnp.dot(attention_output, down_reduced[3], precision=highest_precision)))
    adapter_branch = reduced_backward(jnp.dot(attention_output, attention_output_weight, precision=highest_precision) + ADAPTER_SCALE * jnp.dot(rank_output, up_reduced[3], precision=highest_precision))
    hidden = reduced_precision(jax.nn.gelu(jnp.dot(h_mlp, feedforward_input_weight, precision=highest_precision), approximate=False))
    residual = residual_stream + adapter_branch + jnp.dot(hidden, feedforward_output_weight, precision=highest_precision)
    normed = reduced_precision(layer_norm(residual, norm_gain_vectors[2]))
    valid_mask = (jnp.arange(LEN) < length).astype(jnp.float32)
    block_rows = min(512, LEN)
    block_count = LEN // block_rows

    def block_loss(block_args):
        normed_block, target_block, mask_block = block_args
        logits = reduced_backward(jnp.dot(normed_block, unembed, precision=highest_precision))
        log_norm = jax.nn.logsumexp(logits, axis=-1)
        picked = jnp.take_along_axis(logits, target_block[:, None], axis=-1)[:, 0]
        return jnp.sum((log_norm - picked) * mask_block)
    block_sums = lax.map(jax.checkpoint(block_loss), (normed.reshape(block_count, block_rows, MODEL_DIM), targets.reshape(block_count, block_rows), valid_mask.reshape(block_count, block_rows)))
    loss_sum = jnp.sum(block_sums)
    return (loss_sum / token_total, loss_sum)

def sketch(grad_down, grad_up, seeds):
    matrices = [grad_down[0], grad_down[1], grad_down[2], grad_down[3], grad_up[0].T, grad_up[1].T, grad_up[2].T, grad_up[3].T]
    return jnp.stack([project(matrices[matrix_index], seeds[matrix_index], 0, SK, SK) for matrix_index in range(8)])

def optimizer_step(weight, grad_in, first_in, second_in, clipping_scale):
    grad_clip = grad_in * clipping_scale
    first_new = BETA_ONE * first_in + (1.0 - BETA_ONE) * grad_clip
    second_new = BETA_TWO * second_in + (1.0 - BETA_TWO) * grad_clip * grad_clip
    first_hat = first_new / (1.0 - BETA_ONE ** STEP)
    second_hat = second_new / (1.0 - BETA_TWO ** STEP)
    new_weight = weight - LEARN_RATE * (first_hat / (jnp.sqrt(second_hat) + ADAM_EPS) + WEIGHT_DECAY * weight)
    return (new_weight, first_new, second_new)

def reference(inputs, targets, lengths, norm_gain_vectors, query_key_value_weight, attention_output_weight, feedforward_input_weight, feedforward_output_weight, unembed, adapter_down_maps, adapter_up_maps, down_first_moment, up_first_moment, down_second_moment, up_second_moment, target_gradient_sketches, seeds):
    frozen = (norm_gain_vectors, query_key_value_weight.astype(jnp.float32), attention_output_weight.astype(jnp.float32), feedforward_input_weight.astype(jnp.float32), feedforward_output_weight.astype(jnp.float32), unembed.astype(jnp.float32))
    token_total = jnp.sum(lengths).astype(jnp.float32)
    adapter_params = (adapter_down_maps, adapter_up_maps)
    rates = 1.0 - jnp.arange(CKPTS, dtype=jnp.float32) / CKPTS
    theirs = lax.optimization_barrier(jnp.sum(target_gradient_sketches * target_gradient_sketches, axis=(1, 2, 3)))
    sequence_rows = (inputs.astype(jnp.float32).reshape(SEQS, LEN, MODEL_DIM), targets.reshape(SEQS, LEN), lengths)

    def per_sequence(carry, item):
        residual_stream, target_rows, length = item

        def loss_of(params):
            return sequence_loss(params, frozen, (residual_stream, target_rows, length, token_total))
        mean_part, back_fn, loss_sum = jax.vjp(loss_of, adapter_params, has_aux=True)
        grad_down, grad_up = back_fn(jnp.ones_like(mean_part))[0]
        features = sketch(grad_down * token_total, grad_up * token_total, seeds)
        dot_terms = jnp.einsum('jab,cjab->c', features, target_gradient_sketches, precision=highest_precision)
        own_square = jnp.sum(features * features)
        score = jnp.sum(rates * dot_terms * lax.rsqrt(own_square * theirs + 1e-12))
        return ((carry[0] + grad_down, carry[1] + grad_up), (score, loss_sum))
    initial_carry = (jnp.zeros_like(adapter_down_maps), jnp.zeros_like(adapter_up_maps))
    (down_accumulated, up_accumulated), (influence, losses) = lax.scan(per_sequence, initial_carry, sequence_rows)
    grad_norm = jnp.sqrt(jnp.sum(down_accumulated * down_accumulated) + jnp.sum(up_accumulated * up_accumulated))
    clipping_scale = jnp.minimum(1.0, CLIP_NORM / (grad_norm + 1e-06))
    down_maps_updated, down_first_updated, down_second_updated = optimizer_step(adapter_down_maps, down_accumulated, down_first_moment, down_second_moment, clipping_scale)
    up_maps_updated, up_first_updated, up_second_updated = optimizer_step(adapter_up_maps, up_accumulated, up_first_moment, up_second_moment, clipping_scale)
    loss_parts = jnp.stack([jnp.sum(losses), token_total])
    return (loss_parts, grad_norm[None], influence, down_maps_updated, up_maps_updated, down_first_updated, up_first_updated, down_second_updated, up_second_updated)
```

```python
from functools import partial
import math

import jax
import jax.numpy as jnp
import numpy as np
from jax import lax
from jax.experimental import pallas as pl
from jax.experimental.pallas import tpu as pltpu
from jax.sharding import PartitionSpec as P

HEAD = 64
ROT = 16
STEP = 10

EPS_NORM = 1e-05
ADAPTER_SCALE = 0.25
CLIP_NORM = 0.05
LEARN_RATE = 0.05
BETA_ONE = 0.9
BETA_TWO = 0.99
ADAM_EPS = 1e-08
WEIGHT_DECAY = 0.01

BF = jnp.bfloat16
F32 = jnp.float32
BLOCK = 256
UNIT = 512
TILE_V = 1280
VMEM = 56 * 2**20

PROJ, CORE, YBIT, SEQ, LENGTH = range(5)


def dot_nn(lhs, rhs):
    return lax.dot_general(lhs, rhs, (((1,), (0,)), ((), ())), preferred_element_type=F32)


def dot_nt(lhs, rhs):
    return lax.dot_general(lhs, rhs, (((1,), (1,)), ((), ())), preferred_element_type=F32)


def dot_tn(lhs, rhs):
    return lax.dot_general(lhs, rhs, (((0,), (0,)), ((), ())), preferred_element_type=F32)


def kernel_call(body, name, grid, in_specs, out_specs, out_shape, scratch=(), flops=0, moved=0):
    return pl.pallas_call(
        body,
        grid_spec=pltpu.PrefetchScalarGridSpec(
            num_scalar_prefetch=1,
            grid=grid,
            in_specs=in_specs,
            out_specs=out_specs,
            scratch_shapes=list(scratch),
        ),
        out_shape=out_shape,
        compiler_params=pltpu.CompilerParams(vmem_limit_bytes=VMEM),
        cost_estimate=pl.CostEstimate(flops=flops, bytes_accessed=moved, transcendentals=0),
        name=name,
    )


def whole(shape):
    zeros = (0,) * len(shape)
    return pl.BlockSpec(shape, lambda *_: zeros)


def sds(shape, dtype):
    return jax.ShapeDtypeStruct(shape, dtype)


def normalize(rows):
    center = rows - jnp.mean(rows, axis=-1, keepdims=True)
    spread = jnp.mean(center * center, axis=-1, keepdims=True)
    return center * lax.rsqrt(spread + EPS_NORM)


def columns(index, size):
    return pl.ds(pl.multiple_of(index * size, size), size)


def ffn_body(meta, x_ref, gain_ref, up_ref, down_ref, mine_ref, sib_ref, part_ref):
    hat = normalize(x_ref[...].astype(F32))
    low = (hat * gain_ref[1:2, :]).astype(BF)
    hidden = dot_nn(low, up_ref[...])
    hidden = 0.5 * hidden * (1.0 + lax.erf(hidden * (0.5**0.5)))
    part_ref[...] = dot_nn(hidden.astype(BF), down_ref[...])
    core = meta[CORE]
    mine_ref[0] = part_ref[columns(core, BLOCK), :].astype(BF)
    sib_ref[0] = part_ref[columns(1 - core, BLOCK), :].astype(BF)


def ffn(meta, x, gains, w_up, w_down):
    rows, width = x.shape
    units = rows // UNIT
    half = sds((units, BLOCK, width), BF)
    return kernel_call(
        ffn_body,
        "ffn",
        (units,),
        [
            pl.BlockSpec((UNIT, width), lambda i, m: (i, 0)),
            whole(gains.shape),
            whole(w_up.shape),
            whole(w_down.shape),
        ],
        [pl.BlockSpec((1, BLOCK, width), lambda i, m: (i, 0, 0))] * 2,
        [half, half],
        [pltpu.VMEM((UNIT, width), F32)],
        flops=4 * rows * width * w_up.shape[1],
        moved=4 * w_up.size + 8 * x.size,
    )(meta, x, gains, w_up, w_down)


def qkv_body(meta, x_ref, gain_ref, w_ref, low_ref, out_ref):
    hat = normalize(x_ref[...].astype(F32))
    low = (hat * gain_ref[0:1, :]).astype(BF)
    low_ref[...] = low
    out_ref[...] = dot_nn(low, w_ref[...])


def frozen_qkv(meta, x, gains, w_qkv):
    rows, width = x.shape
    out = w_qkv.shape[1]
    return kernel_call(
        qkv_body,
        "frozen_qkv",
        (rows // UNIT,),
        [
            pl.BlockSpec((UNIT, width), lambda i, m: (i, 0)),
            whole(gains.shape),
            whole(w_qkv.shape),
        ],
        [
            pl.BlockSpec((UNIT, width), lambda i, m: (i, 0)),
            pl.BlockSpec((UNIT, out), lambda i, m: (i, 0)),
        ],
        [sds((rows, width), BF), sds((rows, out), F32)],
        flops=2 * rows * width * out,
        moved=2 * w_qkv.size + 4 * x.size + 4 * rows * out,
    )(meta, x, gains, w_qkv)


def rotary_tables(rows, shard):
    half = ROT // 2
    freq = np.exp(np.arange(half) * (-2.0 * math.log(10000.0) / ROT))
    angles = np.arange(rows)[:, None] * freq[None, :]
    cos, sin = np.cos(angles), np.sin(angles)
    one = np.ones((rows, HEAD))
    one[:, :half] = cos
    one[:, half:ROT] = cos
    up = np.zeros((rows, HEAD))
    up[:, half:ROT] = sin
    down = np.zeros((rows, HEAD))
    down[:, :half] = sin
    heads = shard // HEAD
    return [jnp.asarray(np.tile(table, (1, heads)), F32) for table in (one, up, down)]


def turn(rows, cos, up, down, sign):
    half = ROT // 2
    width = rows.shape[1]
    from_low = pltpu.roll(rows, half, 1)
    from_high = pltpu.roll(rows, width - half, 1)
    return rows * cos + sign * (from_low * up - from_high * down)


def pre_body(
    meta, low_ref, qkv_ref, cos_ref, up_ref, down_ref,
    m_own, m_y, m_sib, m_far, q_ref, k_ref, v_ref, rank_ref,
):
    proj = meta[PROJ]
    shard = q_ref.shape[1]
    rank = m_own.shape[1]
    total = None
    for rel, piece in enumerate((m_own, m_sib, m_y, m_far)):
        low = low_ref[:, columns(proj ^ rel, shard)]
        part = dot_nt(low, piece[0:3].reshape(3 * rank, shard))
        total = part if total is None else total + part
    rank_in = total.astype(BF)
    rank_ref[...] = rank_in
    pre = [
        qkv_ref[:, k * shard : (k + 1) * shard]
        + ADAPTER_SCALE * dot_nn(rank_in[:, k * rank : (k + 1) * rank], m_own[5 + k])
        for k in range(3)
    ]
    tables = (cos_ref[...], up_ref[...], down_ref[...])
    q_ref[...] = turn(pre[0], *tables, 1.0).astype(BF)
    k_ref[...] = turn(pre[1], *tables, 1.0).astype(BF)
    v_ref[...] = pre[2].astype(BF)


def make_qkv(meta, low, qkv, tables, m_own, m_y, m_sib, m_far):
    rows, width = low.shape
    shard = qkv.shape[1] // 3
    rank = m_own.shape[1]
    block = lambda cols: pl.BlockSpec((UNIT, cols), lambda i, m: (i, 0))
    return kernel_call(
        pre_body,
        "adapter_qkv",
        (rows // UNIT,),
        [block(width), block(3 * shard)]
        + [block(shard)] * 3
        + [whole(m_own.shape), whole(m_y.shape), whole(m_sib.shape), whole(m_far.shape)],
        [block(shard)] * 3 + [block(3 * rank)],
        [sds((rows, shard), BF)] * 3 + [sds((rows, 3 * rank), BF)],
        flops=2 * rows * width * 3 * rank,
        moved=rows * (2 * width + 24 * shard),
    )(meta, low, qkv, *tables, m_own, m_y, m_sib, m_far)


def head_mask(shard, head):
    return lax.broadcasted_iota(jnp.int32, (1, shard), 1) // HEAD == head


def diagonal():
    rows = lax.broadcasted_iota(jnp.int32, (BLOCK, BLOCK), 0)
    cols = lax.broadcasted_iota(jnp.int32, (BLOCK, BLOCK), 1)
    return rows >= cols


def block_scores(query, k_ref, prev, causal):
    scale = HEAD**-0.5
    diag = dot_nt(query, k_ref[prev : prev + BLOCK, :]) * scale
    diag = jnp.where(causal, diag, -1e30)
    if prev == 0:
        return diag
    return jnp.concatenate([dot_nt(query, k_ref[0:prev, :]) * scale, diag], axis=1)


def attend_body(unit, meta, q_ref, k_ref, v_ref, mine_ref, sib_ref, lse_ref):
    shard = q_ref.shape[1]
    causal = diagonal()
    lane = lax.broadcasted_iota(jnp.int32, (BLOCK, 128), 1)
    for half in range(UNIT // BLOCK):
        prev = unit * UNIT + half * BLOCK
        query = q_ref[half * BLOCK : (half + 1) * BLOCK, :]
        out = jnp.zeros((BLOCK, shard), F32)
        lse = jnp.zeros((BLOCK, 128), F32)
        for head in range(shard // HEAD):
            mask = head_mask(shard, head)
            scores = block_scores(jnp.where(mask, query, 0), k_ref, prev, causal)
            top = jnp.max(scores, axis=1, keepdims=True)
            prob = jnp.exp(scores - top)
            total = jnp.sum(prob, axis=1, keepdims=True)
            got = dot_nn(prob.astype(BF), v_ref[0 : prev + BLOCK, :]) / total
            out = jnp.where(mask, got, out)
            lse = jnp.where(lane == head, top + jnp.log(total), lse)
        lse_ref[half * BLOCK : (half + 1) * BLOCK, :] = lse
        low = out.astype(BF)

        @pl.when(meta[CORE] == half)
        def _():
            mine_ref[...] = low

        @pl.when(meta[CORE] != half)
        def _():
            sib_ref[...] = low


def attend(meta, unit, queries, keys, values):
    shard = queries.shape[1]
    known = (unit + 1) * UNIT
    return kernel_call(
        partial(attend_body, unit),
        f"attend_{unit}",
        (1,),
        [
            pl.BlockSpec((UNIT, shard), lambda i, m: (unit, 0)),
            pl.BlockSpec((known, shard), lambda i, m: (0, 0)),
            pl.BlockSpec((known, shard), lambda i, m: (0, 0)),
        ],
        [whole((BLOCK, shard)), whole((BLOCK, shard)), whole((UNIT, 128))],
        [sds((BLOCK, shard), BF)] * 2 + [sds((UNIT, 128), F32)],
        flops=16 * UNIT * known * shard,
        moved=8 * known * shard,
    )(meta, queries, keys, values)


def attend_back_body(unit, meta, *refs):
    shard = refs[4].shape[1]
    if unit == 0:
        (g0, g1, g2, g3, q_ref, k_ref, v_ref, lse_ref, cos_ref, up_ref, down_ref,
         dq_ref, dk_ref, dv_ref, grad_ref) = refs
        dk_ref[...] = jnp.zeros_like(dk_ref)
        dv_ref[...] = jnp.zeros_like(dv_ref)
    else:
        (g0, g1, g2, g3, q_ref, k_ref, v_ref, lse_ref, cos_ref, up_ref, down_ref,
         dk_in, dv_in, dq_ref, dk_ref, dv_ref, grad_ref) = refs
        dk_ref[...] = dk_in[...]
        dv_ref[...] = dv_in[...]
    core, ybit = meta[CORE], meta[YBIT]
    quarter = BLOCK // 2
    for rel, piece in enumerate((g0, g1, g2, g3)):
        place = (core ^ (rel & 1)) * 2 + (ybit ^ (rel >> 1))
        grad_ref[columns(place, quarter), :] = piece[...]
    causal = diagonal()
    lane = lax.broadcasted_iota(jnp.int32, (BLOCK, 128), 1)
    scale = HEAD**-0.5
    for half in range(UNIT // BLOCK):
        prev = unit * UNIT + half * BLOCK
        known = prev + BLOCK
        here = slice(half * BLOCK, (half + 1) * BLOCK)
        query = q_ref[here, :]
        grad = grad_ref[here, :]
        lse = lse_ref[here, :]
        dq = jnp.zeros((BLOCK, shard), F32)
        for head in range(shard // HEAD):
            mask = head_mask(shard, head)
            own_q = jnp.where(mask, query, 0)
            own_g = jnp.where(mask, grad, 0)
            own_lse = jnp.sum(jnp.where(lane == head, lse, 0.0), axis=1, keepdims=True)
            prob = jnp.exp(block_scores(own_q, k_ref, prev, causal) - own_lse)
            dweights = dot_nt(own_g, v_ref[0:known, :])
            delta = jnp.sum(prob * dweights, axis=1, keepdims=True)
            dscores = (prob * (dweights - delta)).astype(BF)
            dq = dq + jnp.where(mask, dot_nn(dscores, k_ref[0:known, :]), 0.0)
            dk_ref[0:known, :] += dot_tn(dscores, own_q) * scale
            dv_ref[0:known, :] += dot_tn(prob.astype(BF), own_g)
        dq = turn(dq * scale, cos_ref[here, :], up_ref[here, :], down_ref[here, :], -1.0)
        dq_ref[here, :] = dq.astype(BF)


def attend_back(meta, unit, grads, queries, keys, values, lse, tables, before):
    rows, shard = queries.shape
    known = (unit + 1) * UNIT
    unit_rows = pl.BlockSpec((UNIT, shard), lambda i, m: (unit, 0))
    past = pl.BlockSpec((known, shard), lambda i, m: (0, 0))
    quarter = whole((BLOCK // 2, shard))
    sums = whole((rows, shard))
    return kernel_call(
        partial(attend_back_body, unit),
        f"attend_back_{unit}",
        (1,),
        [quarter] * 4
        + [unit_rows, past, past, whole((UNIT, 128))]
        + [unit_rows] * 3
        + [sums] * len(before),
        [whole((UNIT, shard)), sums, sums],
        [sds((UNIT, shard), BF), sds((rows, shard), F32), sds((rows, shard), F32)],
        [pltpu.VMEM((UNIT, shard), BF)],
        flops=40 * UNIT * known * shard,
        moved=16 * rows * shard,
    )(meta, *grads, queries, keys, values, lse, *tables, *before)


def mix_body(
    meta, x_ref, gain_ref, f_own, f_far, a0, a1, a2, a3, w0, w1, w2, w3,
    m0, m1, m2, m3, norm_ref, res_ref, rank_ref, keep_ref,
):
    proj = meta[PROJ]
    shard = a0.shape[1]
    rank = None
    for a_ref, m_ref in ((a0, m0), (a1, m1), (a2, m2), (a3, m3)):
        part = dot_nt(a_ref[...], m_ref[0])
        rank = part if rank is None else rank + part
    rank = rank.astype(BF)
    total = x_ref[...].astype(F32) + f_own[0].astype(F32) + f_far[...].astype(F32)
    for a_ref, w_ref in ((a0, w0), (a1, w1), (a2, w2), (a3, w3)):
        total = total + dot_nn(a_ref[...], w_ref[...])
    keep_ref[...] = total
    for rel, m_ref in enumerate((m0, m1, m2, m3)):
        here = columns(proj ^ rel, shard)
        keep_ref[:, here] += ADAPTER_SCALE * dot_nn(rank, m_ref[1])
    residual = keep_ref[...]
    norm_ref[...] = (normalize(residual) * gain_ref[2:3, :]).astype(BF)
    mine = columns(meta[YBIT], BLOCK // 2)
    res_ref[...] = keep_ref[mine, :]
    keep_ref[:, 0 : rank.shape[1]] = rank.astype(F32)
    rank_ref[...] = keep_ref[mine, 0 : rank.shape[1]].astype(BF)


def mix(meta, unit, x, gains, f_own, f_far, att, wo, maps):
    rows, width = x.shape
    shard = att[0].shape[1]
    rank = maps[0].shape[1]
    return kernel_call(
        mix_body,
        f"mix_{unit}",
        (1,),
        [
            pl.BlockSpec((BLOCK, width), lambda i, m: (2 * unit + m[CORE], 0)),
            whole(gains.shape),
            pl.BlockSpec((1, BLOCK, width), lambda i, m: (unit, 0, 0)),
            whole((BLOCK, width)),
        ]
        + [whole((BLOCK, shard))] * 4
        + [whole((shard, width))] * 4
        + [whole((2, rank, shard))] * 4,
        [whole((BLOCK, width)), whole((BLOCK // 2, width)), whole((BLOCK // 2, rank))],
        [sds((BLOCK, width), BF), sds((BLOCK // 2, width), F32), sds((BLOCK // 2, rank), BF)],
        [pltpu.VMEM((BLOCK, width), F32)],
        flops=2 * BLOCK * width * width,
        moved=2 * width * width + 8 * BLOCK * width,
    )(meta, x, gains, f_own, f_far, *att, *wo, *maps)


def vocab_grid(vocab):
    steps = -(-vocab // TILE_V)
    return steps, vocab - (steps - 1) * TILE_V


def vocab_stats_body(vocab, meta, mine_ref, sib_ref, u_ref, tm_ref, ts_ref, p_ref, top_ref, st_ref, acc_ref):
    step = pl.program_id(0)
    steps, tail = vocab_grid(vocab)

    @pl.when(step == 0)
    def _():
        acc_ref[...] = jnp.zeros_like(acc_ref)

    def tile(is_tail):
        col = lax.broadcasted_iota(jnp.int32, (BLOCK, TILE_V), 1)
        lane = lax.broadcasted_iota(jnp.int32, (BLOCK, 128), 1)
        for half, (rows_ref, target_ref) in enumerate(((mine_ref, tm_ref), (sib_ref, ts_ref))):
            here = slice(half * BLOCK, (half + 1) * BLOCK)
            logits = dot_nn(rows_ref[...], u_ref[...])
            if is_tail:
                logits = jnp.where(col < tail, logits, -1e30)
            top = jnp.max(logits, axis=1, keepdims=True)
            prob = jnp.exp(logits - top)
            total = jnp.sum(prob, axis=1, keepdims=True)
            hit = col == target_ref[...] - step * TILE_V
            picked = jnp.sum(jnp.where(hit, logits, 0.0), axis=1, keepdims=True)
            p_ref[here, :] = prob.astype(BF)
            acc = acc_ref[here, :]
            acc = jnp.where(lane == step, top, acc)
            acc = jnp.where(lane == step + 32, total, acc)
            acc_ref[here, :] = jnp.where(lane == 64, acc + picked, acc)

    @pl.when(step < steps - 1)
    def _():
        tile(False)

    @pl.when(step == steps - 1)
    def _():
        tile(True)
        acc = acc_ref[...]
        lane = lax.broadcasted_iota(jnp.int32, acc.shape, 1)
        top_ref[...] = acc
        tops = jnp.where(lane < steps, acc, -1e30)
        best = jnp.max(tops, axis=1, keepdims=True)
        totals = pltpu.roll(acc, 128 - 32, 1)
        total = jnp.sum(
            jnp.where(lane < steps, totals * jnp.exp(tops - best), 0.0), axis=1, keepdims=True
        )
        picked = jnp.sum(jnp.where(lane == 64, acc, 0.0), axis=1, keepdims=True)
        pair = jnp.where(lane == 0, best + jnp.log(total), jnp.where(lane == 1, picked, 0.0))
        st_ref[...] = jnp.transpose(pair)[0:8, :]


def vocab_stats(meta, unit, mine, sib, unembed, targets):
    width, vocab = unembed.shape
    steps, _ = vocab_grid(vocab)
    rows = 2 * BLOCK
    return kernel_call(
        partial(vocab_stats_body, vocab),
        f"vocab_stats_{unit}",
        (steps,),
        [
            whole((BLOCK, width)),
            whole((BLOCK, width)),
            pl.BlockSpec((width, TILE_V), lambda i, m: (0, i)),
            pl.BlockSpec((BLOCK, 1), lambda i, m: (2 * unit + m[CORE], 0)),
            pl.BlockSpec((BLOCK, 1), lambda i, m: (2 * unit + 1 - m[CORE], 0)),
        ],
        [pl.BlockSpec((rows, TILE_V), lambda i, m: (0, i)), whole((rows, 128)), whole((8, rows))],
        [
            sds((rows, steps * TILE_V), BF),
            sds((rows, 128), F32),
            sds((8, rows), F32),
        ],
        [pltpu.VMEM((rows, 128), F32)],
        flops=2 * rows * width * vocab,
        moved=2 * width * vocab + 2 * rows * vocab,
    )(meta, mine, sib, unembed, targets, targets)


def swap_halves(pair):
    return jnp.concatenate([pair[:, BLOCK:], pair[:, :BLOCK]], axis=1)


def vocab_back_body(
    vocab, unit, meta, count_ref, p_ref, u_ref, tm_ref, ts_ref, top_ref, s0, s1, s2, s3,
    mine_ref, sib_ref, loss_ref, scale_ref, acc_ref,
):
    step = pl.program_id(0)
    steps, tail = vocab_grid(vocab)
    rows = 2 * BLOCK

    @pl.when(step == 0)
    def _():
        acc_ref[...] = jnp.zeros_like(acc_ref)
        parts = [s0[...], swap_halves(s1[...]), s2[...], swap_halves(s3[...])]
        lses = [part[0:1, :] for part in parts]
        best = jnp.maximum(jnp.maximum(lses[0], lses[1]), jnp.maximum(lses[2], lses[3]))
        total = sum(jnp.exp(one - best) for one in lses)
        log_norm = best + jnp.log(total)
        picked = sum(part[1:2, :] for part in parts)
        place = lax.broadcasted_iota(jnp.int32, (1, rows), 1)
        core = meta[CORE]
        offset = jnp.where(place < BLOCK, core * BLOCK, (1 - core) * BLOCK - BLOCK)
        valid = (unit * UNIT + place + offset < meta[LENGTH]).astype(F32)
        loss_ref[...] = jnp.broadcast_to(
            jnp.sum((log_norm - picked) * valid, axis=1, keepdims=True), (8, 128)
        )
        weight = valid / count_ref[0, 0]
        row = lax.broadcasted_iota(jnp.int32, (128, rows), 0)
        lines = jnp.where(row == 0, log_norm, 0.0)
        lines = jnp.where(row == 1, weight, lines)
        lines = jnp.where(row == 2, (jnp.exp(picked - log_norm) - 1.0) * weight, lines)
        cols = jnp.transpose(lines)
        lane = lax.broadcasted_iota(jnp.int32, (rows, 128), 1)
        take = lambda k: jnp.sum(jnp.where(lane == k, cols, 0.0), axis=1, keepdims=True)
        tops = jnp.where(lane < steps, top_ref[...], -1e30)
        scales = jnp.exp(tops - take(0)) * take(1)
        scale_ref[...] = jnp.where(lane == 64, take(2), scales)

    def tile(is_tail):
        u_tile = u_ref[...]
        if is_tail:
            col = lax.broadcasted_iota(jnp.int32, u_tile.shape, 1)
            u_tile = jnp.where(col < tail, u_tile, jnp.zeros_like(u_tile))
        col = lax.broadcasted_iota(jnp.int32, (BLOCK, TILE_V), 1)
        lane = lax.broadcasted_iota(jnp.int32, (BLOCK, 128), 1)
        for half, target_ref in enumerate((tm_ref, ts_ref)):
            here = slice(half * BLOCK, (half + 1) * BLOCK)
            scales = scale_ref[here, :]
            scale = jnp.sum(jnp.where(lane == step, scales, 0.0), axis=1, keepdims=True)
            at_hit = jnp.sum(jnp.where(lane == 64, scales, 0.0), axis=1, keepdims=True)
            hit = col == target_ref[...] - step * TILE_V
            grad = jnp.where(hit, at_hit, p_ref[here, :].astype(F32) * scale).astype(BF)
            acc_ref[here, :] += dot_nt(grad, u_tile)

    @pl.when(step < steps - 1)
    def _():
        tile(False)

    @pl.when(step == steps - 1)
    def _():
        tile(True)
        mine_ref[...] = acc_ref[0:BLOCK, :].astype(BF)
        sib_ref[...] = acc_ref[BLOCK:, :].astype(BF)


def vocab_back(meta, unit, count, prob, unembed, targets, tops, stats):
    width, vocab = unembed.shape
    steps, _ = vocab_grid(vocab)
    rows = 2 * BLOCK
    return kernel_call(
        partial(vocab_back_body, vocab, unit),
        f"vocab_back_{unit}",
        (steps,),
        [
            whole((1, 1)),
            pl.BlockSpec((rows, TILE_V), lambda i, m: (0, i)),
            pl.BlockSpec((width, TILE_V), lambda i, m: (0, i)),
            pl.BlockSpec((BLOCK, 1), lambda i, m: (2 * unit + m[CORE], 0)),
            pl.BlockSpec((BLOCK, 1), lambda i, m: (2 * unit + 1 - m[CORE], 0)),
            whole((rows, 128)),
        ]
        + [whole((8, rows))] * 4,
        [whole((BLOCK, width)), whole((BLOCK, width)), whole((8, 128))],
        [sds((BLOCK, width), BF), sds((BLOCK, width), BF), sds((8, 128), F32)],
        [pltpu.VMEM((rows, 128), F32), pltpu.VMEM((rows, width), F32)],
        flops=2 * rows * width * vocab,
        moved=2 * width * vocab + 2 * rows * vocab,
    )(meta, count, prob, unembed, targets, targets, tops, *stats)


def split_body(meta, own_ref, got_ref, keep_ref, send_ref, sum_ref):
    sum_ref[...] = own_ref[...].astype(F32) + got_ref[...].astype(F32)
    ybit = meta[YBIT]
    keep_ref[...] = sum_ref[columns(ybit, BLOCK // 2), :]
    send_ref[...] = sum_ref[columns(1 - ybit, BLOCK // 2), :].astype(BF)


def split_sum(meta, unit, own, got):
    rows, width = own.shape
    return kernel_call(
        split_body,
        f"split_sum_{unit}",
        (1,),
        [whole(own.shape), whole(got.shape)],
        [whole((rows // 2, width))] * 2,
        [sds((rows // 2, width), F32), sds((rows // 2, width), BF)],
        [pltpu.VMEM((rows, width), F32)],
        flops=own.size,
        moved=8 * own.size,
    )(meta, own, got)


def norm_back_body(last, meta, *refs):
    (keep_ref, got_ref, res_ref, gain_ref, rank_ref) = refs[:5]
    atts, wos, maps = refs[5:9], refs[9:13], refs[13:17]
    if last:
        before_ref = refs[17]
        outs, (hold_ref,) = refs[18:24], refs[24:]
    else:
        outs, (hold_ref,) = refs[17:22], refs[22:]
    proj = meta[PROJ]
    shard = atts[0].shape[1]
    dnormed = keep_ref[...] + got_ref[...].astype(F32)
    residual = res_ref[...]
    center = residual - jnp.mean(residual, axis=-1, keepdims=True)
    spread = jnp.mean(center * center, axis=-1, keepdims=True)
    inv = lax.rsqrt(spread + EPS_NORM)
    hat = center * inv
    dhat = dnormed * gain_ref[2:3, :]
    dres = inv * (
        dhat
        - jnp.mean(dhat, axis=-1, keepdims=True)
        - hat * jnp.mean(dhat * hat, axis=-1, keepdims=True)
    )
    hold_ref[...] = dres.astype(BF)
    dbranch = hold_ref[...]
    drank = None
    for rel, m_ref in enumerate(maps):
        part = dot_nt(hold_ref[:, columns(proj ^ rel, shard)], m_ref[1])
        drank = part if drank is None else drank + part
    drank = (ADAPTER_SCALE * drank).astype(BF)
    for rel in range(4):
        datt = dot_nt(dbranch, wos[rel][...]) + dot_nn(drank, maps[rel][0])
        outs[rel][...] = datt.astype(BF)
        g_down = dot_tn(drank, atts[rel][...])
        g_up = ADAPTER_SCALE * dot_tn(rank_ref[...], hold_ref[:, columns(proj ^ rel, shard)])
        if last:
            dest = outs[4 + (rel & 1)]
            dest[rel >> 1, 0] = (before_ref[rel, 0] + g_down).astype(BF)
            dest[rel >> 1, 1] = (before_ref[rel, 1] + g_up).astype(BF)
        else:
            outs[4][rel, 0] = g_down
            outs[4][rel, 1] = g_up


def norm_back(meta, unit, last, keep, got, residual, gains, rank_out, att, wo, maps, before):
    quarter, width = keep.shape
    shard = att[0].shape[1]
    rank = rank_out.shape[1]
    if last:
        more_specs = [whole((2, 2, rank, shard))] * 2
        more_shapes = [sds((2, 2, rank, shard), BF)] * 2
    else:
        more_specs = [whole((4, 2, rank, shard))]
        more_shapes = [sds((4, 2, rank, shard), F32)]
    return kernel_call(
        partial(norm_back_body, last),
        f"norm_back_{unit}",
        (1,),
        [whole(keep.shape), whole(got.shape), whole(residual.shape), whole(gains.shape), whole(rank_out.shape)]
        + [pl.BlockSpec((quarter, shard), lambda i, m: (m[YBIT], 0))] * 4
        + [whole((shard, width))] * 4
        + [whole((2, rank, shard))] * 4
        + [whole(one.shape) for one in before],
        [whole((quarter, shard))] * 4 + more_specs,
        [sds((quarter, shard), BF)] * 4 + more_shapes,
        [pltpu.VMEM((quarter, width), BF)],
        flops=2 * quarter * width * width,
        moved=2 * width * width + 12 * quarter * width,
    )(meta, keep, got, residual, gains, rank_out, *att, *wo, *maps, *before)


def grads_body(
    meta, dq0, dq1, dk_ref, dv_ref, cos_ref, up_ref, down_ref, rank_ref, m_own, low_ref,
    keep_ref, send_ref, up_grad_ref, drank_ref,
):
    proj = meta[PROJ]
    rank, shard = m_own.shape[1:]
    dk = turn(dk_ref[...], cos_ref[...], up_ref[...], down_ref[...], -1.0).astype(BF)
    dpre = [jnp.concatenate([dq0[...], dq1[...]], axis=0), dk, dv_ref[...].astype(BF)]
    for k in range(3):
        here = slice(k * rank, (k + 1) * rank)
        up_grad_ref[k] = ADAPTER_SCALE * dot_tn(rank_ref[:, here], dpre[k])
        drank_ref[:, here] = (ADAPTER_SCALE * dot_nt(dpre[k], m_own[5 + k])).astype(BF)
    drank = drank_ref[...]
    for rel in range(4):
        grad = dot_tn(drank, low_ref[:, columns(proj ^ rel, shard)])
        dest = (keep_ref, send_ref)[rel & 1]
        dest[rel >> 1] = grad.reshape(3, rank, shard).astype(BF)


def adapter_grads(meta, dqs, dk, dv, tables, rank_in, m_own, low):
    rows, shard = dk.shape
    rank = m_own.shape[1]
    pair = (2, 3, rank, shard)
    args = (*dqs, dk, dv, *tables, rank_in, m_own, low)
    return kernel_call(
        grads_body,
        "adapter_grads",
        (1,),
        [whole(one.shape) for one in args],
        [whole(pair), whole(pair), whole((3, rank, shard))],
        [sds(pair, BF), sds(pair, BF), sds((3, rank, shard), F32)],
        [pltpu.VMEM((rows, 3 * rank), BF)],
        flops=2 * rows * low.shape[1] * 3 * rank,
        moved=30 * rows * shard,
    )(meta, *args)


def signs(row_ids, col_ids, seed):
    hashed = row_ids * 1640531527 + col_ids * 747796405 + seed * 277803737
    hashed = hashed ^ hashed >> 15 & 131071
    hashed = hashed * 2024237689
    hashed = hashed ^ hashed >> 13 & 524287
    return 1.0 - 2.0 * (hashed >> 17 & 1).astype(F32)


def sketch_body(slice_rank, meta, seeds_ref, count_ref, grad_ref, p0, p1, p2, p3, full_ref):
    mats, rank, shard = grad_ref.shape
    sketch = full_ref.shape[1]
    proj = meta[PROJ]
    left_rows = lax.broadcasted_iota(jnp.int32, (sketch, shard), 1) + proj * shard
    left_cols = lax.broadcasted_iota(jnp.int32, (sketch, shard), 0)
    place = lax.broadcasted_iota(jnp.int32, (rank, sketch), 0)
    right_rows = place ^ (meta[SEQ] * slice_rank)
    right_cols = lax.broadcasted_iota(jnp.int32, (rank, sketch), 1)
    for mat in range(mats):
        seed = seeds_ref[mat]
        left = signs(left_rows, left_cols, 2 * seed).astype(BF)
        right = signs(right_rows, right_cols, 2 * seed + 1)
        inner = dot_nt(left, grad_ref[mat])
        full_ref[mat] = count_ref[0, 0] * jnp.dot(inner, right, precision=lax.Precision.HIGHEST)
    size = sketch // 4
    for rel, out_ref in enumerate((p0, p1, p2, p3)):
        out_ref[...] = full_ref[:, columns(proj ^ rel, size), :]


def sketch(meta, slice_rank, seeds, count, grads, sketch_width):
    mats, rank, shard = grads.shape
    piece = (mats, sketch_width // 4, sketch_width)
    return kernel_call(
        partial(sketch_body, slice_rank),
        "sketch",
        (1,),
        [pl.BlockSpec(memory_space=pltpu.SMEM), whole((1, 1)), whole(grads.shape)],
        [whole(piece)] * 4,
        [sds(piece, F32)] * 4,
        [pltpu.VMEM((mats, sketch_width, sketch_width), F32)],
        flops=2 * mats * rank * shard * sketch_width,
        moved=2 * grads.size,
    )(meta, seeds, count, grads)


def optimizer_step(weight, grad_in, first_in, second_in, clipping_scale):
    grad_clip = grad_in * clipping_scale
    first_new = BETA_ONE * first_in + (1.0 - BETA_ONE) * grad_clip
    second_new = BETA_TWO * second_in + (1.0 - BETA_TWO) * grad_clip * grad_clip
    first_hat = first_new / (1.0 - BETA_ONE**STEP)
    second_hat = second_new / (1.0 - BETA_TWO**STEP)
    new_weight = weight - LEARN_RATE * (
        first_hat / (jnp.sqrt(second_hat) + ADAM_EPS) + WEIGHT_DECAY * weight
    )
    return (new_weight, first_new, second_new)


def to_partner(array, axis, size, offset):
    return lax.ppermute(array, axis, [(i, i ^ offset) for i in range(size)])


def on_device(
    seq_count,
    proj_count,
    inputs,
    targets,
    lengths,
    norm_gain_vectors,
    query_key_value_weight,
    attention_output_weight,
    feedforward_input_weight,
    feedforward_output_weight,
    unembed,
    adapter_down_maps,
    adapter_up_maps,
    down_first_moment,
    up_first_moment,
    down_second_moment,
    up_second_moment,
    target_gradient_sketches,
    seeds,
):
    rows, width = inputs.shape
    shard = attention_output_weight.shape[0]
    vocab_local = unembed.shape[1]
    slice_rank = adapter_up_maps.shape[1]
    rank = slice_rank * seq_count
    sketch_width = target_gradient_sketches.shape[3]
    proj = lax.axis_index("proj")
    seq = lax.axis_index("dp")
    units = rows // UNIT

    over_proj = lambda array, rel: to_partner(array, "proj", proj_count, rel)
    over_seq = lambda array, rel: to_partner(array, "dp", seq_count, rel)

    token_total = jnp.sum(lengths).astype(F32)
    count = token_total.reshape(1, 1)
    length = jnp.sum(jnp.where(jnp.arange(seq_count) == seq, lengths, 0))
    zero = jnp.int32(0)
    meta = jnp.stack([proj, proj & 1, proj >> 1, seq, length, zero, zero, zero]).astype(jnp.int32)

    down_rows = jnp.transpose(adapter_down_maps, (0, 2, 1))
    maps = jnp.concatenate(
        [down_rows, adapter_up_maps[3:], adapter_up_maps[:3]], axis=0
    ).astype(BF)
    offset = 1
    while offset < seq_count:
        maps = jnp.concatenate([maps, over_seq(maps, offset)], axis=1)
        offset *= 2

    wo_y = over_proj(attention_output_weight, 2)
    wo_sib = over_proj(attention_output_weight, 1)
    wo_far = over_proj(wo_y, 1)
    wo = (attention_output_weight, wo_sib, wo_y, wo_far)

    f_mine, f_sib = ffn(
        meta, inputs, norm_gain_vectors, feedforward_input_weight, feedforward_output_weight
    )
    f_got = over_proj(f_sib, 1)
    f_chip = f_mine + f_got
    f_far = [over_proj(f_chip[unit], 2) for unit in range(units)]

    low, qkv = frozen_qkv(
        meta, inputs, norm_gain_vectors, query_key_value_weight.reshape(width, 3 * shard)
    )

    down_in = maps[:3]
    down_y = over_proj(down_in, 2)
    down_sib = over_proj(down_in, 1)
    down_far = over_proj(down_y, 1)
    out_maps = maps[3:5]
    out_y = over_proj(out_maps, 2)
    out_sib = over_proj(out_maps, 1)
    out_far = over_proj(out_y, 1)
    outs = (out_maps, out_sib, out_y, out_far)

    tables = rotary_tables(rows, shard)
    queries, keys, values, rank_in = make_qkv(
        meta, low, qkv, tables, maps, down_y, down_sib, down_far
    )

    local_targets = targets - proj * vocab_local
    inside = (local_targets >= 0) & (local_targets < vocab_local)
    target_cols = jnp.where(inside, local_targets, -1).reshape(rows, 1)

    lses, atts, normeds, residuals, ranks = [], [], [], [], []
    for unit in range(units):
        att_mine, att_sib, lse = attend(meta, unit, queries, keys, values)
        lses.append(lse)
        att = (att_mine, over_proj(att_sib, 1), over_proj(att_mine, 2), over_proj(att_sib, 3))
        atts.append(att)
    for unit in range(units):
        normed, residual, rank_out = mix(
            meta, unit, inputs, norm_gain_vectors, f_chip, f_far[unit], atts[unit], wo, outs
        )
        normeds.append((normed, over_proj(normed, 1)))
        residuals.append(residual)
        ranks.append(rank_out)

    probs, tops, stats = [], [], []
    for unit in range(units):
        prob, top, stat = vocab_stats(meta, unit, *normeds[unit], unembed, target_cols)
        probs.append(prob)
        tops.append(top)
        stats.append((stat, over_proj(stat, 1), over_proj(stat, 2), over_proj(stat, 3)))

    losses, dnormed = [], []
    for unit in range(units):
        d_mine, d_sib, loss = vocab_back(
            meta, unit, count, probs[unit], unembed, target_cols, tops[unit], stats[unit]
        )
        losses.append(loss[0, 0])
        keep, send = split_sum(meta, unit, d_mine, over_proj(d_sib, 1))
        dnormed.append((keep, over_proj(send, 2)))

    dqs, out_grads, sums = [], (), ()
    for unit in range(units):
        last = unit == units - 1
        result = norm_back(
            meta, unit, last, *dnormed[unit], residuals[unit], norm_gain_vectors,
            ranks[unit], atts[unit], wo, outs, out_grads,
        )
        out_grads = tuple(result[4:])
        datt = [result[0]] + [over_proj(result[rel], rel) for rel in (1, 2, 3)]
        dq, dk, dv = attend_back(
            meta, unit, datt, queries, keys, values, lses[unit], tables, sums
        )
        dqs.append(dq)
        sums = (dk, dv)

    def reduce_proj(keep, send):
        half = keep.astype(F32) + over_proj(send, 1).astype(F32)
        return half[0] + over_proj(half[1].astype(BF), 2).astype(F32)

    out_total = reduce_proj(*out_grads)
    in_keep, in_send, up_grads = adapter_grads(meta, dqs, *sums, tables, rank_in, maps, low)
    in_total = reduce_proj(in_keep, in_send)

    grads = jnp.concatenate(
        [in_total, out_total[0:1], up_grads, out_total[1:2]], axis=0
    ).astype(BF)
    pieces = sketch(meta, slice_rank, seeds, count, grads, sketch_width)
    features = pieces[0] + over_proj(pieces[1], 1) + over_proj(pieces[2], 2) + over_proj(pieces[3], 3)

    blocks = grads.reshape(8, seq_count, slice_rank, shard)
    blocks = jnp.transpose(blocks, (1, 0, 2, 3))
    blocks = jnp.take(blocks, jnp.arange(seq_count) ^ seq, axis=0)
    arrived = lax.all_to_all(blocks, "dp", split_axis=0, concat_axis=0, tiled=True)
    total = jnp.sum(arrived.astype(F32), axis=0)
    down_total = jnp.transpose(total[:4], (0, 2, 1))
    up_total = total[4:]

    dot_terms = jnp.sum(features[None] * target_gradient_sketches, axis=(1, 2, 3))
    own_square = jnp.sum(features * features)
    theirs = jnp.sum(target_gradient_sketches * target_gradient_sketches, axis=(1, 2, 3))
    loss_local = jnp.where(proj == 0, sum(losses), 0.0)
    line = jnp.concatenate(
        [jnp.stack([jnp.sum(total * total), loss_local, own_square]), dot_terms, theirs]
    )
    line = jnp.pad(line, (0, 128 - line.shape[0]))
    device_count = seq_count * proj_count
    lines = lax.all_to_all(
        jnp.broadcast_to(line, (device_count, 128)), ("dp", "proj"), split_axis=0, concat_axis=0, tiled=True
    )
    everyone = jnp.sum(lines, axis=0)
    group = jnp.arange(device_count) // proj_count == seq
    ours = jnp.sum(jnp.where(group[:, None], lines, 0.0), axis=0)
    checkpoints = dot_terms.shape[0]
    rates = 1.0 - jnp.arange(checkpoints, dtype=F32) / checkpoints
    dots, squares = ours[3 : 3 + checkpoints], ours[3 + checkpoints : 3 + 2 * checkpoints]
    influence = jnp.sum(rates * dots * lax.rsqrt(ours[2] * squares + 1e-12))
    grad_norm = jnp.sqrt(everyone[0])
    clipping_scale = jnp.minimum(1.0, CLIP_NORM / (grad_norm + 1e-06))
    down_new, down_first, down_second = optimizer_step(
        adapter_down_maps, down_total, down_first_moment, down_second_moment, clipping_scale
    )
    up_new, up_first, up_second = optimizer_step(
        adapter_up_maps, up_total, up_first_moment, up_second_moment, clipping_scale
    )
    return (
        jnp.stack([everyone[1], token_total]),
        grad_norm[None],
        influence[None],
        down_new,
        up_new,
        down_first,
        up_first,
        down_second,
        up_second,
    )


def solution(mesh):
    in_specs = (
        P("dp", None),
        P("dp"),
        P(),
        P(),
        P(None, None, "proj"),
        P("proj", None),
        P(None, "proj"),
        P("proj", None),
        P(None, "proj"),
        P(None, "proj", "dp"),
        P(None, "dp", "proj"),
        P(None, "proj", "dp"),
        P(None, "dp", "proj"),
        P(None, "proj", "dp"),
        P(None, "dp", "proj"),
        P(None, None, "proj", None),
        P(),
    )
    out_specs = (
        P(),
        P(),
        P("dp"),
        P(None, "proj", "dp"),
        P(None, "dp", "proj"),
        P(None, "proj", "dp"),
        P(None, "dp", "proj"),
        P(None, "proj", "dp"),
        P(None, "dp", "proj"),
    )
    return jax.shard_map(
        partial(on_device, mesh.shape["dp"], mesh.shape["proj"]),
        mesh=mesh,
        in_specs=in_specs,
        out_specs=out_specs,
        check_vma=False,
    )
```

```python
from functools import partial
import math

import jax
import jax.numpy as jnp
import numpy as np
from jax import lax
from jax.experimental import pallas as pl
from jax.experimental.pallas import tpu as pltpu
from jax.sharding import PartitionSpec as P

HEAD = 64
ROT = 16
STEP = 10

EPS_NORM = 1e-05
ADAPTER_SCALE = 0.25
CLIP_NORM = 0.05
LEARN_RATE = 0.05
BETA_ONE = 0.9
BETA_TWO = 0.99
ADAM_EPS = 1e-08
WEIGHT_DECAY = 0.01

BF = jnp.bfloat16
F32 = jnp.float32
BLOCK = 256
UNIT = 512
TILE_V = 2560
VMEM = 56 * 2**20

PROJ, CORE, YBIT, SEQ, LENGTH = range(5)


def dot_nn(lhs, rhs):
    return lax.dot_general(lhs, rhs, (((1,), (0,)), ((), ())), preferred_element_type=F32)


def dot_nt(lhs, rhs):
    return lax.dot_general(lhs, rhs, (((1,), (1,)), ((), ())), preferred_element_type=F32)


def dot_tn(lhs, rhs):
    return lax.dot_general(lhs, rhs, (((0,), (0,)), ((), ())), preferred_element_type=F32)


def kernel_call(
    body, name, grid, in_specs, out_specs, out_shape, scratch=(), flops=0, moved=0, after=()
):
    inputs = len(in_specs) + 1
    extra = len(after)

    def run(*refs):
        body(*refs[:inputs], *refs[inputs + extra :])

    call = pl.pallas_call(
        run,
        grid_spec=pltpu.PrefetchScalarGridSpec(
            num_scalar_prefetch=1,
            grid=grid,
            in_specs=list(in_specs) + [pl.BlockSpec(memory_space=pl.ANY)] * extra,
            out_specs=out_specs,
            scratch_shapes=list(scratch),
        ),
        out_shape=out_shape,
        compiler_params=pltpu.CompilerParams(vmem_limit_bytes=VMEM),
        cost_estimate=pl.CostEstimate(flops=flops, bytes_accessed=moved, transcendentals=0),
        name=name,
    )
    return lambda *args: call(*args, *after)


def whole(shape):
    zeros = (0,) * len(shape)
    return pl.BlockSpec(shape, lambda *_: zeros)


def sds(shape, dtype):
    return jax.ShapeDtypeStruct(shape, dtype)


def normalize(rows):
    center = rows - jnp.mean(rows, axis=-1, keepdims=True)
    spread = jnp.mean(center * center, axis=-1, keepdims=True)
    return center * lax.rsqrt(spread + EPS_NORM)


def columns(index, size):
    return pl.ds(pl.multiple_of(index * size, size), size)


def ffn_body(meta, x_ref, gain_ref, up_ref, down_ref, mine_ref, sib_ref, low_ref, part_ref):
    step = pl.program_id(0)

    @pl.when(step == 0)
    def _():
        hat = normalize(x_ref[...].astype(F32))
        low_ref[...] = (hat * gain_ref[1:2, :]).astype(BF)
        part_ref[...] = jnp.zeros_like(part_ref)

    hidden = dot_nn(low_ref[...], up_ref[...])
    hidden = 0.5 * hidden * (1.0 + lax.erf(hidden * (0.5**0.5)))
    part_ref[...] += dot_nn(hidden.astype(BF), down_ref[...])

    @pl.when(step == pl.num_programs(0) - 1)
    def _():
        core = meta[CORE]
        mine_ref[...] = part_ref[columns(core, BLOCK), :].astype(BF)
        sib_ref[...] = part_ref[columns(1 - core, BLOCK), :].astype(BF)


def ffn(meta, unit, x, gains, w_up, w_down, after=()):
    rows, width = x.shape
    chunk = 512
    half = sds((BLOCK, width), BF)
    return kernel_call(
        ffn_body,
        f"ffn_{unit}",
        (w_up.shape[1] // chunk,),
        [
            pl.BlockSpec((UNIT, width), lambda i, m: (unit, 0)),
            whole(gains.shape),
            pl.BlockSpec((width, chunk), lambda i, m: (0, i)),
            pl.BlockSpec((chunk, width), lambda i, m: (i, 0)),
        ],
        [whole((BLOCK, width))] * 2,
        [half, half],
        [pltpu.VMEM((UNIT, width), BF), pltpu.VMEM((UNIT, width), F32)],
        flops=4 * UNIT * width * w_up.shape[1],
        moved=4 * w_up.size + 8 * UNIT * width,
        after=after,
    )(meta, x, gains, w_up, w_down)


def qkv_body(meta, x_ref, gain_ref, w_ref, low_ref, out_ref):
    hat = normalize(x_ref[...].astype(F32))
    low = (hat * gain_ref[0:1, :]).astype(BF)
    low_ref[...] = low
    shard = w_ref.shape[2]
    for k in range(3):
        out_ref[:, k * shard : (k + 1) * shard] = dot_nn(low, w_ref[k])


def frozen_qkv(meta, x, gains, w_qkv, after=()):
    rows, width = x.shape
    out = 3 * w_qkv.shape[2]
    return kernel_call(
        qkv_body,
        "frozen_qkv",
        (rows // UNIT,),
        [
            pl.BlockSpec((UNIT, width), lambda i, m: (i, 0)),
            whole(gains.shape),
            whole(w_qkv.shape),
        ],
        [
            pl.BlockSpec((UNIT, width), lambda i, m: (i, 0)),
            pl.BlockSpec((UNIT, out), lambda i, m: (i, 0)),
        ],
        [sds((rows, width), BF), sds((rows, out), F32)],
        flops=2 * rows * width * out,
        moved=2 * w_qkv.size + 4 * x.size + 4 * rows * out,
        after=after,
    )(meta, x, gains, w_qkv)


def rotary_tables(rows, shard):
    half = ROT // 2
    freq = np.exp(np.arange(half) * (-2.0 * math.log(10000.0) / ROT))
    angles = np.arange(rows)[:, None] * freq[None, :]
    cos, sin = np.cos(angles), np.sin(angles)
    one = np.ones((rows, HEAD))
    one[:, :half] = cos
    one[:, half:ROT] = cos
    up = np.zeros((rows, HEAD))
    up[:, half:ROT] = sin
    down = np.zeros((rows, HEAD))
    down[:, :half] = sin
    heads = min(shard, 128) // HEAD
    return [jnp.asarray(np.tile(table, (1, heads)), F32) for table in (one, up, down)]


def across(table, width):
    return jnp.concatenate([table] * (width // table.shape[1]), axis=1)


def turn(rows, cos, up, down, sign):
    half = ROT // 2
    width = rows.shape[1]
    from_low = pltpu.roll(rows, half, 1)
    from_high = pltpu.roll(rows, width - half, 1)
    cos, up, down = (across(table, width) for table in (cos, up, down))
    return rows * cos + sign * (from_low * up - from_high * down)


def pre_body(
    meta, low_ref, qkv_ref, cos_ref, up_ref, down_ref,
    m_own, m_y, m_sib, m_far, q_ref, k_ref, v_ref, rank_ref,
):
    proj = meta[PROJ]
    shard = q_ref.shape[1]
    rank = m_own.shape[1]
    total = None
    for rel, piece in enumerate((m_own, m_sib, m_y, m_far)):
        low = low_ref[:, columns(proj ^ rel, shard)]
        part = dot_nt(low, piece[0:3].reshape(3 * rank, shard))
        total = part if total is None else total + part
    rank_in = total.astype(BF)
    rank_ref[...] = rank_in
    pre = [
        qkv_ref[:, k * shard : (k + 1) * shard]
        + ADAPTER_SCALE * dot_nn(rank_in[:, k * rank : (k + 1) * rank], m_own[5 + k])
        for k in range(3)
    ]
    tables = (cos_ref[...], up_ref[...], down_ref[...])
    q_ref[...] = turn(pre[0], *tables, 1.0).astype(BF)
    k_ref[...] = turn(pre[1], *tables, 1.0).astype(BF)
    v_ref[...] = pre[2].astype(BF)


def make_qkv(meta, low, qkv, tables, m_own, m_y, m_sib, m_far, after=()):
    rows, width = low.shape
    shard = qkv.shape[1] // 3
    rank = m_own.shape[1]
    block = lambda cols: pl.BlockSpec((UNIT, cols), lambda i, m: (i, 0))
    return kernel_call(
        pre_body,
        "adapter_qkv",
        (rows // UNIT,),
        [block(width), block(3 * shard)]
        + [block(tables[0].shape[1])] * 3
        + [whole(m_own.shape), whole(m_y.shape), whole(m_sib.shape), whole(m_far.shape)],
        [block(shard)] * 3 + [block(3 * rank)],
        [sds((rows, shard), BF)] * 3 + [sds((rows, 3 * rank), BF)],
        flops=2 * rows * width * 3 * rank,
        moved=rows * (2 * width + 24 * shard),
        after=after,
    )(meta, low, qkv, *tables, m_own, m_y, m_sib, m_far)


def head_mask(shard, head):
    return lax.broadcasted_iota(jnp.int32, (1, shard), 1) // HEAD == head


def diagonal():
    rows = lax.broadcasted_iota(jnp.int32, (BLOCK, BLOCK), 0)
    cols = lax.broadcasted_iota(jnp.int32, (BLOCK, BLOCK), 1)
    return rows >= cols


def block_scores(query, k_ref, prev, causal):
    scale = HEAD**-0.5
    diag = dot_nt(query, k_ref[prev : prev + BLOCK, :]) * scale
    diag = jnp.where(causal, diag, -1e30)
    if prev == 0:
        return diag
    return jnp.concatenate([dot_nt(query, k_ref[0:prev, :]) * scale, diag], axis=1)


def attend_body(unit, meta, q_ref, k_ref, v_ref, mine_ref, sib_ref, lse_ref):
    shard = q_ref.shape[1]
    causal = diagonal()
    lane = lax.broadcasted_iota(jnp.int32, (BLOCK, 128), 1)
    for half in range(UNIT // BLOCK):
        prev = unit * UNIT + half * BLOCK
        query = q_ref[half * BLOCK : (half + 1) * BLOCK, :]
        out = jnp.zeros((BLOCK, shard), F32)
        lse = jnp.zeros((BLOCK, 128), F32)
        for head in range(shard // HEAD):
            mask = head_mask(shard, head)
            scores = block_scores(jnp.where(mask, query, 0), k_ref, prev, causal)
            top = jnp.max(scores, axis=1, keepdims=True)
            prob = jnp.exp(scores - top)
            total = jnp.sum(prob, axis=1, keepdims=True)
            got = dot_nn(prob.astype(BF), v_ref[0 : prev + BLOCK, :]) / total
            out = jnp.where(mask, got, out)
            lse = jnp.where(lane == head, top + jnp.log(total), lse)
        lse_ref[half * BLOCK : (half + 1) * BLOCK, :] = lse
        low = out.astype(BF)

        @pl.when(meta[CORE] == half)
        def _():
            mine_ref[...] = low

        @pl.when(meta[CORE] != half)
        def _():
            sib_ref[...] = low


def attend(meta, unit, queries, keys, values):
    shard = queries.shape[1]
    known = (unit + 1) * UNIT
    return kernel_call(
        partial(attend_body, unit),
        f"attend_{unit}",
        (1,),
        [
            pl.BlockSpec((UNIT, shard), lambda i, m: (unit, 0)),
            pl.BlockSpec((known, shard), lambda i, m: (0, 0)),
            pl.BlockSpec((known, shard), lambda i, m: (0, 0)),
        ],
        [whole((BLOCK, shard)), whole((BLOCK, shard)), whole((UNIT, 128))],
        [sds((BLOCK, shard), BF)] * 2 + [sds((UNIT, 128), F32)],
        flops=16 * UNIT * known * shard,
        moved=8 * known * shard,
    )(meta, queries, keys, values)


def attend_back_body(unit, meta, *refs):
    shard = refs[4].shape[1]
    if unit == 0:
        (g0, g1, g2, g3, q_ref, k_ref, v_ref, lse_ref, cos_ref, up_ref, down_ref,
         dq_ref, dk_ref, dv_ref, grad_ref) = refs
        dk_ref[...] = jnp.zeros_like(dk_ref)
        dv_ref[...] = jnp.zeros_like(dv_ref)
    else:
        (g0, g1, g2, g3, q_ref, k_ref, v_ref, lse_ref, cos_ref, up_ref, down_ref,
         dk_in, dv_in, dq_ref, dk_ref, dv_ref, grad_ref) = refs
        dk_ref[...] = dk_in[...]
        dv_ref[...] = dv_in[...]
    core, ybit = meta[CORE], meta[YBIT]
    quarter = BLOCK // 2
    for rel, piece in enumerate((g0, g1, g2, g3)):
        place = (core ^ (rel & 1)) * 2 + (ybit ^ (rel >> 1))
        grad_ref[columns(place, quarter), :] = piece[...]
    causal = diagonal()
    lane = lax.broadcasted_iota(jnp.int32, (BLOCK, 128), 1)
    scale = HEAD**-0.5
    for half in range(UNIT // BLOCK):
        prev = unit * UNIT + half * BLOCK
        known = prev + BLOCK
        here = slice(half * BLOCK, (half + 1) * BLOCK)
        query = q_ref[here, :]
        grad = grad_ref[here, :]
        lse = lse_ref[here, :]
        dq = jnp.zeros((BLOCK, shard), F32)
        for head in range(shard // HEAD):
            mask = head_mask(shard, head)
            own_q = jnp.where(mask, query, 0)
            own_g = jnp.where(mask, grad, 0)
            own_lse = jnp.sum(jnp.where(lane == head, lse, 0.0), axis=1, keepdims=True)
            prob = jnp.exp(block_scores(own_q, k_ref, prev, causal) - own_lse)
            dweights = dot_nt(own_g, v_ref[0:known, :])
            delta = jnp.sum(prob * dweights, axis=1, keepdims=True)
            dscores = (prob * (dweights - delta)).astype(BF)
            dq = dq + jnp.where(mask, dot_nn(dscores, k_ref[0:known, :]), 0.0)
            dk_ref[0:known, :] += dot_tn(dscores, own_q) * scale
            dv_ref[0:known, :] += dot_tn(prob.astype(BF), own_g)
        dq = turn(dq * scale, cos_ref[here, :], up_ref[here, :], down_ref[here, :], -1.0)
        dq_ref[here, :] = dq.astype(BF)


def attend_back(meta, unit, grads, queries, keys, values, lse, tables, before):
    rows, shard = queries.shape
    known = (unit + 1) * UNIT
    unit_rows = pl.BlockSpec((UNIT, shard), lambda i, m: (unit, 0))
    past = pl.BlockSpec((known, shard), lambda i, m: (0, 0))
    quarter = whole((BLOCK // 2, shard))
    sums = whole((rows, shard))
    return kernel_call(
        partial(attend_back_body, unit),
        f"attend_back_{unit}",
        (1,),
        [quarter] * 4
        + [unit_rows, past, past, whole((UNIT, 128))]
        + [pl.BlockSpec((UNIT, tables[0].shape[1]), lambda i, m: (unit, 0))] * 3
        + [sums] * len(before),
        [whole((UNIT, shard)), sums, sums],
        [sds((UNIT, shard), BF), sds((rows, shard), F32), sds((rows, shard), F32)],
        [pltpu.VMEM((UNIT, shard), BF)],
        flops=40 * UNIT * known * shard,
        moved=16 * rows * shard,
    )(meta, *grads, queries, keys, values, lse, *tables, *before)


def mix_body(
    meta, x_ref, gain_ref, f_own, f_far, a0, a1, a2, a3, w0, w1, w2, w3,
    m0, m1, m2, m3, norm_ref, res_ref, rank_ref, keep_ref,
):
    proj = meta[PROJ]
    shard = a0.shape[1]
    rank = None
    for a_ref, m_ref in ((a0, m0), (a1, m1), (a2, m2), (a3, m3)):
        part = dot_nt(a_ref[...], m_ref[0])
        rank = part if rank is None else rank + part
    rank = rank.astype(BF)
    total = x_ref[...].astype(F32) + f_own[...].astype(F32) + f_far[...].astype(F32)
    for a_ref, w_ref in ((a0, w0), (a1, w1), (a2, w2), (a3, w3)):
        total = total + dot_nn(a_ref[...], w_ref[...])
    keep_ref[...] = total
    for rel, m_ref in enumerate((m0, m1, m2, m3)):
        here = columns(proj ^ rel, shard)
        keep_ref[:, here] += ADAPTER_SCALE * dot_nn(rank, m_ref[1])
    residual = keep_ref[...]
    norm_ref[...] = (normalize(residual) * gain_ref[2:3, :]).astype(BF)
    mine = columns(meta[YBIT], BLOCK // 2)
    res_ref[...] = keep_ref[mine, :]
    keep_ref[:, 0 : rank.shape[1]] = rank.astype(F32)
    rank_ref[...] = keep_ref[mine, 0 : rank.shape[1]].astype(BF)


def mix(meta, unit, x, gains, f_own, f_far, att, wo, maps):
    rows, width = x.shape
    shard = att[0].shape[1]
    rank = maps[0].shape[1]
    return kernel_call(
        mix_body,
        f"mix_{unit}",
        (1,),
        [
            pl.BlockSpec((BLOCK, width), lambda i, m: (2 * unit + m[CORE], 0)),
            whole(gains.shape),
            whole((BLOCK, width)),
            whole((BLOCK, width)),
        ]
        + [whole((BLOCK, shard))] * 4
        + [whole((shard, width))] * 4
        + [whole((2, rank, shard))] * 4,
        [whole((BLOCK, width)), whole((BLOCK // 2, width)), whole((BLOCK // 2, rank))],
        [sds((BLOCK, width), BF), sds((BLOCK // 2, width), F32), sds((BLOCK // 2, rank), BF)],
        [pltpu.VMEM((BLOCK, width), F32)],
        flops=2 * BLOCK * width * width,
        moved=2 * width * width + 8 * BLOCK * width,
    )(meta, x, gains, f_own, f_far, *att, *wo, *maps)


def vocab_grid(vocab):
    steps = -(-vocab // TILE_V)
    return steps, vocab - (steps - 1) * TILE_V


def vocab_stats_body(vocab, meta, mine_ref, sib_ref, u_ref, tm_ref, ts_ref, p_ref, top_ref, st_ref, acc_ref):
    step = pl.program_id(0)
    steps, tail = vocab_grid(vocab)

    @pl.when(step == 0)
    def _():
        acc_ref[...] = jnp.zeros_like(acc_ref)

    def tile(is_tail):
        col = lax.broadcasted_iota(jnp.int32, (BLOCK, TILE_V), 1)
        lane = lax.broadcasted_iota(jnp.int32, (BLOCK, 128), 1)
        for half, (rows_ref, target_ref) in enumerate(((mine_ref, tm_ref), (sib_ref, ts_ref))):
            here = slice(half * BLOCK, (half + 1) * BLOCK)
            logits = dot_nt(rows_ref[...], u_ref[...])
            if is_tail:
                logits = jnp.where(col < tail, logits, -1e30)
            top = jnp.max(logits, axis=1, keepdims=True)
            prob = jnp.exp(logits - top)
            total = jnp.sum(prob, axis=1, keepdims=True)
            hit = col == target_ref[...] - step * TILE_V
            picked = jnp.sum(jnp.where(hit, logits, 0.0), axis=1, keepdims=True)
            p_ref[here, :] = prob.astype(BF)
            acc = acc_ref[here, :]
            acc = jnp.where(lane == step, top, acc)
            acc = jnp.where(lane == step + 32, total, acc)
            acc_ref[here, :] = jnp.where(lane == 64, acc + picked, acc)

    @pl.when(step < steps - 1)
    def _():
        tile(False)

    @pl.when(step == steps - 1)
    def _():
        tile(True)
        acc = acc_ref[...]
        lane = lax.broadcasted_iota(jnp.int32, acc.shape, 1)
        top_ref[...] = acc
        tops = jnp.where(lane < steps, acc, -1e30)
        best = jnp.max(tops, axis=1, keepdims=True)
        totals = pltpu.roll(acc, 128 - 32, 1)
        total = jnp.sum(
            jnp.where(lane < steps, totals * jnp.exp(tops - best), 0.0), axis=1, keepdims=True
        )
        picked = jnp.sum(jnp.where(lane == 64, acc, 0.0), axis=1, keepdims=True)
        pair = jnp.where(lane == 0, best + jnp.log(total), jnp.where(lane == 1, picked, 0.0))
        st_ref[...] = jnp.transpose(pair)[0:8, :]


def vocab_stats(meta, unit, mine, sib, unembed, targets):
    vocab, width = unembed.shape
    steps, _ = vocab_grid(vocab)
    rows = 2 * BLOCK
    return kernel_call(
        partial(vocab_stats_body, vocab),
        f"vocab_stats_{unit}",
        (steps,),
        [
            whole((BLOCK, width)),
            whole((BLOCK, width)),
            pl.BlockSpec((TILE_V, width), lambda i, m: (i, 0)),
            pl.BlockSpec((BLOCK, 1), lambda i, m: (2 * unit + m[CORE], 0)),
            pl.BlockSpec((BLOCK, 1), lambda i, m: (2 * unit + 1 - m[CORE], 0)),
        ],
        [pl.BlockSpec((rows, TILE_V), lambda i, m: (0, i)), whole((rows, 128)), whole((8, rows))],
        [
            sds((rows, steps * TILE_V), BF),
            sds((rows, 128), F32),
            sds((8, rows), F32),
        ],
        [pltpu.VMEM((rows, 128), F32)],
        flops=2 * rows * width * vocab,
        moved=2 * width * vocab + 2 * rows * vocab,
    )(meta, mine, sib, unembed, targets, targets)


def swap_halves(pair):
    return jnp.concatenate([pair[:, BLOCK:], pair[:, :BLOCK]], axis=1)


def vocab_back_body(
    vocab, unit, meta, count_ref, p_ref, u_ref, tm_ref, ts_ref, top_ref, s0, s1, s2, s3,
    d0, d1, d2, d3, loss_ref, scale_ref, acc_ref,
):
    step = pl.program_id(0)
    steps, tail = vocab_grid(vocab)
    rows = 2 * BLOCK

    @pl.when(step == 0)
    def _():
        acc_ref[...] = jnp.zeros_like(acc_ref)
        parts = [s0[...], swap_halves(s1[...]), s2[...], swap_halves(s3[...])]
        lses = [part[0:1, :] for part in parts]
        best = jnp.maximum(jnp.maximum(lses[0], lses[1]), jnp.maximum(lses[2], lses[3]))
        total = sum(jnp.exp(one - best) for one in lses)
        log_norm = best + jnp.log(total)
        picked = sum(part[1:2, :] for part in parts)
        place = lax.broadcasted_iota(jnp.int32, (1, rows), 1)
        core = meta[CORE]
        offset = jnp.where(place < BLOCK, core * BLOCK, (1 - core) * BLOCK - BLOCK)
        valid = (unit * UNIT + place + offset < meta[LENGTH]).astype(F32)
        loss_ref[...] = jnp.broadcast_to(
            jnp.sum((log_norm - picked) * valid, axis=1, keepdims=True), (8, 128)
        )
        weight = valid / count_ref[0, 0]
        row = lax.broadcasted_iota(jnp.int32, (128, rows), 0)
        lines = jnp.where(row == 0, log_norm, 0.0)
        lines = jnp.where(row == 1, weight, lines)
        lines = jnp.where(row == 2, (jnp.exp(picked - log_norm) - 1.0) * weight, lines)
        cols = jnp.transpose(lines)
        lane = lax.broadcasted_iota(jnp.int32, (rows, 128), 1)
        take = lambda k: jnp.sum(jnp.where(lane == k, cols, 0.0), axis=1, keepdims=True)
        tops = jnp.where(lane < steps, top_ref[...], -1e30)
        scales = jnp.exp(tops - take(0)) * take(1)
        scale_ref[...] = jnp.where(lane == 64, take(2), scales)

    def tile(is_tail):
        u_tile = u_ref[...]
        if is_tail:
            row = lax.broadcasted_iota(jnp.int32, u_tile.shape, 0)
            u_tile = jnp.where(row < tail, u_tile, jnp.zeros_like(u_tile))
        col = lax.broadcasted_iota(jnp.int32, (BLOCK, TILE_V), 1)
        lane = lax.broadcasted_iota(jnp.int32, (BLOCK, 128), 1)
        for half, target_ref in enumerate((tm_ref, ts_ref)):
            here = slice(half * BLOCK, (half + 1) * BLOCK)
            scales = scale_ref[here, :]
            scale = jnp.sum(jnp.where(lane == step, scales, 0.0), axis=1, keepdims=True)
            at_hit = jnp.sum(jnp.where(lane == 64, scales, 0.0), axis=1, keepdims=True)
            hit = col == target_ref[...] - step * TILE_V
            grad = jnp.where(hit, at_hit, p_ref[here, :].astype(F32) * scale).astype(BF)
            acc_ref[here, :] += dot_nn(grad, u_tile)

    @pl.when(step < steps - 1)
    def _():
        tile(False)

    @pl.when(step == steps - 1)
    def _():
        tile(True)
        quarter = BLOCK // 2
        for rel, out_ref in enumerate((d0, d1, d2, d3)):
            place = (rel & 1) * 2 + (meta[YBIT] ^ (rel >> 1))
            out_ref[...] = acc_ref[columns(place, quarter), :].astype(BF)


def vocab_back(meta, unit, count, prob, unembed, targets, tops, stats):
    vocab, width = unembed.shape
    steps, _ = vocab_grid(vocab)
    rows = 2 * BLOCK
    return kernel_call(
        partial(vocab_back_body, vocab, unit),
        f"vocab_back_{unit}",
        (steps,),
        [
            whole((1, 1)),
            pl.BlockSpec((rows, TILE_V), lambda i, m: (0, i)),
            pl.BlockSpec((TILE_V, width), lambda i, m: (i, 0)),
            pl.BlockSpec((BLOCK, 1), lambda i, m: (2 * unit + m[CORE], 0)),
            pl.BlockSpec((BLOCK, 1), lambda i, m: (2 * unit + 1 - m[CORE], 0)),
            whole((rows, 128)),
        ]
        + [whole((8, rows))] * 4,
        [whole((BLOCK // 2, width))] * 4 + [whole((8, 128))],
        [sds((BLOCK // 2, width), BF)] * 4 + [sds((8, 128), F32)],
        [pltpu.VMEM((rows, 128), F32), pltpu.VMEM((rows, width), F32)],
        flops=2 * rows * width * vocab,
        moved=2 * width * vocab + 2 * rows * vocab,
    )(meta, count, prob, unembed, targets, targets, tops, *stats)


def norm_back_body(last, meta, *refs):
    parts, (res_ref, gain_ref, rank_ref) = refs[:4], refs[4:7]
    atts, wos, maps = refs[7:11], refs[11:15], refs[15:19]
    if last:
        before_ref = refs[19]
        outs, (hold_ref,) = refs[20:26], refs[26:]
    else:
        outs, (hold_ref,) = refs[19:24], refs[24:]
    proj = meta[PROJ]
    shard = atts[0].shape[1]
    dnormed = sum(part[...].astype(F32) for part in parts)
    residual = res_ref[...]
    center = residual - jnp.mean(residual, axis=-1, keepdims=True)
    spread = jnp.mean(center * center, axis=-1, keepdims=True)
    inv = lax.rsqrt(spread + EPS_NORM)
    hat = center * inv
    dhat = dnormed * gain_ref[2:3, :]
    dres = inv * (
        dhat
        - jnp.mean(dhat, axis=-1, keepdims=True)
        - hat * jnp.mean(dhat * hat, axis=-1, keepdims=True)
    )
    hold_ref[...] = dres.astype(BF)
    dbranch = hold_ref[...]
    drank = None
    for rel, m_ref in enumerate(maps):
        part = dot_nt(hold_ref[:, columns(proj ^ rel, shard)], m_ref[1])
        drank = part if drank is None else drank + part
    drank = (ADAPTER_SCALE * drank).astype(BF)
    for rel in range(4):
        datt = dot_nt(dbranch, wos[rel][...]) + dot_nn(drank, maps[rel][0])
        outs[rel][...] = datt.astype(BF)
        g_down = dot_tn(drank, atts[rel][...])
        g_up = ADAPTER_SCALE * dot_tn(rank_ref[...], hold_ref[:, columns(proj ^ rel, shard)])
        if last:
            dest = outs[4 + (rel & 1)]
            dest[rel >> 1, 0] = (before_ref[rel, 0] + g_down).astype(BF)
            dest[rel >> 1, 1] = (before_ref[rel, 1] + g_up).astype(BF)
        else:
            outs[4][rel, 0] = g_down
            outs[4][rel, 1] = g_up


def norm_back(meta, unit, last, parts, residual, gains, rank_out, att, wo, maps, before):
    quarter, width = residual.shape
    shard = att[0].shape[1]
    rank = rank_out.shape[1]
    if last:
        more_specs = [whole((2, 2, rank, shard))] * 2
        more_shapes = [sds((2, 2, rank, shard), BF)] * 2
    else:
        more_specs = [whole((4, 2, rank, shard))]
        more_shapes = [sds((4, 2, rank, shard), F32)]
    return kernel_call(
        partial(norm_back_body, last),
        f"norm_back_{unit}",
        (1,),
        [whole(residual.shape)] * 5
        + [whole(gains.shape), whole(rank_out.shape)]
        + [pl.BlockSpec((quarter, shard), lambda i, m: (m[YBIT], 0))] * 4
        + [whole((shard, width))] * 4
        + [whole((2, rank, shard))] * 4
        + [whole(one.shape) for one in before],
        [whole((quarter, shard))] * 4 + more_specs,
        [sds((quarter, shard), BF)] * 4 + more_shapes,
        [pltpu.VMEM((quarter, width), BF)],
        flops=2 * quarter * width * width,
        moved=2 * width * width + 12 * quarter * width,
    )(meta, *parts, residual, gains, rank_out, *att, *wo, *maps, *before)


def grads_body(
    meta, dq0, dq1, dk_ref, dv_ref, cos_ref, up_ref, down_ref, rank_ref, m_own, low_ref,
    keep_ref, send_ref, up_grad_ref, drank_ref,
):
    proj = meta[PROJ]
    rank, shard = m_own.shape[1:]
    dk = turn(dk_ref[...], cos_ref[...], up_ref[...], down_ref[...], -1.0).astype(BF)
    dpre = [jnp.concatenate([dq0[...], dq1[...]], axis=0), dk, dv_ref[...].astype(BF)]
    for k in range(3):
        here = slice(k * rank, (k + 1) * rank)
        up_grad_ref[k] = ADAPTER_SCALE * dot_tn(rank_ref[:, here], dpre[k])
        drank_ref[:, here] = (ADAPTER_SCALE * dot_nt(dpre[k], m_own[5 + k])).astype(BF)
    drank = drank_ref[...]
    for rel in range(4):
        grad = dot_tn(drank, low_ref[:, columns(proj ^ rel, shard)])
        dest = (keep_ref, send_ref)[rel & 1]
        dest[rel >> 1] = grad.reshape(3, rank, shard).astype(BF)


def adapter_grads(meta, dqs, dk, dv, tables, rank_in, m_own, low):
    rows, shard = dk.shape
    rank = m_own.shape[1]
    pair = (2, 3, rank, shard)
    args = (*dqs, dk, dv, *tables, rank_in, m_own, low)
    return kernel_call(
        grads_body,
        "adapter_grads",
        (1,),
        [whole(one.shape) for one in args],
        [whole(pair), whole(pair), whole((3, rank, shard))],
        [sds(pair, BF), sds(pair, BF), sds((3, rank, shard), F32)],
        [pltpu.VMEM((rows, 3 * rank), BF)],
        flops=2 * rows * low.shape[1] * 3 * rank,
        moved=30 * rows * shard,
    )(meta, *args)


def signs(row_ids, col_ids, seed):
    hashed = row_ids * 1640531527 + col_ids * 747796405 + seed * 277803737
    hashed = hashed ^ hashed >> 15 & 131071
    hashed = hashed * 2024237689
    hashed = hashed ^ hashed >> 13 & 524287
    return 1.0 - 2.0 * (hashed >> 17 & 1).astype(F32)


def sketch_body(meta, seeds_ref, count_ref, grad_ref, p0, p1, p2, p3, full_ref):
    mats, rank, shard = grad_ref.shape
    sketch = full_ref.shape[1]
    proj = meta[PROJ]
    left_rows = lax.broadcasted_iota(jnp.int32, (sketch, shard), 1) + proj * shard
    left_cols = lax.broadcasted_iota(jnp.int32, (sketch, shard), 0)
    right_rows = lax.broadcasted_iota(jnp.int32, (rank, sketch), 0)
    right_cols = lax.broadcasted_iota(jnp.int32, (rank, sketch), 1)
    for mat in range(mats):
        seed = seeds_ref[mat]
        left = signs(left_rows, left_cols, 2 * seed).astype(BF)
        right = signs(right_rows, right_cols, 2 * seed + 1)
        inner = dot_nt(left, grad_ref[mat])
        full_ref[mat] = count_ref[0, 0] * jnp.dot(inner, right, precision=lax.Precision.HIGHEST)
    size = sketch // 4
    for rel, out_ref in enumerate((p0, p1, p2, p3)):
        out_ref[...] = full_ref[:, columns(proj ^ rel, size), :]


def sketch(meta, seeds, count, grads, sketch_width):
    mats, rank, shard = grads.shape
    piece = (mats, sketch_width // 4, sketch_width)
    return kernel_call(
        sketch_body,
        "sketch",
        (1,),
        [pl.BlockSpec(memory_space=pltpu.SMEM), whole((1, 1)), whole(grads.shape)],
        [whole(piece)] * 4,
        [sds(piece, F32)] * 4,
        [pltpu.VMEM((mats, sketch_width, sketch_width), F32)],
        flops=2 * mats * rank * shard * sketch_width,
        moved=2 * grads.size,
    )(meta, seeds, count, grads)


def lane_value(row, lane, place):
    return jnp.sum(jnp.where(lane == place, row, 0.0), axis=1, keepdims=True)


def tally_body(
    units, meta, got_ref, target_ref, f0, f1, f2, f3, *refs
):
    losses, (total_ref, line_ref) = refs[:units], refs[units:]
    total = jnp.sum(got_ref[...].astype(F32), axis=0)
    total_ref[...] = total
    features = f0[...] + f1[...] + f2[...] + f3[...]
    squares = jnp.sum(total * total)
    own = jnp.sum(features * features)
    loss = sum(jnp.sum(one[0:1, 0:1]) for one in losses)
    loss = jnp.where(meta[PROJ] == 0, loss, 0.0)
    lane = lax.broadcasted_iota(jnp.int32, (1, 128), 1)
    line = jnp.where(lane == 0, squares, 0.0)
    line = jnp.where(lane == 1, loss, line)
    line = jnp.where(lane == 2, own, line)
    checkpoints = target_ref.shape[0]
    for c in range(checkpoints):
        theirs = target_ref[c]
        line = jnp.where(lane == 3 + c, jnp.sum(features * theirs), line)
        line = jnp.where(lane == 3 + checkpoints + c, jnp.sum(theirs * theirs), line)
    line_ref[...] = jnp.broadcast_to(line, line_ref.shape)


def tally(meta, devices, got, targets, pieces, losses):
    _, mats, slice_rank, shard = got.shape
    args = (got, targets, *pieces, *losses)
    return kernel_call(
        partial(tally_body, len(losses)),
        "tally",
        (1,),
        [whole(one.shape) for one in args],
        [whole((mats, slice_rank, shard)), whole((devices, 128))],
        [sds((mats, slice_rank, shard), F32), sds((devices, 128), F32)],
        flops=got.size,
        moved=4 * got.size,
    )(meta, *args)


def optimizer_step(weight, grad_in, first_in, second_in, clipping_scale):
    grad_clip = grad_in * clipping_scale
    first_new = BETA_ONE * first_in + (1.0 - BETA_ONE) * grad_clip
    second_new = BETA_TWO * second_in + (1.0 - BETA_TWO) * grad_clip * grad_clip
    first_hat = first_new / (1.0 - BETA_ONE**STEP)
    second_hat = second_new / (1.0 - BETA_TWO**STEP)
    new_weight = weight - LEARN_RATE * (
        first_hat / (jnp.sqrt(second_hat) + ADAM_EPS) + WEIGHT_DECAY * weight
    )
    return (new_weight, first_new, second_new)


def finish_body(
    proj_count, checkpoints, meta, count_ref, lines_ref, total_ref,
    dw, uw, dm, um, ds, us,
    loss_out, norm_out, influence_out, dw_out, uw_out, dm_out, um_out, ds_out, us_out,
):
    lines = lines_ref[...]
    everyone = jnp.sum(lines, axis=0, keepdims=True)
    row = lax.broadcasted_iota(jnp.int32, lines.shape, 0)
    ours = jnp.sum(
        jnp.where(row // proj_count == meta[SEQ], lines, 0.0), axis=0, keepdims=True
    )
    lane = lax.broadcasted_iota(jnp.int32, (1, 128), 1)
    grad_norm = jnp.sqrt(lane_value(everyone, lane, 0))
    own = lane_value(ours, lane, 2)
    influence = jnp.zeros((1, 1), F32)
    for c in range(checkpoints):
        dot = lane_value(ours, lane, 3 + c)
        theirs = lane_value(ours, lane, 3 + checkpoints + c)
        influence += (1.0 - c / checkpoints) * dot * lax.rsqrt(own * theirs + 1e-12)
    loss_out[0] = jnp.sum(lane_value(everyone, lane, 1))
    loss_out[1] = count_ref[0, 0]
    norm_out[0] = jnp.sum(grad_norm)
    influence_out[0] = jnp.sum(influence)
    clip = jnp.minimum(1.0, CLIP_NORM / (grad_norm + 1e-06))
    half = total_ref.shape[0] // 2
    for base, ins, outs in (
        (0, (dw, dm, ds), (dw_out, dm_out, ds_out)),
        (half, (uw, um, us), (uw_out, um_out, us_out)),
    ):
        for k in range(half):
            new = optimizer_step(
                ins[0][k], total_ref[base + k], ins[1][k], ins[2][k], clip
            )
            for out, value in zip(outs, new):
                out[k] = value


def finish(meta, proj_count, checkpoints, count, lines, total, params):
    scalar = pl.BlockSpec(memory_space=pltpu.SMEM)
    block = whole(params[0].shape)
    return kernel_call(
        partial(finish_body, proj_count, checkpoints),
        "finish",
        (1,),
        [scalar, whole(lines.shape), whole(total.shape)] + [block] * 6,
        [scalar] * 3 + [block] * 6,
        [sds((2,), F32), sds((1,), F32), sds((1,), F32)] + [sds(params[0].shape, F32)] * 6,
        flops=20 * total.size,
        moved=28 * total.size,
    )(meta, count, lines, total, *params)


def to_partner(array, axis, size, offset):
    return lax.ppermute(array, axis, [(i, i ^ offset) for i in range(size)])


def on_device(
    seq_count,
    proj_count,
    inputs,
    targets,
    lengths,
    norm_gain_vectors,
    query_key_value_weight,
    attention_output_weight,
    feedforward_input_weight,
    feedforward_output_weight,
    unembed,
    adapter_down_maps,
    adapter_up_maps,
    down_first_moment,
    up_first_moment,
    down_second_moment,
    up_second_moment,
    target_gradient_sketches,
    seeds,
):
    rows, width = inputs.shape
    shard = attention_output_weight.shape[0]
    vocab_local = unembed.shape[1]
    slice_rank = adapter_up_maps.shape[1]
    rank = slice_rank * seq_count
    sketch_width = target_gradient_sketches.shape[3]
    proj = lax.axis_index("proj")
    seq = lax.axis_index("dp")
    units = rows // UNIT

    over_proj = lambda array, rel: to_partner(array, "proj", proj_count, rel)
    over_seq = lambda array, rel: to_partner(array, "dp", seq_count, rel)

    token_total = jnp.sum(lengths).astype(F32)
    count = token_total.reshape(1, 1)
    length = jnp.sum(jnp.where(jnp.arange(seq_count) == seq, lengths, 0))
    zero = jnp.int32(0)
    meta = jnp.stack([proj, proj & 1, proj >> 1, seq, length, zero, zero, zero]).astype(jnp.int32)

    transposed = lambda array: jnp.transpose(array, (0, 2, 1))
    own_maps = jnp.concatenate(
        [transposed(adapter_down_maps), adapter_up_maps[3:], adapter_up_maps[:3]], axis=0
    ).astype(BF)
    maps = lax.all_to_all(
        jnp.broadcast_to(own_maps[None], (seq_count, *own_maps.shape)),
        "dp", split_axis=0, concat_axis=0, tiled=True,
    )
    maps = jnp.transpose(maps, (1, 0, 2, 3)).reshape(8, rank, shard)

    wo_sib = over_proj(attention_output_weight, 1)
    wo_y = over_proj(attention_output_weight, 2)
    wo_far = over_proj(wo_y, 1)
    wo = (attention_output_weight, wo_sib, wo_y, wo_far)

    ffn_unit = lambda unit, after: ffn(
        meta, unit, inputs, norm_gain_vectors,
        feedforward_input_weight, feedforward_output_weight, after,
    )
    low, qkv = frozen_qkv(
        meta, inputs, norm_gain_vectors, jnp.transpose(query_key_value_weight, (1, 0, 2))
    )
    f_parts = []
    for unit in range(units):
        f_mine, f_sib = ffn_unit(unit, (low,) if unit == 0 else (maps,))
        f_parts.append((f_mine, f_sib))

    down_in = maps[:3]
    down_y = over_proj(down_in, 2)
    down_sib = over_proj(down_in, 1)
    down_far = over_proj(down_y, 1)

    tables = rotary_tables(rows, shard)
    queries, keys, values, rank_in = make_qkv(
        meta, low, qkv, tables, maps, down_y, down_sib, down_far, (f_parts[-1][0],)
    )

    f_chip = [mine + over_proj(sib, 1) for mine, sib in f_parts]
    f_far = [over_proj(one, 2) for one in f_chip]
    out_maps = maps[3:5]
    out_y = over_proj(out_maps, 2)
    out_sib = over_proj(out_maps, 1)
    out_far = over_proj(out_y, 1)
    outs = (out_maps, out_sib, out_y, out_far)

    local_targets = targets - proj * vocab_local
    inside = (local_targets >= 0) & (local_targets < vocab_local)
    target_cols = jnp.where(inside, local_targets, -1).reshape(rows, 1)
    table = jnp.transpose(unembed)

    lses, atts, normeds, residuals, ranks = [], [], [], [], []
    for unit in range(units):
        att_mine, att_sib, lse = attend(meta, unit, queries, keys, values)
        lses.append(lse)
        att = (att_mine, over_proj(att_sib, 1), over_proj(att_mine, 2), over_proj(att_sib, 3))
        atts.append(att)
    for unit in range(units):
        normed, residual, rank_out = mix(
            meta, unit, inputs, norm_gain_vectors, f_chip[unit], f_far[unit], atts[unit], wo, outs
        )
        normeds.append((normed, over_proj(normed, 1)))
        residuals.append(residual)
        ranks.append(rank_out)

    probs, tops, stats = [], [], []
    for unit in range(units):
        prob, top, stat = vocab_stats(meta, unit, *normeds[unit], table, target_cols)
        probs.append(prob)
        tops.append(top)
        stats.append((stat, over_proj(stat, 1), over_proj(stat, 2), over_proj(stat, 3)))

    losses, dnormed = [], []
    for unit in range(units):
        *parts, loss = vocab_back(
            meta, unit, count, probs[unit], table, target_cols, tops[unit], stats[unit]
        )
        losses.append(loss)
        dnormed.append(parts[:1] + [over_proj(parts[rel], rel) for rel in (1, 2, 3)])

    def half_sum(keep, send):
        return keep.astype(F32) + over_proj(send, 1).astype(F32)

    def full_sum(half):
        return half[0] + over_proj(half[1].astype(BF), 2).astype(F32)

    dqs, out_grads, sums = [], (), ()
    for unit in range(units):
        last = unit == units - 1
        result = norm_back(
            meta, unit, last, dnormed[unit], residuals[unit], norm_gain_vectors,
            ranks[unit], atts[unit], wo, outs, out_grads,
        )
        out_grads = tuple(result[4:])
        datt = [result[0]] + [over_proj(result[rel], rel) for rel in (1, 2, 3)]
        dq, dk, dv = attend_back(
            meta, unit, datt, queries, keys, values, lses[unit], tables, sums
        )
        dqs.append(dq)
        sums = (dk, dv)

    out_total = full_sum(half_sum(*out_grads))
    in_keep, in_send, up_grads = adapter_grads(meta, dqs, *sums, tables, rank_in, maps, low)
    in_total = full_sum(half_sum(in_keep, in_send))

    grads = jnp.concatenate(
        [in_total, out_total[0:1], up_grads, out_total[1:2]], axis=0
    ).astype(BF)
    blocks = jnp.transpose(grads.reshape(8, seq_count, slice_rank, shard), (1, 0, 2, 3))
    arrived = lax.all_to_all(blocks, "dp", split_axis=0, concat_axis=0, tiled=True)
    pieces = sketch(meta, seeds, count, grads, sketch_width)
    pieces = [pieces[0]] + [over_proj(pieces[rel], rel) for rel in (1, 2, 3)]

    device_count = seq_count * proj_count
    total, lines = tally(meta, device_count, arrived, target_gradient_sketches, pieces, losses)
    lines = lax.all_to_all(lines, ("dp", "proj"), split_axis=0, concat_axis=0, tiled=True)
    params = (
        transposed(adapter_down_maps),
        adapter_up_maps,
        transposed(down_first_moment),
        up_first_moment,
        transposed(down_second_moment),
        up_second_moment,
    )
    loss_parts, grad_norm, influence, dw, uw, dm, um, ds, us = finish(
        meta, proj_count, target_gradient_sketches.shape[0], count, lines, total, params
    )
    return (
        loss_parts,
        grad_norm,
        influence,
        transposed(dw),
        uw,
        transposed(dm),
        um,
        transposed(ds),
        us,
    )


def solution(mesh):
    in_specs = (
        P("dp", None),
        P("dp"),
        P(),
        P(),
        P(None, None, "proj"),
        P("proj", None),
        P(None, "proj"),
        P("proj", None),
        P(None, "proj"),
        P(None, "proj", "dp"),
        P(None, "dp", "proj"),
        P(None, "proj", "dp"),
        P(None, "dp", "proj"),
        P(None, "proj", "dp"),
        P(None, "dp", "proj"),
        P(None, None, "proj", None),
        P(),
    )
    out_specs = (
        P(),
        P(),
        P("dp"),
        P(None, "proj", "dp"),
        P(None, "dp", "proj"),
        P(None, "proj", "dp"),
        P(None, "dp", "proj"),
        P(None, "proj", "dp"),
        P(None, "dp", "proj"),
    )
    return jax.shard_map(
        partial(on_device, mesh.shape["dp"], mesh.shape["proj"]),
        mesh=mesh,
        in_specs=in_specs,
        out_specs=out_specs,
        check_vma=False,
    )
```

```python
from functools import partial
import math

import jax
import jax.numpy as jnp
import numpy as np
from jax import lax
from jax.experimental import pallas as pl
from jax.experimental.pallas import tpu as pltpu
from jax.sharding import PartitionSpec as P

HEAD = 64
ROT = 16
STEP = 10

EPS_NORM = 1e-05
ADAPTER_SCALE = 0.25
CLIP_NORM = 0.05
LEARN_RATE = 0.05
BETA_ONE = 0.9
BETA_TWO = 0.99
ADAM_EPS = 1e-08
WEIGHT_DECAY = 0.01

BF = jnp.bfloat16
F32 = jnp.float32
BLOCK = 256
UNIT = 512
TILE_V = 2560
CHUNK_V = 512
MIB = 2**20

PROJ, SEQ = range(2)


def core_of(meta):
    return meta[PROJ] & 1


def ybit_of(meta):
    return meta[PROJ] >> 1


def token_count(lens_ref):
    return sum(lens_ref[i] for i in range(lens_ref.shape[0])).astype(F32)


def dot_nn(lhs, rhs):
    return lax.dot_general(lhs, rhs, (((1,), (0,)), ((), ())), preferred_element_type=F32)


def dot_nt(lhs, rhs):
    return lax.dot_general(lhs, rhs, (((1,), (1,)), ((), ())), preferred_element_type=F32)


def dot_tn(lhs, rhs):
    return lax.dot_general(lhs, rhs, (((0,), (0,)), ((), ())), preferred_element_type=F32)


def kernel_call(
    body, name, grid, in_specs, out_specs, out_shape, scratch=(), flops=0, moved=0, after=(),
    vmem=24,
):
    inputs = len(in_specs) + 1
    extra = len(after)

    def run(*refs):
        body(*refs[:inputs], *refs[inputs + extra :])

    call = pl.pallas_call(
        run,
        grid_spec=pltpu.PrefetchScalarGridSpec(
            num_scalar_prefetch=1,
            grid=grid,
            in_specs=list(in_specs) + [pl.BlockSpec(memory_space=pl.ANY)] * extra,
            out_specs=out_specs,
            scratch_shapes=list(scratch),
        ),
        out_shape=out_shape,
        compiler_params=pltpu.CompilerParams(vmem_limit_bytes=vmem * MIB),
        cost_estimate=pl.CostEstimate(flops=flops, bytes_accessed=moved, transcendentals=0),
        name=name,
    )
    return lambda *args: call(*args, *after)


def whole(shape):
    zeros = (0,) * len(shape)
    return pl.BlockSpec(shape, lambda *_: zeros)


def slot(array, index):
    place = (index,) + (0,) * (len(array.shape) - 1)
    return pl.BlockSpec((1, *array.shape[1:]), lambda *_: place)


def by_slots(arrays):
    return [slot(array, rel & 1) for rel, array in enumerate(arrays)]


SCALARS = pl.BlockSpec(memory_space=pltpu.SMEM)


def sds(shape, dtype):
    return jax.ShapeDtypeStruct(shape, dtype)


def normalize(rows):
    center = rows - jnp.mean(rows, axis=-1, keepdims=True)
    spread = jnp.mean(center * center, axis=-1, keepdims=True)
    return center * lax.rsqrt(spread + EPS_NORM)


def columns(index, size):
    return pl.ds(pl.multiple_of(index * size, size), size)


def pack_body(meta, down_ref, up_ref, out_ref):
    mats = down_ref.shape[0]
    down, up = down_ref[...].astype(BF), up_ref[...].astype(BF)
    for dest in range(out_ref.shape[0]):
        out_ref[dest, 0] = down[mats - 1]
        out_ref[dest, 1] = up[mats - 1]
        out_ref[dest, 2 : mats + 1] = down[: mats - 1]
        out_ref[dest, mats + 1 :] = up[: mats - 1]


def pack_maps(meta, seq_count, down, up):
    shape = (seq_count, 2 * down.shape[0], *down.shape[1:])
    return kernel_call(
        pack_body, "pack_maps", (1,),
        [whole(down.shape), whole(up.shape)], whole(shape), sds(shape, BF),
        moved=8 * down.size,
    )(meta, down, up)


def unpack_body(meta, got_ref, out_ref, up_ref):
    count, _, size, _ = got_ref.shape
    for block in range(count):
        here = slice(block * size, (block + 1) * size)
        out_ref[:, here, :] = got_ref[block, 0:5]
        up_ref[:, here, :] = got_ref[block, 5:8]


def unpack_maps(meta, got):
    count, mats, size, shard = got.shape
    rank = count * size
    if size % 16:
        maps = jnp.transpose(got, (1, 0, 2, 3)).reshape(mats, rank, shard)
        return maps[:5], maps[5:]
    return kernel_call(
        unpack_body, "unpack_maps", (1,),
        [whole(got.shape)], [whole((5, rank, shard)), whole((3, rank, shard))],
        [sds((5, rank, shard), BF), sds((3, rank, shard), BF)],
        moved=4 * got.size,
    )(meta, got)


def side_sum(refs):
    one_ref, two_ref, out_ref = refs
    out_ref[...] = (one_ref[...].astype(F32) + two_ref[...].astype(F32)).astype(BF)


def ffn_body(unit, meta, x_ref, gain_ref, up_ref, down_ref, *refs):
    if unit == 0:
        mine_ref, sib_ref, low_ref, part_ref = refs
    else:
        one_ref, two_ref, mine_ref, sib_ref, sum_ref, low_ref, part_ref = refs
    step = pl.program_id(0)

    @pl.when(step == 0)
    def _():
        hat = normalize(x_ref[...].astype(F32))
        low_ref[...] = (hat * gain_ref[1:2, :]).astype(BF)
        part_ref[...] = jnp.zeros_like(part_ref)
        if unit:
            side_sum((one_ref, two_ref, sum_ref))

    hidden = dot_nn(low_ref[...], up_ref[...])
    hidden = 0.5 * hidden * (1.0 + lax.erf(hidden * (0.5**0.5)))
    part_ref[...] += dot_nn(hidden.astype(BF), down_ref[...])

    @pl.when(step == pl.num_programs(0) - 1)
    def _():
        core = core_of(meta)
        mine_ref[...] = part_ref[columns(core, BLOCK), :].astype(BF)
        sib_ref[...] = part_ref[columns(1 - core, BLOCK), :].astype(BF)


def ffn(meta, unit, x, gains, w_up, w_down, sums=(), after=()):
    rows, width = x.shape
    chunk = 512
    half = sds((BLOCK, width), BF)
    results = 2 + len(sums) // 2
    return kernel_call(
        partial(ffn_body, unit),
        f"ffn_{unit}",
        (w_up.shape[1] // chunk,),
        [
            pl.BlockSpec((UNIT, width), lambda i, m: (unit, 0)),
            whole(gains.shape),
            pl.BlockSpec((width, chunk), lambda i, m: (0, i)),
            pl.BlockSpec((chunk, width), lambda i, m: (i, 0)),
        ]
        + [whole((BLOCK, width))] * len(sums),
        [whole((BLOCK, width))] * results,
        [half] * results,
        [pltpu.VMEM((UNIT, width), BF), pltpu.VMEM((UNIT, width), F32)],
        flops=4 * UNIT * width * w_up.shape[1],
        moved=4 * w_up.size + 8 * UNIT * width,
        after=after,
    )(meta, x, gains, w_up, w_down, *sums)


def qkv_body(meta, x_ref, gain_ref, w_ref, low_ref, out_ref):
    hat = normalize(x_ref[...].astype(F32))
    low = (hat * gain_ref[0:1, :]).astype(BF)
    low_ref[...] = low
    shard = w_ref.shape[2]
    for k in range(3):
        out_ref[:, k * shard : (k + 1) * shard] = dot_nn(low, w_ref[k])


def frozen_qkv(meta, x, gains, w_qkv, after=()):
    rows, width = x.shape
    out = 3 * w_qkv.shape[2]
    return kernel_call(
        qkv_body,
        "frozen_qkv",
        (rows // UNIT,),
        [
            pl.BlockSpec((UNIT, width), lambda i, m: (i, 0)),
            whole(gains.shape),
            whole(w_qkv.shape),
        ],
        [
            pl.BlockSpec((UNIT, width), lambda i, m: (i, 0)),
            pl.BlockSpec((UNIT, out), lambda i, m: (i, 0)),
        ],
        [sds((rows, width), BF), sds((rows, out), F32)],
        flops=2 * rows * width * out,
        moved=2 * w_qkv.size + 4 * x.size + 4 * rows * out,
        after=after,
    )(meta, x, gains, w_qkv)


def rotary_tables(rows, shard):
    half = ROT // 2
    freq = np.exp(np.arange(half) * (-2.0 * math.log(10000.0) / ROT))
    angles = np.arange(rows)[:, None] * freq[None, :]
    cos, sin = np.cos(angles), np.sin(angles)
    one = np.ones((rows, HEAD))
    one[:, :half] = cos
    one[:, half:ROT] = cos
    up = np.zeros((rows, HEAD))
    up[:, half:ROT] = sin
    down = np.zeros((rows, HEAD))
    down[:, :half] = sin
    heads = min(shard, 128) // HEAD
    return [jnp.asarray(np.tile(table, (1, heads)), F32) for table in (one, up, down)]


def across(table, width):
    return jnp.concatenate([table] * (width // table.shape[1]), axis=1)


def turn(rows, cos, up, down, sign):
    half = ROT // 2
    width = rows.shape[1]
    from_low = pltpu.roll(rows, half, 1)
    from_high = pltpu.roll(rows, width - half, 1)
    cos, up, down = (across(table, width) for table in (cos, up, down))
    return rows * cos + sign * (from_low * up - from_high * down)


def pre_body(
    meta, low_ref, qkv_ref, cos_ref, up_ref, down_ref,
    m_own, m_sib, m_y, m_far, ups, one_ref, two_ref,
    q_ref, k_ref, v_ref, rank_ref, sum_ref,
):
    @pl.when(pl.program_id(0) == 0)
    def _():
        side_sum((one_ref, two_ref, sum_ref))

    proj = meta[PROJ]
    shard = q_ref.shape[1]
    rank = m_own.shape[1]
    total = None
    for rel, piece in enumerate((m_own, m_sib, m_y, m_far)):
        low = low_ref[:, columns(proj ^ rel, shard)]
        part = dot_nt(low, piece[2:5].reshape(3 * rank, shard))
        total = part if total is None else total + part
    rank_in = total.astype(BF)
    rank_ref[...] = rank_in
    pre = [
        qkv_ref[:, k * shard : (k + 1) * shard]
        + ADAPTER_SCALE * dot_nn(rank_in[:, k * rank : (k + 1) * rank], ups[k])
        for k in range(3)
    ]
    tables = (cos_ref[...], up_ref[...], down_ref[...])
    q_ref[...] = turn(pre[0], *tables, 1.0).astype(BF)
    k_ref[...] = turn(pre[1], *tables, 1.0).astype(BF)
    v_ref[...] = pre[2].astype(BF)


def make_qkv(meta, low, qkv, tables, maps, ups, sums, after=()):
    rows, width = low.shape
    shard = qkv.shape[1] // 3
    rank = ups.shape[1]
    block = lambda cols: pl.BlockSpec((UNIT, cols), lambda i, m: (i, 0))
    return kernel_call(
        pre_body,
        "adapter_qkv",
        (rows // UNIT,),
        [block(width), block(3 * shard)]
        + [block(tables[0].shape[1])] * 3
        + [whole(one.shape) for one in (*maps, ups, *sums)],
        [block(shard)] * 3 + [block(3 * rank), whole((BLOCK, width))],
        [sds((rows, shard), BF)] * 3 + [sds((rows, 3 * rank), BF), sds((BLOCK, width), BF)],
        flops=2 * rows * width * 3 * rank,
        moved=rows * (2 * width + 24 * shard),
        after=after,
    )(meta, low, qkv, *tables, *maps, ups, *sums)


def head_mask(shard, head):
    return lax.broadcasted_iota(jnp.int32, (1, shard), 1) // HEAD == head


def diagonal():
    rows = lax.broadcasted_iota(jnp.int32, (BLOCK, BLOCK), 0)
    cols = lax.broadcasted_iota(jnp.int32, (BLOCK, BLOCK), 1)
    return rows >= cols


def block_scores(query, k_ref, prev, causal):
    scale = HEAD**-0.5
    diag = dot_nt(query, k_ref[prev : prev + BLOCK, :]) * scale
    diag = jnp.where(causal, diag, -1e30)
    if prev == 0:
        return diag
    return jnp.concatenate([dot_nt(query, k_ref[0:prev, :]) * scale, diag], axis=1)


def attend_body(unit, meta, q_ref, k_ref, v_ref, out_ref, lse_ref):
    shard = q_ref.shape[1]
    causal = diagonal()
    lane = lax.broadcasted_iota(jnp.int32, (BLOCK, 128), 1)
    for half in range(UNIT // BLOCK):
        prev = unit * UNIT + half * BLOCK
        query = q_ref[half * BLOCK : (half + 1) * BLOCK, :]
        out = jnp.zeros((BLOCK, shard), F32)
        lse = jnp.zeros((BLOCK, 128), F32)
        for head in range(shard // HEAD):
            mask = head_mask(shard, head)
            scores = block_scores(jnp.where(mask, query, 0), k_ref, prev, causal)
            top = jnp.max(scores, axis=1, keepdims=True)
            prob = jnp.exp(scores - top)
            total = jnp.sum(prob, axis=1, keepdims=True)
            got = dot_nn(prob.astype(BF), v_ref[0 : prev + BLOCK, :]) / total
            out = jnp.where(mask, got, out)
            lse = jnp.where(lane == head, top + jnp.log(total), lse)
        lse_ref[half * BLOCK : (half + 1) * BLOCK, :] = lse
        out_ref[half ^ core_of(meta)] = out.astype(BF)


def attend(meta, unit, queries, keys, values, after=()):
    shard = queries.shape[1]
    known = (unit + 1) * UNIT
    return kernel_call(
        partial(attend_body, unit),
        f"attend_{unit}",
        (1,),
        [
            pl.BlockSpec((UNIT, shard), lambda i, m: (unit, 0)),
            pl.BlockSpec((known, shard), lambda i, m: (0, 0)),
            pl.BlockSpec((known, shard), lambda i, m: (0, 0)),
        ],
        [whole((2, BLOCK, shard)), whole((UNIT, 128))],
        [sds((2, BLOCK, shard), BF), sds((UNIT, 128), F32)],
        flops=16 * UNIT * known * shard,
        moved=8 * known * shard,
        after=after,
    )(meta, queries, keys, values)


def attend_back_body(unit, meta, *refs):
    shard = refs[4].shape[1]
    (g0, g1, g2, g3, q_ref, k_ref, v_ref, lse_ref, cos_ref, up_ref, down_ref) = refs[:11]
    if unit == 0:
        dq_ref, dk_ref, dv_ref, grad_ref = refs[11:]
        dk_ref[...] = jnp.zeros_like(dk_ref)
        dv_ref[...] = jnp.zeros_like(dv_ref)
    else:
        (dk_in, dv_in, keep_ref, got_ref,
         dq_ref, dk_ref, dv_ref, own_ref, far_ref, grad_ref) = refs[11:]
        dk_ref[...] = dk_in[...]
        dv_ref[...] = dv_in[...]
        own_ref[...] = keep_ref[0].astype(F32) + got_ref[0].astype(F32)
        far_ref[...] = (keep_ref[1].astype(F32) + got_ref[1].astype(F32)).astype(BF)
    core, ybit = core_of(meta), ybit_of(meta)
    quarter = BLOCK // 2
    for rel, piece in enumerate((g0, g1, g2, g3)):
        place = (core ^ (rel & 1)) * 2 + (ybit ^ (rel >> 1))
        grad_ref[columns(place, quarter), :] = piece[0]
    causal = diagonal()
    lane = lax.broadcasted_iota(jnp.int32, (BLOCK, 128), 1)
    scale = HEAD**-0.5
    for half in range(UNIT // BLOCK):
        prev = unit * UNIT + half * BLOCK
        known = prev + BLOCK
        here = slice(half * BLOCK, (half + 1) * BLOCK)
        query = q_ref[here, :]
        grad = grad_ref[here, :]
        lse = lse_ref[here, :]
        dq = jnp.zeros((BLOCK, shard), F32)
        for head in range(shard // HEAD):
            mask = head_mask(shard, head)
            own_q = jnp.where(mask, query, 0)
            own_g = jnp.where(mask, grad, 0)
            own_lse = jnp.sum(jnp.where(lane == head, lse, 0.0), axis=1, keepdims=True)
            prob = jnp.exp(block_scores(own_q, k_ref, prev, causal) - own_lse)
            dweights = dot_nt(own_g, v_ref[0:known, :])
            delta = jnp.sum(prob * dweights, axis=1, keepdims=True)
            dscores = (prob * (dweights - delta)).astype(BF)
            dq = dq + jnp.where(mask, dot_nn(dscores, k_ref[0:known, :]), 0.0)
            dk_ref[0:known, :] += dot_tn(dscores, own_q) * scale
            dv_ref[0:known, :] += dot_tn(prob.astype(BF), own_g)
        dq = turn(dq * scale, cos_ref[here, :], up_ref[here, :], down_ref[here, :], -1.0)
        dq_ref[here, :] = dq.astype(BF)


def attend_back(meta, unit, grads, queries, keys, values, lse, tables, before=(), pair=(), after=()):
    rows, shard = queries.shape
    known = (unit + 1) * UNIT
    unit_rows = pl.BlockSpec((UNIT, shard), lambda i, m: (unit, 0))
    past = pl.BlockSpec((known, shard), lambda i, m: (0, 0))
    sums = whole((rows, shard))
    more = [one.shape[1:] for one in pair[:1]] * 2
    return kernel_call(
        partial(attend_back_body, unit),
        f"attend_back_{unit}",
        (1,),
        by_slots(grads)
        + [unit_rows, past, past, whole((UNIT, 128))]
        + [pl.BlockSpec((UNIT, tables[0].shape[1]), lambda i, m: (unit, 0))] * 3
        + [sums] * len(before)
        + [whole(one.shape) for one in pair],
        [whole((UNIT, shard)), sums, sums] + [whole(one) for one in more],
        [sds((UNIT, shard), BF), sds((rows, shard), F32), sds((rows, shard), F32)]
        + [sds(one, dtype) for one, dtype in zip(more, (F32, BF))],
        [pltpu.VMEM((UNIT, shard), BF)],
        flops=40 * UNIT * known * shard,
        moved=16 * rows * shard,
        after=after,
    )(meta, *grads, queries, keys, values, lse, *tables, *before, *pair)


def mix_body(
    meta, x_ref, gain_ref, f_own, f_far, a0, a1, a2, a3, w0, w1, w2, w3,
    m0, m1, m2, m3, norm_ref, res_ref, rank_ref, keep_ref,
):
    proj = meta[PROJ]
    shard = a0.shape[1]
    rank = None
    for a_ref, m_ref in ((a0, m0), (a1, m1), (a2, m2), (a3, m3)):
        part = dot_nt(a_ref[0], m_ref[0])
        rank = part if rank is None else rank + part
    rank = rank.astype(BF)
    total = x_ref[...].astype(F32) + f_own[...].astype(F32) + f_far[...].astype(F32)
    for a_ref, w_ref in ((a0, w0), (a1, w1), (a2, w2), (a3, w3)):
        total = total + dot_nn(a_ref[0], w_ref[...])
    keep_ref[...] = total
    for rel, m_ref in enumerate((m0, m1, m2, m3)):
        here = columns(proj ^ rel, shard)
        keep_ref[:, here] += ADAPTER_SCALE * dot_nn(rank, m_ref[1])
    residual = keep_ref[...]
    norm_ref[...] = (normalize(residual) * gain_ref[2:3, :]).astype(BF)
    mine = columns(ybit_of(meta), BLOCK // 2)
    res_ref[...] = keep_ref[mine, :]
    keep_ref[:, 0 : rank.shape[1]] = rank.astype(F32)
    rank_ref[...] = keep_ref[mine, 0 : rank.shape[1]].astype(BF)


def mix(meta, unit, x, gains, f_own, f_far, att, wo, maps, after=()):
    rows, width = x.shape
    shard = att[0].shape[2]
    rank = maps[0].shape[1]
    return kernel_call(
        mix_body,
        f"mix_{unit}",
        (1,),
        [
            pl.BlockSpec((BLOCK, width), lambda i, m: (2 * unit + core_of(m), 0)),
            whole(gains.shape),
            whole((BLOCK, width)),
            whole((BLOCK, width)),
        ]
        + by_slots(att)
        + [whole((shard, width))] * 4
        + [whole((2, rank, shard))] * 4,
        [whole((BLOCK, width)), whole((BLOCK // 2, width)), whole((BLOCK // 2, rank))],
        [sds((BLOCK, width), BF), sds((BLOCK // 2, width), F32), sds((BLOCK // 2, rank), BF)],
        [pltpu.VMEM((BLOCK, width), F32)],
        flops=2 * BLOCK * width * width,
        moved=2 * width * width + 8 * BLOCK * width,
        after=after,
    )(meta, x, gains, f_own, f_far, *att, *wo, *maps)


def vocab_grid(vocab):
    steps = -(-vocab // TILE_V)
    return steps, vocab - (steps - 1) * TILE_V


def local_columns(unit, meta, vocab, target_ref, out_ref):
    for group in range(4):
        half = core_of(meta) ^ (group >> 1)
        ids = target_ref[pl.ds((unit * 2 + half) * 2 + (group & 1), 1), :] - meta[PROJ] * vocab
        ids = jnp.where((ids >= 0) & (ids < vocab), ids, -1)
        square = jnp.transpose(jnp.broadcast_to(ids.astype(F32), (128, 128)))
        out_ref[group * 128 : (group + 1) * 128, :] = square.astype(jnp.int32)


def vocab_stats_body(
    unit, vocab, meta, mine_ref, sib_ref, u_ref, target_ref, p_ref, top_ref, st_ref, acc_ref, col_ref
):
    step = pl.program_id(0)
    steps, tail = vocab_grid(vocab)
    chunks = TILE_V // CHUNK_V

    @pl.when(step == 0)
    def _():
        acc_ref[...] = jnp.zeros_like(acc_ref)
        local_columns(unit, meta, vocab, target_ref, col_ref)

    def tile(is_tail):
        col = lax.broadcasted_iota(jnp.int32, (BLOCK, CHUNK_V), 1)
        lane = lax.broadcasted_iota(jnp.int32, (BLOCK, 128), 1)
        for chunk in range(chunks):
            inside = slice(chunk * CHUNK_V, (chunk + 1) * CHUNK_V)
            place = step * chunks + chunk
            for half, rows_ref in enumerate((mine_ref, sib_ref)):
                here = slice(half * BLOCK, (half + 1) * BLOCK)
                logits = dot_nt(rows_ref[...], u_ref[inside, :])
                if is_tail and inside.stop > tail:
                    logits = jnp.where(col < tail - inside.start, logits, -1e30)
                top = jnp.max(logits, axis=1, keepdims=True)
                prob = jnp.exp(logits - top)
                total = jnp.sum(prob, axis=1, keepdims=True)
                hit = col == col_ref[here, 0:1] - place * CHUNK_V
                picked = jnp.sum(jnp.where(hit, logits, 0.0), axis=1, keepdims=True)
                p_ref[here, inside] = prob.astype(BF)
                acc = acc_ref[here, :]
                acc = jnp.where(lane == place, top, acc)
                acc = jnp.where(lane == place + 32, total, acc)
                acc_ref[here, :] = jnp.where(lane == 64, acc + picked, acc)

    @pl.when(step < steps - 1)
    def _():
        tile(False)

    @pl.when(step == steps - 1)
    def _():
        tile(True)
        acc = acc_ref[...]
        lane = lax.broadcasted_iota(jnp.int32, acc.shape, 1)
        top_ref[...] = acc
        tops = jnp.where(lane < steps * chunks, acc, -1e30)
        best = jnp.max(tops, axis=1, keepdims=True)
        totals = pltpu.roll(acc, 128 - 32, 1)
        total = jnp.sum(
            jnp.where(lane < steps * chunks, totals * jnp.exp(tops - best), 0.0),
            axis=1, keepdims=True,
        )
        picked = jnp.sum(jnp.where(lane == 64, acc, 0.0), axis=1, keepdims=True)
        pair = jnp.where(lane == 0, best + jnp.log(total), jnp.where(lane == 1, picked, 0.0))
        st_ref[...] = jnp.transpose(pair)[0:8, :]


def vocab_stats(meta, unit, mine, sib, unembed, targets, after=()):
    vocab, width = unembed.shape
    steps, _ = vocab_grid(vocab)
    rows = 2 * BLOCK
    return kernel_call(
        partial(vocab_stats_body, unit, vocab),
        f"vocab_stats_{unit}",
        (steps,),
        [
            whole((BLOCK, width)),
            whole((BLOCK, width)),
            pl.BlockSpec((TILE_V, width), lambda i, m: (i, 0)),
            whole(targets.shape),
        ],
        [
            pl.BlockSpec((rows, TILE_V), lambda i, m: (0, i)),
            whole((rows, 128)),
            whole((8, rows)),
        ],
        [
            sds((rows, steps * TILE_V), BF),
            sds((rows, 128), F32),
            sds((8, rows), F32),
        ],
        [pltpu.VMEM((rows, 128), F32), pltpu.VMEM((rows, 128), jnp.int32)],
        flops=2 * rows * width * vocab,
        moved=2 * width * vocab + 2 * rows * vocab,
        vmem=40,
        after=after,
    )(meta, mine, sib, unembed, targets)


def swap_halves(pair):
    return jnp.concatenate([pair[:, BLOCK:], pair[:, :BLOCK]], axis=1)


def vocab_back_body(
    vocab, unit, meta, lens_ref, p_ref, u_ref, target_ref, top_ref, s0, s1, s2, s3,
    near_ref, far_ref, loss_ref, scale_ref, acc_ref, col_ref,
):
    step = pl.program_id(0)
    steps, tail = vocab_grid(vocab)
    chunks = TILE_V // CHUNK_V
    rows = 2 * BLOCK

    @pl.when(step == 0)
    def _():
        acc_ref[...] = jnp.zeros_like(acc_ref)
        local_columns(unit, meta, vocab, target_ref, col_ref)
        parts = [s0[...], swap_halves(s1[...]), s2[...], swap_halves(s3[...])]
        lses = [part[0:1, :] for part in parts]
        best = jnp.maximum(jnp.maximum(lses[0], lses[1]), jnp.maximum(lses[2], lses[3]))
        total = sum(jnp.exp(one - best) for one in lses)
        log_norm = best + jnp.log(total)
        picked = sum(part[1:2, :] for part in parts)
        place = lax.broadcasted_iota(jnp.int32, (1, rows), 1)
        core = core_of(meta)
        offset = jnp.where(place < BLOCK, core * BLOCK, (1 - core) * BLOCK - BLOCK)
        valid = (unit * UNIT + place + offset < lens_ref[meta[SEQ]]).astype(F32)
        loss_ref[...] = jnp.broadcast_to(
            jnp.sum((log_norm - picked) * valid, axis=1, keepdims=True), (8, 128)
        )
        weight = valid / token_count(lens_ref)
        row = lax.broadcasted_iota(jnp.int32, (128, rows), 0)
        lines = jnp.where(row == 0, log_norm, 0.0)
        lines = jnp.where(row == 1, weight, lines)
        lines = jnp.where(row == 2, (jnp.exp(picked - log_norm) - 1.0) * weight, lines)
        cols = jnp.transpose(lines)
        lane = lax.broadcasted_iota(jnp.int32, (rows, 128), 1)
        take = lambda k: jnp.sum(jnp.where(lane == k, cols, 0.0), axis=1, keepdims=True)
        tops = jnp.where(lane < steps * chunks, top_ref[...], -1e30)
        scales = jnp.exp(tops - take(0)) * take(1)
        scale_ref[...] = jnp.where(lane == 64, take(2), scales)

    def tile(is_tail):
        u_tile = u_ref[...]
        if is_tail:
            row = lax.broadcasted_iota(jnp.int32, u_tile.shape, 0)
            u_tile = jnp.where(row < tail, u_tile, jnp.zeros_like(u_tile))
        col = lax.broadcasted_iota(jnp.int32, (BLOCK, CHUNK_V), 1)
        lane = lax.broadcasted_iota(jnp.int32, (BLOCK, 128), 1)
        for half in range(2):
            here = slice(half * BLOCK, (half + 1) * BLOCK)
            scales = scale_ref[here, :]
            at_hit = jnp.sum(jnp.where(lane == 64, scales, 0.0), axis=1, keepdims=True)
            for chunk in range(chunks):
                inside = slice(chunk * CHUNK_V, (chunk + 1) * CHUNK_V)
                place = step * chunks + chunk
                scale = jnp.sum(jnp.where(lane == place, scales, 0.0), axis=1, keepdims=True)
                hit = col == col_ref[here, 0:1] - place * CHUNK_V
                grad = jnp.where(hit, at_hit, p_ref[here, inside].astype(F32) * scale)
                acc_ref[here, :] += dot_nn(grad.astype(BF), u_tile[inside, :])

    @pl.when(step < steps - 1)
    def _():
        tile(False)

    @pl.when(step == steps - 1)
    def _():
        tile(True)
        quarter = BLOCK // 2
        for rel in range(4):
            place = (rel & 1) * 2 + (ybit_of(meta) ^ (rel >> 1))
            dest = (near_ref, far_ref)[rel >> 1]
            dest[rel & 1] = acc_ref[columns(place, quarter), :].astype(BF)


def vocab_back(meta, unit, lens, prob, unembed, targets, tops, stats, after=()):
    vocab, width = unembed.shape
    steps, _ = vocab_grid(vocab)
    rows = 2 * BLOCK
    pair = (2, BLOCK // 2, width)
    return kernel_call(
        partial(vocab_back_body, vocab, unit),
        f"vocab_back_{unit}",
        (steps,),
        [
            SCALARS,
            pl.BlockSpec((rows, TILE_V), lambda i, m: (0, i)),
            pl.BlockSpec((TILE_V, width), lambda i, m: (i, 0)),
            whole(targets.shape),
            whole((rows, 128)),
        ]
        + [whole((8, rows))] * 4,
        [whole(pair), whole(pair), whole((8, 128))],
        [sds(pair, BF), sds(pair, BF), sds((8, 128), F32)],
        [
            pltpu.VMEM((rows, 128), F32),
            pltpu.VMEM((rows, width), F32),
            pltpu.VMEM((rows, 128), jnp.int32),
        ],
        flops=2 * rows * width * vocab,
        moved=2 * width * vocab + 2 * rows * vocab,
        vmem=40,
        after=after,
    )(meta, lens, prob, unembed, targets, tops, *stats)


def norm_back_body(last, meta, *refs):
    parts, (res_ref, gain_ref, rank_ref) = refs[:4], refs[4:7]
    atts, wos, maps = refs[7:11], refs[11:15], refs[15:19]
    if last:
        before_ref, near_ref, far_ref, keep_ref, send_ref, hold_ref = refs[19:]
    else:
        near_ref, far_ref, sum_ref, hold_ref = refs[19:]
    proj = meta[PROJ]
    shard = atts[0].shape[2]
    dnormed = sum(part[0].astype(F32) for part in parts)
    residual = res_ref[...]
    center = residual - jnp.mean(residual, axis=-1, keepdims=True)
    spread = jnp.mean(center * center, axis=-1, keepdims=True)
    inv = lax.rsqrt(spread + EPS_NORM)
    hat = center * inv
    dhat = dnormed * gain_ref[2:3, :]
    dres = inv * (
        dhat
        - jnp.mean(dhat, axis=-1, keepdims=True)
        - hat * jnp.mean(dhat * hat, axis=-1, keepdims=True)
    )
    hold_ref[...] = dres.astype(BF)
    dbranch = hold_ref[...]
    drank = None
    for rel, m_ref in enumerate(maps):
        part = dot_nt(hold_ref[:, columns(proj ^ rel, shard)], m_ref[1])
        drank = part if drank is None else drank + part
    drank = (ADAPTER_SCALE * drank).astype(BF)
    for rel in range(4):
        datt = dot_nt(dbranch, wos[rel][...]) + dot_nn(drank, maps[rel][0])
        (near_ref, far_ref)[rel >> 1][rel & 1] = datt.astype(BF)
        g_down = dot_tn(drank, atts[rel][0])
        g_up = ADAPTER_SCALE * dot_tn(rank_ref[...], hold_ref[:, columns(proj ^ rel, shard)])
        if last:
            dest = (keep_ref, send_ref)[rel & 1]
            dest[rel >> 1, 0] = (before_ref[rel, 0] + g_down).astype(BF)
            dest[rel >> 1, 1] = (before_ref[rel, 1] + g_up).astype(BF)
        else:
            sum_ref[rel, 0] = g_down
            sum_ref[rel, 1] = g_up


def norm_back(meta, unit, last, parts, residual, gains, rank_out, att, wo, maps, before, after=()):
    quarter, width = residual.shape
    shard = att[0].shape[2]
    rank = rank_out.shape[1]
    pair = (2, quarter, shard)
    if last:
        more = [sds((2, 2, rank, shard), BF)] * 2
    else:
        more = [sds((4, 2, rank, shard), F32)]
    return kernel_call(
        partial(norm_back_body, last),
        f"norm_back_{unit}",
        (1,),
        by_slots(parts)
        + [whole(residual.shape), whole(gains.shape), whole(rank_out.shape)]
        + [
            pl.BlockSpec((1, quarter, shard), partial(lambda rel, i, m: (rel & 1, ybit_of(m), 0), rel))
            for rel in range(4)
        ]
        + [whole((shard, width))] * 4
        + [whole((2, rank, shard))] * 4
        + [whole(one.shape) for one in before],
        [whole(pair)] * 2 + [whole(one.shape) for one in more],
        [sds(pair, BF)] * 2 + more,
        [pltpu.VMEM((quarter, width), BF)],
        flops=2 * quarter * width * width,
        moved=2 * width * width + 12 * quarter * width,
        after=after,
    )(meta, *parts, residual, gains, rank_out, *att, *wo, *maps, *before)


def grads_body(
    meta, dq0, dq1, dk_ref, dv_ref, cos_ref, up_ref, down_ref, rank_ref, ups, low_ref,
    keep_ref, send_ref, up_grad_ref, drank_ref,
):
    proj = meta[PROJ]
    rank, shard = ups.shape[1:]
    dk = turn(dk_ref[...], cos_ref[...], up_ref[...], down_ref[...], -1.0).astype(BF)
    dpre = [jnp.concatenate([dq0[...], dq1[...]], axis=0), dk, dv_ref[...].astype(BF)]
    for k in range(3):
        here = slice(k * rank, (k + 1) * rank)
        up_grad_ref[k] = ADAPTER_SCALE * dot_tn(rank_ref[:, here], dpre[k])
        drank_ref[:, here] = (ADAPTER_SCALE * dot_nt(dpre[k], ups[k])).astype(BF)
    drank = drank_ref[...]
    for rel in range(4):
        grad = dot_tn(drank, low_ref[:, columns(proj ^ rel, shard)])
        dest = (keep_ref, send_ref)[rel & 1]
        dest[rel >> 1] = grad.reshape(3, rank, shard).astype(BF)


def adapter_grads(meta, dqs, dk, dv, tables, rank_in, ups, low):
    rows, shard = dk.shape
    rank = ups.shape[1]
    pair = (2, 3, rank, shard)
    args = (*dqs, dk, dv, *tables, rank_in, ups, low)
    return kernel_call(
        grads_body,
        "adapter_grads",
        (1,),
        [whole(one.shape) for one in args],
        [whole(pair), whole(pair), whole((3, rank, shard))],
        [sds(pair, BF), sds(pair, BF), sds((3, rank, shard), F32)],
        [pltpu.VMEM((rows, 3 * rank), BF)],
        flops=2 * rows * low.shape[1] * 3 * rank,
        moved=30 * rows * shard,
    )(meta, *args)


def signs(row_ids, col_ids, seed):
    hashed = row_ids * 1640531527 + col_ids * 747796405 + seed * 277803737
    hashed = hashed ^ hashed >> 15 & 131071
    hashed = hashed * 2024237689
    hashed = hashed ^ hashed >> 13 & 524287
    return 1.0 - 2.0 * (hashed >> 17 & 1).astype(F32)


def sketch_one(meta, seed, grad, sketch):
    rank, shard = grad.shape
    left_rows = lax.broadcasted_iota(jnp.int32, (sketch, shard), 1) + meta[PROJ] * shard
    left_cols = lax.broadcasted_iota(jnp.int32, (sketch, shard), 0)
    right_rows = lax.broadcasted_iota(jnp.int32, (rank, sketch), 0)
    right_cols = lax.broadcasted_iota(jnp.int32, (rank, sketch), 1)
    left = signs(left_rows, left_cols, 2 * seed).astype(BF)
    right = signs(right_rows, right_cols, 2 * seed + 1)
    return jnp.dot(dot_nt(left, grad), right, precision=lax.Precision.HIGHEST)


def local_sketch_body(meta, seeds_ref, lens_ref, own_ref, far_ref, up_ref, block_ref, full_ref):
    size = block_ref.shape[2]
    count = token_count(lens_ref)
    out = own_ref[...] + far_ref[...].astype(F32)
    for place, grad in enumerate((out[0], up_ref[0], up_ref[1], up_ref[2], out[1])):
        for dest in range(block_ref.shape[0]):
            block_ref[dest, place] = grad[dest * size : (dest + 1) * size].astype(BF)
        full_ref[place] = count * sketch_one(
            meta, seeds_ref[3 + place], grad.astype(BF), full_ref.shape[1]
        )


def local_sketch(meta, seeds, lens, own, far, ups, sketch_width):
    _, rank, shard = own.shape
    count = lens.shape[0]
    blocks = (count, 5, rank // count, shard)
    full = (5, sketch_width, sketch_width)
    return kernel_call(
        local_sketch_body, "local_sketch", (1,),
        [SCALARS, SCALARS, whole(own.shape), whole(far.shape), whole(ups.shape)],
        [whole(blocks), whole(full)],
        [sds(blocks, BF), sds(full, F32)],
        flops=10 * rank * shard * sketch_width,
        moved=16 * own.size,
    )(meta, seeds, lens, own, far, ups)


def gather_body(meta, keep_ref, got_ref, far_ref, five_ref, block_ref, grad_ref):
    size = block_ref.shape[2]
    total = keep_ref[0].astype(F32) + got_ref[0].astype(F32) + far_ref[...].astype(F32)
    grad_ref[...] = total.astype(BF)
    for dest in range(block_ref.shape[0]):
        for mat in range(3):
            block_ref[dest, mat] = total[mat, dest * size : (dest + 1) * size].astype(BF)
        block_ref[dest, 3:8] = five_ref[dest]


def gather_blocks(meta, keep, got, far, five):
    count, _, size, shard = five.shape
    blocks = (count, 8, size, shard)
    pair = pl.BlockSpec((1, *keep.shape[1:]), lambda i, m: (0, 0, 0, 0))
    return kernel_call(
        gather_body, "gather_blocks", (1,),
        [pair, pair, whole(far.shape), whole(five.shape)],
        [whole(blocks), whole(far.shape)],
        [sds(blocks, BF), sds(far.shape, BF)],
        moved=16 * far.size,
    )(meta, keep, got, far, five)


def sketch_body(meta, seeds_ref, lens_ref, grad_ref, five_ref, near_ref, far_ref, full_ref):
    count = token_count(lens_ref)
    sketch = full_ref.shape[1]
    full_ref[3:8] = five_ref[...]
    for mat in range(3):
        full_ref[mat] = count * sketch_one(meta, seeds_ref[mat], grad_ref[mat], sketch)
    size = sketch // 4
    for rel in range(4):
        dest = (near_ref, far_ref)[rel >> 1]
        dest[rel & 1] = full_ref[:, columns(meta[PROJ] ^ rel, size), :]


def sketch(meta, seeds, lens, grads, five):
    sketch_width = five.shape[1]
    pair = (2, 8, sketch_width // 4, sketch_width)
    return kernel_call(
        sketch_body, "sketch", (1,),
        [SCALARS, SCALARS, whole(grads.shape), whole(five.shape)],
        [whole(pair)] * 2,
        [sds(pair, F32)] * 2,
        [pltpu.VMEM((8, sketch_width, sketch_width), F32)],
        flops=2 * grads.size * sketch_width,
        moved=2 * grads.size,
    )(meta, seeds, lens, grads, five)


def lane_value(row, lane, place):
    return jnp.sum(jnp.where(lane == place, row, 0.0), axis=1, keepdims=True)


def tally_body(
    units, meta, got_ref, target_ref, f0, f1, f2, f3, *refs
):
    losses, (total_ref, line_ref) = refs[:units], refs[units:]
    total = jnp.sum(got_ref[...].astype(F32), axis=0)
    total_ref[...] = total
    features = f0[0] + f1[0] + f2[0] + f3[0]
    squares = jnp.sum(total * total)
    own = jnp.sum(features * features)
    loss = sum(jnp.sum(one[0:1, 0:1]) for one in losses)
    loss = jnp.where(meta[PROJ] == 0, loss, 0.0)
    lane = lax.broadcasted_iota(jnp.int32, (1, 128), 1)
    line = jnp.where(lane == 0, squares, 0.0)
    line = jnp.where(lane == 1, loss, line)
    line = jnp.where(lane == 2, own, line)
    checkpoints = target_ref.shape[0]
    for c in range(checkpoints):
        theirs = target_ref[c]
        line = jnp.where(lane == 3 + c, jnp.sum(features * theirs), line)
        line = jnp.where(lane == 3 + checkpoints + c, jnp.sum(theirs * theirs), line)
    line_ref[...] = jnp.broadcast_to(line, line_ref.shape)


def tally(meta, devices, got, targets, pieces, losses):
    _, mats, slice_rank, shard = got.shape
    args = (got, targets, *pieces, *losses)
    return kernel_call(
        partial(tally_body, len(losses)),
        "tally",
        (1,),
        [whole(got.shape), whole(targets.shape)]
        + by_slots(pieces)
        + [whole(one.shape) for one in losses],
        [whole((mats, slice_rank, shard)), whole((devices, 128))],
        [sds((mats, slice_rank, shard), F32), sds((devices, 128), F32)],
        flops=got.size,
        moved=4 * got.size,
    )(meta, *args)


def optimizer_step(weight, grad_in, first_in, second_in, clipping_scale):
    grad_clip = grad_in * clipping_scale
    first_new = BETA_ONE * first_in + (1.0 - BETA_ONE) * grad_clip
    second_new = BETA_TWO * second_in + (1.0 - BETA_TWO) * grad_clip * grad_clip
    first_hat = first_new / (1.0 - BETA_ONE**STEP)
    second_hat = second_new / (1.0 - BETA_TWO**STEP)
    new_weight = weight - LEARN_RATE * (
        first_hat / (jnp.sqrt(second_hat) + ADAM_EPS) + WEIGHT_DECAY * weight
    )
    return (new_weight, first_new, second_new)


def finish_body(
    proj_count, checkpoints, meta, lens_ref, lines_ref, total_ref,
    dw, uw, dm, um, ds, us,
    loss_out, norm_out, influence_out, dw_out, uw_out, dm_out, um_out, ds_out, us_out,
):
    lines = lines_ref[...]
    everyone = jnp.sum(lines, axis=0, keepdims=True)
    row = lax.broadcasted_iota(jnp.int32, lines.shape, 0)
    ours = jnp.sum(
        jnp.where(row // proj_count == meta[SEQ], lines, 0.0), axis=0, keepdims=True
    )
    lane = lax.broadcasted_iota(jnp.int32, (1, 128), 1)
    grad_norm = jnp.sqrt(lane_value(everyone, lane, 0))
    own = lane_value(ours, lane, 2)
    influence = jnp.zeros((1, 1), F32)
    for c in range(checkpoints):
        dot = lane_value(ours, lane, 3 + c)
        theirs = lane_value(ours, lane, 3 + checkpoints + c)
        influence += (1.0 - c / checkpoints) * dot * lax.rsqrt(own * theirs + 1e-12)
    loss_out[0] = jnp.sum(lane_value(everyone, lane, 1))
    loss_out[1] = token_count(lens_ref)
    norm_out[0] = jnp.sum(grad_norm)
    influence_out[0] = jnp.sum(influence)
    clip = jnp.minimum(1.0, CLIP_NORM / (grad_norm + 1e-06))
    half = total_ref.shape[0] // 2
    for base, ins, outs in (
        (0, (dw, dm, ds), (dw_out, dm_out, ds_out)),
        (half, (uw, um, us), (uw_out, um_out, us_out)),
    ):
        for k in range(half):
            new = optimizer_step(
                ins[0][k], total_ref[base + k], ins[1][k], ins[2][k], clip
            )
            for out, value in zip(outs, new):
                out[k] = value


def finish(meta, proj_count, checkpoints, lens, lines, total, params):
    block = whole(params[0].shape)
    return kernel_call(
        partial(finish_body, proj_count, checkpoints),
        "finish",
        (1,),
        [SCALARS, whole(lines.shape), whole(total.shape)] + [block] * 6,
        [SCALARS] * 3 + [block] * 6,
        [sds((2,), F32), sds((1,), F32), sds((1,), F32)] + [sds(params[0].shape, F32)] * 6,
        flops=20 * total.size,
        moved=28 * total.size,
    )(meta, lens, lines, total, *params)


def to_partner(array, axis, size, offset):
    return lax.ppermute(array, axis, [(i, i ^ offset) for i in range(size)])


def on_device(
    seq_count,
    proj_count,
    inputs,
    targets,
    lengths,
    norm_gain_vectors,
    query_key_value_weight,
    attention_output_weight,
    feedforward_input_weight,
    feedforward_output_weight,
    unembed,
    adapter_down_maps,
    adapter_up_maps,
    down_first_moment,
    up_first_moment,
    down_second_moment,
    up_second_moment,
    target_gradient_sketches,
    seeds,
):
    rows, width = inputs.shape
    shard = attention_output_weight.shape[0]
    vocab_local = unembed.shape[1]
    slice_rank = adapter_up_maps.shape[1]
    rank = slice_rank * seq_count
    sketch_width = target_gradient_sketches.shape[3]
    proj = lax.axis_index("proj")
    seq = lax.axis_index("dp")
    units = rows // UNIT

    over_proj = lambda array, rel: to_partner(array, "proj", proj_count, rel)
    over_seq = lambda array, rel: to_partner(array, "dp", seq_count, rel)

    meta = jnp.stack([proj, seq]).astype(jnp.int32)
    targets = targets.reshape(rows // 128, 128)
    table = jnp.transpose(unembed)
    tables = rotary_tables(rows, shard)
    transposed = lambda array: jnp.transpose(array, (0, 2, 1))

    def from_all(near, far=None):
        y = over_proj(near if far is None else far, 2)
        return (near, over_proj(near, 1), y, over_proj(y, 1))

    packed = pack_maps(meta, seq_count, transposed(adapter_down_maps), adapter_up_maps)
    maps, ups = unpack_maps(
        meta, lax.all_to_all(packed, "dp", split_axis=0, concat_axis=0, tiled=True)
    )
    maps = from_all(maps)
    wo = from_all(attention_output_weight)

    w_ffn = (feedforward_input_weight, feedforward_output_weight)
    f0_mine, f0_sib = ffn(meta, 0, inputs, norm_gain_vectors, *w_ffn)
    low, qkv = frozen_qkv(
        meta, inputs, norm_gain_vectors, jnp.transpose(query_key_value_weight, (1, 0, 2)),
        (f0_mine,),
    )
    f1_mine, f1_sib, f0_chip = ffn(
        meta, 1, inputs, norm_gain_vectors, *w_ffn, (f0_mine, over_proj(f0_sib, 1)), (maps[0],)
    )
    queries, keys, values, rank_in, f1_chip = make_qkv(
        meta, low, qkv, tables, maps, ups, (f1_mine, over_proj(f1_sib, 1))
    )
    f_chip = (f0_chip, f1_chip)
    f_far = [over_proj(one, 2) for one in f_chip]

    att, lse = [None, None], [None, None]
    for unit in range(2):
        out, lse[unit] = attend(meta, unit, queries, keys, values, (lse[0],) if unit else ())
        att[unit] = from_all(out)

    def mix_unit(unit, after):
        normed, residual, rank_out = mix(
            meta, unit, inputs, norm_gain_vectors, f_chip[unit], f_far[unit], att[unit], wo, maps, after
        )
        return (normed, over_proj(normed, 1)), residual, rank_out

    def stats_unit(unit, normed, after):
        prob, top, stat = vocab_stats(meta, unit, *normed, table, targets, after)
        return prob, top, from_all(stat)

    def back_unit(unit, prob, top, stats, after):
        near, far, loss = vocab_back(meta, unit, lengths, prob, table, targets, top, stats, after)
        return from_all(near, far), loss

    def norm_unit(unit, parts, residual, rank_out, before, after):
        near, far, *grads = norm_back(
            meta, unit, unit == 1, parts, residual, norm_gain_vectors,
            rank_out, att[unit], wo, maps, before, after,
        )
        return from_all(near, far), grads

    normed0, residual0, rank0 = mix_unit(0, (lse[1],))
    prob0, top0, stats0 = stats_unit(0, normed0, ())
    normed1, residual1, rank1 = mix_unit(1, (stats0[0],))
    dnormed0, loss0 = back_unit(0, prob0, top0, stats0, (rank1,))
    prob1, top1, stats1 = stats_unit(1, normed1, (loss0,))
    datt0, out_grads = norm_unit(0, dnormed0, residual0, rank0, (), (stats1[0],))
    dnormed1, loss1 = back_unit(1, prob1, top1, stats1, (datt0[0],))
    dq0, dk, dv = attend_back(
        meta, 0, datt0, queries, keys, values, lse[0], tables, after=(loss1,)
    )
    datt1, (out_keep, out_send) = norm_unit(1, dnormed1, residual1, rank1, out_grads, (dq0,))
    dq1, dk, dv, out_own, out_far = attend_back(
        meta, 1, datt1, queries, keys, values, lse[1], tables,
        (dk, dv), (out_keep, over_proj(out_send, 1)),
    )
    out_far = over_proj(out_far, 2)

    in_keep, in_send, up_grads = adapter_grads(
        meta, (dq0, dq1), dk, dv, tables, rank_in, ups, low
    )
    in_got = over_proj(in_send, 1)
    in_far = over_proj((in_keep[1].astype(F32) + in_got[1].astype(F32)).astype(BF), 2)
    blocks, five = local_sketch(meta, seeds, lengths, out_own, out_far, up_grads, sketch_width)
    blocks, in_grads = gather_blocks(meta, in_keep, in_got, in_far, blocks)
    arrived = lax.all_to_all(blocks, "dp", split_axis=0, concat_axis=0, tiled=True)
    pieces = from_all(*sketch(meta, seeds, lengths, in_grads, five))

    device_count = seq_count * proj_count
    total, lines = tally(
        meta, device_count, arrived, target_gradient_sketches, pieces, (loss0, loss1)
    )
    lines = lax.all_to_all(lines, ("dp", "proj"), split_axis=0, concat_axis=0, tiled=True)
    params = (
        transposed(adapter_down_maps),
        adapter_up_maps,
        transposed(down_first_moment),
        up_first_moment,
        transposed(down_second_moment),
        up_second_moment,
    )
    loss_parts, grad_norm, influence, dw, uw, dm, um, ds, us = finish(
        meta, proj_count, target_gradient_sketches.shape[0], lengths, lines, total, params
    )
    return (
        loss_parts,
        grad_norm,
        influence,
        transposed(dw),
        uw,
        transposed(dm),
        um,
        transposed(ds),
        us,
    )


def solution(mesh):
    in_specs = (
        P("dp", None),
        P("dp"),
        P(),
        P(),
        P(None, None, "proj"),
        P("proj", None),
        P(None, "proj"),
        P("proj", None),
        P(None, "proj"),
        P(None, "proj", "dp"),
        P(None, "dp", "proj"),
        P(None, "proj", "dp"),
        P(None, "dp", "proj"),
        P(None, "proj", "dp"),
        P(None, "dp", "proj"),
        P(None, None, "proj", None),
        P(),
    )
    out_specs = (
        P(),
        P(),
        P("dp"),
        P(None, "proj", "dp"),
        P(None, "dp", "proj"),
        P(None, "proj", "dp"),
        P(None, "dp", "proj"),
        P(None, "proj", "dp"),
        P(None, "dp", "proj"),
    )
    return jax.shard_map(
        partial(on_device, mesh.shape["dp"], mesh.shape["proj"]),
        mesh=mesh,
        in_specs=in_specs,
        out_specs=out_specs,
        check_vma=False,
    )
```

```python
from functools import partial
import math

import jax
import jax.numpy as jnp
import numpy as np
from jax import lax
from jax.experimental import pallas as pl
from jax.experimental.pallas import tpu as pltpu
from jax.sharding import PartitionSpec as P

HEAD = 64
ROT = 16
STEP = 10

EPS_NORM = 1e-05
ADAPTER_SCALE = 0.25
CLIP_NORM = 0.05
LEARN_RATE = 0.05
BETA_ONE = 0.9
BETA_TWO = 0.99
ADAM_EPS = 1e-08
WEIGHT_DECAY = 0.01

BF = jnp.bfloat16
F32 = jnp.float32
BLOCK = 256
UNIT = 512
TILE_V = 2560
CHUNK_V = 512
MIB = 2**20

PROJ, SEQ = range(2)


def core_of(meta):
    return meta[PROJ] & 1


def ybit_of(meta):
    return meta[PROJ] >> 1


def token_count(lens_ref):
    return sum(lens_ref[i] for i in range(lens_ref.shape[0])).astype(F32)


def dot_nn(lhs, rhs):
    return lax.dot_general(lhs, rhs, (((1,), (0,)), ((), ())), preferred_element_type=F32)


def dot_nt(lhs, rhs):
    return lax.dot_general(lhs, rhs, (((1,), (1,)), ((), ())), preferred_element_type=F32)


def dot_tn(lhs, rhs):
    return lax.dot_general(lhs, rhs, (((0,), (0,)), ((), ())), preferred_element_type=F32)


def kernel_call(
    body, name, grid, in_specs, out_specs, out_shape, scratch=(), flops=0, moved=0, after=(),
    vmem=24,
):
    inputs = len(in_specs) + 1
    extra = len(after)

    def run(*refs):
        body(*refs[:inputs], *refs[inputs + extra :])

    call = pl.pallas_call(
        run,
        grid_spec=pltpu.PrefetchScalarGridSpec(
            num_scalar_prefetch=1,
            grid=grid,
            in_specs=list(in_specs) + [pl.BlockSpec(memory_space=pl.ANY)] * extra,
            out_specs=out_specs,
            scratch_shapes=list(scratch),
        ),
        out_shape=out_shape,
        compiler_params=pltpu.CompilerParams(vmem_limit_bytes=vmem * MIB),
        cost_estimate=pl.CostEstimate(flops=10**12, bytes_accessed=1000, transcendentals=0),
        name=name,
    )
    return lambda *args: call(*args, *after)


def whole(shape):
    zeros = (0,) * len(shape)
    return pl.BlockSpec(shape, lambda *_: zeros)


SCALARS = pl.BlockSpec(memory_space=pltpu.SMEM)


def sds(shape, dtype):
    return jax.ShapeDtypeStruct(shape, dtype)


def normalize(rows):
    center = rows - jnp.mean(rows, axis=-1, keepdims=True)
    spread = jnp.mean(center * center, axis=-1, keepdims=True)
    return center * lax.rsqrt(spread + EPS_NORM)


def columns(index, size):
    return pl.ds(pl.multiple_of(index * size, size), size)


def pack_body(meta, down_ref, up_ref, out_ref):
    mats = down_ref.shape[0]
    down, up = down_ref[...].astype(BF), up_ref[...].astype(BF)
    for dest in range(out_ref.shape[0]):
        out_ref[dest, 0] = down[mats - 1]
        out_ref[dest, 1] = up[mats - 1]
        out_ref[dest, 2 : mats + 1] = down[: mats - 1]
        out_ref[dest, mats + 1 :] = up[: mats - 1]


def pack_maps(meta, seq_count, down, up):
    shape = (seq_count, 2 * down.shape[0], *down.shape[1:])
    return kernel_call(
        pack_body, "pack_maps", (1,),
        [whole(down.shape), whole(up.shape)], whole(shape), sds(shape, BF),
        moved=8 * down.size,
    )(meta, down, up)


def unpack_body(meta, got_ref, out_ref, up_ref):
    count, _, size, _ = got_ref.shape
    for block in range(count):
        here = slice(block * size, (block + 1) * size)
        out_ref[:, here, :] = got_ref[block, 0:5]
        up_ref[:, here, :] = got_ref[block, 5:8]


def unpack_maps(meta, got, after):
    count, mats, size, shard = got.shape
    rank = count * size
    if size % 16:
        maps = jnp.transpose(got, (1, 0, 2, 3)).reshape(mats, rank, shard)
        return maps[:5], maps[5:]
    return kernel_call(
        unpack_body, "unpack_maps", (1,),
        [whole(got.shape)], [whole((5, rank, shard)), whole((3, rank, shard))],
        [sds((5, rank, shard), BF), sds((3, rank, shard), BF)],
        moved=4 * got.size,
        after=after,
    )(meta, got)


def side_sum(refs):
    one_ref, two_ref, out_ref = refs
    out_ref[...] = (one_ref[...].astype(F32) + two_ref[...].astype(F32)).astype(BF)


def ffn_body(unit, meta, x_ref, gain_ref, up_ref, down_ref, *refs):
    if unit == 0:
        mine_ref, sib_ref, low_ref, part_ref = refs
    else:
        one_ref, two_ref, mine_ref, sib_ref, sum_ref, low_ref, part_ref = refs
    step = pl.program_id(0)

    @pl.when(step == 0)
    def _():
        hat = normalize(x_ref[...].astype(F32))
        low_ref[...] = (hat * gain_ref[1:2, :]).astype(BF)
        part_ref[...] = jnp.zeros_like(part_ref)
        if unit:
            side_sum((one_ref, two_ref, sum_ref))

    hidden = dot_nn(low_ref[...], up_ref[...])
    hidden = 0.5 * hidden * (1.0 + lax.erf(hidden * (0.5**0.5)))
    part_ref[...] += dot_nn(hidden.astype(BF), down_ref[...])

    @pl.when(step == pl.num_programs(0) - 1)
    def _():
        core = core_of(meta)
        mine_ref[...] = part_ref[columns(core, BLOCK), :].astype(BF)
        sib_ref[...] = part_ref[columns(1 - core, BLOCK), :].astype(BF)


def ffn(meta, unit, x, gains, w_up, w_down, sums=(), after=()):
    rows, width = x.shape
    chunk = 512
    half = sds((BLOCK, width), BF)
    results = 2 + len(sums) // 2
    return kernel_call(
        partial(ffn_body, unit),
        f"ffn_{unit}",
        (w_up.shape[1] // chunk,),
        [
            pl.BlockSpec((UNIT, width), lambda i, m: (unit, 0)),
            whole(gains.shape),
            pl.BlockSpec((width, chunk), lambda i, m: (0, i)),
            pl.BlockSpec((chunk, width), lambda i, m: (i, 0)),
        ]
        + [whole((BLOCK, width))] * len(sums),
        [whole((BLOCK, width))] * results,
        [half] * results,
        [pltpu.VMEM((UNIT, width), BF), pltpu.VMEM((UNIT, width), F32)],
        flops=4 * UNIT * width * w_up.shape[1],
        moved=4 * w_up.size + 8 * UNIT * width,
        vmem=58,
        after=after,
    )(meta, x, gains, w_up, w_down, *sums)


def qkv_body(meta, x_ref, gain_ref, w_ref, low_ref, out_ref):
    hat = normalize(x_ref[...].astype(F32))
    low = (hat * gain_ref[0:1, :]).astype(BF)
    low_ref[...] = low
    shard = w_ref.shape[2]
    for k in range(3):
        out_ref[:, k * shard : (k + 1) * shard] = dot_nn(low, w_ref[k])


def frozen_qkv(meta, x, gains, w_qkv, after=()):
    rows, width = x.shape
    out = 3 * w_qkv.shape[2]
    return kernel_call(
        qkv_body,
        "frozen_qkv",
        (rows // UNIT,),
        [
            pl.BlockSpec((UNIT, width), lambda i, m: (i, 0)),
            whole(gains.shape),
            whole(w_qkv.shape),
        ],
        [
            pl.BlockSpec((UNIT, width), lambda i, m: (i, 0)),
            pl.BlockSpec((UNIT, out), lambda i, m: (i, 0)),
        ],
        [sds((rows, width), BF), sds((rows, out), F32)],
        flops=2 * rows * width * out,
        moved=2 * w_qkv.size + 4 * x.size + 4 * rows * out,
        vmem=58,
        after=after,
    )(meta, x, gains, w_qkv)


def rotary_tables(rows, shard):
    half = ROT // 2
    freq = np.exp(np.arange(half) * (-2.0 * math.log(10000.0) / ROT))
    angles = np.arange(rows)[:, None] * freq[None, :]
    cos, sin = np.cos(angles), np.sin(angles)
    one = np.ones((rows, HEAD))
    one[:, :half] = cos
    one[:, half:ROT] = cos
    up = np.zeros((rows, HEAD))
    up[:, half:ROT] = sin
    down = np.zeros((rows, HEAD))
    down[:, :half] = sin
    heads = min(shard, 128) // HEAD
    return [jnp.asarray(np.tile(table, (1, heads)), F32) for table in (one, up, down)]


def across(table, width):
    return jnp.concatenate([table] * (width // table.shape[1]), axis=1)


def turn(rows, cos, up, down, sign):
    half = ROT // 2
    width = rows.shape[1]
    from_low = pltpu.roll(rows, half, 1)
    from_high = pltpu.roll(rows, width - half, 1)
    cos, up, down = (across(table, width) for table in (cos, up, down))
    return rows * cos + sign * (from_low * up - from_high * down)


def pre_body(
    meta, low_ref, qkv_ref, cos_ref, up_ref, down_ref,
    m_own, m_sib, m_y, m_far, ups, one_ref, two_ref,
    q_ref, k_ref, v_ref, rank_ref, sum_ref,
):
    @pl.when(pl.program_id(0) == 0)
    def _():
        side_sum((one_ref, two_ref, sum_ref))

    proj = meta[PROJ]
    shard = q_ref.shape[1]
    rank = m_own.shape[1]
    total = None
    for rel, piece in enumerate((m_own, m_sib, m_y, m_far)):
        low = low_ref[:, columns(proj ^ rel, shard)]
        part = dot_nt(low, piece[2:5].reshape(3 * rank, shard))
        total = part if total is None else total + part
    rank_in = total.astype(BF)
    rank_ref[...] = rank_in
    pre = [
        qkv_ref[:, k * shard : (k + 1) * shard]
        + ADAPTER_SCALE * dot_nn(rank_in[:, k * rank : (k + 1) * rank], ups[k])
        for k in range(3)
    ]
    tables = (cos_ref[...], up_ref[...], down_ref[...])
    q_ref[...] = turn(pre[0], *tables, 1.0).astype(BF)
    k_ref[...] = turn(pre[1], *tables, 1.0).astype(BF)
    v_ref[...] = pre[2].astype(BF)


def make_qkv(meta, low, qkv, tables, maps, ups, sums, after=()):
    rows, width = low.shape
    shard = qkv.shape[1] // 3
    rank = ups.shape[1]
    block = lambda cols: pl.BlockSpec((UNIT, cols), lambda i, m: (i, 0))
    return kernel_call(
        pre_body,
        "adapter_qkv",
        (rows // UNIT,),
        [block(width), block(3 * shard)]
        + [block(tables[0].shape[1])] * 3
        + [whole(one.shape) for one in (*maps, ups, *sums)],
        [block(shard)] * 3 + [block(3 * rank), whole((BLOCK, width))],
        [sds((rows, shard), BF)] * 3 + [sds((rows, 3 * rank), BF), sds((BLOCK, width), BF)],
        flops=2 * rows * width * 3 * rank,
        moved=rows * (2 * width + 24 * shard),
        after=after,
    )(meta, low, qkv, *tables, *maps, ups, *sums)


def head_mask(shard, head):
    return lax.broadcasted_iota(jnp.int32, (1, shard), 1) // HEAD == head


def diagonal():
    rows = lax.broadcasted_iota(jnp.int32, (BLOCK, BLOCK), 0)
    cols = lax.broadcasted_iota(jnp.int32, (BLOCK, BLOCK), 1)
    return rows >= cols


def block_scores(query, k_ref, prev, causal):
    scale = HEAD**-0.5
    diag = dot_nt(query, k_ref[prev : prev + BLOCK, :]) * scale
    diag = jnp.where(causal, diag, -1e30)
    if prev == 0:
        return diag
    return jnp.concatenate([dot_nt(query, k_ref[0:prev, :]) * scale, diag], axis=1)


def attend_body(unit, meta, q_ref, k_ref, v_ref, mine_ref, sib_ref, lse_ref):
    shard = q_ref.shape[1]
    causal = diagonal()
    lane = lax.broadcasted_iota(jnp.int32, (BLOCK, 128), 1)
    for half in range(UNIT // BLOCK):
        prev = unit * UNIT + half * BLOCK
        query = q_ref[half * BLOCK : (half + 1) * BLOCK, :]
        out = jnp.zeros((BLOCK, shard), F32)
        lse = jnp.zeros((BLOCK, 128), F32)
        for head in range(shard // HEAD):
            mask = head_mask(shard, head)
            scores = block_scores(jnp.where(mask, query, 0), k_ref, prev, causal)
            top = jnp.max(scores, axis=1, keepdims=True)
            prob = jnp.exp(scores - top)
            total = jnp.sum(prob, axis=1, keepdims=True)
            got = dot_nn(prob.astype(BF), v_ref[0 : prev + BLOCK, :]) / total
            out = jnp.where(mask, got, out)
            lse = jnp.where(lane == head, top + jnp.log(total), lse)
        lse_ref[half * BLOCK : (half + 1) * BLOCK, :] = lse
        low = out.astype(BF)

        @pl.when(core_of(meta) == half)
        def _():
            mine_ref[...] = low

        @pl.when(core_of(meta) != half)
        def _():
            sib_ref[...] = low


def attend(meta, unit, queries, keys, values, after=()):
    shard = queries.shape[1]
    known = (unit + 1) * UNIT
    return kernel_call(
        partial(attend_body, unit),
        f"attend_{unit}",
        (1,),
        [
            pl.BlockSpec((UNIT, shard), lambda i, m: (unit, 0)),
            pl.BlockSpec((known, shard), lambda i, m: (0, 0)),
            pl.BlockSpec((known, shard), lambda i, m: (0, 0)),
        ],
        [whole((BLOCK, shard))] * 2 + [whole((UNIT, 128))],
        [sds((BLOCK, shard), BF)] * 2 + [sds((UNIT, 128), F32)],
        flops=16 * UNIT * known * shard,
        moved=8 * known * shard,
        after=after,
    )(meta, queries, keys, values)


def attend_back_body(unit, meta, *refs):
    shard = refs[4].shape[1]
    (g0, g1, g2, g3, q_ref, k_ref, v_ref, lse_ref, cos_ref, up_ref, down_ref) = refs[:11]
    if unit == 0:
        dq_ref, dk_ref, dv_ref, grad_ref = refs[11:]
        dk_ref[...] = jnp.zeros_like(dk_ref)
        dv_ref[...] = jnp.zeros_like(dv_ref)
    else:
        (dk_in, dv_in, keep_ref, got_ref,
         dq_ref, dk_ref, dv_ref, own_ref, far_ref, grad_ref) = refs[11:]
        dk_ref[...] = dk_in[...]
        dv_ref[...] = dv_in[...]
        own_ref[...] = keep_ref[0].astype(F32) + got_ref[0].astype(F32)
        far_ref[...] = (keep_ref[1].astype(F32) + got_ref[1].astype(F32)).astype(BF)
    core, ybit = core_of(meta), ybit_of(meta)
    quarter = BLOCK // 2
    for rel, piece in enumerate((g0, g1, g2, g3)):
        place = (core ^ (rel & 1)) * 2 + (ybit ^ (rel >> 1))
        grad_ref[columns(place, quarter), :] = piece[...]
    causal = diagonal()
    lane = lax.broadcasted_iota(jnp.int32, (BLOCK, 128), 1)
    scale = HEAD**-0.5
    for half in range(UNIT // BLOCK):
        prev = unit * UNIT + half * BLOCK
        known = prev + BLOCK
        here = slice(half * BLOCK, (half + 1) * BLOCK)
        query = q_ref[here, :]
        grad = grad_ref[here, :]
        lse = lse_ref[here, :]
        dq = jnp.zeros((BLOCK, shard), F32)
        for head in range(shard // HEAD):
            mask = head_mask(shard, head)
            own_q = jnp.where(mask, query, 0)
            own_g = jnp.where(mask, grad, 0)
            own_lse = jnp.sum(jnp.where(lane == head, lse, 0.0), axis=1, keepdims=True)
            prob = jnp.exp(block_scores(own_q, k_ref, prev, causal) - own_lse)
            dweights = dot_nt(own_g, v_ref[0:known, :])
            delta = jnp.sum(prob * dweights, axis=1, keepdims=True)
            dscores = (prob * (dweights - delta)).astype(BF)
            dq = dq + jnp.where(mask, dot_nn(dscores, k_ref[0:known, :]), 0.0)
            dk_ref[0:known, :] += dot_tn(dscores, own_q) * scale
            dv_ref[0:known, :] += dot_tn(prob.astype(BF), own_g)
        dq = turn(dq * scale, cos_ref[here, :], up_ref[here, :], down_ref[here, :], -1.0)
        dq_ref[here, :] = dq.astype(BF)


def attend_back(meta, unit, grads, queries, keys, values, lse, tables, before=(), pair=(), after=()):
    rows, shard = queries.shape
    known = (unit + 1) * UNIT
    unit_rows = pl.BlockSpec((UNIT, shard), lambda i, m: (unit, 0))
    past = pl.BlockSpec((known, shard), lambda i, m: (0, 0))
    sums = whole((rows, shard))
    more = [one.shape[1:] for one in pair[:1]] * 2
    return kernel_call(
        partial(attend_back_body, unit),
        f"attend_back_{unit}",
        (1,),
        [whole(one.shape) for one in grads]
        + [unit_rows, past, past, whole((UNIT, 128))]
        + [pl.BlockSpec((UNIT, tables[0].shape[1]), lambda i, m: (unit, 0))] * 3
        + [sums] * len(before)
        + [whole(one.shape) for one in pair],
        [whole((UNIT, shard)), sums, sums] + [whole(one) for one in more],
        [sds((UNIT, shard), BF), sds((rows, shard), F32), sds((rows, shard), F32)]
        + [sds(one, dtype) for one, dtype in zip(more, (F32, BF))],
        [pltpu.VMEM((UNIT, shard), BF)],
        flops=40 * UNIT * known * shard,
        moved=16 * rows * shard,
        after=after,
    )(meta, *grads, queries, keys, values, lse, *tables, *before, *pair)


def mix_body(
    meta, x_ref, gain_ref, f_own, f_far, a0, a1, a2, a3, w0, w1, w2, w3,
    m0, m1, m2, m3, norm_ref, res_ref, rank_ref, keep_ref,
):
    proj = meta[PROJ]
    shard = a0.shape[1]
    rank = None
    for a_ref, m_ref in ((a0, m0), (a1, m1), (a2, m2), (a3, m3)):
        part = dot_nt(a_ref[...], m_ref[0])
        rank = part if rank is None else rank + part
    rank = rank.astype(BF)
    total = x_ref[...].astype(F32) + f_own[...].astype(F32) + f_far[...].astype(F32)
    for a_ref, w_ref in ((a0, w0), (a1, w1), (a2, w2), (a3, w3)):
        total = total + dot_nn(a_ref[...], w_ref[...])
    keep_ref[...] = total
    for rel, m_ref in enumerate((m0, m1, m2, m3)):
        here = columns(proj ^ rel, shard)
        keep_ref[:, here] += ADAPTER_SCALE * dot_nn(rank, m_ref[1])
    residual = keep_ref[...]
    norm_ref[...] = (normalize(residual) * gain_ref[2:3, :]).astype(BF)
    mine = columns(ybit_of(meta), BLOCK // 2)
    res_ref[...] = keep_ref[mine, :]
    keep_ref[:, 0 : rank.shape[1]] = rank.astype(F32)
    rank_ref[...] = keep_ref[mine, 0 : rank.shape[1]].astype(BF)


def mix(meta, unit, x, gains, f_own, f_far, att, wo, maps, after=()):
    rows, width = x.shape
    shard = att[0].shape[1]
    rank = maps[0].shape[1]
    return kernel_call(
        mix_body,
        f"mix_{unit}",
        (1,),
        [
            pl.BlockSpec((BLOCK, width), lambda i, m: (2 * unit + core_of(m), 0)),
            whole(gains.shape),
            whole((BLOCK, width)),
            whole((BLOCK, width)),
        ]
        + [whole(one.shape) for one in att]
        + [whole((shard, width))] * 4
        + [whole((2, rank, shard))] * 4,
        [whole((BLOCK, width)), whole((BLOCK // 2, width)), whole((BLOCK // 2, rank))],
        [sds((BLOCK, width), BF), sds((BLOCK // 2, width), F32), sds((BLOCK // 2, rank), BF)],
        [pltpu.VMEM((BLOCK, width), F32)],
        flops=2 * BLOCK * width * width,
        moved=2 * width * width + 8 * BLOCK * width,
        after=after,
    )(meta, x, gains, f_own, f_far, *att, *wo, *maps)


def vocab_grid(vocab):
    steps = -(-vocab // TILE_V)
    return steps, vocab - (steps - 1) * TILE_V


def local_columns(unit, meta, vocab, target_ref, out_ref):
    for group in range(4):
        half = core_of(meta) ^ (group >> 1)
        ids = target_ref[pl.ds((unit * 2 + half) * 2 + (group & 1), 1), :] - meta[PROJ] * vocab
        ids = jnp.where((ids >= 0) & (ids < vocab), ids, -1)
        square = jnp.transpose(jnp.broadcast_to(ids.astype(F32), (128, 128)))
        out_ref[group * 128 : (group + 1) * 128, :] = square.astype(jnp.int32)


def vocab_stats_body(
    unit, vocab, meta, mine_ref, sib_ref, u_ref, target_ref, p_ref, top_ref, st_ref, acc_ref, col_ref
):
    step = pl.program_id(0)
    steps, tail = vocab_grid(vocab)
    chunks = TILE_V // CHUNK_V

    @pl.when(step == 0)
    def _():
        acc_ref[...] = jnp.zeros_like(acc_ref)
        local_columns(unit, meta, vocab, target_ref, col_ref)

    def tile(is_tail):
        col = lax.broadcasted_iota(jnp.int32, (BLOCK, CHUNK_V), 1)
        lane = lax.broadcasted_iota(jnp.int32, (BLOCK, 128), 1)
        for chunk in range(chunks):
            inside = slice(chunk * CHUNK_V, (chunk + 1) * CHUNK_V)
            place = step * chunks + chunk
            for half, rows_ref in enumerate((mine_ref, sib_ref)):
                here = slice(half * BLOCK, (half + 1) * BLOCK)
                logits = dot_nt(rows_ref[...], u_ref[inside, :])
                if is_tail and inside.stop > tail:
                    logits = jnp.where(col < tail - inside.start, logits, -1e30)
                top = jnp.max(logits, axis=1, keepdims=True)
                prob = jnp.exp(logits - top)
                total = jnp.sum(prob, axis=1, keepdims=True)
                hit = col == col_ref[here, 0:1] - place * CHUNK_V
                picked = jnp.sum(jnp.where(hit, logits, 0.0), axis=1, keepdims=True)
                p_ref[here, inside] = prob.astype(BF)
                acc = acc_ref[here, :]
                acc = jnp.where(lane == place, top, acc)
                acc = jnp.where(lane == place + 32, total, acc)
                acc_ref[here, :] = jnp.where(lane == 64, acc + picked, acc)

    @pl.when(step < steps - 1)
    def _():
        tile(False)

    @pl.when(step == steps - 1)
    def _():
        tile(True)
        acc = acc_ref[...]
        lane = lax.broadcasted_iota(jnp.int32, acc.shape, 1)
        top_ref[...] = acc
        tops = jnp.where(lane < steps * chunks, acc, -1e30)
        best = jnp.max(tops, axis=1, keepdims=True)
        totals = pltpu.roll(acc, 128 - 32, 1)
        total = jnp.sum(
            jnp.where(lane < steps * chunks, totals * jnp.exp(tops - best), 0.0),
            axis=1, keepdims=True,
        )
        picked = jnp.sum(jnp.where(lane == 64, acc, 0.0), axis=1, keepdims=True)
        pair = jnp.where(lane == 0, best + jnp.log(total), jnp.where(lane == 1, picked, 0.0))
        st_ref[...] = jnp.transpose(pair)[0:8, :]


def vocab_stats(meta, unit, mine, sib, unembed, targets, after=()):
    vocab, width = unembed.shape
    steps, _ = vocab_grid(vocab)
    rows = 2 * BLOCK
    return kernel_call(
        partial(vocab_stats_body, unit, vocab),
        f"vocab_stats_{unit}",
        (steps,),
        [
            whole((BLOCK, width)),
            whole((BLOCK, width)),
            pl.BlockSpec((TILE_V, width), lambda i, m: (i, 0)),
            whole(targets.shape),
        ],
        [
            pl.BlockSpec((rows, TILE_V), lambda i, m: (0, i)),
            whole((rows, 128)),
            whole((8, rows)),
        ],
        [
            sds((rows, steps * TILE_V), BF),
            sds((rows, 128), F32),
            sds((8, rows), F32),
        ],
        [pltpu.VMEM((rows, 128), F32), pltpu.VMEM((rows, 128), jnp.int32)],
        flops=2 * rows * width * vocab,
        moved=2 * width * vocab + 2 * rows * vocab,
        vmem=52,
        after=after,
    )(meta, mine, sib, unembed, targets)


def swap_halves(pair):
    return jnp.concatenate([pair[:, BLOCK:], pair[:, :BLOCK]], axis=1)


def vocab_back_body(
    vocab, unit, meta, lens_ref, p_ref, u_ref, target_ref, top_ref, s0, s1, s2, s3,
    d0, d1, d2, d3, loss_ref, scale_ref, acc_ref, col_ref,
):
    step = pl.program_id(0)
    steps, tail = vocab_grid(vocab)
    chunks = TILE_V // CHUNK_V
    rows = 2 * BLOCK

    @pl.when(step == 0)
    def _():
        acc_ref[...] = jnp.zeros_like(acc_ref)
        local_columns(unit, meta, vocab, target_ref, col_ref)
        parts = [s0[...], swap_halves(s1[...]), s2[...], swap_halves(s3[...])]
        lses = [part[0:1, :] for part in parts]
        best = jnp.maximum(jnp.maximum(lses[0], lses[1]), jnp.maximum(lses[2], lses[3]))
        total = sum(jnp.exp(one - best) for one in lses)
        log_norm = best + jnp.log(total)
        picked = sum(part[1:2, :] for part in parts)
        place = lax.broadcasted_iota(jnp.int32, (1, rows), 1)
        core = core_of(meta)
        offset = jnp.where(place < BLOCK, core * BLOCK, (1 - core) * BLOCK - BLOCK)
        valid = (unit * UNIT + place + offset < lens_ref[meta[SEQ]]).astype(F32)
        loss_ref[...] = jnp.broadcast_to(
            jnp.sum((log_norm - picked) * valid, axis=1, keepdims=True), (8, 128)
        )
        weight = valid / token_count(lens_ref)
        row = lax.broadcasted_iota(jnp.int32, (128, rows), 0)
        lines = jnp.where(row == 0, log_norm, 0.0)
        lines = jnp.where(row == 1, weight, lines)
        lines = jnp.where(row == 2, (jnp.exp(picked - log_norm) - 1.0) * weight, lines)
        cols = jnp.transpose(lines)
        lane = lax.broadcasted_iota(jnp.int32, (rows, 128), 1)
        take = lambda k: jnp.sum(jnp.where(lane == k, cols, 0.0), axis=1, keepdims=True)
        tops = jnp.where(lane < steps * chunks, top_ref[...], -1e30)
        scales = jnp.exp(tops - take(0)) * take(1)
        scale_ref[...] = jnp.where(lane == 64, take(2), scales)

    def tile(is_tail):
        u_tile = u_ref[...]
        if is_tail:
            row = lax.broadcasted_iota(jnp.int32, u_tile.shape, 0)
            u_tile = jnp.where(row < tail, u_tile, jnp.zeros_like(u_tile))
        col = lax.broadcasted_iota(jnp.int32, (BLOCK, CHUNK_V), 1)
        lane = lax.broadcasted_iota(jnp.int32, (BLOCK, 128), 1)
        for half in range(2):
            here = slice(half * BLOCK, (half + 1) * BLOCK)
            scales = scale_ref[here, :]
            at_hit = jnp.sum(jnp.where(lane == 64, scales, 0.0), axis=1, keepdims=True)
            for chunk in range(chunks):
                inside = slice(chunk * CHUNK_V, (chunk + 1) * CHUNK_V)
                place = step * chunks + chunk
                scale = jnp.sum(jnp.where(lane == place, scales, 0.0), axis=1, keepdims=True)
                hit = col == col_ref[here, 0:1] - place * CHUNK_V
                grad = jnp.where(hit, at_hit, p_ref[here, inside].astype(F32) * scale)
                acc_ref[here, :] += dot_nn(grad.astype(BF), u_tile[inside, :])

    @pl.when(step < steps - 1)
    def _():
        tile(False)

    @pl.when(step == steps - 1)
    def _():
        tile(True)
        quarter = BLOCK // 2
        for rel, out_ref in enumerate((d0, d1, d2, d3)):
            place = (rel & 1) * 2 + (ybit_of(meta) ^ (rel >> 1))
            out_ref[...] = acc_ref[columns(place, quarter), :].astype(BF)


def vocab_back(meta, unit, lens, prob, unembed, targets, tops, stats, after=()):
    vocab, width = unembed.shape
    steps, _ = vocab_grid(vocab)
    rows = 2 * BLOCK
    quarter = (BLOCK // 2, width)
    return kernel_call(
        partial(vocab_back_body, vocab, unit),
        f"vocab_back_{unit}",
        (steps,),
        [
            SCALARS,
            pl.BlockSpec((rows, TILE_V), lambda i, m: (0, i)),
            pl.BlockSpec((TILE_V, width), lambda i, m: (i, 0)),
            whole(targets.shape),
            whole((rows, 128)),
        ]
        + [whole((8, rows))] * 4,
        [whole(quarter)] * 4 + [whole((8, 128))],
        [sds(quarter, BF)] * 4 + [sds((8, 128), F32)],
        [
            pltpu.VMEM((rows, 128), F32),
            pltpu.VMEM((rows, width), F32),
            pltpu.VMEM((rows, 128), jnp.int32),
        ],
        flops=2 * rows * width * vocab,
        moved=2 * width * vocab + 2 * rows * vocab,
        vmem=52,
        after=after,
    )(meta, lens, prob, unembed, targets, tops, *stats)


def norm_back_body(last, meta, *refs):
    parts, (res_ref, gain_ref, rank_ref) = refs[:4], refs[4:7]
    atts, wos, maps = refs[7:11], refs[11:15], refs[15:19]
    if last:
        before_ref, *outs, keep_ref, send_ref, hold_ref = refs[19:]
    else:
        *outs, sum_ref, hold_ref = refs[19:]
    proj = meta[PROJ]
    shard = atts[0].shape[1]
    dnormed = sum(part[...].astype(F32) for part in parts)
    residual = res_ref[...]
    center = residual - jnp.mean(residual, axis=-1, keepdims=True)
    spread = jnp.mean(center * center, axis=-1, keepdims=True)
    inv = lax.rsqrt(spread + EPS_NORM)
    hat = center * inv
    dhat = dnormed * gain_ref[2:3, :]
    dres = inv * (
        dhat
        - jnp.mean(dhat, axis=-1, keepdims=True)
        - hat * jnp.mean(dhat * hat, axis=-1, keepdims=True)
    )
    hold_ref[...] = dres.astype(BF)
    dbranch = hold_ref[...]
    drank = None
    for rel, m_ref in enumerate(maps):
        part = dot_nt(hold_ref[:, columns(proj ^ rel, shard)], m_ref[1])
        drank = part if drank is None else drank + part
    drank = (ADAPTER_SCALE * drank).astype(BF)
    for rel in range(4):
        datt = dot_nt(dbranch, wos[rel][...]) + dot_nn(drank, maps[rel][0])
        outs[rel][...] = datt.astype(BF)
        g_down = dot_tn(drank, atts[rel][...])
        g_up = ADAPTER_SCALE * dot_tn(rank_ref[...], hold_ref[:, columns(proj ^ rel, shard)])
        if last:
            dest = (keep_ref, send_ref)[rel & 1]
            dest[rel >> 1, 0] = (before_ref[rel, 0] + g_down).astype(BF)
            dest[rel >> 1, 1] = (before_ref[rel, 1] + g_up).astype(BF)
        else:
            sum_ref[rel, 0] = g_down
            sum_ref[rel, 1] = g_up


def norm_back(meta, unit, last, parts, residual, gains, rank_out, att, wo, maps, before, after=()):
    quarter, width = residual.shape
    shard = att[0].shape[1]
    rank = rank_out.shape[1]
    piece = (quarter, shard)
    if last:
        more = [sds((2, 2, rank, shard), BF)] * 2
    else:
        more = [sds((4, 2, rank, shard), F32)]
    return kernel_call(
        partial(norm_back_body, last),
        f"norm_back_{unit}",
        (1,),
        [whole(one.shape) for one in parts]
        + [whole(residual.shape), whole(gains.shape), whole(rank_out.shape)]
        + [pl.BlockSpec(piece, lambda i, m: (ybit_of(m), 0))] * 4
        + [whole((shard, width))] * 4
        + [whole((2, rank, shard))] * 4
        + [whole(one.shape) for one in before],
        [whole(piece)] * 4 + [whole(one.shape) for one in more],
        [sds(piece, BF)] * 4 + more,
        [pltpu.VMEM((quarter, width), BF)],
        flops=2 * quarter * width * width,
        moved=2 * width * width + 12 * quarter * width,
        after=after,
    )(meta, *parts, residual, gains, rank_out, *att, *wo, *maps, *before)


def grads_body(
    meta, dq0, dq1, dk_ref, dv_ref, cos_ref, up_ref, down_ref, rank_ref, ups, low_ref,
    keep_ref, send_ref, up_grad_ref, drank_ref,
):
    proj = meta[PROJ]
    rank, shard = ups.shape[1:]
    dk = turn(dk_ref[...], cos_ref[...], up_ref[...], down_ref[...], -1.0).astype(BF)
    dpre = [jnp.concatenate([dq0[...], dq1[...]], axis=0), dk, dv_ref[...].astype(BF)]
    for k in range(3):
        here = slice(k * rank, (k + 1) * rank)
        up_grad_ref[k] = ADAPTER_SCALE * dot_tn(rank_ref[:, here], dpre[k])
        drank_ref[:, here] = (ADAPTER_SCALE * dot_nt(dpre[k], ups[k])).astype(BF)
    drank = drank_ref[...]
    for rel in range(4):
        grad = dot_tn(drank, low_ref[:, columns(proj ^ rel, shard)])
        dest = (keep_ref, send_ref)[rel & 1]
        dest[rel >> 1] = grad.reshape(3, rank, shard).astype(BF)


def adapter_grads(meta, dqs, dk, dv, tables, rank_in, ups, low):
    rows, shard = dk.shape
    rank = ups.shape[1]
    pair = (2, 3, rank, shard)
    args = (*dqs, dk, dv, *tables, rank_in, ups, low)
    return kernel_call(
        grads_body,
        "adapter_grads",
        (1,),
        [whole(one.shape) for one in args],
        [whole(pair), whole(pair), whole((3, rank, shard))],
        [sds(pair, BF), sds(pair, BF), sds((3, rank, shard), F32)],
        [pltpu.VMEM((rows, 3 * rank), BF)],
        flops=2 * rows * low.shape[1] * 3 * rank,
        moved=30 * rows * shard,
    )(meta, *args)


def signs(row_ids, col_ids, seed):
    hashed = row_ids * 1640531527 + col_ids * 747796405 + seed * 277803737
    hashed = hashed ^ hashed >> 15 & 131071
    hashed = hashed * 2024237689
    hashed = hashed ^ hashed >> 13 & 524287
    return 1.0 - 2.0 * (hashed >> 17 & 1).astype(F32)


def sketch_one(meta, seed, grad, sketch):
    rank, shard = grad.shape
    left_rows = lax.broadcasted_iota(jnp.int32, (sketch, shard), 1) + meta[PROJ] * shard
    left_cols = lax.broadcasted_iota(jnp.int32, (sketch, shard), 0)
    right_rows = lax.broadcasted_iota(jnp.int32, (rank, sketch), 0)
    right_cols = lax.broadcasted_iota(jnp.int32, (rank, sketch), 1)
    left = signs(left_rows, left_cols, 2 * seed).astype(BF)
    right = signs(right_rows, right_cols, 2 * seed + 1)
    return jnp.dot(dot_nt(left, grad), right, precision=lax.Precision.HIGHEST)


def local_sketch_body(meta, seeds_ref, lens_ref, own_ref, far_ref, up_ref, block_ref, full_ref):
    size = block_ref.shape[2]
    count = token_count(lens_ref)
    out = own_ref[...] + far_ref[...].astype(F32)
    for place, grad in enumerate((out[0], up_ref[0], up_ref[1], up_ref[2], out[1])):
        for dest in range(block_ref.shape[0]):
            block_ref[dest, place] = grad[dest * size : (dest + 1) * size].astype(BF)
        full_ref[place] = count * sketch_one(
            meta, seeds_ref[3 + place], grad.astype(BF), full_ref.shape[1]
        )


def local_sketch(meta, seeds, lens, own, far, ups, sketch_width):
    _, rank, shard = own.shape
    count = lens.shape[0]
    blocks = (count, 5, rank // count, shard)
    full = (5, sketch_width, sketch_width)
    return kernel_call(
        local_sketch_body, "local_sketch", (1,),
        [SCALARS, SCALARS, whole(own.shape), whole(far.shape), whole(ups.shape)],
        [whole(blocks), whole(full)],
        [sds(blocks, BF), sds(full, F32)],
        flops=10 * rank * shard * sketch_width,
        moved=16 * own.size,
    )(meta, seeds, lens, own, far, ups)


def gather_body(meta, keep_ref, got_ref, far_ref, five_ref, block_ref, grad_ref):
    size = block_ref.shape[2]
    total = keep_ref[0].astype(F32) + got_ref[0].astype(F32) + far_ref[...].astype(F32)
    grad_ref[...] = total.astype(BF)
    for dest in range(block_ref.shape[0]):
        for mat in range(3):
            block_ref[dest, mat] = total[mat, dest * size : (dest + 1) * size].astype(BF)
        block_ref[dest, 3:8] = five_ref[dest]


def gather_blocks(meta, keep, got, far, five):
    count, _, size, shard = five.shape
    blocks = (count, 8, size, shard)
    pair = pl.BlockSpec((1, *keep.shape[1:]), lambda i, m: (0, 0, 0, 0))
    return kernel_call(
        gather_body, "gather_blocks", (1,),
        [pair, pair, whole(far.shape), whole(five.shape)],
        [whole(blocks), whole(far.shape)],
        [sds(blocks, BF), sds(far.shape, BF)],
        moved=16 * far.size,
    )(meta, keep, got, far, five)


def sketch_body(meta, seeds_ref, lens_ref, grad_ref, five_ref, f0, f1, f2, f3, full_ref):
    count = token_count(lens_ref)
    sketch = full_ref.shape[1]
    full_ref[3:8] = five_ref[...]
    for mat in range(3):
        full_ref[mat] = count * sketch_one(meta, seeds_ref[mat], grad_ref[mat], sketch)
    size = sketch // 4
    for rel, out_ref in enumerate((f0, f1, f2, f3)):
        out_ref[...] = full_ref[:, columns(meta[PROJ] ^ rel, size), :]


def sketch(meta, seeds, lens, grads, five):
    sketch_width = five.shape[1]
    piece = (8, sketch_width // 4, sketch_width)
    return kernel_call(
        sketch_body, "sketch", (1,),
        [SCALARS, SCALARS, whole(grads.shape), whole(five.shape)],
        [whole(piece)] * 4,
        [sds(piece, F32)] * 4,
        [pltpu.VMEM((8, sketch_width, sketch_width), F32)],
        flops=2 * grads.size * sketch_width,
        moved=2 * grads.size,
    )(meta, seeds, lens, grads, five)


def lane_value(row, lane, place):
    return jnp.sum(jnp.where(lane == place, row, 0.0), axis=1, keepdims=True)


def tally_body(
    units, meta, got_ref, target_ref, f0, f1, f2, f3, *refs
):
    losses, (total_ref, line_ref) = refs[:units], refs[units:]
    total = jnp.sum(got_ref[...].astype(F32), axis=0)
    total_ref[...] = total
    features = f0[...] + f1[...] + f2[...] + f3[...]
    squares = jnp.sum(total * total)
    own = jnp.sum(features * features)
    loss = sum(jnp.sum(one[0:1, 0:1]) for one in losses)
    loss = jnp.where(meta[PROJ] == 0, loss, 0.0)
    lane = lax.broadcasted_iota(jnp.int32, (1, 128), 1)
    line = jnp.where(lane == 0, squares, 0.0)
    line = jnp.where(lane == 1, loss, line)
    line = jnp.where(lane == 2, own, line)
    checkpoints = target_ref.shape[0]
    for c in range(checkpoints):
        theirs = target_ref[c]
        line = jnp.where(lane == 3 + c, jnp.sum(features * theirs), line)
        line = jnp.where(lane == 3 + checkpoints + c, jnp.sum(theirs * theirs), line)
    line_ref[...] = jnp.broadcast_to(line, line_ref.shape)


def tally(meta, devices, got, targets, pieces, losses):
    _, mats, slice_rank, shard = got.shape
    args = (got, targets, *pieces, *losses)
    return kernel_call(
        partial(tally_body, len(losses)),
        "tally",
        (1,),
        [whole(one.shape) for one in args],
        [whole((mats, slice_rank, shard)), whole((devices, 128))],
        [sds((mats, slice_rank, shard), F32), sds((devices, 128), F32)],
        flops=got.size,
        moved=4 * got.size,
    )(meta, *args)


def optimizer_step(weight, grad_in, first_in, second_in, clipping_scale):
    grad_clip = grad_in * clipping_scale
    first_new = BETA_ONE * first_in + (1.0 - BETA_ONE) * grad_clip
    second_new = BETA_TWO * second_in + (1.0 - BETA_TWO) * grad_clip * grad_clip
    first_hat = first_new / (1.0 - BETA_ONE**STEP)
    second_hat = second_new / (1.0 - BETA_TWO**STEP)
    new_weight = weight - LEARN_RATE * (
        first_hat / (jnp.sqrt(second_hat) + ADAM_EPS) + WEIGHT_DECAY * weight
    )
    return (new_weight, first_new, second_new)


def finish_body(
    proj_count, checkpoints, meta, lens_ref, lines_ref, total_ref,
    dw, uw, dm, um, ds, us,
    loss_out, norm_out, influence_out, dw_out, uw_out, dm_out, um_out, ds_out, us_out,
):
    lines = lines_ref[...]
    everyone = jnp.sum(lines, axis=0, keepdims=True)
    row = lax.broadcasted_iota(jnp.int32, lines.shape, 0)
    ours = jnp.sum(
        jnp.where(row // proj_count == meta[SEQ], lines, 0.0), axis=0, keepdims=True
    )
    lane = lax.broadcasted_iota(jnp.int32, (1, 128), 1)
    grad_norm = jnp.sqrt(lane_value(everyone, lane, 0))
    own = lane_value(ours, lane, 2)
    influence = jnp.zeros((1, 1), F32)
    for c in range(checkpoints):
        dot = lane_value(ours, lane, 3 + c)
        theirs = lane_value(ours, lane, 3 + checkpoints + c)
        influence += (1.0 - c / checkpoints) * dot * lax.rsqrt(own * theirs + 1e-12)
    loss_out[0] = jnp.sum(lane_value(everyone, lane, 1))
    loss_out[1] = token_count(lens_ref)
    norm_out[0] = jnp.sum(grad_norm)
    influence_out[0] = jnp.sum(influence)
    clip = jnp.minimum(1.0, CLIP_NORM / (grad_norm + 1e-06))
    half = total_ref.shape[0] // 2
    for base, ins, outs in (
        (0, (dw, dm, ds), (dw_out, dm_out, ds_out)),
        (half, (uw, um, us), (uw_out, um_out, us_out)),
    ):
        for k in range(half):
            new = optimizer_step(
                ins[0][k], total_ref[base + k], ins[1][k], ins[2][k], clip
            )
            for out, value in zip(outs, new):
                out[k] = value


def finish(meta, proj_count, checkpoints, lens, lines, total, params):
    block = whole(params[0].shape)
    return kernel_call(
        partial(finish_body, proj_count, checkpoints),
        "finish",
        (1,),
        [SCALARS, whole(lines.shape), whole(total.shape)] + [block] * 6,
        [SCALARS] * 3 + [block] * 6,
        [sds((2,), F32), sds((1,), F32), sds((1,), F32)] + [sds(params[0].shape, F32)] * 6,
        flops=20 * total.size,
        moved=28 * total.size,
    )(meta, lens, lines, total, *params)


def to_partner(array, axis, size, offset):
    return lax.ppermute(array, axis, [(i, i ^ offset) for i in range(size)])


def on_device(
    seq_count,
    proj_count,
    inputs,
    targets,
    lengths,
    norm_gain_vectors,
    query_key_value_weight,
    attention_output_weight,
    feedforward_input_weight,
    feedforward_output_weight,
    unembed,
    adapter_down_maps,
    adapter_up_maps,
    down_first_moment,
    up_first_moment,
    down_second_moment,
    up_second_moment,
    target_gradient_sketches,
    seeds,
):
    rows, width = inputs.shape
    shard = attention_output_weight.shape[0]
    vocab_local = unembed.shape[1]
    slice_rank = adapter_up_maps.shape[1]
    rank = slice_rank * seq_count
    sketch_width = target_gradient_sketches.shape[3]
    proj = lax.axis_index("proj")
    seq = lax.axis_index("dp")
    units = rows // UNIT

    over_proj = lambda array, rel: to_partner(array, "proj", proj_count, rel)
    over_seq = lambda array, rel: to_partner(array, "dp", seq_count, rel)

    meta = jnp.stack([proj, seq]).astype(jnp.int32)
    targets = targets.reshape(rows // 128, 128)
    table = jnp.transpose(unembed)
    tables = rotary_tables(rows, shard)
    transposed = lambda array: jnp.transpose(array, (0, 2, 1))

    def from_all(array):
        y = over_proj(array, 2)
        return (array, over_proj(array, 1), y, over_proj(y, 1))

    def exchange(*pieces):
        return [pieces[0]] + [over_proj(pieces[rel], rel) for rel in (1, 2, 3)]

    packed = pack_maps(meta, seq_count, transposed(adapter_down_maps), adapter_up_maps)
    arrived = lax.all_to_all(packed, "dp", split_axis=0, concat_axis=0, tiled=True)
    wo = from_all(attention_output_weight)

    w_ffn = (feedforward_input_weight, feedforward_output_weight)
    f0_mine, f0_sib = ffn(meta, 0, inputs, norm_gain_vectors, *w_ffn)
    low, qkv = frozen_qkv(
        meta, inputs, norm_gain_vectors, jnp.transpose(query_key_value_weight, (1, 0, 2)),
        (f0_mine,),
    )
    maps, ups = unpack_maps(meta, arrived, (low,))
    maps = from_all(maps)
    f1_mine, f1_sib, f0_chip = ffn(
        meta, 1, inputs, norm_gain_vectors, *w_ffn, (f0_mine, over_proj(f0_sib, 1)), (maps[0],)
    )
    queries, keys, values, rank_in, f1_chip = make_qkv(
        meta, low, qkv, tables, maps, ups, (f1_mine, over_proj(f1_sib, 1))
    )
    f_chip = (f0_chip, f1_chip)
    f_far = [over_proj(one, 2) for one in f_chip]

    att, lse = [None, None], [None, None]
    for unit in range(2):
        mine, sib, lse[unit] = attend(
            meta, unit, queries, keys, values, (lse[0],) if unit else ()
        )
        att[unit] = exchange(mine, sib, mine, sib)

    def mix_unit(unit, after):
        normed, residual, rank_out = mix(
            meta, unit, inputs, norm_gain_vectors, f_chip[unit], f_far[unit], att[unit], wo, maps, after
        )
        return (normed, over_proj(normed, 1)), residual, rank_out

    def stats_unit(unit, normed, after):
        prob, top, stat = vocab_stats(meta, unit, *normed, table, targets, after)
        return prob, top, exchange(stat, stat, stat, stat)

    def back_unit(unit, prob, top, stats, after):
        *parts, loss = vocab_back(meta, unit, lengths, prob, table, targets, top, stats, after)
        return exchange(*parts), loss

    def norm_unit(unit, parts, residual, rank_out, before, after):
        d0, d1, d2, d3, *grads = norm_back(
            meta, unit, unit == 1, parts, residual, norm_gain_vectors,
            rank_out, att[unit], wo, maps, before, after,
        )
        return exchange(d0, d1, d2, d3), grads

    normed0, residual0, rank0 = mix_unit(0, (lse[1],))
    prob0, top0, stats0 = stats_unit(0, normed0, ())
    normed1, residual1, rank1 = mix_unit(1, (stats0[0],))
    dnormed0, loss0 = back_unit(0, prob0, top0, stats0, (rank1,))
    prob1, top1, stats1 = stats_unit(1, normed1, (loss0,))
    datt0, out_grads = norm_unit(0, dnormed0, residual0, rank0, (), (stats1[0],))
    dnormed1, loss1 = back_unit(1, prob1, top1, stats1, (datt0[0],))
    dq0, dk, dv = attend_back(
        meta, 0, datt0, queries, keys, values, lse[0], tables, after=(loss1,)
    )
    datt1, (out_keep, out_send) = norm_unit(
        1, dnormed1, residual1, rank1, out_grads, (dq0,)
    )
    dq1, dk, dv, out_own, out_far = attend_back(
        meta, 1, datt1, queries, keys, values, lse[1], tables,
        (dk, dv), (out_keep, over_proj(out_send, 1)),
    )
    out_far = over_proj(out_far, 2)

    in_keep, in_send, up_grads = adapter_grads(
        meta, (dq0, dq1), dk, dv, tables, rank_in, ups, low
    )
    in_got = over_proj(in_send, 1)
    in_far = over_proj((in_keep[1].astype(F32) + in_got[1].astype(F32)).astype(BF), 2)
    blocks, five = local_sketch(meta, seeds, lengths, out_own, out_far, up_grads, sketch_width)
    blocks, in_grads = gather_blocks(meta, in_keep, in_got, in_far, blocks)
    arrived = lax.all_to_all(blocks, "dp", split_axis=0, concat_axis=0, tiled=True)
    pieces = exchange(*sketch(meta, seeds, lengths, in_grads, five))

    device_count = seq_count * proj_count
    total, lines = tally(
        meta, device_count, arrived, target_gradient_sketches, pieces, (loss0, loss1)
    )
    lines = lax.all_to_all(lines, ("dp", "proj"), split_axis=0, concat_axis=0, tiled=True)
    params = (
        transposed(adapter_down_maps),
        adapter_up_maps,
        transposed(down_first_moment),
        up_first_moment,
        transposed(down_second_moment),
        up_second_moment,
    )
    loss_parts, grad_norm, influence, dw, uw, dm, um, ds, us = finish(
        meta, proj_count, target_gradient_sketches.shape[0], lengths, lines, total, params
    )
    return (
        loss_parts,
        grad_norm,
        influence,
        transposed(dw),
        uw,
        transposed(dm),
        um,
        transposed(ds),
        us,
    )


def solution(mesh):
    in_specs = (
        P("dp", None),
        P("dp"),
        P(),
        P(),
        P(None, None, "proj"),
        P("proj", None),
        P(None, "proj"),
        P("proj", None),
        P(None, "proj"),
        P(None, "proj", "dp"),
        P(None, "dp", "proj"),
        P(None, "proj", "dp"),
        P(None, "dp", "proj"),
        P(None, "proj", "dp"),
        P(None, "dp", "proj"),
        P(None, None, "proj", None),
        P(),
    )
    out_specs = (
        P(),
        P(),
        P("dp"),
        P(None, "proj", "dp"),
        P(None, "dp", "proj"),
        P(None, "proj", "dp"),
        P(None, "dp", "proj"),
        P(None, "proj", "dp"),
        P(None, "dp", "proj"),
    )
    return jax.shard_map(
        partial(on_device, mesh.shape["dp"], mesh.shape["proj"]),
        mesh=mesh,
        in_specs=in_specs,
        out_specs=out_specs,
        check_vma=False,
    )
```

```python
from functools import partial
import math

import jax
import jax.numpy as jnp
import numpy as np
from jax import lax
from jax.experimental import pallas as pl
from jax.experimental.pallas import tpu as pltpu
from jax.sharding import PartitionSpec as P

HEAD = 64
ROT = 16
STEP = 10

EPS_NORM = 1e-05
ADAPTER_SCALE = 0.25
CLIP_NORM = 0.05
LEARN_RATE = 0.05
BETA_ONE = 0.9
BETA_TWO = 0.99
ADAM_EPS = 1e-08
WEIGHT_DECAY = 0.01

BF = jnp.bfloat16
F32 = jnp.float32
BLOCK = 256
UNIT = 512
FIRST_GROUPS = (3, 3, 3, 3)
SECOND_GROUPS = (5, 4, 4)
CHUNK_V = 512
MIB = 2**20

PROJ, SEQ = range(2)


def core_of(meta):
    return meta[PROJ] & 1


def ybit_of(meta):
    return meta[PROJ] >> 1


def token_count(lens_ref):
    return sum(lens_ref[i] for i in range(lens_ref.shape[0])).astype(F32)


def dot_nn(lhs, rhs):
    return lax.dot_general(lhs, rhs, (((1,), (0,)), ((), ())), preferred_element_type=F32)


def dot_nt(lhs, rhs):
    return lax.dot_general(lhs, rhs, (((1,), (1,)), ((), ())), preferred_element_type=F32)


def dot_tn(lhs, rhs):
    return lax.dot_general(lhs, rhs, (((0,), (0,)), ((), ())), preferred_element_type=F32)


def kernel_call(
    body, name, grid, in_specs, out_specs, out_shape, scratch=(), flops=0, moved=0, after=(),
    vmem=22, keep=(), use_keep=False,
):
    single = not isinstance(out_shape, (list, tuple))
    if single:
        out_specs, out_shape = [out_specs], [out_shape]
    first_keep = 1 + len(in_specs) + len(after)
    first_out = first_keep + len(keep)
    first_kept = first_out + len(out_shape)
    first_scratch = first_kept + len(keep)

    def run(*refs):
        kept = refs[first_keep:first_out] + refs[first_kept:first_scratch]
        body(
            refs[0],
            *(kept if use_keep else ()),
            *refs[1 : 1 + len(in_specs)],
            *refs[first_out:first_kept],
            *refs[first_scratch:],
        )

    anywhere = pl.BlockSpec(memory_space=pl.ANY)
    keep_spec = IN_VMEM if use_keep else anywhere
    call = pl.pallas_call(
        run,
        grid_spec=pltpu.PrefetchScalarGridSpec(
            num_scalar_prefetch=1,
            grid=grid,
            in_specs=list(in_specs) + [anywhere] * len(after) + [keep_spec] * len(keep),
            out_specs=list(out_specs) + [keep_spec] * len(keep),
            scratch_shapes=list(scratch),
        ),
        out_shape=list(out_shape) + [pltpu.VMEM(one.shape, one.dtype) for one in keep],
        input_output_aliases={
            first_keep + i: len(out_shape) + i for i in range(len(keep))
        },
        compiler_params=pltpu.CompilerParams(vmem_limit_bytes=vmem * MIB),
        cost_estimate=pl.CostEstimate(flops=10**12, bytes_accessed=1000, transcendentals=0),
        name=name,
    )

    def apply(*args):
        results = call(*args, *after, *[held(one) for one in keep])
        return results[0] if single else results

    return apply


def whole(shape):
    zeros = (0,) * len(shape)
    return pl.BlockSpec(shape, lambda *_: zeros)


SCALARS = pl.BlockSpec(memory_space=pltpu.SMEM)
IN_VMEM = pl.BlockSpec(memory_space=pltpu.VMEM)


def held(array):
    return pltpu.with_memory_space_constraint(array, pltpu.VMEM)


def sds(shape, dtype):
    return jax.ShapeDtypeStruct(shape, dtype)


def normalize(rows):
    center = rows - jnp.mean(rows, axis=-1, keepdims=True)
    spread = jnp.mean(center * center, axis=-1, keepdims=True)
    return center * lax.rsqrt(spread + EPS_NORM)


def columns(index, size):
    return pl.ds(pl.multiple_of(index * size, size), size)


def pack_body(meta, down_ref, up_ref, out_ref):
    mats = down_ref.shape[0]
    down, up = down_ref[...].astype(BF), up_ref[...].astype(BF)
    for dest in range(out_ref.shape[0]):
        out_ref[dest, 0] = down[mats - 1]
        out_ref[dest, 1] = up[mats - 1]
        out_ref[dest, 2 : mats + 1] = down[: mats - 1]
        out_ref[dest, mats + 1 :] = up[: mats - 1]


def pack_maps(meta, seq_count, down, up):
    shape = (seq_count, 2 * down.shape[0], *down.shape[1:])
    return kernel_call(
        pack_body, "pack_maps", (1,),
        [whole(down.shape), whole(up.shape)], whole(shape), sds(shape, BF),
        vmem=58,
    )(meta, down, up)


def unpack_body(meta, got_ref, out_ref, up_ref):
    count, _, size, _ = got_ref.shape
    for block in range(count):
        here = slice(block * size, (block + 1) * size)
        out_ref[:, here, :] = got_ref[block, 0:5]
        up_ref[:, here, :] = got_ref[block, 5:8]


def unpack_maps(meta, got, after):
    count, mats, size, shard = got.shape
    rank = count * size
    if size % 16:
        maps = jnp.transpose(got, (1, 0, 2, 3)).reshape(mats, rank, shard)
        return maps[:5], maps[5:]
    return kernel_call(
        unpack_body, "unpack_maps", (1,),
        [whole(got.shape)], [whole((5, rank, shard)), whole((3, rank, shard))],
        [sds((5, rank, shard), BF), sds((3, rank, shard), BF)],
        moved=4 * got.size,
        after=after,
    )(meta, got)


def side_sum(refs):
    one_ref, two_ref, out_ref = refs
    out_ref[...] = (one_ref[...].astype(F32) + two_ref[...].astype(F32)).astype(BF)


def ffn_body(unit, meta, x_ref, gain_ref, up_ref, down_ref, *refs):
    if unit == 0:
        mine_ref, sib_ref, low_ref, part_ref = refs
    else:
        one_ref, two_ref, mine_ref, sib_ref, sum_ref, low_ref, part_ref = refs
    step = pl.program_id(0)

    @pl.when(step == 0)
    def _():
        hat = normalize(x_ref[...].astype(F32))
        low_ref[...] = (hat * gain_ref[1:2, :]).astype(BF)
        part_ref[...] = jnp.zeros_like(part_ref)
        if unit:
            side_sum((one_ref, two_ref, sum_ref))

    hidden = dot_nn(low_ref[...], up_ref[...])
    hidden = 0.5 * hidden * (1.0 + lax.erf(hidden * (0.5**0.5)))
    part_ref[...] += dot_nn(hidden.astype(BF), down_ref[...])

    @pl.when(step == pl.num_programs(0) - 1)
    def _():
        core = core_of(meta)
        mine_ref[...] = part_ref[columns(core, BLOCK), :].astype(BF)
        sib_ref[...] = part_ref[columns(1 - core, BLOCK), :].astype(BF)


def ffn(meta, unit, x, gains, w_up, w_down, sums=(), after=()):
    rows, width = x.shape
    chunk = 512
    half = sds((BLOCK, width), BF)
    results = 2 + len(sums) // 2
    return kernel_call(
        partial(ffn_body, unit),
        f"ffn_{unit}",
        (w_up.shape[1] // chunk,),
        [
            pl.BlockSpec((UNIT, width), lambda i, m: (unit, 0)),
            whole(gains.shape),
            pl.BlockSpec((width, chunk), lambda i, m: (0, i)),
            pl.BlockSpec((chunk, width), lambda i, m: (i, 0)),
        ]
        + [whole((BLOCK, width))] * len(sums),
        [whole((BLOCK, width))] * results,
        [half] * results,
        [pltpu.VMEM((UNIT, width), BF), pltpu.VMEM((UNIT, width), F32)],
        flops=4 * UNIT * width * w_up.shape[1],
        moved=4 * w_up.size + 8 * UNIT * width,
        vmem=58,
        after=after,
    )(meta, x, gains, w_up, w_down, *sums)


def qkv_body(meta, x_ref, gain_ref, w_ref, low_ref, out_ref):
    hat = normalize(x_ref[...].astype(F32))
    low = (hat * gain_ref[0:1, :]).astype(BF)
    low_ref[...] = low
    shard = w_ref.shape[2]
    for k in range(3):
        out_ref[:, k * shard : (k + 1) * shard] = dot_nn(low, w_ref[k])


def frozen_qkv(meta, x, gains, w_qkv, after=()):
    rows, width = x.shape
    out = 3 * w_qkv.shape[2]
    return kernel_call(
        qkv_body,
        "frozen_qkv",
        (rows // UNIT,),
        [
            pl.BlockSpec((UNIT, width), lambda i, m: (i, 0)),
            whole(gains.shape),
            whole(w_qkv.shape),
        ],
        [
            pl.BlockSpec((UNIT, width), lambda i, m: (i, 0)),
            pl.BlockSpec((UNIT, out), lambda i, m: (i, 0)),
        ],
        [sds((rows, width), BF), sds((rows, out), F32)],
        flops=2 * rows * width * out,
        moved=2 * w_qkv.size + 4 * x.size + 4 * rows * out,
        vmem=58,
        after=after,
    )(meta, x, gains, w_qkv)


def rotary_tables(rows, shard):
    half = ROT // 2
    freq = np.exp(np.arange(half) * (-2.0 * math.log(10000.0) / ROT))
    angles = np.arange(rows)[:, None] * freq[None, :]
    cos, sin = np.cos(angles), np.sin(angles)
    one = np.ones((rows, HEAD))
    one[:, :half] = cos
    one[:, half:ROT] = cos
    up = np.zeros((rows, HEAD))
    up[:, half:ROT] = sin
    down = np.zeros((rows, HEAD))
    down[:, :half] = sin
    heads = min(shard, 128) // HEAD
    return [jnp.asarray(np.tile(table, (1, heads)), F32) for table in (one, up, down)]


def across(table, width):
    return jnp.concatenate([table] * (width // table.shape[1]), axis=1)


def turn(rows, cos, up, down, sign):
    half = ROT // 2
    width = rows.shape[1]
    from_low = pltpu.roll(rows, half, 1)
    from_high = pltpu.roll(rows, width - half, 1)
    cos, up, down = (across(table, width) for table in (cos, up, down))
    return rows * cos + sign * (from_low * up - from_high * down)


def pre_body(
    meta, low_ref, qkv_ref, cos_ref, up_ref, down_ref,
    m_own, m_sib, m_y, m_far, ups, one_ref, two_ref,
    q_ref, k_ref, v_ref, rank_ref, sum_ref,
):
    @pl.when(pl.program_id(0) == 0)
    def _():
        side_sum((one_ref, two_ref, sum_ref))

    proj = meta[PROJ]
    shard = q_ref.shape[1]
    rank = m_own.shape[1]
    total = None
    for rel, piece in enumerate((m_own, m_sib, m_y, m_far)):
        low = low_ref[:, columns(proj ^ rel, shard)]
        part = dot_nt(low, piece[2:5].reshape(3 * rank, shard))
        total = part if total is None else total + part
    rank_in = total.astype(BF)
    rank_ref[...] = rank_in
    pre = [
        qkv_ref[:, k * shard : (k + 1) * shard]
        + ADAPTER_SCALE * dot_nn(rank_in[:, k * rank : (k + 1) * rank], ups[k])
        for k in range(3)
    ]
    tables = (cos_ref[...], up_ref[...], down_ref[...])
    q_ref[...] = turn(pre[0], *tables, 1.0).astype(BF)
    k_ref[...] = turn(pre[1], *tables, 1.0).astype(BF)
    v_ref[...] = pre[2].astype(BF)


def make_qkv(meta, low, qkv, tables, maps, ups, sums, after=()):
    rows, width = low.shape
    shard = qkv.shape[1] // 3
    rank = ups.shape[1]
    block = lambda cols: pl.BlockSpec((UNIT, cols), lambda i, m: (i, 0))
    return kernel_call(
        pre_body,
        "adapter_qkv",
        (rows // UNIT,),
        [block(width), block(3 * shard)]
        + [block(tables[0].shape[1])] * 3
        + [whole(one.shape) for one in (*maps, ups, *sums)],
        [block(shard)] * 3 + [block(3 * rank), whole((BLOCK, width))],
        [sds((rows, shard), BF)] * 3 + [sds((rows, 3 * rank), BF), sds((BLOCK, width), BF)],
        flops=2 * rows * width * 3 * rank,
        moved=rows * (2 * width + 24 * shard),
        after=after,
    )(meta, low, qkv, *tables, *maps, ups, *sums)


def vocab_chunks(vocab):
    return [(start, min(CHUNK_V, vocab - start)) for start in range(0, vocab, CHUNK_V)]


def table_loads(table_ref, dest_ref, sem, first, groups):
    loads = {}
    for index, group in enumerate(groups):
        start = first * CHUNK_V
        stop = min(start + group * CHUNK_V, table_ref.shape[0])
        here = pl.ds(start, stop - start)
        loads[start] = pltpu.make_async_copy(table_ref.at[here], dest_ref.at[here], sem.at[index])
        first += group
    return loads


def vocab_buffers(vocab, width):
    return [
        pltpu.VMEM((vocab, width), BF),
        pltpu.VMEM((len(vocab_chunks(vocab)), UNIT, CHUNK_V), BF),
    ]


def head_mask(shard, head):
    return lax.broadcasted_iota(jnp.int32, (1, shard), 1) // HEAD == head


def diagonal():
    rows = lax.broadcasted_iota(jnp.int32, (BLOCK, BLOCK), 0)
    cols = lax.broadcasted_iota(jnp.int32, (BLOCK, BLOCK), 1)
    return rows >= cols


def block_scores(query, k_ref, prev, causal):
    scale = HEAD**-0.5
    diag = dot_nt(query, k_ref[prev : prev + BLOCK, :]) * scale
    diag = jnp.where(causal, diag, -1e30)
    if prev == 0:
        return diag
    return jnp.concatenate([dot_nt(query, k_ref[0:prev, :]) * scale, diag], axis=1)


def attend_body(unit, meta, q_ref, k_ref, v_ref, *refs):
    if unit == 0:
        mine_ref, sib_ref, lse_ref = refs
        loads = []
    else:
        table_ref, mine_ref, sib_ref, lse_ref, held_ref, _, sem = refs
        loads = list(table_loads(table_ref, held_ref, sem, 0, FIRST_GROUPS).values())
    for load in loads:
        load.start()
    shard = q_ref.shape[1]
    causal = diagonal()
    lane = lax.broadcasted_iota(jnp.int32, (BLOCK, 128), 1)
    for half in range(UNIT // BLOCK):
        prev = unit * UNIT + half * BLOCK
        query = q_ref[half * BLOCK : (half + 1) * BLOCK, :]
        out = jnp.zeros((BLOCK, shard), F32)
        lse = jnp.zeros((BLOCK, 128), F32)
        for head in range(shard // HEAD):
            mask = head_mask(shard, head)
            scores = block_scores(jnp.where(mask, query, 0), k_ref, prev, causal)
            top = jnp.max(scores, axis=1, keepdims=True)
            prob = jnp.exp(scores - top)
            total = jnp.sum(prob, axis=1, keepdims=True)
            got = dot_nn(prob.astype(BF), v_ref[0 : prev + BLOCK, :]) / total
            out = jnp.where(mask, got, out)
            lse = jnp.where(lane == head, top + jnp.log(total), lse)
        lse_ref[half * BLOCK : (half + 1) * BLOCK, :] = lse
        low = out.astype(BF)

        @pl.when(core_of(meta) == half)
        def _():
            mine_ref[...] = low

        @pl.when(core_of(meta) != half)
        def _():
            sib_ref[...] = low

    for load in loads:
        load.wait()


def attend(meta, unit, queries, keys, values, table, after=()):
    shard = queries.shape[1]
    known = (unit + 1) * UNIT
    return kernel_call(
        partial(attend_body, unit),
        f"attend_{unit}",
        (1,),
        [
            pl.BlockSpec((UNIT, shard), lambda i, m: (unit, 0)),
            pl.BlockSpec((known, shard), lambda i, m: (0, 0)),
            pl.BlockSpec((known, shard), lambda i, m: (0, 0)),
        ]
        + [pl.BlockSpec(memory_space=pl.ANY)] * unit,
        [whole((BLOCK, shard))] * 2 + [whole((UNIT, 128))] + [pl.BlockSpec(memory_space=pl.ANY)] * 2 * unit,
        [sds((BLOCK, shard), BF)] * 2
        + [sds((UNIT, 128), F32)]
        + vocab_buffers(*table.shape) * unit,
        [pltpu.SemaphoreType.DMA((len(FIRST_GROUPS),))] * unit,
        flops=16 * UNIT * known * shard,
        moved=8 * known * shard,
        after=after,
    )(meta, queries, keys, values, *((table,) * unit))


def attend_back_body(unit, meta, *refs):
    shard = refs[4].shape[1]
    (g0, g1, g2, g3, q_ref, k_ref, v_ref, lse_ref, cos_ref, up_ref, down_ref) = refs[:11]
    if unit == 0:
        dq_ref, dk_ref, dv_ref, grad_ref = refs[11:]
        dk_ref[...] = jnp.zeros_like(dk_ref)
        dv_ref[...] = jnp.zeros_like(dv_ref)
    else:
        (dk_in, dv_in, keep_ref, got_ref,
         dq_ref, dk_ref, dv_ref, own_ref, far_ref, grad_ref) = refs[11:]
        dk_ref[...] = dk_in[...]
        dv_ref[...] = dv_in[...]
        own_ref[...] = keep_ref[0].astype(F32) + got_ref[0].astype(F32)
        far_ref[...] = (keep_ref[1].astype(F32) + got_ref[1].astype(F32)).astype(BF)
    core, ybit = core_of(meta), ybit_of(meta)
    quarter = BLOCK // 2
    for rel, piece in enumerate((g0, g1, g2, g3)):
        place = (core ^ (rel & 1)) * 2 + (ybit ^ (rel >> 1))
        grad_ref[columns(place, quarter), :] = piece[...]
    causal = diagonal()
    lane = lax.broadcasted_iota(jnp.int32, (BLOCK, 128), 1)
    scale = HEAD**-0.5
    for half in range(UNIT // BLOCK):
        prev = unit * UNIT + half * BLOCK
        known = prev + BLOCK
        here = slice(half * BLOCK, (half + 1) * BLOCK)
        query = q_ref[here, :]
        grad = grad_ref[here, :]
        lse = lse_ref[here, :]
        dq = jnp.zeros((BLOCK, shard), F32)
        for head in range(shard // HEAD):
            mask = head_mask(shard, head)
            own_q = jnp.where(mask, query, 0)
            own_g = jnp.where(mask, grad, 0)
            own_lse = jnp.sum(jnp.where(lane == head, lse, 0.0), axis=1, keepdims=True)
            prob = jnp.exp(block_scores(own_q, k_ref, prev, causal) - own_lse)
            dweights = dot_nt(own_g, v_ref[0:known, :])
            delta = jnp.sum(prob * dweights, axis=1, keepdims=True)
            dscores = (prob * (dweights - delta)).astype(BF)
            dq = dq + jnp.where(mask, dot_nn(dscores, k_ref[0:known, :]), 0.0)
            dk_ref[0:known, :] += dot_tn(dscores, own_q) * scale
            dv_ref[0:known, :] += dot_tn(prob.astype(BF), own_g)
        dq = turn(dq * scale, cos_ref[here, :], up_ref[here, :], down_ref[here, :], -1.0)
        dq_ref[here, :] = dq.astype(BF)


def attend_back(meta, unit, grads, queries, keys, values, lse, tables, before=(), pair=(), after=()):
    rows, shard = queries.shape
    known = (unit + 1) * UNIT
    unit_rows = pl.BlockSpec((UNIT, shard), lambda i, m: (unit, 0))
    past = pl.BlockSpec((known, shard), lambda i, m: (0, 0))
    sums = whole((rows, shard))
    more = [one.shape[1:] for one in pair[:1]] * 2
    return kernel_call(
        partial(attend_back_body, unit),
        f"attend_back_{unit}",
        (1,),
        [whole(one.shape) for one in grads]
        + [unit_rows, past, past, whole((UNIT, 128))]
        + [pl.BlockSpec((UNIT, tables[0].shape[1]), lambda i, m: (unit, 0))] * 3
        + [sums] * len(before)
        + [whole(one.shape) for one in pair],
        [whole((UNIT, shard)), sums, sums] + [whole(one) for one in more],
        [sds((UNIT, shard), BF), sds((rows, shard), F32), sds((rows, shard), F32)]
        + [sds(one, dtype) for one, dtype in zip(more, (F32, BF))],
        [pltpu.VMEM((UNIT, shard), BF)],
        flops=40 * UNIT * known * shard,
        moved=16 * rows * shard,
        after=after,
    )(meta, *grads, queries, keys, values, lse, *tables, *before, *pair)


def mix_body(
    meta, x_ref, gain_ref, f_own, f_far, a0, a1, a2, a3, w0, w1, w2, w3,
    m0, m1, m2, m3, norm_ref, res_ref, rank_ref, keep_ref,
):
    proj = meta[PROJ]
    shard = a0.shape[1]
    rank = None
    for a_ref, m_ref in ((a0, m0), (a1, m1), (a2, m2), (a3, m3)):
        part = dot_nt(a_ref[...], m_ref[0])
        rank = part if rank is None else rank + part
    rank = rank.astype(BF)
    total = x_ref[...].astype(F32) + f_own[...].astype(F32) + f_far[...].astype(F32)
    for a_ref, w_ref in ((a0, w0), (a1, w1), (a2, w2), (a3, w3)):
        total = total + dot_nn(a_ref[...], w_ref[...])
    keep_ref[...] = total
    for rel, m_ref in enumerate((m0, m1, m2, m3)):
        here = columns(proj ^ rel, shard)
        keep_ref[:, here] += ADAPTER_SCALE * dot_nn(rank, m_ref[1])
    residual = keep_ref[...]
    norm_ref[...] = (normalize(residual) * gain_ref[2:3, :]).astype(BF)
    mine = columns(ybit_of(meta), BLOCK // 2)
    res_ref[...] = keep_ref[mine, :]
    keep_ref[:, 0 : rank.shape[1]] = rank.astype(F32)
    rank_ref[...] = keep_ref[mine, 0 : rank.shape[1]].astype(BF)


def mix(meta, unit, x, gains, f_own, f_far, att, wo, maps, after=(), keep=()):
    rows, width = x.shape
    shard = att[0].shape[1]
    rank = maps[0].shape[1]
    return kernel_call(
        mix_body,
        f"mix_{unit}",
        (1,),
        [
            pl.BlockSpec((BLOCK, width), lambda i, m: (2 * unit + core_of(m), 0)),
            whole(gains.shape),
            whole((BLOCK, width)),
            whole((BLOCK, width)),
        ]
        + [whole(one.shape) for one in att]
        + [whole((shard, width))] * 4
        + [whole((2, rank, shard))] * 4,
        [whole((BLOCK, width)), whole((BLOCK // 2, width)), whole((BLOCK // 2, rank))],
        [sds((BLOCK, width), BF), sds((BLOCK // 2, width), F32), sds((BLOCK // 2, rank), BF)],
        [pltpu.VMEM((BLOCK, width), F32)],
        flops=2 * BLOCK * width * width,
        moved=2 * width * width + 8 * BLOCK * width,
        after=after,
        keep=keep,
    )(meta, x, gains, f_own, f_far, *att, *wo, *maps)


def local_columns(unit, meta, vocab, target_ref, out_ref):
    for group in range(4):
        half = core_of(meta) ^ (group >> 1)
        ids = target_ref[pl.ds((unit * 2 + half) * 2 + (group & 1), 1), :] - meta[PROJ] * vocab
        ids = jnp.where((ids >= 0) & (ids < vocab), ids, -1)
        square = jnp.transpose(jnp.broadcast_to(ids.astype(F32), (128, 128)))
        out_ref[group * 128 : (group + 1) * 128, :] = square.astype(jnp.int32)


def vocab_stats_body(unit, meta, _u, _p, u_ref, p_ref, *refs):
    vocab = u_ref.shape[0]
    chunks = vocab_chunks(vocab)
    if unit == 0:
        mine_ref, sib_ref, target_ref, table_ref, top_ref, st_ref, acc_ref, col_ref, sem = refs
        loads = table_loads(table_ref, u_ref, sem, sum(FIRST_GROUPS), SECOND_GROUPS)
    else:
        mine_ref, sib_ref, target_ref, top_ref, st_ref, acc_ref, col_ref = refs
        loads = {}
    for load in loads.values():
        load.start()
    acc_ref[...] = jnp.zeros_like(acc_ref)
    local_columns(unit, meta, vocab, target_ref, col_ref)
    lane = lax.broadcasted_iota(jnp.int32, (BLOCK, 128), 1)
    for place, (start, size) in enumerate(chunks):
        if start in loads:
            loads[start].wait()
        col = lax.broadcasted_iota(jnp.int32, (BLOCK, size), 1)
        for half, rows_ref in enumerate((mine_ref, sib_ref)):
            here = slice(half * BLOCK, (half + 1) * BLOCK)
            logits = dot_nt(rows_ref[...], u_ref[start : start + size, :])
            top = jnp.max(logits, axis=1, keepdims=True)
            prob = jnp.exp(logits - top)
            total = jnp.sum(prob, axis=1, keepdims=True)
            hit = col == col_ref[here, 0:1] - start
            picked = jnp.sum(jnp.where(hit, logits, 0.0), axis=1, keepdims=True)
            p_ref[place, here, 0:size] = prob.astype(BF)
            acc = acc_ref[here, :]
            acc = jnp.where(lane == place, top, acc)
            acc = jnp.where(lane == place + 32, total, acc)
            acc_ref[here, :] = jnp.where(lane == 64, acc + picked, acc)
    acc = acc_ref[...]
    lane = lax.broadcasted_iota(jnp.int32, acc.shape, 1)
    top_ref[...] = acc
    tops = jnp.where(lane < len(chunks), acc, -1e30)
    best = jnp.max(tops, axis=1, keepdims=True)
    totals = pltpu.roll(acc, 128 - 32, 1)
    total = jnp.sum(
        jnp.where(lane < len(chunks), totals * jnp.exp(tops - best), 0.0), axis=1, keepdims=True
    )
    picked = jnp.sum(jnp.where(lane == 64, acc, 0.0), axis=1, keepdims=True)
    pair = jnp.where(lane == 0, best + jnp.log(total), jnp.where(lane == 1, picked, 0.0))
    st_ref[...] = jnp.transpose(pair)[0:8, :]


def vocab_stats(meta, unit, mine, sib, targets, table, keep, after=()):
    rows = 2 * BLOCK
    first = unit == 0
    return kernel_call(
        partial(vocab_stats_body, unit),
        f"vocab_stats_{unit}",
        (),
        [IN_VMEM] * 3 + [pl.BlockSpec(memory_space=pl.ANY)] * first,
        [IN_VMEM] * 2,
        [sds((rows, 128), F32), sds((8, rows), F32)],
        [pltpu.VMEM((rows, 128), F32), pltpu.VMEM((rows, 128), jnp.int32)]
        + [pltpu.SemaphoreType.DMA((len(SECOND_GROUPS),))] * first,
        after=after,
        keep=keep,
        use_keep=True,
    )(meta, mine, sib, targets, *((table,) * first))


def swap_halves(pair):
    return jnp.concatenate([pair[:, BLOCK:], pair[:, :BLOCK]], axis=1)


def vocab_back_body(
    unit, meta, u_ref, p_ref, _u, _p, lens_ref, target_ref, top_ref, s0, s1, s2, s3,
    d0, d1, d2, d3, loss_ref, scale_ref, acc_ref, col_ref,
):
    vocab = u_ref.shape[0]
    chunks = vocab_chunks(vocab)
    rows = 2 * BLOCK
    acc_ref[...] = jnp.zeros_like(acc_ref)
    local_columns(unit, meta, vocab, target_ref, col_ref)
    parts = [s0[...], swap_halves(s1[...]), s2[...], swap_halves(s3[...])]
    lses = [part[0:1, :] for part in parts]
    best = jnp.maximum(jnp.maximum(lses[0], lses[1]), jnp.maximum(lses[2], lses[3]))
    total = sum(jnp.exp(one - best) for one in lses)
    log_norm = best + jnp.log(total)
    picked = sum(part[1:2, :] for part in parts)
    place = lax.broadcasted_iota(jnp.int32, (1, rows), 1)
    core = core_of(meta)
    offset = jnp.where(place < BLOCK, core * BLOCK, (1 - core) * BLOCK - BLOCK)
    valid = (unit * UNIT + place + offset < lens_ref[meta[SEQ]]).astype(F32)
    loss_ref[...] = jnp.broadcast_to(
        jnp.sum((log_norm - picked) * valid, axis=1, keepdims=True), (8, 128)
    )
    weight = valid / token_count(lens_ref)
    row = lax.broadcasted_iota(jnp.int32, (128, rows), 0)
    lines = jnp.where(row == 0, log_norm, 0.0)
    lines = jnp.where(row == 1, weight, lines)
    lines = jnp.where(row == 2, (jnp.exp(picked - log_norm) - 1.0) * weight, lines)
    cols = jnp.transpose(lines)
    lane = lax.broadcasted_iota(jnp.int32, (rows, 128), 1)
    take = lambda k: jnp.sum(jnp.where(lane == k, cols, 0.0), axis=1, keepdims=True)
    tops = jnp.where(lane < len(chunks), top_ref[...], -1e30)
    scales = jnp.exp(tops - take(0)) * take(1)
    scale_ref[...] = jnp.where(lane == 64, take(2), scales)

    lane = lax.broadcasted_iota(jnp.int32, (BLOCK, 128), 1)
    for place, (start, size) in enumerate(chunks):
        col = lax.broadcasted_iota(jnp.int32, (BLOCK, size), 1)
        for half in range(2):
            here = slice(half * BLOCK, (half + 1) * BLOCK)
            scales = scale_ref[here, :]
            at_hit = jnp.sum(jnp.where(lane == 64, scales, 0.0), axis=1, keepdims=True)
            scale = jnp.sum(jnp.where(lane == place, scales, 0.0), axis=1, keepdims=True)
            hit = col == col_ref[here, 0:1] - start
            grad = jnp.where(hit, at_hit, p_ref[place, here, 0:size].astype(F32) * scale)
            acc_ref[here, :] += dot_nn(grad.astype(BF), u_ref[start : start + size, :])

    quarter = BLOCK // 2
    for rel, out_ref in enumerate((d0, d1, d2, d3)):
        place = (rel & 1) * 2 + (ybit_of(meta) ^ (rel >> 1))
        out_ref[...] = acc_ref[columns(place, quarter), :].astype(BF)


def vocab_back(meta, unit, lens, targets, tops, stats, keep, after=()):
    width = keep[0].shape[1]
    rows = 2 * BLOCK
    quarter = sds((BLOCK // 2, width), BF)
    return kernel_call(
        partial(vocab_back_body, unit),
        f"vocab_back_{unit}",
        (),
        [SCALARS] + [IN_VMEM] * 6,
        [IN_VMEM] * 5,
        [quarter] * 4 + [sds((8, 128), F32)],
        [
            pltpu.VMEM((rows, 128), F32),
            pltpu.VMEM((rows, width), F32),
            pltpu.VMEM((rows, 128), jnp.int32),
        ],
        after=after,
        keep=keep,
        use_keep=True,
    )(meta, lens, targets, tops, *stats)


def norm_back_body(last, meta, *refs):
    parts, (res_ref, gain_ref, rank_ref) = refs[:4], refs[4:7]
    atts, wos, maps = refs[7:11], refs[11:15], refs[15:19]
    if last:
        before_ref, *outs, keep_ref, send_ref, hold_ref = refs[19:]
    else:
        *outs, sum_ref, hold_ref = refs[19:]
    proj = meta[PROJ]
    shard = atts[0].shape[1]
    dnormed = sum(part[...].astype(F32) for part in parts)
    residual = res_ref[...]
    center = residual - jnp.mean(residual, axis=-1, keepdims=True)
    spread = jnp.mean(center * center, axis=-1, keepdims=True)
    inv = lax.rsqrt(spread + EPS_NORM)
    hat = center * inv
    dhat = dnormed * gain_ref[2:3, :]
    dres = inv * (
        dhat
        - jnp.mean(dhat, axis=-1, keepdims=True)
        - hat * jnp.mean(dhat * hat, axis=-1, keepdims=True)
    )
    hold_ref[...] = dres.astype(BF)
    dbranch = hold_ref[...]
    drank = None
    for rel, m_ref in enumerate(maps):
        part = dot_nt(hold_ref[:, columns(proj ^ rel, shard)], m_ref[1])
        drank = part if drank is None else drank + part
    drank = (ADAPTER_SCALE * drank).astype(BF)
    for rel in range(4):
        datt = dot_nt(dbranch, wos[rel][...]) + dot_nn(drank, maps[rel][0])
        outs[rel][...] = datt.astype(BF)
        g_down = dot_tn(drank, atts[rel][...])
        g_up = ADAPTER_SCALE * dot_tn(rank_ref[...], hold_ref[:, columns(proj ^ rel, shard)])
        if last:
            dest = (keep_ref, send_ref)[rel & 1]
            dest[rel >> 1, 0] = (before_ref[rel, 0] + g_down).astype(BF)
            dest[rel >> 1, 1] = (before_ref[rel, 1] + g_up).astype(BF)
        else:
            sum_ref[rel, 0] = g_down
            sum_ref[rel, 1] = g_up


def norm_back(
    meta, unit, last, parts, residual, gains, rank_out, att, wo, maps, before, after=(), keep=()
):
    quarter, width = residual.shape
    shard = att[0].shape[1]
    rank = rank_out.shape[1]
    piece = (quarter, shard)
    if last:
        more = [sds((2, 2, rank, shard), BF)] * 2
    else:
        more = [sds((4, 2, rank, shard), F32)]
    return kernel_call(
        partial(norm_back_body, last),
        f"norm_back_{unit}",
        (1,),
        [whole(one.shape) for one in parts]
        + [whole(residual.shape), whole(gains.shape), whole(rank_out.shape)]
        + [pl.BlockSpec(piece, lambda i, m: (ybit_of(m), 0))] * 4
        + [whole((shard, width))] * 4
        + [whole((2, rank, shard))] * 4
        + [whole(one.shape) for one in before],
        [whole(piece)] * 4 + [whole(one.shape) for one in more],
        [sds(piece, BF)] * 4 + more,
        [pltpu.VMEM((quarter, width), BF)],
        flops=2 * quarter * width * width,
        moved=2 * width * width + 12 * quarter * width,
        after=after,
        keep=keep,
    )(meta, *parts, residual, gains, rank_out, *att, *wo, *maps, *before)


def grads_body(
    meta, dq0, dq1, dk_ref, dv_ref, cos_ref, up_ref, down_ref, rank_ref, ups, low_ref,
    keep_ref, send_ref, up_grad_ref, drank_ref,
):
    proj = meta[PROJ]
    rank, shard = ups.shape[1:]
    dk = turn(dk_ref[...], cos_ref[...], up_ref[...], down_ref[...], -1.0).astype(BF)
    dpre = [jnp.concatenate([dq0[...], dq1[...]], axis=0), dk, dv_ref[...].astype(BF)]
    for k in range(3):
        here = slice(k * rank, (k + 1) * rank)
        up_grad_ref[k] = ADAPTER_SCALE * dot_tn(rank_ref[:, here], dpre[k])
        drank_ref[:, here] = (ADAPTER_SCALE * dot_nt(dpre[k], ups[k])).astype(BF)
    drank = drank_ref[...]
    for rel in range(4):
        grad = dot_tn(drank, low_ref[:, columns(proj ^ rel, shard)])
        dest = (keep_ref, send_ref)[rel & 1]
        dest[rel >> 1] = grad.reshape(3, rank, shard).astype(BF)


def adapter_grads(meta, dqs, dk, dv, tables, rank_in, ups, low):
    rows, shard = dk.shape
    rank = ups.shape[1]
    pair = (2, 3, rank, shard)
    args = (*dqs, dk, dv, *tables, rank_in, ups, low)
    return kernel_call(
        grads_body,
        "adapter_grads",
        (1,),
        [whole(one.shape) for one in args],
        [whole(pair), whole(pair), whole((3, rank, shard))],
        [sds(pair, BF), sds(pair, BF), sds((3, rank, shard), F32)],
        [pltpu.VMEM((rows, 3 * rank), BF)],
        flops=2 * rows * low.shape[1] * 3 * rank,
        moved=30 * rows * shard,
    )(meta, *args)


def signs(row_ids, col_ids, seed):
    hashed = row_ids * 1640531527 + col_ids * 747796405 + seed * 277803737
    hashed = hashed ^ hashed >> 15 & 131071
    hashed = hashed * 2024237689
    hashed = hashed ^ hashed >> 13 & 524287
    return 1.0 - 2.0 * (hashed >> 17 & 1).astype(F32)


def sketch_one(meta, seed, grad, sketch):
    rank, shard = grad.shape
    left_rows = lax.broadcasted_iota(jnp.int32, (sketch, shard), 1) + meta[PROJ] * shard
    left_cols = lax.broadcasted_iota(jnp.int32, (sketch, shard), 0)
    right_rows = lax.broadcasted_iota(jnp.int32, (rank, sketch), 0)
    right_cols = lax.broadcasted_iota(jnp.int32, (rank, sketch), 1)
    left = signs(left_rows, left_cols, 2 * seed).astype(BF)
    right = signs(right_rows, right_cols, 2 * seed + 1)
    return jnp.dot(dot_nt(left, grad), right, precision=lax.Precision.HIGHEST)


def local_sketch_body(meta, seeds_ref, lens_ref, own_ref, far_ref, up_ref, block_ref, full_ref):
    size = block_ref.shape[2]
    count = token_count(lens_ref)
    out = own_ref[...] + far_ref[...].astype(F32)
    for place, grad in enumerate((out[0], up_ref[0], up_ref[1], up_ref[2], out[1])):
        for dest in range(block_ref.shape[0]):
            block_ref[dest, place] = grad[dest * size : (dest + 1) * size].astype(BF)
        full_ref[place] = count * sketch_one(
            meta, seeds_ref[3 + place], grad.astype(BF), full_ref.shape[1]
        )


def local_sketch(meta, seeds, lens, own, far, ups, sketch_width):
    _, rank, shard = own.shape
    count = lens.shape[0]
    blocks = (count, 5, rank // count, shard)
    full = (5, sketch_width, sketch_width)
    return kernel_call(
        local_sketch_body, "local_sketch", (1,),
        [SCALARS, SCALARS, whole(own.shape), whole(far.shape), whole(ups.shape)],
        [whole(blocks), whole(full)],
        [sds(blocks, BF), sds(full, F32)],
        flops=10 * rank * shard * sketch_width,
        moved=16 * own.size,
    )(meta, seeds, lens, own, far, ups)


def gather_body(meta, keep_ref, got_ref, far_ref, five_ref, block_ref, grad_ref):
    size = block_ref.shape[2]
    total = keep_ref[0].astype(F32) + got_ref[0].astype(F32) + far_ref[...].astype(F32)
    grad_ref[...] = total.astype(BF)
    for dest in range(block_ref.shape[0]):
        for mat in range(3):
            block_ref[dest, mat] = total[mat, dest * size : (dest + 1) * size].astype(BF)
        block_ref[dest, 3:8] = five_ref[dest]


def gather_blocks(meta, keep, got, far, five):
    count, _, size, shard = five.shape
    blocks = (count, 8, size, shard)
    pair = pl.BlockSpec((1, *keep.shape[1:]), lambda i, m: (0, 0, 0, 0))
    return kernel_call(
        gather_body, "gather_blocks", (1,),
        [pair, pair, whole(far.shape), whole(five.shape)],
        [whole(blocks), whole(far.shape)],
        [sds(blocks, BF), sds(far.shape, BF)],
    )(meta, keep, got, far, five)


def sketch_body(meta, seeds_ref, lens_ref, grad_ref, five_ref, f0, f1, f2, f3, full_ref):
    count = token_count(lens_ref)
    sketch = full_ref.shape[1]
    full_ref[3:8] = five_ref[...]
    for mat in range(3):
        full_ref[mat] = count * sketch_one(meta, seeds_ref[mat], grad_ref[mat], sketch)
    size = sketch // 4
    for rel, out_ref in enumerate((f0, f1, f2, f3)):
        out_ref[...] = full_ref[:, columns(meta[PROJ] ^ rel, size), :]


def sketch(meta, seeds, lens, grads, five):
    sketch_width = five.shape[1]
    piece = (8, sketch_width // 4, sketch_width)
    return kernel_call(
        sketch_body, "sketch", (1,),
        [SCALARS, SCALARS, whole(grads.shape), whole(five.shape)],
        [whole(piece)] * 4,
        [sds(piece, F32)] * 4,
        [pltpu.VMEM((8, sketch_width, sketch_width), F32)],
        flops=2 * grads.size * sketch_width,
        moved=2 * grads.size,
    )(meta, seeds, lens, grads, five)


def lane_value(row, lane, place):
    return jnp.sum(jnp.where(lane == place, row, 0.0), axis=1, keepdims=True)


def tally_body(
    units, meta, got_ref, target_ref, f0, f1, f2, f3, *refs
):
    losses, (total_ref, line_ref) = refs[:units], refs[units:]
    total = jnp.sum(got_ref[...].astype(F32), axis=0)
    total_ref[...] = total
    features = f0[...] + f1[...] + f2[...] + f3[...]
    squares = jnp.sum(total * total)
    own = jnp.sum(features * features)
    loss = sum(jnp.sum(one[0:1, 0:1]) for one in losses)
    loss = jnp.where(meta[PROJ] == 0, loss, 0.0)
    lane = lax.broadcasted_iota(jnp.int32, (1, 128), 1)
    line = jnp.where(lane == 0, squares, 0.0)
    line = jnp.where(lane == 1, loss, line)
    line = jnp.where(lane == 2, own, line)
    checkpoints = target_ref.shape[0]
    for c in range(checkpoints):
        theirs = target_ref[c]
        line = jnp.where(lane == 3 + c, jnp.sum(features * theirs), line)
        line = jnp.where(lane == 3 + checkpoints + c, jnp.sum(theirs * theirs), line)
    line_ref[...] = jnp.broadcast_to(line, line_ref.shape)


def tally(meta, devices, got, targets, pieces, losses):
    _, mats, slice_rank, shard = got.shape
    args = (got, targets, *pieces, *losses)
    return kernel_call(
        partial(tally_body, len(losses)),
        "tally",
        (1,),
        [whole(one.shape) for one in args],
        [whole((mats, slice_rank, shard)), whole((devices, 128))],
        [sds((mats, slice_rank, shard), F32), sds((devices, 128), F32)],
    )(meta, *args)


def optimizer_step(weight, grad_in, first_in, second_in, clipping_scale):
    grad_clip = grad_in * clipping_scale
    first_new = BETA_ONE * first_in + (1.0 - BETA_ONE) * grad_clip
    second_new = BETA_TWO * second_in + (1.0 - BETA_TWO) * grad_clip * grad_clip
    first_hat = first_new / (1.0 - BETA_ONE**STEP)
    second_hat = second_new / (1.0 - BETA_TWO**STEP)
    new_weight = weight - LEARN_RATE * (
        first_hat / (jnp.sqrt(second_hat) + ADAM_EPS) + WEIGHT_DECAY * weight
    )
    return (new_weight, first_new, second_new)


def finish_body(
    proj_count, checkpoints, meta, lens_ref, lines_ref, total_ref,
    dw, uw, dm, um, ds, us,
    loss_out, norm_out, influence_out, dw_out, uw_out, dm_out, um_out, ds_out, us_out,
):
    lines = lines_ref[...]
    everyone = jnp.sum(lines, axis=0, keepdims=True)
    row = lax.broadcasted_iota(jnp.int32, lines.shape, 0)
    ours = jnp.sum(
        jnp.where(row // proj_count == meta[SEQ], lines, 0.0), axis=0, keepdims=True
    )
    lane = lax.broadcasted_iota(jnp.int32, (1, 128), 1)
    grad_norm = jnp.sqrt(lane_value(everyone, lane, 0))
    own = lane_value(ours, lane, 2)
    influence = jnp.zeros((1, 1), F32)
    for c in range(checkpoints):
        dot = lane_value(ours, lane, 3 + c)
        theirs = lane_value(ours, lane, 3 + checkpoints + c)
        influence += (1.0 - c / checkpoints) * dot * lax.rsqrt(own * theirs + 1e-12)
    loss_out[0] = jnp.sum(lane_value(everyone, lane, 1))
    loss_out[1] = token_count(lens_ref)
    norm_out[0] = jnp.sum(grad_norm)
    influence_out[0] = jnp.sum(influence)
    clip = jnp.minimum(1.0, CLIP_NORM / (grad_norm + 1e-06))
    half = total_ref.shape[0] // 2
    for base, ins, outs in (
        (0, (dw, dm, ds), (dw_out, dm_out, ds_out)),
        (half, (uw, um, us), (uw_out, um_out, us_out)),
    ):
        for k in range(half):
            new = optimizer_step(
                ins[0][k], total_ref[base + k], ins[1][k], ins[2][k], clip
            )
            for out, value in zip(outs, new):
                out[k] = value


def finish(meta, proj_count, checkpoints, lens, lines, total, params):
    block = whole(params[0].shape)
    return kernel_call(
        partial(finish_body, proj_count, checkpoints),
        "finish",
        (1,),
        [SCALARS, whole(lines.shape), whole(total.shape)] + [block] * 6,
        [SCALARS] * 3 + [block] * 6,
        [sds((2,), F32), sds((1,), F32), sds((1,), F32)] + [sds(params[0].shape, F32)] * 6,
        flops=20 * total.size,
        moved=28 * total.size,
    )(meta, lens, lines, total, *params)


def to_partner(array, axis, size, offset):
    return lax.ppermute(array, axis, [(i, i ^ offset) for i in range(size)])


def on_device(
    seq_count,
    proj_count,
    inputs,
    targets,
    lengths,
    norm_gain_vectors,
    query_key_value_weight,
    attention_output_weight,
    feedforward_input_weight,
    feedforward_output_weight,
    unembed,
    adapter_down_maps,
    adapter_up_maps,
    down_first_moment,
    up_first_moment,
    down_second_moment,
    up_second_moment,
    target_gradient_sketches,
    seeds,
):
    rows, width = inputs.shape
    shard = attention_output_weight.shape[0]
    vocab_local = unembed.shape[1]
    slice_rank = adapter_up_maps.shape[1]
    rank = slice_rank * seq_count
    sketch_width = target_gradient_sketches.shape[3]
    proj = lax.axis_index("proj")
    seq = lax.axis_index("dp")
    units = rows // UNIT

    over_proj = lambda array, rel: to_partner(array, "proj", proj_count, rel)
    over_seq = lambda array, rel: to_partner(array, "dp", seq_count, rel)

    meta = jnp.stack([proj, seq]).astype(jnp.int32)
    targets = targets.reshape(rows // 128, 128)
    table = jnp.transpose(unembed)
    tables = rotary_tables(rows, shard)
    transposed = lambda array: jnp.transpose(array, (0, 2, 1))

    def from_all(array):
        y = over_proj(array, 2)
        return (array, over_proj(array, 1), y, over_proj(y, 1))

    def exchange(*pieces):
        return [pieces[0]] + [over_proj(pieces[rel], rel) for rel in (1, 2, 3)]

    packed = pack_maps(meta, seq_count, transposed(adapter_down_maps), adapter_up_maps)
    arrived = lax.all_to_all(packed, "dp", split_axis=0, concat_axis=0, tiled=True)
    wo = from_all(attention_output_weight)

    w_ffn = (feedforward_input_weight, feedforward_output_weight)
    f0_mine, f0_sib = ffn(meta, 0, inputs, norm_gain_vectors, *w_ffn)
    low, qkv = frozen_qkv(
        meta, inputs, norm_gain_vectors, jnp.transpose(query_key_value_weight, (1, 0, 2)),
        (f0_mine,),
    )
    maps, ups = unpack_maps(meta, arrived, (low,))
    maps = from_all(maps)
    f1_mine, f1_sib, f0_chip = ffn(
        meta, 1, inputs, norm_gain_vectors, *w_ffn, (f0_mine, over_proj(f0_sib, 1)), (maps[0],)
    )
    queries, keys, values, rank_in, f1_chip = make_qkv(
        meta, low, qkv, tables, maps, ups, (f1_mine, over_proj(f1_sib, 1))
    )
    f_chip = (f0_chip, f1_chip)
    f_far = [over_proj(one, 2) for one in f_chip]

    att, lse = [None, None], [None, None]
    for unit in range(2):
        mine, sib, lse[unit], *buffers = attend(
            meta, unit, queries, keys, values, table, (lse[0],) if unit else ()
        )
        att[unit] = exchange(mine, sib, mine, sib)

    def mix_unit(unit, after, keep=()):
        normed, residual, rank_out, *keep = mix(
            meta, unit, inputs, norm_gain_vectors, f_chip[unit], f_far[unit], att[unit], wo, maps,
            after, keep,
        )
        return (normed, over_proj(normed, 1)), residual, rank_out, keep

    def stats_unit(unit, normed, keep, after=()):
        top, stat, *keep = vocab_stats(meta, unit, *normed, targets, table, keep, after)
        return top, exchange(stat, stat, stat, stat), keep

    def back_unit(unit, top, stats, keep, after):
        d0, d1, d2, d3, loss, *keep = vocab_back(
            meta, unit, lengths, targets, top, stats, keep, after
        )
        return exchange(d0, d1, d2, d3), loss, keep

    def norm_unit(unit, parts, residual, rank_out, before, after, keep=()):
        d0, d1, d2, d3, *more = norm_back(
            meta, unit, unit == 1, parts, residual, norm_gain_vectors,
            rank_out, att[unit], wo, maps, before, after, keep,
        )
        grads = more[: 1 + unit]
        return exchange(d0, d1, d2, d3), grads, more[1 + unit :]

    normed0, residual0, rank0, keep = mix_unit(0, (lse[1],), buffers)
    top0, stats0, keep = stats_unit(0, normed0, keep)
    normed1, residual1, rank1, keep = mix_unit(1, (stats0[0],), keep)
    dnormed0, loss0, keep = back_unit(0, top0, stats0, keep, (rank1,))
    top1, stats1, keep = stats_unit(1, normed1, keep, (loss0,))
    datt0, out_grads, keep = norm_unit(
        0, dnormed0, residual0, rank0, (), (stats1[0],), keep
    )
    dnormed1, loss1, _ = back_unit(1, top1, stats1, keep, (datt0[0],))
    dq0, dk, dv = attend_back(
        meta, 0, datt0, queries, keys, values, lse[0], tables, after=(loss1,)
    )
    datt1, (out_keep, out_send), _ = norm_unit(
        1, dnormed1, residual1, rank1, out_grads, (dq0,)
    )
    dq1, dk, dv, out_own, out_far = attend_back(
        meta, 1, datt1, queries, keys, values, lse[1], tables,
        (dk, dv), (out_keep, over_proj(out_send, 1)),
    )
    out_far = over_proj(out_far, 2)

    in_keep, in_send, up_grads = adapter_grads(
        meta, (dq0, dq1), dk, dv, tables, rank_in, ups, low
    )
    in_got = over_proj(in_send, 1)
    in_far = over_proj((in_keep[1].astype(F32) + in_got[1].astype(F32)).astype(BF), 2)
    blocks, five = local_sketch(meta, seeds, lengths, out_own, out_far, up_grads, sketch_width)
    blocks, in_grads = gather_blocks(meta, in_keep, in_got, in_far, blocks)
    arrived = lax.all_to_all(blocks, "dp", split_axis=0, concat_axis=0, tiled=True)
    pieces = exchange(*sketch(meta, seeds, lengths, in_grads, five))

    device_count = seq_count * proj_count
    total, lines = tally(
        meta, device_count, arrived, target_gradient_sketches, pieces, (loss0, loss1)
    )
    lines = lax.all_to_all(lines, ("dp", "proj"), split_axis=0, concat_axis=0, tiled=True)
    params = (
        transposed(adapter_down_maps),
        adapter_up_maps,
        transposed(down_first_moment),
        up_first_moment,
        transposed(down_second_moment),
        up_second_moment,
    )
    loss_parts, grad_norm, influence, dw, uw, dm, um, ds, us = finish(
        meta, proj_count, target_gradient_sketches.shape[0], lengths, lines, total, params
    )
    return (
        loss_parts,
        grad_norm,
        influence,
        transposed(dw),
        uw,
        transposed(dm),
        um,
        transposed(ds),
        us,
    )


def solution(mesh):
    in_specs = (
        P("dp", None),
        P("dp"),
        P(),
        P(),
        P(None, None, "proj"),
        P("proj", None),
        P(None, "proj"),
        P("proj", None),
        P(None, "proj"),
        P(None, "proj", "dp"),
        P(None, "dp", "proj"),
        P(None, "proj", "dp"),
        P(None, "dp", "proj"),
        P(None, "proj", "dp"),
        P(None, "dp", "proj"),
        P(None, None, "proj", None),
        P(),
    )
    out_specs = (
        P(),
        P(),
        P("dp"),
        P(None, "proj", "dp"),
        P(None, "dp", "proj"),
        P(None, "proj", "dp"),
        P(None, "dp", "proj"),
        P(None, "proj", "dp"),
        P(None, "dp", "proj"),
    )
    return jax.shard_map(
        partial(on_device, mesh.shape["dp"], mesh.shape["proj"]),
        mesh=mesh,
        in_specs=in_specs,
        out_specs=out_specs,
        check_vma=False,
    )
```

```python
from functools import partial
import math

import jax
import jax.numpy as jnp
import numpy as np
from jax import lax
from jax.experimental import pallas as pl
from jax.experimental.pallas import tpu as pltpu
from jax.sharding import PartitionSpec as P

HEAD = 64
ROT = 16
STEP = 10

EPS_NORM = 1e-05
ADAPTER_SCALE = 0.25
CLIP_NORM = 0.05
LEARN_RATE = 0.05
BETA_ONE = 0.9
BETA_TWO = 0.99
ADAM_EPS = 1e-08
WEIGHT_DECAY = 0.01

BF = jnp.bfloat16
F32 = jnp.float32
BLOCK = 256
UNIT = 512
FIRST_GROUPS = (3, 3, 3, 3)
SECOND_GROUPS = (5, 4, 4)
CHUNK_V = 512
MIB = 2**20

PROJ, SEQ = range(2)


def core_of(meta):
    return meta[PROJ] & 1


def ybit_of(meta):
    return meta[PROJ] >> 1


def token_count(lens_ref):
    return sum(lens_ref[i] for i in range(lens_ref.shape[0])).astype(F32)


def dot_nn(lhs, rhs):
    return lax.dot_general(lhs, rhs, (((1,), (0,)), ((), ())), preferred_element_type=F32)


def dot_nt(lhs, rhs):
    return lax.dot_general(lhs, rhs, (((1,), (1,)), ((), ())), preferred_element_type=F32)


def dot_tn(lhs, rhs):
    return lax.dot_general(lhs, rhs, (((0,), (0,)), ((), ())), preferred_element_type=F32)


def kernel_call(
    body, name, grid, in_specs, out_specs, out_shape, scratch=(), flops=0, moved=0, after=(),
    vmem=20, keep=(), use_keep=False,
):
    single = not isinstance(out_shape, (list, tuple))
    if single:
        out_specs, out_shape = [out_specs], [out_shape]
    first_keep = 1 + len(in_specs) + len(after)
    first_out = first_keep + len(keep)
    first_kept = first_out + len(out_shape)
    first_scratch = first_kept + len(keep)

    def run(*refs):
        kept = refs[first_keep:first_out] + refs[first_kept:first_scratch]
        body(
            refs[0],
            *(kept if use_keep else ()),
            *refs[1 : 1 + len(in_specs)],
            *refs[first_out:first_kept],
            *refs[first_scratch:],
        )

    anywhere = pl.BlockSpec(memory_space=pl.ANY)
    keep_spec = IN_VMEM if use_keep else anywhere
    call = pl.pallas_call(
        run,
        grid_spec=pltpu.PrefetchScalarGridSpec(
            num_scalar_prefetch=1,
            grid=grid,
            in_specs=list(in_specs) + [anywhere] * len(after) + [keep_spec] * len(keep),
            out_specs=list(out_specs) + [keep_spec] * len(keep),
            scratch_shapes=list(scratch),
        ),
        out_shape=list(out_shape) + [pltpu.VMEM(one.shape, one.dtype) for one in keep],
        input_output_aliases={
            first_keep + i: len(out_shape) + i for i in range(len(keep))
        },
        compiler_params=pltpu.CompilerParams(vmem_limit_bytes=vmem * MIB),
        cost_estimate=pl.CostEstimate(flops=10**12, bytes_accessed=1000, transcendentals=0),
        name=name,
    )

    def apply(*args):
        results = call(*args, *after, *[held(one) for one in keep])
        return results[0] if single else results

    return apply


def whole(shape):
    zeros = (0,) * len(shape)
    return pl.BlockSpec(shape, lambda *_: zeros)


SCALARS = pl.BlockSpec(memory_space=pltpu.SMEM)
IN_VMEM = pl.BlockSpec(memory_space=pltpu.VMEM)


def held(array):
    return pltpu.with_memory_space_constraint(array, pltpu.VMEM)


def sds(shape, dtype):
    return jax.ShapeDtypeStruct(shape, dtype)


def normalize(rows):
    center = rows - jnp.mean(rows, axis=-1, keepdims=True)
    spread = jnp.mean(center * center, axis=-1, keepdims=True)
    return center * lax.rsqrt(spread + EPS_NORM)


def columns(index, size):
    return pl.ds(pl.multiple_of(index * size, size), size)


def pack_body(meta, down_ref, up_ref, out_ref):
    mats = down_ref.shape[0]
    down, up = down_ref[...].astype(BF), up_ref[...].astype(BF)
    for dest in range(out_ref.shape[0]):
        out_ref[dest, 0] = down[mats - 1]
        out_ref[dest, 1] = up[mats - 1]
        out_ref[dest, 2 : mats + 1] = down[: mats - 1]
        out_ref[dest, mats + 1 :] = up[: mats - 1]


def pack_maps(meta, seq_count, down, up):
    shape = (seq_count, 2 * down.shape[0], *down.shape[1:])
    return kernel_call(
        pack_body, "pack_maps", (1,),
        [whole(down.shape), whole(up.shape)], whole(shape), sds(shape, BF),
        vmem=58,
    )(meta, down, up)


def unpack_body(meta, got_ref, out_ref, up_ref):
    count, _, size, _ = got_ref.shape
    for block in range(count):
        here = slice(block * size, (block + 1) * size)
        out_ref[:, here, :] = got_ref[block, 0:5]
        up_ref[:, here, :] = got_ref[block, 5:8]


def unpack_maps(meta, got, after):
    count, mats, size, shard = got.shape
    rank = count * size
    if size % 16:
        maps = jnp.transpose(got, (1, 0, 2, 3)).reshape(mats, rank, shard)
        return maps[:5], maps[5:]
    return kernel_call(
        unpack_body, "unpack_maps", (1,),
        [whole(got.shape)], [whole((5, rank, shard)), whole((3, rank, shard))],
        [sds((5, rank, shard), BF), sds((3, rank, shard), BF)],
        vmem=58,
        after=after,
    )(meta, got)


def side_sum(refs):
    one_ref, two_ref, out_ref = refs
    out_ref[...] = (one_ref[...].astype(F32) + two_ref[...].astype(F32)).astype(BF)


def ffn_body(unit, meta, x_ref, gain_ref, up_ref, down_ref, *refs):
    if unit == 0:
        mine_ref, sib_ref, low_ref, part_ref = refs
    else:
        one_ref, two_ref, mine_ref, sib_ref, sum_ref, low_ref, part_ref = refs
    step = pl.program_id(0)

    @pl.when(step == 0)
    def _():
        hat = normalize(x_ref[...].astype(F32))
        low_ref[...] = (hat * gain_ref[1:2, :]).astype(BF)
        part_ref[...] = jnp.zeros_like(part_ref)
        if unit:
            side_sum((one_ref, two_ref, sum_ref))

    hidden = dot_nn(low_ref[...], up_ref[...])
    hidden = 0.5 * hidden * (1.0 + lax.erf(hidden * (0.5**0.5)))
    part_ref[...] += dot_nn(hidden.astype(BF), down_ref[...])

    @pl.when(step == pl.num_programs(0) - 1)
    def _():
        core = core_of(meta)
        mine_ref[...] = part_ref[columns(core, BLOCK), :].astype(BF)
        sib_ref[...] = part_ref[columns(1 - core, BLOCK), :].astype(BF)


def ffn(meta, unit, x, gains, w_up, w_down, sums=(), after=()):
    rows, width = x.shape
    chunk = 512
    half = sds((BLOCK, width), BF)
    results = 2 + len(sums) // 2
    return kernel_call(
        partial(ffn_body, unit),
        f"ffn_{unit}",
        (w_up.shape[1] // chunk,),
        [
            pl.BlockSpec((UNIT, width), lambda i, m: (unit, 0)),
            whole(gains.shape),
            pl.BlockSpec((width, chunk), lambda i, m: (0, i)),
            pl.BlockSpec((chunk, width), lambda i, m: (i, 0)),
        ]
        + [whole((BLOCK, width))] * len(sums),
        [whole((BLOCK, width))] * results,
        [half] * results,
        [pltpu.VMEM((UNIT, width), BF), pltpu.VMEM((UNIT, width), F32)],
        flops=4 * UNIT * width * w_up.shape[1],
        moved=4 * w_up.size + 8 * UNIT * width,
        vmem=58,
        after=after,
    )(meta, x, gains, w_up, w_down, *sums)


def qkv_body(meta, x_ref, gain_ref, w_ref, low_ref, out_ref):
    hat = normalize(x_ref[...].astype(F32))
    low = (hat * gain_ref[0:1, :]).astype(BF)
    low_ref[...] = low
    shard = w_ref.shape[2]
    for k in range(3):
        out_ref[:, k * shard : (k + 1) * shard] = dot_nn(low, w_ref[k])


def frozen_qkv(meta, x, gains, w_qkv, after=()):
    rows, width = x.shape
    out = 3 * w_qkv.shape[2]
    return kernel_call(
        qkv_body,
        "frozen_qkv",
        (rows // UNIT,),
        [
            pl.BlockSpec((UNIT, width), lambda i, m: (i, 0)),
            whole(gains.shape),
            whole(w_qkv.shape),
        ],
        [
            pl.BlockSpec((UNIT, width), lambda i, m: (i, 0)),
            pl.BlockSpec((UNIT, out), lambda i, m: (i, 0)),
        ],
        [sds((rows, width), BF), sds((rows, out), F32)],
        flops=2 * rows * width * out,
        moved=2 * w_qkv.size + 4 * x.size + 4 * rows * out,
        vmem=58,
        after=after,
    )(meta, x, gains, w_qkv)


def rotary_tables(rows, shard):
    half = ROT // 2
    freq = np.exp(np.arange(half) * (-2.0 * math.log(10000.0) / ROT))
    angles = np.arange(rows)[:, None] * freq[None, :]
    cos, sin = np.cos(angles), np.sin(angles)
    one = np.ones((rows, HEAD))
    one[:, :half] = cos
    one[:, half:ROT] = cos
    up = np.zeros((rows, HEAD))
    up[:, half:ROT] = sin
    down = np.zeros((rows, HEAD))
    down[:, :half] = sin
    heads = min(shard, 128) // HEAD
    return [jnp.asarray(np.tile(table, (1, heads)), F32) for table in (one, up, down)]


def across(table, width):
    return jnp.concatenate([table] * (width // table.shape[1]), axis=1)


def turn(rows, cos, up, down, sign):
    half = ROT // 2
    width = rows.shape[1]
    from_low = pltpu.roll(rows, half, 1)
    from_high = pltpu.roll(rows, width - half, 1)
    cos, up, down = (across(table, width) for table in (cos, up, down))
    return rows * cos + sign * (from_low * up - from_high * down)


def project_unit(
    meta, low_ref, qkv_ref, cos_ref, up_ref, down_ref, maps, ups, q_ref, k_ref, v_ref, rank_ref
):
    proj = meta[PROJ]
    shard = q_ref.shape[1]
    rank = ups.shape[1]
    total = None
    for rel, piece in enumerate(maps):
        low = low_ref[:, columns(proj ^ rel, shard)]
        part = dot_nt(low, piece[2:5].reshape(3 * rank, shard))
        total = part if total is None else total + part
    rank_in = total.astype(BF)
    rank_ref[...] = rank_in
    pre = [
        qkv_ref[:, k * shard : (k + 1) * shard]
        + ADAPTER_SCALE * dot_nn(rank_in[:, k * rank : (k + 1) * rank], ups[k])
        for k in range(3)
    ]
    tables = (cos_ref[...], up_ref[...], down_ref[...])
    q_ref[...] = turn(pre[0], *tables, 1.0).astype(BF)
    k_ref[...] = turn(pre[1], *tables, 1.0).astype(BF)
    v_ref[...] = pre[2].astype(BF)


def vocab_chunks(vocab):
    return [(start, min(CHUNK_V, vocab - start)) for start in range(0, vocab, CHUNK_V)]


def table_loads(table_ref, dest_ref, sem, first, groups):
    loads = {}
    for index, group in enumerate(groups):
        start = first * CHUNK_V
        stop = min(start + group * CHUNK_V, table_ref.shape[0])
        here = pl.ds(start, stop - start)
        loads[start] = pltpu.make_async_copy(table_ref.at[here], dest_ref.at[here], sem.at[index])
        first += group
    return loads


def vocab_buffers(vocab, width):
    return [
        pltpu.VMEM((vocab, width), BF),
        pltpu.VMEM((len(vocab_chunks(vocab)), UNIT, CHUNK_V), BF),
    ]


def head_mask(shard, head):
    return lax.broadcasted_iota(jnp.int32, (1, shard), 1) // HEAD == head


def diagonal():
    rows = lax.broadcasted_iota(jnp.int32, (BLOCK, BLOCK), 0)
    cols = lax.broadcasted_iota(jnp.int32, (BLOCK, BLOCK), 1)
    return rows >= cols


def block_scores(query, k_ref, prev, causal):
    scale = HEAD**-0.5
    diag = dot_nt(query, k_ref[prev : prev + BLOCK, :]) * scale
    diag = jnp.where(causal, diag, -1e30)
    if prev == 0:
        return diag
    return jnp.concatenate([dot_nt(query, k_ref[0:prev, :]) * scale, diag], axis=1)


def attend_unit(unit, meta, q_ref, k_ref, v_ref, mine_ref, sib_ref, lse_ref):
    shard = q_ref.shape[1]
    causal = diagonal()
    lane = lax.broadcasted_iota(jnp.int32, (BLOCK, 128), 1)
    for half in range(UNIT // BLOCK):
        prev = unit * UNIT + half * BLOCK
        query = q_ref[half * BLOCK : (half + 1) * BLOCK, :]
        out = jnp.zeros((BLOCK, shard), F32)
        lse = jnp.zeros((BLOCK, 128), F32)
        for head in range(shard // HEAD):
            mask = head_mask(shard, head)
            scores = block_scores(jnp.where(mask, query, 0), k_ref, prev, causal)
            top = jnp.max(scores, axis=1, keepdims=True)
            prob = jnp.exp(scores - top)
            total = jnp.sum(prob, axis=1, keepdims=True)
            got = dot_nn(prob.astype(BF), v_ref[0 : prev + BLOCK, :]) / total
            out = jnp.where(mask, got, out)
            lse = jnp.where(lane == head, top + jnp.log(total), lse)
        lse_ref[half * BLOCK : (half + 1) * BLOCK, :] = lse
        low = out.astype(BF)

        @pl.when(core_of(meta) == half)
        def _():
            mine_ref[...] = low

        @pl.when(core_of(meta) != half)
        def _():
            sib_ref[...] = low


def attend_first_body(
    meta, low_ref, qkv_ref, cos_ref, up_ref, down_ref, m0, m1, m2, m3, ups, one_ref, two_ref,
    w0, w1, w2, w3,
    q_ref, k_ref, v_ref, rank_ref, mine_ref, sib_ref, lse_ref, sum_ref, wo_ref, _u, _p, sem,
):
    shard = w0.shape[0]
    loads = [
        pltpu.make_async_copy(piece, wo_ref.at[pl.ds(rel * shard, shard)], sem.at[rel])
        for rel, piece in enumerate((w0, w1, w2, w3))
    ]
    for load in loads:
        load.start()
    side_sum((one_ref, two_ref, sum_ref))
    project_unit(
        meta, low_ref, qkv_ref, cos_ref, up_ref, down_ref, (m0, m1, m2, m3), ups,
        q_ref, k_ref, v_ref, rank_ref,
    )
    attend_unit(0, meta, q_ref, k_ref, v_ref, mine_ref, sib_ref, lse_ref)
    for load in loads:
        load.wait()


def attend_second_body(
    meta, _wo, _u, _p, _wo_out, held_ref, _p_out,
    low_ref, qkv_ref, cos_ref, up_ref, down_ref, m0, m1, m2, m3, ups, k_past, v_past, table_ref,
    q_ref, k_ref, v_ref, rank_ref, mine_ref, sib_ref, lse_ref, keys_ref, values_ref, sem,
):
    loads = list(table_loads(table_ref, held_ref, sem, 0, FIRST_GROUPS).values())
    for load in loads:
        load.start()
    project_unit(
        meta, low_ref, qkv_ref, cos_ref, up_ref, down_ref, (m0, m1, m2, m3), ups,
        q_ref, k_ref, v_ref, rank_ref,
    )
    for past, new, every in ((k_past, k_ref, keys_ref), (v_past, v_ref, values_ref)):
        every[0:UNIT, :] = past[...]
        every[UNIT:, :] = new[...]
    attend_unit(1, meta, q_ref, keys_ref, values_ref, mine_ref, sib_ref, lse_ref)
    for load in loads:
        load.wait()


def attend(meta, unit, low, qkv, tables, maps, ups, table, sums=(), wo=(), past=(), keep=()):
    rows, width = low.shape
    shard = qkv.shape[1] // 3
    rank = ups.shape[1]
    anywhere = pl.BlockSpec(memory_space=pl.ANY)
    block = lambda cols: pl.BlockSpec((UNIT, cols), lambda i, m: (unit, 0))
    in_specs = (
        [block(width), block(3 * shard)]
        + [block(tables[0].shape[1])] * 3
        + [whole(one.shape) for one in (*maps, ups)]
    )
    out_specs = [whole((UNIT, shard))] * 3 + [whole((UNIT, 3 * rank))]
    out_specs += [whole((BLOCK, shard))] * 2 + [whole((UNIT, 128))]
    out_shape = [sds((UNIT, shard), BF)] * 3 + [sds((UNIT, 3 * rank), BF)]
    out_shape += [sds((BLOCK, shard), BF)] * 2 + [sds((UNIT, 128), F32)]
    if unit == 0:
        body = attend_first_body
        args = (*sums, *wo)
        in_specs += [whole(one.shape) for one in sums] + [anywhere] * 4
        out_specs += [whole((BLOCK, width))] + [anywhere] * 3
        out_shape += [sds((BLOCK, width), BF), pltpu.VMEM((4 * shard, width), BF)]
        out_shape += vocab_buffers(*table.shape)
        scratch = [pltpu.SemaphoreType.DMA((4,))]
    else:
        body = attend_second_body
        args = (*past, table)
        in_specs += [whole((UNIT, shard))] * 2 + [anywhere]
        scratch = [pltpu.VMEM((rows, shard), BF)] * 2
        scratch += [pltpu.SemaphoreType.DMA((len(FIRST_GROUPS),))]
    return kernel_call(
        body, f"attend_{unit}", (1,), in_specs, out_specs, out_shape, scratch,
        keep=keep, use_keep=unit == 1,
    )(meta, low, qkv, *tables, *maps, ups, *args)


def attend_back_body(unit, meta, *refs):
    shard = refs[4].shape[1]
    (g0, g1, g2, g3, q_ref, lse_ref, cos_ref, up_ref, down_ref) = refs[:9]
    if unit == 0:
        k_ref, v_ref, dq_ref, dk_ref, dv_ref, grad_ref = refs[9:]
        dk_ref[...] = jnp.zeros_like(dk_ref)
        dv_ref[...] = jnp.zeros_like(dv_ref)
    else:
        (k0, v0, k1, v1, dk_in, dv_in, keep_ref, got_ref,
         dq_ref, dk_ref, dv_ref, own_ref, far_ref, grad_ref, k_ref, v_ref) = refs[9:]
        for first, second, every in ((k0, k1, k_ref), (v0, v1, v_ref)):
            every[0:UNIT, :] = first[...]
            every[UNIT:, :] = second[...]
        dk_ref[...] = dk_in[...]
        dv_ref[...] = dv_in[...]
        own_ref[...] = keep_ref[0].astype(F32) + got_ref[0].astype(F32)
        far_ref[...] = (keep_ref[1].astype(F32) + got_ref[1].astype(F32)).astype(BF)
    core, ybit = core_of(meta), ybit_of(meta)
    quarter = BLOCK // 2
    for rel, piece in enumerate((g0, g1, g2, g3)):
        place = (core ^ (rel & 1)) * 2 + (ybit ^ (rel >> 1))
        grad_ref[columns(place, quarter), :] = piece[...]
    causal = diagonal()
    lane = lax.broadcasted_iota(jnp.int32, (BLOCK, 128), 1)
    scale = HEAD**-0.5
    for half in range(UNIT // BLOCK):
        prev = unit * UNIT + half * BLOCK
        known = prev + BLOCK
        here = slice(half * BLOCK, (half + 1) * BLOCK)
        query = q_ref[here, :]
        grad = grad_ref[here, :]
        lse = lse_ref[here, :]
        dq = jnp.zeros((BLOCK, shard), F32)
        for head in range(shard // HEAD):
            mask = head_mask(shard, head)
            own_q = jnp.where(mask, query, 0)
            own_g = jnp.where(mask, grad, 0)
            own_lse = jnp.sum(jnp.where(lane == head, lse, 0.0), axis=1, keepdims=True)
            prob = jnp.exp(block_scores(own_q, k_ref, prev, causal) - own_lse)
            dweights = dot_nt(own_g, v_ref[0:known, :])
            delta = jnp.sum(prob * dweights, axis=1, keepdims=True)
            dscores = (prob * (dweights - delta)).astype(BF)
            dq = dq + jnp.where(mask, dot_nn(dscores, k_ref[0:known, :]), 0.0)
            dk_ref[0:known, :] += dot_tn(dscores, own_q) * scale
            dv_ref[0:known, :] += dot_tn(prob.astype(BF), own_g)
        dq = turn(dq * scale, cos_ref[here, :], up_ref[here, :], down_ref[here, :], -1.0)
        dq_ref[here, :] = dq.astype(BF)


def attend_back(meta, unit, rows, grads, query, lse, tables, known, before=(), pair=(), after=(), keep=()):
    shard = query.shape[1]
    sums = (rows, shard)
    more = [one.shape[1:] for one in pair[:1]] * 2
    table = pl.BlockSpec((UNIT, tables[0].shape[1]), lambda i, m: (unit, 0))
    rest = (*known, *before, *pair)
    return kernel_call(
        partial(attend_back_body, unit),
        f"attend_back_{unit}",
        (1,),
        [whole(one.shape) for one in (*grads, query, lse)]
        + [table] * 3
        + [whole(one.shape) for one in rest],
        [whole((UNIT, shard)), whole(sums), whole(sums)] + [whole(one) for one in more],
        [sds((UNIT, shard), BF), sds(sums, F32), sds(sums, F32)]
        + [sds(one, dtype) for one, dtype in zip(more, (F32, BF))],
        [pltpu.VMEM((UNIT, shard), BF)] + [pltpu.VMEM(sums, BF)] * 2 * unit,
        after=after,
        keep=keep,
    )(meta, *grads, query, lse, *tables, *rest)


def mix_body(
    meta, wo_ref, _u, _p, _wo, _u_out, _p_out, x_ref, gain_ref, f_own, f_far, a0, a1, a2, a3,
    m0, m1, m2, m3, norm_ref, res_ref, rank_ref, keep_ref,
):
    proj = meta[PROJ]
    shard = a0.shape[1]
    rank = None
    for a_ref, m_ref in ((a0, m0), (a1, m1), (a2, m2), (a3, m3)):
        part = dot_nt(a_ref[...], m_ref[0])
        rank = part if rank is None else rank + part
    rank = rank.astype(BF)
    total = x_ref[...].astype(F32) + f_own[...].astype(F32) + f_far[...].astype(F32)
    for rel, a_ref in enumerate((a0, a1, a2, a3)):
        total = total + dot_nn(a_ref[...], wo_ref[rel * shard : (rel + 1) * shard, :])
    keep_ref[...] = total
    for rel, m_ref in enumerate((m0, m1, m2, m3)):
        here = columns(proj ^ rel, shard)
        keep_ref[:, here] += ADAPTER_SCALE * dot_nn(rank, m_ref[1])
    residual = keep_ref[...]
    norm_ref[...] = (normalize(residual) * gain_ref[2:3, :]).astype(BF)
    mine = columns(ybit_of(meta), BLOCK // 2)
    res_ref[...] = keep_ref[mine, :]
    keep_ref[:, 0 : rank.shape[1]] = rank.astype(F32)
    rank_ref[...] = keep_ref[mine, 0 : rank.shape[1]].astype(BF)


def mix(meta, unit, x, gains, f_own, f_far, att, maps, keep, after=()):
    rows, width = x.shape
    shard = att[0].shape[1]
    rank = maps[0].shape[1]
    return kernel_call(
        mix_body,
        f"mix_{unit}",
        (1,),
        [
            pl.BlockSpec((BLOCK, width), lambda i, m: (2 * unit + core_of(m), 0)),
            whole(gains.shape),
            whole((BLOCK, width)),
            whole((BLOCK, width)),
        ]
        + [whole(one.shape) for one in att]
        + [whole((2, rank, shard))] * 4,
        [whole((BLOCK, width)), whole((BLOCK // 2, width)), whole((BLOCK // 2, rank))],
        [sds((BLOCK, width), BF), sds((BLOCK // 2, width), F32), sds((BLOCK // 2, rank), BF)],
        [pltpu.VMEM((BLOCK, width), F32)],
        after=after,
        keep=keep,
        use_keep=True,
    )(meta, x, gains, f_own, f_far, *att, *maps)


def local_columns(unit, meta, vocab, target_ref, out_ref):
    for group in range(4):
        half = core_of(meta) ^ (group >> 1)
        ids = target_ref[pl.ds((unit * 2 + half) * 2 + (group & 1), 1), :] - meta[PROJ] * vocab
        ids = jnp.where((ids >= 0) & (ids < vocab), ids, -1)
        square = jnp.transpose(jnp.broadcast_to(ids.astype(F32), (128, 128)))
        out_ref[group * 128 : (group + 1) * 128, :] = square.astype(jnp.int32)


def vocab_stats_body(unit, meta, _wo, _u, _p, _wo_out, u_ref, p_ref, *refs):
    vocab = u_ref.shape[0]
    chunks = vocab_chunks(vocab)
    if unit == 0:
        mine_ref, sib_ref, target_ref, table_ref, top_ref, st_ref, acc_ref, col_ref, sem = refs
        loads = table_loads(table_ref, u_ref, sem, sum(FIRST_GROUPS), SECOND_GROUPS)
    else:
        mine_ref, sib_ref, target_ref, top_ref, st_ref, acc_ref, col_ref = refs
        loads = {}
    for load in loads.values():
        load.start()
    acc_ref[...] = jnp.zeros_like(acc_ref)
    local_columns(unit, meta, vocab, target_ref, col_ref)
    lane = lax.broadcasted_iota(jnp.int32, (BLOCK, 128), 1)
    for place, (start, size) in enumerate(chunks):
        if start in loads:
            loads[start].wait()
        col = lax.broadcasted_iota(jnp.int32, (BLOCK, size), 1)
        for half, rows_ref in enumerate((mine_ref, sib_ref)):
            here = slice(half * BLOCK, (half + 1) * BLOCK)
            logits = dot_nt(rows_ref[...], u_ref[start : start + size, :])
            top = jnp.max(logits, axis=1, keepdims=True)
            prob = jnp.exp(logits - top)
            total = jnp.sum(prob, axis=1, keepdims=True)
            hit = col == col_ref[here, 0:1] - start
            picked = jnp.sum(jnp.where(hit, logits, 0.0), axis=1, keepdims=True)
            p_ref[place, here, 0:size] = prob.astype(BF)
            acc = acc_ref[here, :]
            acc = jnp.where(lane == place, top, acc)
            acc = jnp.where(lane == place + 32, total, acc)
            acc_ref[here, :] = jnp.where(lane == 64, acc + picked, acc)
    acc = acc_ref[...]
    lane = lax.broadcasted_iota(jnp.int32, acc.shape, 1)
    top_ref[...] = acc
    tops = jnp.where(lane < len(chunks), acc, -1e30)
    best = jnp.max(tops, axis=1, keepdims=True)
    totals = pltpu.roll(acc, 128 - 32, 1)
    total = jnp.sum(
        jnp.where(lane < len(chunks), totals * jnp.exp(tops - best), 0.0), axis=1, keepdims=True
    )
    picked = jnp.sum(jnp.where(lane == 64, acc, 0.0), axis=1, keepdims=True)
    pair = jnp.where(lane == 0, best + jnp.log(total), jnp.where(lane == 1, picked, 0.0))
    st_ref[...] = jnp.transpose(pair)[0:8, :]


def vocab_stats(meta, unit, mine, sib, targets, table, keep, after=()):
    rows = 2 * BLOCK
    first = unit == 0
    return kernel_call(
        partial(vocab_stats_body, unit),
        f"vocab_stats_{unit}",
        (),
        [IN_VMEM] * 3 + [pl.BlockSpec(memory_space=pl.ANY)] * first,
        [IN_VMEM] * 2,
        [sds((rows, 128), F32), sds((8, rows), F32)],
        [pltpu.VMEM((rows, 128), F32), pltpu.VMEM((rows, 128), jnp.int32)]
        + [pltpu.SemaphoreType.DMA((len(SECOND_GROUPS),))] * first,
        after=after,
        keep=keep,
        use_keep=True,
    )(meta, mine, sib, targets, *((table,) * first))


def swap_halves(pair):
    return jnp.concatenate([pair[:, BLOCK:], pair[:, :BLOCK]], axis=1)


def vocab_back_body(
    unit, meta, _wo, u_ref, p_ref, _wo_out, _u, _p, lens_ref, target_ref, top_ref, s0, s1, s2, s3,
    d0, d1, d2, d3, loss_ref, scale_ref, acc_ref, col_ref,
):
    vocab = u_ref.shape[0]
    chunks = vocab_chunks(vocab)
    rows = 2 * BLOCK
    acc_ref[...] = jnp.zeros_like(acc_ref)
    local_columns(unit, meta, vocab, target_ref, col_ref)
    parts = [s0[...], swap_halves(s1[...]), s2[...], swap_halves(s3[...])]
    lses = [part[0:1, :] for part in parts]
    best = jnp.maximum(jnp.maximum(lses[0], lses[1]), jnp.maximum(lses[2], lses[3]))
    total = sum(jnp.exp(one - best) for one in lses)
    log_norm = best + jnp.log(total)
    picked = sum(part[1:2, :] for part in parts)
    place = lax.broadcasted_iota(jnp.int32, (1, rows), 1)
    core = core_of(meta)
    offset = jnp.where(place < BLOCK, core * BLOCK, (1 - core) * BLOCK - BLOCK)
    valid = (unit * UNIT + place + offset < lens_ref[meta[SEQ]]).astype(F32)
    loss_ref[...] = jnp.broadcast_to(
        jnp.sum((log_norm - picked) * valid, axis=1, keepdims=True), (8, 128)
    )
    weight = valid / token_count(lens_ref)
    row = lax.broadcasted_iota(jnp.int32, (128, rows), 0)
    lines = jnp.where(row == 0, log_norm, 0.0)
    lines = jnp.where(row == 1, weight, lines)
    lines = jnp.where(row == 2, (jnp.exp(picked - log_norm) - 1.0) * weight, lines)
    cols = jnp.transpose(lines)
    lane = lax.broadcasted_iota(jnp.int32, (rows, 128), 1)
    take = lambda k: jnp.sum(jnp.where(lane == k, cols, 0.0), axis=1, keepdims=True)
    tops = jnp.where(lane < len(chunks), top_ref[...], -1e30)
    scales = jnp.exp(tops - take(0)) * take(1)
    scale_ref[...] = jnp.where(lane == 64, take(2), scales)

    lane = lax.broadcasted_iota(jnp.int32, (BLOCK, 128), 1)
    for place, (start, size) in enumerate(chunks):
        col = lax.broadcasted_iota(jnp.int32, (BLOCK, size), 1)
        for half in range(2):
            here = slice(half * BLOCK, (half + 1) * BLOCK)
            scales = scale_ref[here, :]
            at_hit = jnp.sum(jnp.where(lane == 64, scales, 0.0), axis=1, keepdims=True)
            scale = jnp.sum(jnp.where(lane == place, scales, 0.0), axis=1, keepdims=True)
            hit = col == col_ref[here, 0:1] - start
            grad = jnp.where(hit, at_hit, p_ref[place, here, 0:size].astype(F32) * scale)
            acc_ref[here, :] += dot_nn(grad.astype(BF), u_ref[start : start + size, :])

    quarter = BLOCK // 2
    for rel, out_ref in enumerate((d0, d1, d2, d3)):
        place = (rel & 1) * 2 + (ybit_of(meta) ^ (rel >> 1))
        out_ref[...] = acc_ref[columns(place, quarter), :].astype(BF)


def vocab_back(meta, unit, lens, targets, tops, stats, keep, after=()):
    width = keep[1].shape[1]
    rows = 2 * BLOCK
    quarter = sds((BLOCK // 2, width), BF)
    return kernel_call(
        partial(vocab_back_body, unit),
        f"vocab_back_{unit}",
        (),
        [SCALARS] + [IN_VMEM] * 6,
        [IN_VMEM] * 5,
        [quarter] * 4 + [sds((8, 128), F32)],
        [
            pltpu.VMEM((rows, 128), F32),
            pltpu.VMEM((rows, width), F32),
            pltpu.VMEM((rows, 128), jnp.int32),
        ],
        after=after,
        keep=keep,
        use_keep=True,
    )(meta, lens, targets, tops, *stats)


def norm_back_body(last, meta, wo_ref, *refs):
    refs = refs[1:] if last else refs[5:]
    parts, (res_ref, gain_ref, rank_ref) = refs[:4], refs[4:7]
    atts, maps = refs[7:11], refs[11:15]
    if last:
        before_ref, *outs, keep_ref, send_ref, hold_ref = refs[15:]
    else:
        *outs, sum_ref, hold_ref = refs[15:]
    proj = meta[PROJ]
    shard = atts[0].shape[1]
    dnormed = sum(part[...].astype(F32) for part in parts)
    residual = res_ref[...]
    center = residual - jnp.mean(residual, axis=-1, keepdims=True)
    spread = jnp.mean(center * center, axis=-1, keepdims=True)
    inv = lax.rsqrt(spread + EPS_NORM)
    hat = center * inv
    dhat = dnormed * gain_ref[2:3, :]
    dres = inv * (
        dhat
        - jnp.mean(dhat, axis=-1, keepdims=True)
        - hat * jnp.mean(dhat * hat, axis=-1, keepdims=True)
    )
    hold_ref[...] = dres.astype(BF)
    dbranch = hold_ref[...]
    drank = None
    for rel, m_ref in enumerate(maps):
        part = dot_nt(hold_ref[:, columns(proj ^ rel, shard)], m_ref[1])
        drank = part if drank is None else drank + part
    drank = (ADAPTER_SCALE * drank).astype(BF)
    for rel in range(4):
        w_piece = wo_ref[rel * shard : (rel + 1) * shard, :]
        datt = dot_nt(dbranch, w_piece) + dot_nn(drank, maps[rel][0])
        outs[rel][...] = datt.astype(BF)
        g_down = dot_tn(drank, atts[rel][...])
        g_up = ADAPTER_SCALE * dot_tn(rank_ref[...], hold_ref[:, columns(proj ^ rel, shard)])
        if last:
            dest = (keep_ref, send_ref)[rel & 1]
            dest[rel >> 1, 0] = (before_ref[rel, 0] + g_down).astype(BF)
            dest[rel >> 1, 1] = (before_ref[rel, 1] + g_up).astype(BF)
        else:
            sum_ref[rel, 0] = g_down
            sum_ref[rel, 1] = g_up


def norm_back(
    meta, unit, last, parts, residual, gains, rank_out, att, maps, before, keep, after=()
):
    quarter, width = residual.shape
    shard = att[0].shape[1]
    rank = rank_out.shape[1]
    piece = (quarter, shard)
    if last:
        more = [sds((2, 2, rank, shard), BF)] * 2
    else:
        more = [sds((4, 2, rank, shard), F32)]
    return kernel_call(
        partial(norm_back_body, last),
        f"norm_back_{unit}",
        (1,),
        [whole(one.shape) for one in parts]
        + [whole(residual.shape), whole(gains.shape), whole(rank_out.shape)]
        + [pl.BlockSpec(piece, lambda i, m: (ybit_of(m), 0))] * 4
        + [whole((2, rank, shard))] * 4
        + [whole(one.shape) for one in before],
        [whole(piece)] * 4 + [whole(one.shape) for one in more],
        [sds(piece, BF)] * 4 + more,
        [pltpu.VMEM((quarter, width), BF)],
        after=after,
        keep=keep,
        use_keep=True,
    )(meta, *parts, residual, gains, rank_out, *att, *maps, *before)


def grads_body(
    meta, dq0, dq1, dk_ref, dv_ref, cos_ref, up_ref, down_ref, rank0, rank1, ups, low_ref,
    keep_ref, send_ref, up_grad_ref, drank_ref,
):
    proj = meta[PROJ]
    rank, shard = ups.shape[1:]
    dk = turn(dk_ref[...], cos_ref[...], up_ref[...], down_ref[...], -1.0).astype(BF)
    dpre = [jnp.concatenate([dq0[...], dq1[...]], axis=0), dk, dv_ref[...].astype(BF)]
    rank_in = jnp.concatenate([rank0[...], rank1[...]], axis=0)
    for k in range(3):
        here = slice(k * rank, (k + 1) * rank)
        up_grad_ref[k] = ADAPTER_SCALE * dot_tn(rank_in[:, here], dpre[k])
        drank_ref[:, here] = (ADAPTER_SCALE * dot_nt(dpre[k], ups[k])).astype(BF)
    drank = drank_ref[...]
    for rel in range(4):
        grad = dot_tn(drank, low_ref[:, columns(proj ^ rel, shard)])
        dest = (keep_ref, send_ref)[rel & 1]
        dest[rel >> 1] = grad.reshape(3, rank, shard).astype(BF)


def adapter_grads(meta, dqs, dk, dv, tables, rank_in, ups, low):
    rows, shard = dk.shape
    rank = ups.shape[1]
    pair = (2, 3, rank, shard)
    args = (*dqs, dk, dv, *tables, *rank_in, ups, low)
    return kernel_call(
        grads_body,
        "adapter_grads",
        (1,),
        [whole(one.shape) for one in args],
        [whole(pair), whole(pair), whole((3, rank, shard))],
        [sds(pair, BF), sds(pair, BF), sds((3, rank, shard), F32)],
        [pltpu.VMEM((rows, 3 * rank), BF)],
        flops=2 * rows * low.shape[1] * 3 * rank,
        moved=30 * rows * shard,
    )(meta, *args)


def signs(row_ids, col_ids, seed):
    hashed = row_ids * 1640531527 + col_ids * 747796405 + seed * 277803737
    hashed = hashed ^ hashed >> 15 & 131071
    hashed = hashed * 2024237689
    hashed = hashed ^ hashed >> 13 & 524287
    return 1.0 - 2.0 * (hashed >> 17 & 1).astype(F32)


def sketch_one(meta, seed, grad, sketch):
    rank, shard = grad.shape
    left_rows = lax.broadcasted_iota(jnp.int32, (sketch, shard), 1) + meta[PROJ] * shard
    left_cols = lax.broadcasted_iota(jnp.int32, (sketch, shard), 0)
    right_rows = lax.broadcasted_iota(jnp.int32, (rank, sketch), 0)
    right_cols = lax.broadcasted_iota(jnp.int32, (rank, sketch), 1)
    left = signs(left_rows, left_cols, 2 * seed).astype(BF)
    right = signs(right_rows, right_cols, 2 * seed + 1)
    return jnp.dot(dot_nt(left, grad), right, precision=lax.Precision.HIGHEST)


def local_sketch_body(meta, seeds_ref, lens_ref, own_ref, far_ref, up_ref, block_ref, full_ref):
    size = block_ref.shape[2]
    count = token_count(lens_ref)
    out = own_ref[...] + far_ref[...].astype(F32)
    for place, grad in enumerate((out[0], up_ref[0], up_ref[1], up_ref[2], out[1])):
        for dest in range(block_ref.shape[0]):
            block_ref[dest, place] = grad[dest * size : (dest + 1) * size].astype(BF)
        full_ref[place] = count * sketch_one(
            meta, seeds_ref[3 + place], grad.astype(BF), full_ref.shape[1]
        )


def local_sketch(meta, seeds, lens, own, far, ups, sketch_width):
    _, rank, shard = own.shape
    count = lens.shape[0]
    blocks = (count, 5, rank // count, shard)
    full = (5, sketch_width, sketch_width)
    return kernel_call(
        local_sketch_body, "local_sketch", (1,),
        [SCALARS, SCALARS, whole(own.shape), whole(far.shape), whole(ups.shape)],
        [whole(blocks), whole(full)],
        [sds(blocks, BF), sds(full, F32)],
        flops=10 * rank * shard * sketch_width,
        moved=16 * own.size,
    )(meta, seeds, lens, own, far, ups)


def gather_body(meta, keep_ref, got_ref, far_ref, five_ref, block_ref, grad_ref):
    size = block_ref.shape[2]
    total = keep_ref[0].astype(F32) + got_ref[0].astype(F32) + far_ref[...].astype(F32)
    grad_ref[...] = total.astype(BF)
    for dest in range(block_ref.shape[0]):
        for mat in range(3):
            block_ref[dest, mat] = total[mat, dest * size : (dest + 1) * size].astype(BF)
        block_ref[dest, 3:8] = five_ref[dest]


def gather_blocks(meta, keep, got, far, five):
    count, _, size, shard = five.shape
    blocks = (count, 8, size, shard)
    pair = pl.BlockSpec((1, *keep.shape[1:]), lambda i, m: (0, 0, 0, 0))
    return kernel_call(
        gather_body, "gather_blocks", (1,),
        [pair, pair, whole(far.shape), whole(five.shape)],
        [whole(blocks), whole(far.shape)],
        [sds(blocks, BF), sds(far.shape, BF)],
    )(meta, keep, got, far, five)


def sketch_body(meta, seeds_ref, lens_ref, grad_ref, five_ref, f0, f1, f2, f3, full_ref):
    count = token_count(lens_ref)
    sketch = full_ref.shape[1]
    full_ref[3:8] = five_ref[...]
    for mat in range(3):
        full_ref[mat] = count * sketch_one(meta, seeds_ref[mat], grad_ref[mat], sketch)
    size = sketch // 4
    for rel, out_ref in enumerate((f0, f1, f2, f3)):
        out_ref[...] = full_ref[:, columns(meta[PROJ] ^ rel, size), :]


def sketch(meta, seeds, lens, grads, five):
    sketch_width = five.shape[1]
    piece = (8, sketch_width // 4, sketch_width)
    return kernel_call(
        sketch_body, "sketch", (1,),
        [SCALARS, SCALARS, whole(grads.shape), whole(five.shape)],
        [whole(piece)] * 4,
        [sds(piece, F32)] * 4,
        [pltpu.VMEM((8, sketch_width, sketch_width), F32)],
        flops=2 * grads.size * sketch_width,
        moved=2 * grads.size,
    )(meta, seeds, lens, grads, five)


def lane_value(row, lane, place):
    return jnp.sum(jnp.where(lane == place, row, 0.0), axis=1, keepdims=True)


def tally_body(
    units, meta, got_ref, target_ref, f0, f1, f2, f3, *refs
):
    losses, (total_ref, line_ref) = refs[:units], refs[units:]
    total = jnp.sum(got_ref[...].astype(F32), axis=0)
    total_ref[...] = total
    features = f0[...] + f1[...] + f2[...] + f3[...]
    squares = jnp.sum(total * total)
    own = jnp.sum(features * features)
    loss = sum(jnp.sum(one[0:1, 0:1]) for one in losses)
    loss = jnp.where(meta[PROJ] == 0, loss, 0.0)
    lane = lax.broadcasted_iota(jnp.int32, (1, 128), 1)
    line = jnp.where(lane == 0, squares, 0.0)
    line = jnp.where(lane == 1, loss, line)
    line = jnp.where(lane == 2, own, line)
    checkpoints = target_ref.shape[0]
    for c in range(checkpoints):
        theirs = target_ref[c]
        line = jnp.where(lane == 3 + c, jnp.sum(features * theirs), line)
        line = jnp.where(lane == 3 + checkpoints + c, jnp.sum(theirs * theirs), line)
    line_ref[...] = jnp.broadcast_to(line, line_ref.shape)


def tally(meta, devices, got, targets, pieces, losses):
    _, mats, slice_rank, shard = got.shape
    args = (got, targets, *pieces, *losses)
    return kernel_call(
        partial(tally_body, len(losses)),
        "tally",
        (1,),
        [whole(one.shape) for one in args],
        [whole((mats, slice_rank, shard)), whole((devices, 128))],
        [sds((mats, slice_rank, shard), F32), sds((devices, 128), F32)],
    )(meta, *args)


def optimizer_step(weight, grad_in, first_in, second_in, clipping_scale):
    grad_clip = grad_in * clipping_scale
    first_new = BETA_ONE * first_in + (1.0 - BETA_ONE) * grad_clip
    second_new = BETA_TWO * second_in + (1.0 - BETA_TWO) * grad_clip * grad_clip
    first_hat = first_new / (1.0 - BETA_ONE**STEP)
    second_hat = second_new / (1.0 - BETA_TWO**STEP)
    new_weight = weight - LEARN_RATE * (
        first_hat / (jnp.sqrt(second_hat) + ADAM_EPS) + WEIGHT_DECAY * weight
    )
    return (new_weight, first_new, second_new)


def finish_body(
    proj_count, checkpoints, meta, lens_ref, lines_ref, total_ref,
    dw, uw, dm, um, ds, us,
    loss_out, norm_out, influence_out, dw_out, uw_out, dm_out, um_out, ds_out, us_out,
):
    lines = lines_ref[...]
    everyone = jnp.sum(lines, axis=0, keepdims=True)
    row = lax.broadcasted_iota(jnp.int32, lines.shape, 0)
    ours = jnp.sum(
        jnp.where(row // proj_count == meta[SEQ], lines, 0.0), axis=0, keepdims=True
    )
    lane = lax.broadcasted_iota(jnp.int32, (1, 128), 1)
    grad_norm = jnp.sqrt(lane_value(everyone, lane, 0))
    own = lane_value(ours, lane, 2)
    influence = jnp.zeros((1, 1), F32)
    for c in range(checkpoints):
        dot = lane_value(ours, lane, 3 + c)
        theirs = lane_value(ours, lane, 3 + checkpoints + c)
        influence += (1.0 - c / checkpoints) * dot * lax.rsqrt(own * theirs + 1e-12)
    loss_out[0] = jnp.sum(lane_value(everyone, lane, 1))
    loss_out[1] = token_count(lens_ref)
    norm_out[0] = jnp.sum(grad_norm)
    influence_out[0] = jnp.sum(influence)
    clip = jnp.minimum(1.0, CLIP_NORM / (grad_norm + 1e-06))
    half = total_ref.shape[0] // 2
    for base, ins, outs in (
        (0, (dw, dm, ds), (dw_out, dm_out, ds_out)),
        (half, (uw, um, us), (uw_out, um_out, us_out)),
    ):
        for k in range(half):
            new = optimizer_step(
                ins[0][k], total_ref[base + k], ins[1][k], ins[2][k], clip
            )
            for out, value in zip(outs, new):
                out[k] = value


def finish(meta, proj_count, checkpoints, lens, lines, total, params):
    block = whole(params[0].shape)
    return kernel_call(
        partial(finish_body, proj_count, checkpoints),
        "finish",
        (1,),
        [SCALARS, whole(lines.shape), whole(total.shape)] + [block] * 6,
        [SCALARS] * 3 + [block] * 6,
        [sds((2,), F32), sds((1,), F32), sds((1,), F32)] + [sds(params[0].shape, F32)] * 6,
        flops=20 * total.size,
        moved=28 * total.size,
    )(meta, lens, lines, total, *params)


def to_partner(array, axis, size, offset):
    return lax.ppermute(array, axis, [(i, i ^ offset) for i in range(size)])


def on_device(
    seq_count,
    proj_count,
    inputs,
    targets,
    lengths,
    norm_gain_vectors,
    query_key_value_weight,
    attention_output_weight,
    feedforward_input_weight,
    feedforward_output_weight,
    unembed,
    adapter_down_maps,
    adapter_up_maps,
    down_first_moment,
    up_first_moment,
    down_second_moment,
    up_second_moment,
    target_gradient_sketches,
    seeds,
):
    rows, width = inputs.shape
    shard = attention_output_weight.shape[0]
    vocab_local = unembed.shape[1]
    slice_rank = adapter_up_maps.shape[1]
    rank = slice_rank * seq_count
    sketch_width = target_gradient_sketches.shape[3]
    proj = lax.axis_index("proj")
    seq = lax.axis_index("dp")

    over_proj = lambda array, rel: to_partner(array, "proj", proj_count, rel)
    over_seq = lambda array, rel: to_partner(array, "dp", seq_count, rel)

    meta = jnp.stack([proj, seq]).astype(jnp.int32)
    targets = targets.reshape(rows // 128, 128)
    table = jnp.transpose(unembed)
    tables = rotary_tables(rows, shard)
    transposed = lambda array: jnp.transpose(array, (0, 2, 1))

    def from_all(array):
        y = over_proj(array, 2)
        return (array, over_proj(array, 1), y, over_proj(y, 1))

    def exchange(*pieces):
        return [pieces[0]] + [over_proj(pieces[rel], rel) for rel in (1, 2, 3)]

    packed = pack_maps(meta, seq_count, transposed(adapter_down_maps), adapter_up_maps)
    arrived = lax.all_to_all(packed, "dp", split_axis=0, concat_axis=0, tiled=True)
    wo = from_all(attention_output_weight)

    w_ffn = (feedforward_input_weight, feedforward_output_weight)
    f0_mine, f0_sib = ffn(meta, 0, inputs, norm_gain_vectors, *w_ffn)
    low, qkv = frozen_qkv(
        meta, inputs, norm_gain_vectors, jnp.transpose(query_key_value_weight, (1, 0, 2)),
        (f0_mine,),
    )
    maps, ups = unpack_maps(meta, arrived, (low,))
    maps = from_all(maps)
    f1_mine, f1_sib, f0_chip = ffn(
        meta, 1, inputs, norm_gain_vectors, *w_ffn, (f0_mine, over_proj(f0_sib, 1)), (maps[0],)
    )
    q0, k0, v0, rank_in0, mine, sib, lse0, f1_chip, *keep = attend(
        meta, 0, low, qkv, tables, maps, ups, table, (f1_mine, over_proj(f1_sib, 1)), wo
    )
    att0 = exchange(mine, sib, mine, sib)
    q1, k1, v1, rank_in1, mine, sib, lse1, *keep = attend(
        meta, 1, low, qkv, tables, maps, ups, table, past=(k0, v0), keep=keep
    )
    att1 = exchange(mine, sib, mine, sib)
    f_chip = (f0_chip, f1_chip)
    f_far = [over_proj(one, 2) for one in f_chip]

    def mix_unit(unit, att, keep, after):
        normed, residual, rank_out, *keep = mix(
            meta, unit, inputs, norm_gain_vectors, f_chip[unit], f_far[unit], att, maps, keep, after
        )
        return (normed, over_proj(normed, 1)), residual, rank_out, keep

    def stats_unit(unit, normed, keep, after=()):
        top, stat, *keep = vocab_stats(meta, unit, *normed, targets, table, keep, after)
        return top, exchange(stat, stat, stat, stat), keep

    def back_unit(unit, top, stats, keep, after):
        d0, d1, d2, d3, loss, *keep = vocab_back(
            meta, unit, lengths, targets, top, stats, keep, after
        )
        return exchange(d0, d1, d2, d3), loss, keep

    def norm_unit(unit, parts, residual, rank_out, att, before, keep, after):
        d0, d1, d2, d3, *more = norm_back(
            meta, unit, unit == 1, parts, residual, norm_gain_vectors,
            rank_out, att, maps, before, keep, after,
        )
        grads = more[: 1 + unit]
        return exchange(d0, d1, d2, d3), grads, more[1 + unit :]

    normed0, residual0, rank0, keep = mix_unit(0, att0, keep, (lse1,))
    top0, stats0, keep = stats_unit(0, normed0, keep)
    normed1, residual1, rank1, keep = mix_unit(1, att1, keep, (stats0[0],))
    dnormed0, loss0, keep = back_unit(0, top0, stats0, keep, (rank1,))
    top1, stats1, keep = stats_unit(1, normed1, keep, (loss0,))
    datt0, out_grads, keep = norm_unit(
        0, dnormed0, residual0, rank0, att0, (), keep, (stats1[0],)
    )
    dnormed1, loss1, keep = back_unit(1, top1, stats1, keep, (datt0[0],))
    dq0, dk, dv, *keep = attend_back(
        meta, 0, rows, datt0, q0, lse0, tables, (k0, v0), after=(loss1,), keep=keep[:1]
    )
    datt1, (out_keep, out_send), _ = norm_unit(
        1, dnormed1, residual1, rank1, att1, out_grads, keep, (dq0,)
    )
    dq1, dk, dv, out_own, out_far = attend_back(
        meta, 1, rows, datt1, q1, lse1, tables, (k0, v0, k1, v1),
        (dk, dv), (out_keep, over_proj(out_send, 1)),
    )
    out_far = over_proj(out_far, 2)

    in_keep, in_send, up_grads = adapter_grads(
        meta, (dq0, dq1), dk, dv, tables, (rank_in0, rank_in1), ups, low
    )
    in_got = over_proj(in_send, 1)
    in_far = over_proj((in_keep[1].astype(F32) + in_got[1].astype(F32)).astype(BF), 2)
    blocks, five = local_sketch(meta, seeds, lengths, out_own, out_far, up_grads, sketch_width)
    blocks, in_grads = gather_blocks(meta, in_keep, in_got, in_far, blocks)
    arrived = lax.all_to_all(blocks, "dp", split_axis=0, concat_axis=0, tiled=True)
    pieces = exchange(*sketch(meta, seeds, lengths, in_grads, five))

    device_count = seq_count * proj_count
    total, lines = tally(
        meta, device_count, arrived, target_gradient_sketches, pieces, (loss0, loss1)
    )
    lines = lax.all_to_all(lines, ("dp", "proj"), split_axis=0, concat_axis=0, tiled=True)
    params = (
        transposed(adapter_down_maps),
        adapter_up_maps,
        transposed(down_first_moment),
        up_first_moment,
        transposed(down_second_moment),
        up_second_moment,
    )
    loss_parts, grad_norm, influence, dw, uw, dm, um, ds, us = finish(
        meta, proj_count, target_gradient_sketches.shape[0], lengths, lines, total, params
    )
    return (
        loss_parts,
        grad_norm,
        influence,
        transposed(dw),
        uw,
        transposed(dm),
        um,
        transposed(ds),
        us,
    )


def solution(mesh):
    in_specs = (
        P("dp", None),
        P("dp"),
        P(),
        P(),
        P(None, None, "proj"),
        P("proj", None),
        P(None, "proj"),
        P("proj", None),
        P(None, "proj"),
        P(None, "proj", "dp"),
        P(None, "dp", "proj"),
        P(None, "proj", "dp"),
        P(None, "dp", "proj"),
        P(None, "proj", "dp"),
        P(None, "dp", "proj"),
        P(None, None, "proj", None),
        P(),
    )
    out_specs = (
        P(),
        P(),
        P("dp"),
        P(None, "proj", "dp"),
        P(None, "dp", "proj"),
        P(None, "proj", "dp"),
        P(None, "dp", "proj"),
        P(None, "proj", "dp"),
        P(None, "dp", "proj"),
    )
    return jax.shard_map(
        partial(on_device, mesh.shape["dp"], mesh.shape["proj"]),
        mesh=mesh,
        in_specs=in_specs,
        out_specs=out_specs,
        check_vma=False,
    )
```

```python
from functools import partial
import math

import jax
import jax.numpy as jnp
import numpy as np
from jax import lax
from jax.experimental import pallas as pl
from jax.experimental.pallas import tpu as pltpu
from jax.sharding import PartitionSpec as P

HEAD = 64
ROT = 16
STEP = 10

EPS_NORM = 1e-05
ADAPTER_SCALE = 0.25
CLIP_NORM = 0.05
LEARN_RATE = 0.05
BETA_ONE = 0.9
BETA_TWO = 0.99
ADAM_EPS = 1e-08
WEIGHT_DECAY = 0.01

BF = jnp.bfloat16
F32 = jnp.float32
BLOCK = 256
UNIT = 512
FIRST_GROUPS = (3, 3, 3, 3)
SECOND_GROUPS = (5, 4, 4)
TOGETHER_V = 6
CHUNK_V = 512
MIB = 2**20

PROJ, SEQ = range(2)


def core_of(meta):
    return meta[PROJ] & 1


def ybit_of(meta):
    return meta[PROJ] >> 1


def token_count(lens_ref):
    return sum(lens_ref[i] for i in range(lens_ref.shape[0])).astype(F32)


def dot_nn(lhs, rhs):
    return lax.dot_general(lhs, rhs, (((1,), (0,)), ((), ())), preferred_element_type=F32)


def dot_nt(lhs, rhs):
    return lax.dot_general(lhs, rhs, (((1,), (1,)), ((), ())), preferred_element_type=F32)


def dot_tn(lhs, rhs):
    return lax.dot_general(lhs, rhs, (((0,), (0,)), ((), ())), preferred_element_type=F32)


def kernel_call(
    body, name, grid, in_specs, out_specs, out_shape, scratch=(), flops=0, moved=0, after=(),
    vmem=20, keep=(), use_keep=False,
):
    single = not isinstance(out_shape, (list, tuple))
    if single:
        out_specs, out_shape = [out_specs], [out_shape]
    first_keep = 1 + len(in_specs) + len(after)
    first_out = first_keep + len(keep)
    first_kept = first_out + len(out_shape)
    first_scratch = first_kept + len(keep)

    def run(*refs):
        kept = refs[first_keep:first_out] + refs[first_kept:first_scratch]
        body(
            refs[0],
            *(kept if use_keep else ()),
            *refs[1 : 1 + len(in_specs)],
            *refs[first_out:first_kept],
            *refs[first_scratch:],
        )

    anywhere = pl.BlockSpec(memory_space=pl.ANY)
    keep_spec = IN_VMEM if use_keep else anywhere
    call = pl.pallas_call(
        run,
        grid_spec=pltpu.PrefetchScalarGridSpec(
            num_scalar_prefetch=1,
            grid=grid,
            in_specs=list(in_specs) + [anywhere] * len(after) + [keep_spec] * len(keep),
            out_specs=list(out_specs) + [keep_spec] * len(keep),
            scratch_shapes=list(scratch),
        ),
        out_shape=list(out_shape) + [pltpu.VMEM(one.shape, one.dtype) for one in keep],
        input_output_aliases={
            first_keep + i: len(out_shape) + i for i in range(len(keep))
        },
        compiler_params=pltpu.CompilerParams(vmem_limit_bytes=vmem * MIB),
        cost_estimate=pl.CostEstimate(flops=10**12, bytes_accessed=1000, transcendentals=0),
        name=name,
    )

    def apply(*args):
        results = call(*args, *after, *[held(one) for one in keep])
        return results[0] if single else results

    return apply


def whole(shape):
    zeros = (0,) * len(shape)
    return pl.BlockSpec(shape, lambda *_: zeros)


SCALARS = pl.BlockSpec(memory_space=pltpu.SMEM)
IN_VMEM = pl.BlockSpec(memory_space=pltpu.VMEM)


def held(array):
    return pltpu.with_memory_space_constraint(array, pltpu.VMEM)


def sds(shape, dtype):
    return jax.ShapeDtypeStruct(shape, dtype)


def normalize(rows):
    center = rows - jnp.mean(rows, axis=-1, keepdims=True)
    spread = jnp.mean(center * center, axis=-1, keepdims=True)
    return center * lax.rsqrt(spread + EPS_NORM)


def columns(index, size):
    return pl.ds(pl.multiple_of(index * size, size), size)


def pack_body(meta, down_ref, up_ref, out_ref):
    mats = down_ref.shape[0]
    down, up = down_ref[...].astype(BF), up_ref[...].astype(BF)
    for dest in range(out_ref.shape[0]):
        out_ref[dest, 0] = down[mats - 1]
        out_ref[dest, 1] = up[mats - 1]
        out_ref[dest, 2 : mats + 1] = down[: mats - 1]
        out_ref[dest, mats + 1 :] = up[: mats - 1]


def pack_maps(meta, seq_count, down, up):
    shape = (seq_count, 2 * down.shape[0], *down.shape[1:])
    return kernel_call(
        pack_body, "pack_maps", (1,),
        [whole(down.shape), whole(up.shape)], whole(shape), sds(shape, BF),
        vmem=58,
    )(meta, down, up)


def unpack_body(meta, got_ref, out_ref, up_ref):
    count, _, size, _ = got_ref.shape
    for block in range(count):
        here = slice(block * size, (block + 1) * size)
        out_ref[:, here, :] = got_ref[block, 0:5]
        up_ref[:, here, :] = got_ref[block, 5:8]


def unpack_maps(meta, got, after):
    count, mats, size, shard = got.shape
    rank = count * size
    if size % 16:
        maps = jnp.transpose(got, (1, 0, 2, 3)).reshape(mats, rank, shard)
        return maps[:5], maps[5:]
    return kernel_call(
        unpack_body, "unpack_maps", (1,),
        [whole(got.shape)], [whole((5, rank, shard)), whole((3, rank, shard))],
        [sds((5, rank, shard), BF), sds((3, rank, shard), BF)],
        vmem=58,
        after=after,
    )(meta, got)


def side_sum(refs):
    one_ref, two_ref, out_ref = refs
    out_ref[...] = (one_ref[...].astype(F32) + two_ref[...].astype(F32)).astype(BF)


def ffn_body(unit, meta, x_ref, gain_ref, up_ref, down_ref, *refs):
    if unit == 0:
        mine_ref, sib_ref, low_ref, part_ref = refs
    else:
        one_ref, two_ref, mine_ref, sib_ref, sum_ref, low_ref, part_ref = refs
    step = pl.program_id(0)

    @pl.when(step == 0)
    def _():
        hat = normalize(x_ref[...].astype(F32))
        low_ref[...] = (hat * gain_ref[1:2, :]).astype(BF)
        part_ref[...] = jnp.zeros_like(part_ref)
        if unit:
            side_sum((one_ref, two_ref, sum_ref))

    hidden = dot_nn(low_ref[...], up_ref[...])
    hidden = 0.5 * hidden * (1.0 + lax.erf(hidden * (0.5**0.5)))
    part_ref[...] += dot_nn(hidden.astype(BF), down_ref[...])

    @pl.when(step == pl.num_programs(0) - 1)
    def _():
        core = core_of(meta)
        mine_ref[...] = part_ref[columns(core, BLOCK), :].astype(BF)
        sib_ref[...] = part_ref[columns(1 - core, BLOCK), :].astype(BF)


def ffn(meta, unit, x, gains, w_up, w_down, sums=(), after=()):
    rows, width = x.shape
    chunk = 512
    half = sds((BLOCK, width), BF)
    results = 2 + len(sums) // 2
    return kernel_call(
        partial(ffn_body, unit),
        f"ffn_{unit}",
        (w_up.shape[1] // chunk,),
        [
            pl.BlockSpec((UNIT, width), lambda i, m: (unit, 0)),
            whole(gains.shape),
            pl.BlockSpec((width, chunk), lambda i, m: (0, i)),
            pl.BlockSpec((chunk, width), lambda i, m: (i, 0)),
        ]
        + [whole((BLOCK, width))] * len(sums),
        [whole((BLOCK, width))] * results,
        [half] * results,
        [pltpu.VMEM((UNIT, width), BF), pltpu.VMEM((UNIT, width), F32)],
        flops=4 * UNIT * width * w_up.shape[1],
        moved=4 * w_up.size + 8 * UNIT * width,
        vmem=58,
        after=after,
    )(meta, x, gains, w_up, w_down, *sums)


def qkv_body(meta, x_ref, gain_ref, w_ref, low_ref, out_ref):
    hat = normalize(x_ref[...].astype(F32))
    low = (hat * gain_ref[0:1, :]).astype(BF)
    low_ref[...] = low
    shard = w_ref.shape[2]
    for k in range(3):
        out_ref[:, k * shard : (k + 1) * shard] = dot_nn(low, w_ref[k])


def frozen_qkv(meta, x, gains, w_qkv, after=()):
    rows, width = x.shape
    out = 3 * w_qkv.shape[2]
    return kernel_call(
        qkv_body,
        "frozen_qkv",
        (rows // UNIT,),
        [
            pl.BlockSpec((UNIT, width), lambda i, m: (i, 0)),
            whole(gains.shape),
            whole(w_qkv.shape),
        ],
        [
            pl.BlockSpec((UNIT, width), lambda i, m: (i, 0)),
            pl.BlockSpec((UNIT, out), lambda i, m: (i, 0)),
        ],
        [sds((rows, width), BF), sds((rows, out), F32)],
        flops=2 * rows * width * out,
        moved=2 * w_qkv.size + 4 * x.size + 4 * rows * out,
        vmem=58,
        after=after,
    )(meta, x, gains, w_qkv)


def rotary_tables(rows, shard):
    half = ROT // 2
    freq = np.exp(np.arange(half) * (-2.0 * math.log(10000.0) / ROT))
    angles = np.arange(rows)[:, None] * freq[None, :]
    cos, sin = np.cos(angles), np.sin(angles)
    one = np.ones((rows, HEAD))
    one[:, :half] = cos
    one[:, half:ROT] = cos
    up = np.zeros((rows, HEAD))
    up[:, half:ROT] = sin
    down = np.zeros((rows, HEAD))
    down[:, :half] = sin
    heads = min(shard, 128) // HEAD
    return [jnp.asarray(np.tile(table, (1, heads)), F32) for table in (one, up, down)]


def across(table, width):
    return jnp.concatenate([table] * (width // table.shape[1]), axis=1)


def turn(rows, cos, up, down, sign):
    half = ROT // 2
    width = rows.shape[1]
    from_low = pltpu.roll(rows, half, 1)
    from_high = pltpu.roll(rows, width - half, 1)
    cos, up, down = (across(table, width) for table in (cos, up, down))
    return rows * cos + sign * (from_low * up - from_high * down)


def project_unit(
    meta, low_ref, qkv_ref, cos_ref, up_ref, down_ref, maps, ups, q_ref, k_ref, v_ref, rank_ref
):
    proj = meta[PROJ]
    shard = q_ref.shape[1]
    rank = ups.shape[1]
    total = None
    for rel, piece in enumerate(maps):
        low = low_ref[:, columns(proj ^ rel, shard)]
        part = dot_nt(low, piece[2:5].reshape(3 * rank, shard))
        total = part if total is None else total + part
    rank_in = total.astype(BF)
    rank_ref[...] = rank_in
    pre = [
        qkv_ref[:, k * shard : (k + 1) * shard]
        + ADAPTER_SCALE * dot_nn(rank_in[:, k * rank : (k + 1) * rank], ups[k])
        for k in range(3)
    ]
    tables = (cos_ref[...], up_ref[...], down_ref[...])
    q_ref[...] = turn(pre[0], *tables, 1.0).astype(BF)
    k_ref[...] = turn(pre[1], *tables, 1.0).astype(BF)
    v_ref[...] = pre[2].astype(BF)


def vocab_chunks(vocab):
    return [(start, min(CHUNK_V, vocab - start)) for start in range(0, vocab, CHUNK_V)]


def for_chunks(vocab, first, last, together, run):
    whole_chunks = min(last, vocab // CHUNK_V)
    steps = (whole_chunks - first) // together

    def several(step, carry):
        for k in range(together):
            place = first + step * together + k
            run(place, pl.multiple_of(place * CHUNK_V, CHUNK_V), CHUNK_V)
        return carry

    if steps > 1:
        lax.fori_loop(0, steps, several, 0)
        first += steps * together
    for place in range(first, last):
        run(place, place * CHUNK_V, min(CHUNK_V, vocab - place * CHUNK_V))


def table_loads(table_ref, dest_ref, sem, first, groups):
    loads = {}
    for index, group in enumerate(groups):
        start = first * CHUNK_V
        stop = min(start + group * CHUNK_V, table_ref.shape[0])
        here = pl.ds(start, stop - start)
        loads[start] = pltpu.make_async_copy(table_ref.at[here], dest_ref.at[here], sem.at[index])
        first += group
    return loads


def vocab_buffers(vocab, width):
    return [
        pltpu.VMEM((vocab, width), BF),
        pltpu.VMEM((len(vocab_chunks(vocab)), UNIT, CHUNK_V), BF),
    ]


def head_mask(shard, head):
    return lax.broadcasted_iota(jnp.int32, (1, shard), 1) // HEAD == head


def diagonal():
    rows = lax.broadcasted_iota(jnp.int32, (BLOCK, BLOCK), 0)
    cols = lax.broadcasted_iota(jnp.int32, (BLOCK, BLOCK), 1)
    return rows >= cols


def block_scores(query, k_ref, prev, causal):
    scale = HEAD**-0.5
    diag = dot_nt(query, k_ref[prev : prev + BLOCK, :]) * scale
    diag = jnp.where(causal, diag, -1e30)
    if prev == 0:
        return diag
    return jnp.concatenate([dot_nt(query, k_ref[0:prev, :]) * scale, diag], axis=1)


def attend_unit(unit, meta, q_ref, k_ref, v_ref, mine_ref, sib_ref, lse_ref):
    shard = q_ref.shape[1]
    causal = diagonal()
    lane = lax.broadcasted_iota(jnp.int32, (BLOCK, 128), 1)
    for half in range(UNIT // BLOCK):
        prev = unit * UNIT + half * BLOCK
        query = q_ref[half * BLOCK : (half + 1) * BLOCK, :]
        out = jnp.zeros((BLOCK, shard), F32)
        lse = jnp.zeros((BLOCK, 128), F32)
        for head in range(shard // HEAD):
            mask = head_mask(shard, head)
            scores = block_scores(jnp.where(mask, query, 0), k_ref, prev, causal)
            top = jnp.max(scores, axis=1, keepdims=True)
            prob = jnp.exp(scores - top)
            total = jnp.sum(prob, axis=1, keepdims=True)
            got = dot_nn(prob.astype(BF), v_ref[0 : prev + BLOCK, :]) / total
            out = jnp.where(mask, got, out)
            lse = jnp.where(lane == head, top + jnp.log(total), lse)
        lse_ref[half * BLOCK : (half + 1) * BLOCK, :] = lse
        low = out.astype(BF)

        @pl.when(core_of(meta) == half)
        def _():
            mine_ref[...] = low

        @pl.when(core_of(meta) != half)
        def _():
            sib_ref[...] = low


def attend_first_body(
    meta, low_ref, qkv_ref, cos_ref, up_ref, down_ref, m0, m1, m2, m3, ups, one_ref, two_ref,
    w0, w1, w2, w3,
    q_ref, k_ref, v_ref, rank_ref, mine_ref, sib_ref, lse_ref, sum_ref, wo_ref, _u, _p, sem,
):
    shard = w0.shape[0]
    loads = [
        pltpu.make_async_copy(piece, wo_ref.at[pl.ds(rel * shard, shard)], sem.at[rel])
        for rel, piece in enumerate((w0, w1, w2, w3))
    ]
    for load in loads:
        load.start()
    side_sum((one_ref, two_ref, sum_ref))
    project_unit(
        meta, low_ref, qkv_ref, cos_ref, up_ref, down_ref, (m0, m1, m2, m3), ups,
        q_ref, k_ref, v_ref, rank_ref,
    )
    attend_unit(0, meta, q_ref, k_ref, v_ref, mine_ref, sib_ref, lse_ref)
    for load in loads:
        load.wait()


def attend_second_body(
    meta, _wo, _u, _p, _wo_out, held_ref, _p_out,
    low_ref, qkv_ref, cos_ref, up_ref, down_ref, m0, m1, m2, m3, ups, k_past, v_past, table_ref,
    q_ref, k_ref, v_ref, rank_ref, mine_ref, sib_ref, lse_ref, keys_ref, values_ref, sem,
):
    loads = list(table_loads(table_ref, held_ref, sem, 0, FIRST_GROUPS).values())
    for load in loads:
        load.start()
    project_unit(
        meta, low_ref, qkv_ref, cos_ref, up_ref, down_ref, (m0, m1, m2, m3), ups,
        q_ref, k_ref, v_ref, rank_ref,
    )
    for past, new, every in ((k_past, k_ref, keys_ref), (v_past, v_ref, values_ref)):
        every[0:UNIT, :] = past[...]
        every[UNIT:, :] = new[...]
    attend_unit(1, meta, q_ref, keys_ref, values_ref, mine_ref, sib_ref, lse_ref)
    for load in loads:
        load.wait()


def attend(meta, unit, low, qkv, tables, maps, ups, table, sums=(), wo=(), past=(), keep=()):
    rows, width = low.shape
    shard = qkv.shape[1] // 3
    rank = ups.shape[1]
    anywhere = pl.BlockSpec(memory_space=pl.ANY)
    block = lambda cols: pl.BlockSpec((UNIT, cols), lambda i, m: (unit, 0))
    in_specs = (
        [block(width), block(3 * shard)]
        + [block(tables[0].shape[1])] * 3
        + [whole(one.shape) for one in (*maps, ups)]
    )
    out_specs = [whole((UNIT, shard))] * 3 + [whole((UNIT, 3 * rank))]
    out_specs += [whole((BLOCK, shard))] * 2 + [whole((UNIT, 128))]
    out_shape = [sds((UNIT, shard), BF)] * 3 + [sds((UNIT, 3 * rank), BF)]
    out_shape += [sds((BLOCK, shard), BF)] * 2 + [sds((UNIT, 128), F32)]
    if unit == 0:
        body = attend_first_body
        args = (*sums, *wo)
        in_specs += [whole(one.shape) for one in sums] + [anywhere] * 4
        out_specs += [whole((BLOCK, width))] + [anywhere] * 3
        out_shape += [sds((BLOCK, width), BF), pltpu.VMEM((4 * shard, width), BF)]
        out_shape += vocab_buffers(*table.shape)
        scratch = [pltpu.SemaphoreType.DMA((4,))]
    else:
        body = attend_second_body
        args = (*past, table)
        in_specs += [whole((UNIT, shard))] * 2 + [anywhere]
        scratch = [pltpu.VMEM((rows, shard), BF)] * 2
        scratch += [pltpu.SemaphoreType.DMA((len(FIRST_GROUPS),))]
    return kernel_call(
        body, f"attend_{unit}", (1,), in_specs, out_specs, out_shape, scratch,
        keep=keep, use_keep=unit == 1,
    )(meta, low, qkv, *tables, *maps, ups, *args)


def place_grads(meta, pieces, grad_ref):
    core, ybit = core_of(meta), ybit_of(meta)
    for rel, piece in enumerate(pieces):
        place = (core ^ (rel & 1)) * 2 + (ybit ^ (rel >> 1))
        grad_ref[columns(place, BLOCK // 2), :] = piece[...]


def attend_back_unit(unit, grad_ref, q_ref, k_ref, v_ref, lse_ref, tables, dk_ref, dv_ref):
    shard = q_ref.shape[1]
    causal = diagonal()
    lane = lax.broadcasted_iota(jnp.int32, (BLOCK, 128), 1)
    scale = HEAD**-0.5
    dqs = []
    for half in range(UNIT // BLOCK):
        prev = unit * UNIT + half * BLOCK
        known = prev + BLOCK
        here = slice(half * BLOCK, (half + 1) * BLOCK)
        query = q_ref[here, :]
        grad = grad_ref[here, :]
        lse = lse_ref[here, :]
        dq = jnp.zeros((BLOCK, shard), F32)
        for head in range(shard // HEAD):
            mask = head_mask(shard, head)
            own_q = jnp.where(mask, query, 0)
            own_g = jnp.where(mask, grad, 0)
            own_lse = jnp.sum(jnp.where(lane == head, lse, 0.0), axis=1, keepdims=True)
            prob = jnp.exp(block_scores(own_q, k_ref, prev, causal) - own_lse)
            dweights = dot_nt(own_g, v_ref[0:known, :])
            delta = jnp.sum(prob * dweights, axis=1, keepdims=True)
            dscores = (prob * (dweights - delta)).astype(BF)
            dq = dq + jnp.where(mask, dot_nn(dscores, k_ref[0:known, :]), 0.0)
            dk_ref[0:known, :] += dot_tn(dscores, own_q) * scale
            dv_ref[0:known, :] += dot_tn(prob.astype(BF), own_g)
        rows = slice(prev, known)
        dq = turn(dq * scale, *(one[rows, :] for one in tables), -1.0)
        dqs.append(dq.astype(BF))
    return dqs


def attend_back_first_body(
    meta, g0, g1, g2, g3, q_ref, lse_ref, cos_ref, up_ref, down_ref, k_ref, v_ref,
    dq_ref, dk_ref, dv_ref, grad_ref,
):
    dk_ref[...] = jnp.zeros_like(dk_ref)
    dv_ref[...] = jnp.zeros_like(dv_ref)
    place_grads(meta, (g0, g1, g2, g3), grad_ref)
    dqs = attend_back_unit(
        0, grad_ref, q_ref, k_ref, v_ref, lse_ref, (cos_ref, up_ref, down_ref), dk_ref, dv_ref
    )
    dq_ref[...] = jnp.concatenate(dqs, axis=0)


def attend_back_first(meta, rows, grads, query, lse, tables, known, after, keep):
    shard = query.shape[1]
    args = (*grads, query, lse, *tables, *known)
    sums = (rows, shard)
    return kernel_call(
        attend_back_first_body, "attend_back_0", (1,),
        [whole(one.shape) for one in args],
        [whole((UNIT, shard)), whole(sums), whole(sums)],
        [sds((UNIT, shard), BF), sds(sums, F32), sds(sums, F32)],
        [pltpu.VMEM((UNIT, shard), BF)],
        after=after,
        keep=keep,
    )(meta, *args)


def attend_back_second_body(
    meta, g0, g1, g2, g3, q_ref, lse_ref, cos_ref, up_ref, down_ref, k0, v0, k1, v1,
    dk_in, dv_in, pair_ref, got_ref, dq0, rank0, rank1, ups, low_ref,
    own_ref, far_ref, keep_ref, send_ref, up_grad_ref,
    grad_ref, k_ref, v_ref, dk_ref, dv_ref, drank_ref,
):
    own_ref[...] = pair_ref[0].astype(F32) + got_ref[0].astype(F32)
    far_ref[...] = (pair_ref[1].astype(F32) + got_ref[1].astype(F32)).astype(BF)
    for first, second, every in ((k0, k1, k_ref), (v0, v1, v_ref)):
        every[0:UNIT, :] = first[...]
        every[UNIT:, :] = second[...]
    dk_ref[...] = dk_in[...]
    dv_ref[...] = dv_in[...]
    place_grads(meta, (g0, g1, g2, g3), grad_ref)
    tables = (cos_ref, up_ref, down_ref)
    dqs = attend_back_unit(1, grad_ref, q_ref, k_ref, v_ref, lse_ref, tables, dk_ref, dv_ref)
    proj = meta[PROJ]
    rank, shard = ups.shape[1:]
    dk = turn(dk_ref[...], *(one[...] for one in tables), -1.0).astype(BF)
    dpre = [jnp.concatenate([dq0[...], *dqs], axis=0), dk, dv_ref[...].astype(BF)]
    rank_in = jnp.concatenate([rank0[...], rank1[...]], axis=0)
    for k in range(3):
        here = slice(k * rank, (k + 1) * rank)
        up_grad_ref[k] = ADAPTER_SCALE * dot_tn(rank_in[:, here], dpre[k])
        drank_ref[:, here] = (ADAPTER_SCALE * dot_nt(dpre[k], ups[k])).astype(BF)
    drank = drank_ref[...]
    for rel in range(4):
        grad = dot_tn(drank, low_ref[:, columns(proj ^ rel, shard)])
        dest = (keep_ref, send_ref)[rel & 1]
        dest[rel >> 1] = grad.reshape(3, rank, shard).astype(BF)


def attend_back_second(meta, grads, query, lse, tables, known, sums, pair, dq0, rank_in, ups, low):
    rows, shard = sums[0].shape
    rank = ups.shape[1]
    args = (*grads, query, lse, *tables, *known, *sums, *pair, dq0, *rank_in, ups, low)
    out_shape = [
        sds((2, rank, shard), F32), sds((2, rank, shard), BF),
        sds((2, 3, rank, shard), BF), sds((2, 3, rank, shard), BF), sds((3, rank, shard), F32),
    ]
    return kernel_call(
        attend_back_second_body, "attend_back_1", (1,),
        [whole(one.shape) for one in args],
        [whole(one.shape) for one in out_shape],
        out_shape,
        [pltpu.VMEM((UNIT, shard), BF)]
        + [pltpu.VMEM((rows, shard), BF)] * 2
        + [pltpu.VMEM((rows, shard), F32)] * 2
        + [pltpu.VMEM((rows, 3 * rank), BF)],
        vmem=40,
    )(meta, *args)


def mix_body(
    meta, wo_ref, _u, _p, _wo, _u_out, _p_out, x_ref, gain_ref, f_own, f_far, a0, a1, a2, a3,
    m0, m1, m2, m3, norm_ref, res_ref, rank_ref, keep_ref,
):
    proj = meta[PROJ]
    shard = a0.shape[1]
    rank = None
    for a_ref, m_ref in ((a0, m0), (a1, m1), (a2, m2), (a3, m3)):
        part = dot_nt(a_ref[...], m_ref[0])
        rank = part if rank is None else rank + part
    rank = rank.astype(BF)
    total = x_ref[...].astype(F32) + f_own[...].astype(F32) + f_far[...].astype(F32)
    for rel, a_ref in enumerate((a0, a1, a2, a3)):
        total = total + dot_nn(a_ref[...], wo_ref[rel * shard : (rel + 1) * shard, :])
    keep_ref[...] = total
    for rel, m_ref in enumerate((m0, m1, m2, m3)):
        here = columns(proj ^ rel, shard)
        keep_ref[:, here] += ADAPTER_SCALE * dot_nn(rank, m_ref[1])
    residual = keep_ref[...]
    norm_ref[...] = (normalize(residual) * gain_ref[2:3, :]).astype(BF)
    mine = columns(ybit_of(meta), BLOCK // 2)
    res_ref[...] = keep_ref[mine, :]
    keep_ref[:, 0 : rank.shape[1]] = rank.astype(F32)
    rank_ref[...] = keep_ref[mine, 0 : rank.shape[1]].astype(BF)


def mix(meta, unit, x, gains, f_own, f_far, att, maps, keep, after=()):
    rows, width = x.shape
    shard = att[0].shape[1]
    rank = maps[0].shape[1]
    return kernel_call(
        mix_body,
        f"mix_{unit}",
        (1,),
        [
            pl.BlockSpec((BLOCK, width), lambda i, m: (2 * unit + core_of(m), 0)),
            whole(gains.shape),
            whole((BLOCK, width)),
            whole((BLOCK, width)),
        ]
        + [whole(one.shape) for one in att]
        + [whole((2, rank, shard))] * 4,
        [whole((BLOCK, width)), whole((BLOCK // 2, width)), whole((BLOCK // 2, rank))],
        [sds((BLOCK, width), BF), sds((BLOCK // 2, width), F32), sds((BLOCK // 2, rank), BF)],
        [pltpu.VMEM((BLOCK, width), F32)],
        after=after,
        keep=keep,
        use_keep=True,
    )(meta, x, gains, f_own, f_far, *att, *maps)


def local_columns(unit, meta, vocab, target_ref, out_ref):
    for group in range(4):
        half = core_of(meta) ^ (group >> 1)
        ids = target_ref[pl.ds((unit * 2 + half) * 2 + (group & 1), 1), :] - meta[PROJ] * vocab
        ids = jnp.where((ids >= 0) & (ids < vocab), ids, -1)
        square = jnp.transpose(jnp.broadcast_to(ids.astype(F32), (128, 128)))
        out_ref[group * 128 : (group + 1) * 128, :] = square.astype(jnp.int32)


def vocab_stats_body(unit, meta, _wo, _u, _p, _wo_out, u_ref, p_ref, *refs):
    vocab = u_ref.shape[0]
    chunks = vocab_chunks(vocab)
    if unit == 0:
        mine_ref, sib_ref, target_ref, table_ref, top_ref, st_ref, acc_ref, col_ref, sem = refs
        loads = table_loads(table_ref, u_ref, sem, sum(FIRST_GROUPS), SECOND_GROUPS)
    else:
        mine_ref, sib_ref, target_ref, top_ref, st_ref, acc_ref, col_ref = refs
        loads = {}
    for load in loads.values():
        load.start()
    acc_ref[...] = jnp.zeros_like(acc_ref)
    local_columns(unit, meta, vocab, target_ref, col_ref)
    lane = lax.broadcasted_iota(jnp.int32, (BLOCK, 128), 1)

    def chunk(place, start, size):
        col = lax.broadcasted_iota(jnp.int32, (BLOCK, size), 1)
        for half, rows_ref in enumerate((mine_ref, sib_ref)):
            here = slice(half * BLOCK, (half + 1) * BLOCK)
            logits = dot_nt(rows_ref[...], u_ref[pl.ds(start, size), :])
            top = jnp.max(logits, axis=1, keepdims=True)
            prob = jnp.exp(logits - top)
            total = jnp.sum(prob, axis=1, keepdims=True)
            hit = col == col_ref[here, 0:1] - start
            picked = jnp.sum(jnp.where(hit, logits, 0.0), axis=1, keepdims=True)
            p_ref[place, here, 0:size] = prob.astype(BF)
            acc = acc_ref[here, :]
            acc = jnp.where(lane == place, top, acc)
            acc = jnp.where(lane == place + 32, total, acc)
            acc_ref[here, :] = jnp.where(lane == 64, acc + picked, acc)

    if unit == 0:
        for_chunks(vocab, 0, sum(FIRST_GROUPS), TOGETHER_V, chunk)
        for load in loads.values():
            load.wait()
        for_chunks(vocab, sum(FIRST_GROUPS), len(chunks), TOGETHER_V, chunk)
    else:
        for_chunks(vocab, 0, len(chunks), len(chunks), chunk)
    acc = acc_ref[...]
    lane = lax.broadcasted_iota(jnp.int32, acc.shape, 1)
    top_ref[...] = acc
    tops = jnp.where(lane < len(chunks), acc, -1e30)
    best = jnp.max(tops, axis=1, keepdims=True)
    totals = pltpu.roll(acc, 128 - 32, 1)
    total = jnp.sum(
        jnp.where(lane < len(chunks), totals * jnp.exp(tops - best), 0.0), axis=1, keepdims=True
    )
    picked = jnp.sum(jnp.where(lane == 64, acc, 0.0), axis=1, keepdims=True)
    pair = jnp.where(lane == 0, best + jnp.log(total), jnp.where(lane == 1, picked, 0.0))
    st_ref[...] = jnp.transpose(pair)[0:8, :]


def vocab_stats(meta, unit, mine, sib, targets, table, keep, after=()):
    rows = 2 * BLOCK
    first = unit == 0
    return kernel_call(
        partial(vocab_stats_body, unit),
        f"vocab_stats_{unit}",
        (),
        [IN_VMEM] * 3 + [pl.BlockSpec(memory_space=pl.ANY)] * first,
        [IN_VMEM] * 2,
        [sds((rows, 128), F32), sds((8, rows), F32)],
        [pltpu.VMEM((rows, 128), F32), pltpu.VMEM((rows, 128), jnp.int32)]
        + [pltpu.SemaphoreType.DMA((len(SECOND_GROUPS),))] * first,
        after=after,
        keep=keep,
        use_keep=True,
    )(meta, mine, sib, targets, *((table,) * first))


def swap_halves(pair):
    return jnp.concatenate([pair[:, BLOCK:], pair[:, :BLOCK]], axis=1)


def vocab_back_body(
    unit, meta, _wo, u_ref, p_ref, _wo_out, _u, _p, lens_ref, target_ref, top_ref, s0, s1, s2, s3,
    d0, d1, d2, d3, loss_ref, scale_ref, acc_ref, col_ref,
):
    vocab = u_ref.shape[0]
    chunks = vocab_chunks(vocab)
    rows = 2 * BLOCK
    acc_ref[...] = jnp.zeros_like(acc_ref)
    local_columns(unit, meta, vocab, target_ref, col_ref)
    parts = [s0[...], swap_halves(s1[...]), s2[...], swap_halves(s3[...])]
    lses = [part[0:1, :] for part in parts]
    best = jnp.maximum(jnp.maximum(lses[0], lses[1]), jnp.maximum(lses[2], lses[3]))
    total = sum(jnp.exp(one - best) for one in lses)
    log_norm = best + jnp.log(total)
    picked = sum(part[1:2, :] for part in parts)
    place = lax.broadcasted_iota(jnp.int32, (1, rows), 1)
    core = core_of(meta)
    offset = jnp.where(place < BLOCK, core * BLOCK, (1 - core) * BLOCK - BLOCK)
    valid = (unit * UNIT + place + offset < lens_ref[meta[SEQ]]).astype(F32)
    loss_ref[...] = jnp.broadcast_to(
        jnp.sum((log_norm - picked) * valid, axis=1, keepdims=True), (8, 128)
    )
    weight = valid / token_count(lens_ref)
    row = lax.broadcasted_iota(jnp.int32, (128, rows), 0)
    lines = jnp.where(row == 0, log_norm, 0.0)
    lines = jnp.where(row == 1, weight, lines)
    lines = jnp.where(row == 2, (jnp.exp(picked - log_norm) - 1.0) * weight, lines)
    cols = jnp.transpose(lines)
    lane = lax.broadcasted_iota(jnp.int32, (rows, 128), 1)
    take = lambda k: jnp.sum(jnp.where(lane == k, cols, 0.0), axis=1, keepdims=True)
    tops = jnp.where(lane < len(chunks), top_ref[...], -1e30)
    scales = jnp.exp(tops - take(0)) * take(1)
    scale_ref[...] = jnp.where(lane == 64, take(2), scales)

    lane = lax.broadcasted_iota(jnp.int32, (BLOCK, 128), 1)
    for place, (start, size) in enumerate(chunks):
        col = lax.broadcasted_iota(jnp.int32, (BLOCK, size), 1)
        for half in range(2):
            here = slice(half * BLOCK, (half + 1) * BLOCK)
            scales = scale_ref[here, :]
            at_hit = jnp.sum(jnp.where(lane == 64, scales, 0.0), axis=1, keepdims=True)
            scale = jnp.sum(jnp.where(lane == place, scales, 0.0), axis=1, keepdims=True)
            hit = col == col_ref[here, 0:1] - start
            grad = jnp.where(hit, at_hit, p_ref[place, here, 0:size].astype(F32) * scale)
            acc_ref[here, :] += dot_nn(grad.astype(BF), u_ref[start : start + size, :])

    quarter = BLOCK // 2
    for rel, out_ref in enumerate((d0, d1, d2, d3)):
        place = (rel & 1) * 2 + (ybit_of(meta) ^ (rel >> 1))
        out_ref[...] = acc_ref[columns(place, quarter), :].astype(BF)


def vocab_back(meta, unit, lens, targets, tops, stats, keep, after=()):
    width = keep[1].shape[1]
    rows = 2 * BLOCK
    quarter = sds((BLOCK // 2, width), BF)
    return kernel_call(
        partial(vocab_back_body, unit),
        f"vocab_back_{unit}",
        (),
        [SCALARS] + [IN_VMEM] * 6,
        [IN_VMEM] * 5,
        [quarter] * 4 + [sds((8, 128), F32)],
        [
            pltpu.VMEM((rows, 128), F32),
            pltpu.VMEM((rows, width), F32),
            pltpu.VMEM((rows, 128), jnp.int32),
        ],
        after=after,
        keep=keep,
        use_keep=True,
    )(meta, lens, targets, tops, *stats)


def norm_back_body(last, meta, wo_ref, *refs):
    refs = refs[1:] if last else refs[5:]
    parts, (res_ref, gain_ref, rank_ref) = refs[:4], refs[4:7]
    atts, maps = refs[7:11], refs[11:15]
    if last:
        before_ref, *outs, keep_ref, send_ref, hold_ref = refs[15:]
    else:
        *outs, sum_ref, hold_ref = refs[15:]
    proj = meta[PROJ]
    shard = atts[0].shape[1]
    dnormed = sum(part[...].astype(F32) for part in parts)
    residual = res_ref[...]
    center = residual - jnp.mean(residual, axis=-1, keepdims=True)
    spread = jnp.mean(center * center, axis=-1, keepdims=True)
    inv = lax.rsqrt(spread + EPS_NORM)
    hat = center * inv
    dhat = dnormed * gain_ref[2:3, :]
    dres = inv * (
        dhat
        - jnp.mean(dhat, axis=-1, keepdims=True)
        - hat * jnp.mean(dhat * hat, axis=-1, keepdims=True)
    )
    hold_ref[...] = dres.astype(BF)
    dbranch = hold_ref[...]
    drank = None
    for rel, m_ref in enumerate(maps):
        part = dot_nt(hold_ref[:, columns(proj ^ rel, shard)], m_ref[1])
        drank = part if drank is None else drank + part
    drank = (ADAPTER_SCALE * drank).astype(BF)
    for rel in range(4):
        w_piece = wo_ref[rel * shard : (rel + 1) * shard, :]
        datt = dot_nt(dbranch, w_piece) + dot_nn(drank, maps[rel][0])
        outs[rel][...] = datt.astype(BF)
        g_down = dot_tn(drank, atts[rel][...])
        g_up = ADAPTER_SCALE * dot_tn(rank_ref[...], hold_ref[:, columns(proj ^ rel, shard)])
        if last:
            dest = (keep_ref, send_ref)[rel & 1]
            dest[rel >> 1, 0] = (before_ref[rel, 0] + g_down).astype(BF)
            dest[rel >> 1, 1] = (before_ref[rel, 1] + g_up).astype(BF)
        else:
            sum_ref[rel, 0] = g_down
            sum_ref[rel, 1] = g_up


def norm_back(
    meta, unit, last, parts, residual, gains, rank_out, att, maps, before, keep, after=()
):
    quarter, width = residual.shape
    shard = att[0].shape[1]
    rank = rank_out.shape[1]
    piece = (quarter, shard)
    if last:
        more = [sds((2, 2, rank, shard), BF)] * 2
    else:
        more = [sds((4, 2, rank, shard), F32)]
    return kernel_call(
        partial(norm_back_body, last),
        f"norm_back_{unit}",
        (1,),
        [whole(one.shape) for one in parts]
        + [whole(residual.shape), whole(gains.shape), whole(rank_out.shape)]
        + [pl.BlockSpec(piece, lambda i, m: (ybit_of(m), 0))] * 4
        + [whole((2, rank, shard))] * 4
        + [whole(one.shape) for one in before],
        [whole(piece)] * 4 + [whole(one.shape) for one in more],
        [sds(piece, BF)] * 4 + more,
        [pltpu.VMEM((quarter, width), BF)],
        after=after,
        keep=keep,
        use_keep=True,
    )(meta, *parts, residual, gains, rank_out, *att, *maps, *before)


def signs(row_ids, col_ids, seed):
    hashed = row_ids * 1640531527 + col_ids * 747796405 + seed * 277803737
    hashed = hashed ^ hashed >> 15 & 131071
    hashed = hashed * 2024237689
    hashed = hashed ^ hashed >> 13 & 524287
    return 1.0 - 2.0 * (hashed >> 17 & 1).astype(F32)


def sketch_one(meta, seed, grad, sketch):
    rank, shard = grad.shape
    left_rows = lax.broadcasted_iota(jnp.int32, (sketch, shard), 1) + meta[PROJ] * shard
    left_cols = lax.broadcasted_iota(jnp.int32, (sketch, shard), 0)
    right_rows = lax.broadcasted_iota(jnp.int32, (rank, sketch), 0)
    right_cols = lax.broadcasted_iota(jnp.int32, (rank, sketch), 1)
    left = signs(left_rows, left_cols, 2 * seed).astype(BF)
    right = signs(right_rows, right_cols, 2 * seed + 1)
    return jnp.dot(dot_nt(left, grad), right, precision=lax.Precision.HIGHEST)


def local_sketch_body(meta, seeds_ref, lens_ref, own_ref, far_ref, up_ref, block_ref, full_ref):
    size = block_ref.shape[2]
    count = token_count(lens_ref)
    out = own_ref[...] + far_ref[...].astype(F32)
    for place, grad in enumerate((out[0], up_ref[0], up_ref[1], up_ref[2], out[1])):
        for dest in range(block_ref.shape[0]):
            block_ref[dest, place] = grad[dest * size : (dest + 1) * size].astype(BF)
        full_ref[place] = count * sketch_one(
            meta, seeds_ref[3 + place], grad.astype(BF), full_ref.shape[1]
        )


def local_sketch(meta, seeds, lens, own, far, ups, sketch_width):
    _, rank, shard = own.shape
    count = lens.shape[0]
    blocks = (count, 5, rank // count, shard)
    full = (5, sketch_width, sketch_width)
    return kernel_call(
        local_sketch_body, "local_sketch", (1,),
        [SCALARS, SCALARS, whole(own.shape), whole(far.shape), whole(ups.shape)],
        [whole(blocks), whole(full)],
        [sds(blocks, BF), sds(full, F32)],
        flops=10 * rank * shard * sketch_width,
        moved=16 * own.size,
    )(meta, seeds, lens, own, far, ups)


def gather_body(meta, keep_ref, got_ref, far_ref, five_ref, block_ref, grad_ref):
    size = block_ref.shape[2]
    total = keep_ref[0].astype(F32) + got_ref[0].astype(F32) + far_ref[...].astype(F32)
    grad_ref[...] = total.astype(BF)
    for dest in range(block_ref.shape[0]):
        for mat in range(3):
            block_ref[dest, mat] = total[mat, dest * size : (dest + 1) * size].astype(BF)
        block_ref[dest, 3:8] = five_ref[dest]


def gather_blocks(meta, keep, got, far, five):
    count, _, size, shard = five.shape
    blocks = (count, 8, size, shard)
    pair = pl.BlockSpec((1, *keep.shape[1:]), lambda i, m: (0, 0, 0, 0))
    return kernel_call(
        gather_body, "gather_blocks", (1,),
        [pair, pair, whole(far.shape), whole(five.shape)],
        [whole(blocks), whole(far.shape)],
        [sds(blocks, BF), sds(far.shape, BF)],
    )(meta, keep, got, far, five)


def sketch_body(meta, seeds_ref, lens_ref, grad_ref, five_ref, f0, f1, f2, f3, full_ref):
    count = token_count(lens_ref)
    sketch = full_ref.shape[1]
    full_ref[3:8] = five_ref[...]
    for mat in range(3):
        full_ref[mat] = count * sketch_one(meta, seeds_ref[mat], grad_ref[mat], sketch)
    size = sketch // 4
    for rel, out_ref in enumerate((f0, f1, f2, f3)):
        out_ref[...] = full_ref[:, columns(meta[PROJ] ^ rel, size), :]


def sketch(meta, seeds, lens, grads, five):
    sketch_width = five.shape[1]
    piece = (8, sketch_width // 4, sketch_width)
    return kernel_call(
        sketch_body, "sketch", (1,),
        [SCALARS, SCALARS, whole(grads.shape), whole(five.shape)],
        [whole(piece)] * 4,
        [sds(piece, F32)] * 4,
        [pltpu.VMEM((8, sketch_width, sketch_width), F32)],
        flops=2 * grads.size * sketch_width,
        moved=2 * grads.size,
    )(meta, seeds, lens, grads, five)


def lane_value(row, lane, place):
    return jnp.sum(jnp.where(lane == place, row, 0.0), axis=1, keepdims=True)


def tally_body(
    units, meta, got_ref, target_ref, f0, f1, f2, f3, *refs
):
    losses, (total_ref, line_ref) = refs[:units], refs[units:]
    total = jnp.sum(got_ref[...].astype(F32), axis=0)
    total_ref[...] = total
    features = f0[...] + f1[...] + f2[...] + f3[...]
    squares = jnp.sum(total * total)
    own = jnp.sum(features * features)
    loss = sum(jnp.sum(one[0:1, 0:1]) for one in losses)
    loss = jnp.where(meta[PROJ] == 0, loss, 0.0)
    lane = lax.broadcasted_iota(jnp.int32, (1, 128), 1)
    line = jnp.where(lane == 0, squares, 0.0)
    line = jnp.where(lane == 1, loss, line)
    line = jnp.where(lane == 2, own, line)
    checkpoints = target_ref.shape[0]
    for c in range(checkpoints):
        theirs = target_ref[c]
        line = jnp.where(lane == 3 + c, jnp.sum(features * theirs), line)
        line = jnp.where(lane == 3 + checkpoints + c, jnp.sum(theirs * theirs), line)
    line_ref[...] = jnp.broadcast_to(line, line_ref.shape)


def tally(meta, devices, got, targets, pieces, losses):
    _, mats, slice_rank, shard = got.shape
    args = (got, targets, *pieces, *losses)
    return kernel_call(
        partial(tally_body, len(losses)),
        "tally",
        (1,),
        [whole(one.shape) for one in args],
        [whole((mats, slice_rank, shard)), whole((devices, 128))],
        [sds((mats, slice_rank, shard), F32), sds((devices, 128), F32)],
    )(meta, *args)


def optimizer_step(weight, grad_in, first_in, second_in, clipping_scale):
    grad_clip = grad_in * clipping_scale
    first_new = BETA_ONE * first_in + (1.0 - BETA_ONE) * grad_clip
    second_new = BETA_TWO * second_in + (1.0 - BETA_TWO) * grad_clip * grad_clip
    first_hat = first_new / (1.0 - BETA_ONE**STEP)
    second_hat = second_new / (1.0 - BETA_TWO**STEP)
    new_weight = weight - LEARN_RATE * (
        first_hat / (jnp.sqrt(second_hat) + ADAM_EPS) + WEIGHT_DECAY * weight
    )
    return (new_weight, first_new, second_new)


def finish_body(
    proj_count, checkpoints, meta, lens_ref, lines_ref, total_ref,
    dw, uw, dm, um, ds, us,
    loss_out, norm_out, influence_out, dw_out, uw_out, dm_out, um_out, ds_out, us_out,
):
    lines = lines_ref[...]
    everyone = jnp.sum(lines, axis=0, keepdims=True)
    row = lax.broadcasted_iota(jnp.int32, lines.shape, 0)
    ours = jnp.sum(
        jnp.where(row // proj_count == meta[SEQ], lines, 0.0), axis=0, keepdims=True
    )
    lane = lax.broadcasted_iota(jnp.int32, (1, 128), 1)
    grad_norm = jnp.sqrt(lane_value(everyone, lane, 0))
    own = lane_value(ours, lane, 2)
    influence = jnp.zeros((1, 1), F32)
    for c in range(checkpoints):
        dot = lane_value(ours, lane, 3 + c)
        theirs = lane_value(ours, lane, 3 + checkpoints + c)
        influence += (1.0 - c / checkpoints) * dot * lax.rsqrt(own * theirs + 1e-12)
    loss_out[0] = jnp.sum(lane_value(everyone, lane, 1))
    loss_out[1] = token_count(lens_ref)
    norm_out[0] = jnp.sum(grad_norm)
    influence_out[0] = jnp.sum(influence)
    clip = jnp.minimum(1.0, CLIP_NORM / (grad_norm + 1e-06))
    half = total_ref.shape[0] // 2
    for base, ins, outs in (
        (0, (dw, dm, ds), (dw_out, dm_out, ds_out)),
        (half, (uw, um, us), (uw_out, um_out, us_out)),
    ):
        for k in range(half):
            new = optimizer_step(
                ins[0][k], total_ref[base + k], ins[1][k], ins[2][k], clip
            )
            for out, value in zip(outs, new):
                out[k] = value


def finish(meta, proj_count, checkpoints, lens, lines, total, params):
    block = whole(params[0].shape)
    return kernel_call(
        partial(finish_body, proj_count, checkpoints),
        "finish",
        (1,),
        [SCALARS, whole(lines.shape), whole(total.shape)] + [block] * 6,
        [SCALARS] * 3 + [block] * 6,
        [sds((2,), F32), sds((1,), F32), sds((1,), F32)] + [sds(params[0].shape, F32)] * 6,
        flops=20 * total.size,
        moved=28 * total.size,
    )(meta, lens, lines, total, *params)


def to_partner(array, axis, size, offset):
    return lax.ppermute(array, axis, [(i, i ^ offset) for i in range(size)])


def on_device(
    seq_count,
    proj_count,
    inputs,
    targets,
    lengths,
    norm_gain_vectors,
    query_key_value_weight,
    attention_output_weight,
    feedforward_input_weight,
    feedforward_output_weight,
    unembed,
    adapter_down_maps,
    adapter_up_maps,
    down_first_moment,
    up_first_moment,
    down_second_moment,
    up_second_moment,
    target_gradient_sketches,
    seeds,
):
    rows, width = inputs.shape
    shard = attention_output_weight.shape[0]
    vocab_local = unembed.shape[1]
    slice_rank = adapter_up_maps.shape[1]
    rank = slice_rank * seq_count
    sketch_width = target_gradient_sketches.shape[3]
    proj = lax.axis_index("proj")
    seq = lax.axis_index("dp")

    over_proj = lambda array, rel: to_partner(array, "proj", proj_count, rel)
    over_seq = lambda array, rel: to_partner(array, "dp", seq_count, rel)

    meta = jnp.stack([proj, seq]).astype(jnp.int32)
    targets = targets.reshape(rows // 128, 128)
    table = jnp.transpose(unembed)
    tables = rotary_tables(rows, shard)
    transposed = lambda array: jnp.transpose(array, (0, 2, 1))

    def from_all(array):
        y = over_proj(array, 2)
        return (array, over_proj(array, 1), y, over_proj(y, 1))

    def exchange(*pieces):
        return [pieces[0]] + [over_proj(pieces[rel], rel) for rel in (1, 2, 3)]

    packed = pack_maps(meta, seq_count, transposed(adapter_down_maps), adapter_up_maps)
    arrived = lax.all_to_all(packed, "dp", split_axis=0, concat_axis=0, tiled=True)
    wo = from_all(attention_output_weight)

    w_ffn = (feedforward_input_weight, feedforward_output_weight)
    f0_mine, f0_sib = ffn(meta, 0, inputs, norm_gain_vectors, *w_ffn)
    low, qkv = frozen_qkv(
        meta, inputs, norm_gain_vectors, jnp.transpose(query_key_value_weight, (1, 0, 2)),
        (f0_mine,),
    )
    maps, ups = unpack_maps(meta, arrived, (low,))
    maps = from_all(maps)
    f1_mine, f1_sib, f0_chip = ffn(
        meta, 1, inputs, norm_gain_vectors, *w_ffn, (f0_mine, over_proj(f0_sib, 1)), (maps[0],)
    )
    q0, k0, v0, rank_in0, mine, sib, lse0, f1_chip, *keep = attend(
        meta, 0, low, qkv, tables, maps, ups, table, (f1_mine, over_proj(f1_sib, 1)), wo
    )
    att0 = exchange(mine, sib, mine, sib)
    q1, k1, v1, rank_in1, mine, sib, lse1, *keep = attend(
        meta, 1, low, qkv, tables, maps, ups, table, past=(k0, v0), keep=keep
    )
    att1 = exchange(mine, sib, mine, sib)
    f_chip = (f0_chip, f1_chip)
    f_far = [over_proj(one, 2) for one in f_chip]

    def mix_unit(unit, att, keep, after):
        normed, residual, rank_out, *keep = mix(
            meta, unit, inputs, norm_gain_vectors, f_chip[unit], f_far[unit], att, maps, keep, after
        )
        return (normed, over_proj(normed, 1)), residual, rank_out, keep

    def stats_unit(unit, normed, keep, after=()):
        top, stat, *keep = vocab_stats(meta, unit, *normed, targets, table, keep, after)
        return top, exchange(stat, stat, stat, stat), keep

    def back_unit(unit, top, stats, keep, after):
        d0, d1, d2, d3, loss, *keep = vocab_back(
            meta, unit, lengths, targets, top, stats, keep, after
        )
        return exchange(d0, d1, d2, d3), loss, keep

    def norm_unit(unit, parts, residual, rank_out, att, before, keep, after):
        d0, d1, d2, d3, *more = norm_back(
            meta, unit, unit == 1, parts, residual, norm_gain_vectors,
            rank_out, att, maps, before, keep, after,
        )
        grads = more[: 1 + unit]
        return exchange(d0, d1, d2, d3), grads, more[1 + unit :]

    normed0, residual0, rank0, keep = mix_unit(0, att0, keep, (lse1,))
    top0, stats0, keep = stats_unit(0, normed0, keep)
    normed1, residual1, rank1, keep = mix_unit(1, att1, keep, (stats0[0],))
    dnormed0, loss0, keep = back_unit(0, top0, stats0, keep, (rank1,))
    top1, stats1, keep = stats_unit(1, normed1, keep, (loss0,))
    datt0, out_grads, keep = norm_unit(
        0, dnormed0, residual0, rank0, att0, (), keep, (stats1[0],)
    )
    dnormed1, loss1, keep = back_unit(1, top1, stats1, keep, (datt0[0],))
    dq0, dk, dv, *keep = attend_back_first(
        meta, rows, datt0, q0, lse0, tables, (k0, v0), (loss1,), keep[:1]
    )
    datt1, (out_keep, out_send), _ = norm_unit(
        1, dnormed1, residual1, rank1, att1, out_grads, keep, (dq0,)
    )
    out_own, out_far, in_keep, in_send, up_grads = attend_back_second(
        meta, datt1, q1, lse1, tables, (k0, v0, k1, v1), (dk, dv),
        (out_keep, over_proj(out_send, 1)), dq0, (rank_in0, rank_in1), ups, low,
    )
    out_far = over_proj(out_far, 2)
    in_got = over_proj(in_send, 1)
    in_far = over_proj((in_keep[1].astype(F32) + in_got[1].astype(F32)).astype(BF), 2)
    blocks, five = local_sketch(meta, seeds, lengths, out_own, out_far, up_grads, sketch_width)
    blocks, in_grads = gather_blocks(meta, in_keep, in_got, in_far, blocks)
    arrived = lax.all_to_all(blocks, "dp", split_axis=0, concat_axis=0, tiled=True)
    pieces = exchange(*sketch(meta, seeds, lengths, in_grads, five))

    device_count = seq_count * proj_count
    total, lines = tally(
        meta, device_count, arrived, target_gradient_sketches, pieces, (loss0, loss1)
    )
    lines = lax.all_to_all(lines, ("dp", "proj"), split_axis=0, concat_axis=0, tiled=True)
    params = (
        transposed(adapter_down_maps),
        adapter_up_maps,
        transposed(down_first_moment),
        up_first_moment,
        transposed(down_second_moment),
        up_second_moment,
    )
    loss_parts, grad_norm, influence, dw, uw, dm, um, ds, us = finish(
        meta, proj_count, target_gradient_sketches.shape[0], lengths, lines, total, params
    )
    return (
        loss_parts,
        grad_norm,
        influence,
        transposed(dw),
        uw,
        transposed(dm),
        um,
        transposed(ds),
        us,
    )


def solution(mesh):
    in_specs = (
        P("dp", None),
        P("dp"),
        P(),
        P(),
        P(None, None, "proj"),
        P("proj", None),
        P(None, "proj"),
        P("proj", None),
        P(None, "proj"),
        P(None, "proj", "dp"),
        P(None, "dp", "proj"),
        P(None, "proj", "dp"),
        P(None, "dp", "proj"),
        P(None, "proj", "dp"),
        P(None, "dp", "proj"),
        P(None, None, "proj", None),
        P(),
    )
    out_specs = (
        P(),
        P(),
        P("dp"),
        P(None, "proj", "dp"),
        P(None, "dp", "proj"),
        P(None, "proj", "dp"),
        P(None, "dp", "proj"),
        P(None, "proj", "dp"),
        P(None, "dp", "proj"),
    )
    return jax.shard_map(
        partial(on_device, mesh.shape["dp"], mesh.shape["proj"]),
        mesh=mesh,
        in_specs=in_specs,
        out_specs=out_specs,
        check_vma=False,
    )
```

```python
from functools import partial
import math

import jax
import jax.numpy as jnp
import numpy as np
from jax import lax
from jax.experimental import pallas as pl
from jax.experimental.pallas import tpu as pltpu
from jax.sharding import PartitionSpec as P

HEAD = 64
ROT = 16
STEP = 10

EPS_NORM = 1e-05
ADAPTER_SCALE = 0.25
CLIP_NORM = 0.05
LEARN_RATE = 0.05
BETA_ONE = 0.9
BETA_TWO = 0.99
ADAM_EPS = 1e-08
WEIGHT_DECAY = 0.01

BF = jnp.bfloat16
F32 = jnp.float32
BLOCK = 256
UNIT = 512
FIRST_GROUPS = (4, 4, 4, 3)
SECOND_GROUPS = (5, 5)
TOGETHER_V = 5
CHUNK_V = 512
MIB = 2**20

PROJ, SEQ = range(2)


def core_of(meta):
    return meta[PROJ] & 1


def ybit_of(meta):
    return meta[PROJ] >> 1


def token_count(lens_ref):
    return sum(lens_ref[i] for i in range(lens_ref.shape[0])).astype(F32)


def dot_nn(lhs, rhs):
    return lax.dot_general(lhs, rhs, (((1,), (0,)), ((), ())), preferred_element_type=F32)


def dot_nt(lhs, rhs):
    return lax.dot_general(lhs, rhs, (((1,), (1,)), ((), ())), preferred_element_type=F32)


def dot_tn(lhs, rhs):
    return lax.dot_general(lhs, rhs, (((0,), (0,)), ((), ())), preferred_element_type=F32)


def kernel_call(
    body, name, grid, in_specs, out_specs, out_shape, scratch=(), flops=0, moved=0, after=(),
    vmem=20, keep=(), use_keep=False,
):
    single = not isinstance(out_shape, (list, tuple))
    if single:
        out_specs, out_shape = [out_specs], [out_shape]
    first_keep = 1 + len(in_specs) + len(after)
    first_out = first_keep + len(keep)
    first_kept = first_out + len(out_shape)
    first_scratch = first_kept + len(keep)

    def run(*refs):
        kept = refs[first_keep:first_out] + refs[first_kept:first_scratch]
        body(
            refs[0],
            *(kept if use_keep else ()),
            *refs[1 : 1 + len(in_specs)],
            *refs[first_out:first_kept],
            *refs[first_scratch:],
        )

    anywhere = pl.BlockSpec(memory_space=pl.ANY)
    keep_spec = IN_VMEM if use_keep else anywhere
    call = pl.pallas_call(
        run,
        grid_spec=pltpu.PrefetchScalarGridSpec(
            num_scalar_prefetch=1,
            grid=grid,
            in_specs=list(in_specs) + [anywhere] * len(after) + [keep_spec] * len(keep),
            out_specs=list(out_specs) + [keep_spec] * len(keep),
            scratch_shapes=list(scratch),
        ),
        out_shape=list(out_shape) + [pltpu.VMEM(one.shape, one.dtype) for one in keep],
        input_output_aliases={
            first_keep + i: len(out_shape) + i for i in range(len(keep))
        },
        compiler_params=pltpu.CompilerParams(vmem_limit_bytes=vmem * MIB),
        cost_estimate=pl.CostEstimate(flops=10**12, bytes_accessed=1000, transcendentals=0),
        name=name,
    )

    def apply(*args):
        results = call(*args, *after, *[held(one) for one in keep])
        return results[0] if single else results

    return apply


def whole(shape):
    zeros = (0,) * len(shape)
    return pl.BlockSpec(shape, lambda *_: zeros)


SCALARS = pl.BlockSpec(memory_space=pltpu.SMEM)
IN_VMEM = pl.BlockSpec(memory_space=pltpu.VMEM)


def held(array):
    return pltpu.with_memory_space_constraint(array, pltpu.VMEM)


def sds(shape, dtype):
    return jax.ShapeDtypeStruct(shape, dtype)


def normalize(rows):
    center = rows - jnp.mean(rows, axis=-1, keepdims=True)
    spread = jnp.mean(center * center, axis=-1, keepdims=True)
    return center * lax.rsqrt(spread + EPS_NORM)


def columns(index, size):
    return pl.ds(pl.multiple_of(index * size, size), size)


def pack_body(meta, down_ref, up_ref, out_ref):
    mats = down_ref.shape[0]
    down, up = down_ref[...].astype(BF), up_ref[...].astype(BF)
    for dest in range(out_ref.shape[0]):
        out_ref[dest, 0] = down[mats - 1]
        out_ref[dest, 1] = up[mats - 1]
        out_ref[dest, 2 : mats + 1] = down[: mats - 1]
        out_ref[dest, mats + 1 :] = up[: mats - 1]


def pack_maps(meta, seq_count, down, up):
    shape = (seq_count, 2 * down.shape[0], *down.shape[1:])
    return kernel_call(
        pack_body, "pack_maps", (1,),
        [whole(down.shape), whole(up.shape)], whole(shape), sds(shape, BF),
        vmem=58,
    )(meta, down, up)


def unpack_body(meta, got_ref, out_ref, up_ref):
    count, _, size, _ = got_ref.shape
    for block in range(count):
        here = slice(block * size, (block + 1) * size)
        out_ref[:, here, :] = got_ref[block, 0:5]
        up_ref[:, here, :] = got_ref[block, 5:8]


def unpack_maps(meta, got, after):
    count, mats, size, shard = got.shape
    rank = count * size
    if size % 16:
        maps = jnp.transpose(got, (1, 0, 2, 3)).reshape(mats, rank, shard)
        return maps[:5], maps[5:]
    return kernel_call(
        unpack_body, "unpack_maps", (1,),
        [whole(got.shape)], [whole((5, rank, shard)), whole((3, rank, shard))],
        [sds((5, rank, shard), BF), sds((3, rank, shard), BF)],
        vmem=58,
        after=after,
    )(meta, got)


def side_sum(refs):
    one_ref, two_ref, out_ref = refs
    out_ref[...] = (one_ref[...].astype(F32) + two_ref[...].astype(F32)).astype(BF)


def ffn_body(unit, meta, x_ref, gain_ref, up_ref, down_ref, *refs):
    if unit == 0:
        mine_ref, sib_ref, low_ref, part_ref = refs
    else:
        one_ref, two_ref, mine_ref, sib_ref, sum_ref, low_ref, part_ref = refs
    step = pl.program_id(0)

    @pl.when(step == 0)
    def _():
        hat = normalize(x_ref[...].astype(F32))
        low_ref[...] = (hat * gain_ref[1:2, :]).astype(BF)
        part_ref[...] = jnp.zeros_like(part_ref)
        if unit:
            side_sum((one_ref, two_ref, sum_ref))

    hidden = dot_nn(low_ref[...], up_ref[...])
    hidden = 0.5 * hidden * (1.0 + lax.erf(hidden * (0.5**0.5)))
    part_ref[...] += dot_nn(hidden.astype(BF), down_ref[...])

    @pl.when(step == pl.num_programs(0) - 1)
    def _():
        core = core_of(meta)
        mine_ref[...] = part_ref[columns(core, BLOCK), :].astype(BF)
        sib_ref[...] = part_ref[columns(1 - core, BLOCK), :].astype(BF)


def ffn(meta, unit, x, gains, w_up, w_down, sums=(), after=()):
    rows, width = x.shape
    chunk = 512
    half = sds((BLOCK, width), BF)
    results = 2 + len(sums) // 2
    return kernel_call(
        partial(ffn_body, unit),
        f"ffn_{unit}",
        (w_up.shape[1] // chunk,),
        [
            pl.BlockSpec((UNIT, width), lambda i, m: (unit, 0)),
            whole(gains.shape),
            pl.BlockSpec((width, chunk), lambda i, m: (0, i)),
            pl.BlockSpec((chunk, width), lambda i, m: (i, 0)),
        ]
        + [whole((BLOCK, width))] * len(sums),
        [whole((BLOCK, width))] * results,
        [half] * results,
        [pltpu.VMEM((UNIT, width), BF), pltpu.VMEM((UNIT, width), F32)],
        flops=4 * UNIT * width * w_up.shape[1],
        moved=4 * w_up.size + 8 * UNIT * width,
        vmem=58,
        after=after,
    )(meta, x, gains, w_up, w_down, *sums)


def qkv_body(meta, x_ref, gain_ref, w_ref, low_ref, out_ref):
    hat = normalize(x_ref[...].astype(F32))
    low = (hat * gain_ref[0:1, :]).astype(BF)
    low_ref[...] = low
    shard = w_ref.shape[2]
    for k in range(3):
        out_ref[:, k * shard : (k + 1) * shard] = dot_nn(low, w_ref[k]).astype(BF)


def frozen_qkv(meta, x, gains, w_qkv, after=()):
    rows, width = x.shape
    out = 3 * w_qkv.shape[2]
    return kernel_call(
        qkv_body,
        "frozen_qkv",
        (rows // UNIT,),
        [
            pl.BlockSpec((UNIT, width), lambda i, m: (i, 0)),
            whole(gains.shape),
            whole(w_qkv.shape),
        ],
        [
            pl.BlockSpec((UNIT, width), lambda i, m: (i, 0)),
            pl.BlockSpec((UNIT, out), lambda i, m: (i, 0)),
        ],
        [sds((rows, width), BF), sds((rows, out), BF)],
        flops=2 * rows * width * out,
        moved=2 * w_qkv.size + 4 * x.size + 4 * rows * out,
        vmem=58,
        after=after,
    )(meta, x, gains, w_qkv)


def rotary_tables(rows, shard):
    half = ROT // 2
    freq = np.exp(np.arange(half) * (-2.0 * math.log(10000.0) / ROT))
    angles = np.arange(rows)[:, None] * freq[None, :]
    cos, sin = np.cos(angles), np.sin(angles)
    one = np.ones((rows, HEAD))
    one[:, :half] = cos
    one[:, half:ROT] = cos
    up = np.zeros((rows, HEAD))
    up[:, half:ROT] = sin
    down = np.zeros((rows, HEAD))
    down[:, :half] = sin
    heads = min(shard, 128) // HEAD
    return [jnp.asarray(np.tile(table, (1, heads)), F32) for table in (one, up, down)]


def across(table, width):
    return jnp.concatenate([table] * (width // table.shape[1]), axis=1)


def turn(rows, cos, up, down, sign):
    half = ROT // 2
    width = rows.shape[1]
    from_low = pltpu.roll(rows, half, 1)
    from_high = pltpu.roll(rows, width - half, 1)
    cos, up, down = (across(table, width) for table in (cos, up, down))
    return rows * cos + sign * (from_low * up - from_high * down)


def project_unit(
    meta, low_ref, qkv_ref, cos_ref, up_ref, down_ref, maps, ups, q_ref, k_ref, v_ref, rank_ref
):
    proj = meta[PROJ]
    shard = q_ref.shape[1]
    rank = ups.shape[1]
    total = None
    for rel, piece in enumerate(maps):
        low = low_ref[:, columns(proj ^ rel, shard)]
        part = dot_nt(low, piece[2:5].reshape(3 * rank, shard))
        total = part if total is None else total + part
    rank_in = total.astype(BF)
    rank_ref[...] = rank_in
    pre = [
        qkv_ref[:, k * shard : (k + 1) * shard].astype(F32)
        + ADAPTER_SCALE * dot_nn(rank_in[:, k * rank : (k + 1) * rank], ups[k])
        for k in range(3)
    ]
    tables = (cos_ref[...], up_ref[...], down_ref[...])
    q_ref[...] = turn(pre[0], *tables, 1.0).astype(BF)
    k_ref[...] = turn(pre[1], *tables, 1.0).astype(BF)
    v_ref[...] = pre[2].astype(BF)


def vocab_chunks(vocab):
    return [(start, min(CHUNK_V, vocab - start)) for start in range(0, vocab, CHUNK_V)]


def for_chunks(vocab, first, last, together, run):
    whole_chunks = min(last, vocab // CHUNK_V)
    steps = (whole_chunks - first) // together

    def several(step, carry):
        for k in range(together):
            place = first + step * together + k
            run(place, pl.multiple_of(place * CHUNK_V, CHUNK_V), CHUNK_V)
        return carry

    if steps > 1:
        lax.fori_loop(0, steps, several, 0)
        first += steps * together
    for place in range(first, last):
        run(place, place * CHUNK_V, min(CHUNK_V, vocab - place * CHUNK_V))


def table_loads(table_ref, dest_ref, sem, first, groups):
    loads = {}
    for index, group in enumerate(groups):
        start = first * CHUNK_V
        stop = min(start + group * CHUNK_V, table_ref.shape[0])
        here = pl.ds(start, stop - start)
        loads[start] = pltpu.make_async_copy(table_ref.at[here], dest_ref.at[here], sem.at[index])
        first += group
    return loads


def vocab_buffers(vocab, width):
    return [
        pltpu.VMEM((vocab, width), BF),
        pltpu.VMEM((len(vocab_chunks(vocab)), UNIT, CHUNK_V), BF),
    ]


def head_mask(shard, head):
    return lax.broadcasted_iota(jnp.int32, (1, shard), 1) // HEAD == head


def diagonal():
    rows = lax.broadcasted_iota(jnp.int32, (BLOCK, BLOCK), 0)
    cols = lax.broadcasted_iota(jnp.int32, (BLOCK, BLOCK), 1)
    return rows >= cols


def block_scores(query, k_ref, prev, causal):
    scale = HEAD**-0.5
    diag = dot_nt(query, k_ref[prev : prev + BLOCK, :]) * scale
    diag = jnp.where(causal, diag, -1e30)
    if prev == 0:
        return diag
    return jnp.concatenate([dot_nt(query, k_ref[0:prev, :]) * scale, diag], axis=1)


def attend_unit(unit, meta, q_ref, k_ref, v_ref, mine_ref, sib_ref, lse_ref):
    shard = q_ref.shape[1]
    causal = diagonal()
    lane = lax.broadcasted_iota(jnp.int32, (BLOCK, 128), 1)
    for half in range(UNIT // BLOCK):
        prev = unit * UNIT + half * BLOCK
        query = q_ref[half * BLOCK : (half + 1) * BLOCK, :]
        out = jnp.zeros((BLOCK, shard), F32)
        lse = jnp.zeros((BLOCK, 128), F32)
        for head in range(shard // HEAD):
            mask = head_mask(shard, head)
            scores = block_scores(jnp.where(mask, query, 0), k_ref, prev, causal)
            top = jnp.max(scores, axis=1, keepdims=True)
            prob = jnp.exp(scores - top)
            total = jnp.sum(prob, axis=1, keepdims=True)
            got = dot_nn(prob.astype(BF), v_ref[0 : prev + BLOCK, :]) / total
            out = jnp.where(mask, got, out)
            lse = jnp.where(lane == head, top + jnp.log(total), lse)
        lse_ref[half * BLOCK : (half + 1) * BLOCK, :] = lse
        low = out.astype(BF)

        @pl.when(core_of(meta) == half)
        def _():
            mine_ref[...] = low

        @pl.when(core_of(meta) != half)
        def _():
            sib_ref[...] = low


def attend_first_body(
    meta, low_ref, qkv_ref, cos_ref, up_ref, down_ref, m0, m1, m2, m3, ups, one_ref, two_ref,
    w0, w1, w2, w3,
    q_ref, k_ref, v_ref, rank_ref, mine_ref, sib_ref, lse_ref, sum_ref, wo_ref, _u, _p, sem,
):
    shard = w0.shape[0]
    loads = [
        pltpu.make_async_copy(piece, wo_ref.at[pl.ds(rel * shard, shard)], sem.at[rel])
        for rel, piece in enumerate((w0, w1, w2, w3))
    ]
    for load in loads:
        load.start()
    side_sum((one_ref, two_ref, sum_ref))
    project_unit(
        meta, low_ref, qkv_ref, cos_ref, up_ref, down_ref, (m0, m1, m2, m3), ups,
        q_ref, k_ref, v_ref, rank_ref,
    )
    attend_unit(0, meta, q_ref, k_ref, v_ref, mine_ref, sib_ref, lse_ref)
    for load in loads:
        load.wait()


def attend_second_body(
    meta, _wo, _u, _p, _wo_out, held_ref, _p_out,
    low_ref, qkv_ref, cos_ref, up_ref, down_ref, m0, m1, m2, m3, ups, k_past, v_past, table_ref,
    q_ref, k_ref, v_ref, rank_ref, mine_ref, sib_ref, lse_ref, keys_ref, values_ref, sem,
):
    loads = list(table_loads(table_ref, held_ref, sem, 0, FIRST_GROUPS).values())
    for load in loads:
        load.start()
    project_unit(
        meta, low_ref, qkv_ref, cos_ref, up_ref, down_ref, (m0, m1, m2, m3), ups,
        q_ref, k_ref, v_ref, rank_ref,
    )
    for past, new, every in ((k_past, k_ref, keys_ref), (v_past, v_ref, values_ref)):
        every[0:UNIT, :] = past[...]
        every[UNIT:, :] = new[...]
    attend_unit(1, meta, q_ref, keys_ref, values_ref, mine_ref, sib_ref, lse_ref)
    for load in loads:
        load.wait()


def attend(meta, unit, low, qkv, tables, maps, ups, table, sums=(), wo=(), past=(), keep=()):
    rows, width = low.shape
    shard = qkv.shape[1] // 3
    rank = ups.shape[1]
    anywhere = pl.BlockSpec(memory_space=pl.ANY)
    block = lambda cols: pl.BlockSpec((UNIT, cols), lambda i, m: (unit, 0))
    in_specs = (
        [block(width), block(3 * shard)]
        + [block(tables[0].shape[1])] * 3
        + [whole(one.shape) for one in (*maps, ups)]
    )
    out_specs = [whole((UNIT, shard))] * 3 + [whole((UNIT, 3 * rank))]
    out_specs += [whole((BLOCK, shard))] * 2 + [whole((UNIT, 128))]
    out_shape = [sds((UNIT, shard), BF)] * 3 + [sds((UNIT, 3 * rank), BF)]
    out_shape += [sds((BLOCK, shard), BF)] * 2 + [sds((UNIT, 128), F32)]
    if unit == 0:
        body = attend_first_body
        args = (*sums, *wo)
        in_specs += [whole(one.shape) for one in sums] + [anywhere] * 4
        out_specs += [whole((BLOCK, width))] + [anywhere] * 3
        out_shape += [sds((BLOCK, width), BF), pltpu.VMEM((4 * shard, width), BF)]
        out_shape += vocab_buffers(*table.shape)
        scratch = [pltpu.SemaphoreType.DMA((4,))]
    else:
        body = attend_second_body
        args = (*past, table)
        in_specs += [whole((UNIT, shard))] * 2 + [anywhere]
        scratch = [pltpu.VMEM((rows, shard), BF)] * 2
        scratch += [pltpu.SemaphoreType.DMA((len(FIRST_GROUPS),))]
    return kernel_call(
        body, f"attend_{unit}", (1,), in_specs, out_specs, out_shape, scratch,
        keep=keep, use_keep=unit == 1,
    )(meta, low, qkv, *tables, *maps, ups, *args)


def place_grads(meta, pieces, grad_ref):
    core, ybit = core_of(meta), ybit_of(meta)
    for rel, piece in enumerate(pieces):
        place = (core ^ (rel & 1)) * 2 + (ybit ^ (rel >> 1))
        grad_ref[columns(place, BLOCK // 2), :] = piece[...]


def attend_back_unit(unit, grad_ref, q_ref, k_ref, v_ref, lse_ref, tables, dk_ref, dv_ref):
    shard = q_ref.shape[1]
    causal = diagonal()
    lane = lax.broadcasted_iota(jnp.int32, (BLOCK, 128), 1)
    scale = HEAD**-0.5
    dqs = []
    for half in range(UNIT // BLOCK):
        prev = unit * UNIT + half * BLOCK
        known = prev + BLOCK
        here = slice(half * BLOCK, (half + 1) * BLOCK)
        query = q_ref[here, :]
        grad = grad_ref[here, :]
        lse = lse_ref[here, :]
        dq = jnp.zeros((BLOCK, shard), F32)
        for head in range(shard // HEAD):
            mask = head_mask(shard, head)
            own_q = jnp.where(mask, query, 0)
            own_g = jnp.where(mask, grad, 0)
            own_lse = jnp.sum(jnp.where(lane == head, lse, 0.0), axis=1, keepdims=True)
            prob = jnp.exp(block_scores(own_q, k_ref, prev, causal) - own_lse)
            dweights = dot_nt(own_g, v_ref[0:known, :])
            delta = jnp.sum(prob * dweights, axis=1, keepdims=True)
            dscores = (prob * (dweights - delta)).astype(BF)
            dq = dq + jnp.where(mask, dot_nn(dscores, k_ref[0:known, :]), 0.0)
            dk_ref[0:known, :] += dot_tn(dscores, own_q) * scale
            dv_ref[0:known, :] += dot_tn(prob.astype(BF), own_g)
        rows = slice(prev, known)
        dq = turn(dq * scale, *(one[rows, :] for one in tables), -1.0)
        dqs.append(dq.astype(BF))
    return dqs


def attend_back_first_body(
    meta, g0, g1, g2, g3, q_ref, lse_ref, cos_ref, up_ref, down_ref, k_ref, v_ref,
    dq_ref, dk_ref, dv_ref, grad_ref,
):
    dk_ref[...] = jnp.zeros_like(dk_ref)
    dv_ref[...] = jnp.zeros_like(dv_ref)
    place_grads(meta, (g0, g1, g2, g3), grad_ref)
    dqs = attend_back_unit(
        0, grad_ref, q_ref, k_ref, v_ref, lse_ref, (cos_ref, up_ref, down_ref), dk_ref, dv_ref
    )
    dq_ref[...] = jnp.concatenate(dqs, axis=0)


def attend_back_first(meta, rows, grads, query, lse, tables, known, after, keep):
    shard = query.shape[1]
    args = (*grads, query, lse, *tables, *known)
    sums = (rows, shard)
    return kernel_call(
        attend_back_first_body, "attend_back_0", (1,),
        [whole(one.shape) for one in args],
        [whole((UNIT, shard)), whole(sums), whole(sums)],
        [sds((UNIT, shard), BF), sds(sums, F32), sds(sums, F32)],
        [pltpu.VMEM((UNIT, shard), BF)],
        after=after,
        keep=keep,
    )(meta, *args)


def attend_back_second_body(
    meta, g0, g1, g2, g3, q_ref, lse_ref, cos_ref, up_ref, down_ref, k0, v0, k1, v1,
    dk_in, dv_in, pair_ref, got_ref, dq0, rank0, rank1, ups, low_ref,
    own_ref, far_ref, keep_ref, send_ref, up_grad_ref,
    grad_ref, k_ref, v_ref, dk_ref, dv_ref, drank_ref,
):
    own_ref[...] = pair_ref[0].astype(F32) + got_ref[0].astype(F32)
    far_ref[...] = (pair_ref[1].astype(F32) + got_ref[1].astype(F32)).astype(BF)
    for first, second, every in ((k0, k1, k_ref), (v0, v1, v_ref)):
        every[0:UNIT, :] = first[...]
        every[UNIT:, :] = second[...]
    dk_ref[...] = dk_in[...]
    dv_ref[...] = dv_in[...]
    place_grads(meta, (g0, g1, g2, g3), grad_ref)
    tables = (cos_ref, up_ref, down_ref)
    dqs = attend_back_unit(1, grad_ref, q_ref, k_ref, v_ref, lse_ref, tables, dk_ref, dv_ref)
    proj = meta[PROJ]
    rank, shard = ups.shape[1:]
    dk = turn(dk_ref[...], *(one[...] for one in tables), -1.0).astype(BF)
    dpre = [jnp.concatenate([dq0[...], *dqs], axis=0), dk, dv_ref[...].astype(BF)]
    rank_in = jnp.concatenate([rank0[...], rank1[...]], axis=0)
    for k in range(3):
        here = slice(k * rank, (k + 1) * rank)
        up_grad_ref[k] = ADAPTER_SCALE * dot_tn(rank_in[:, here], dpre[k])
        drank_ref[:, here] = (ADAPTER_SCALE * dot_nt(dpre[k], ups[k])).astype(BF)
    drank = drank_ref[...]
    for rel in range(4):
        grad = dot_tn(drank, low_ref[:, columns(proj ^ rel, shard)])
        dest = (keep_ref, send_ref)[rel & 1]
        dest[rel >> 1] = grad.reshape(3, rank, shard).astype(BF)


def attend_back_second(meta, grads, query, lse, tables, known, sums, pair, dq0, rank_in, ups, low):
    rows, shard = sums[0].shape
    rank = ups.shape[1]
    args = (*grads, query, lse, *tables, *known, *sums, *pair, dq0, *rank_in, ups, low)
    out_shape = [
        sds((2, rank, shard), F32), sds((2, rank, shard), BF),
        sds((2, 3, rank, shard), BF), sds((2, 3, rank, shard), BF), sds((3, rank, shard), F32),
    ]
    return kernel_call(
        attend_back_second_body, "attend_back_1", (1,),
        [whole(one.shape) for one in args],
        [whole(one.shape) for one in out_shape],
        out_shape,
        [pltpu.VMEM((UNIT, shard), BF)]
        + [pltpu.VMEM((rows, shard), BF)] * 2
        + [pltpu.VMEM((rows, shard), F32)] * 2
        + [pltpu.VMEM((rows, 3 * rank), BF)],
        vmem=40,
    )(meta, *args)


def mix_body(
    meta, wo_ref, _u, _p, _wo, _u_out, _p_out, x_ref, gain_ref, f_own, f_far, a0, a1, a2, a3,
    m0, m1, m2, m3, norm_ref, res_ref, rank_ref, keep_ref,
):
    proj = meta[PROJ]
    shard = a0.shape[1]
    rank = None
    for a_ref, m_ref in ((a0, m0), (a1, m1), (a2, m2), (a3, m3)):
        part = dot_nt(a_ref[...], m_ref[0])
        rank = part if rank is None else rank + part
    rank = rank.astype(BF)
    total = x_ref[...].astype(F32) + f_own[...].astype(F32) + f_far[...].astype(F32)
    for rel, a_ref in enumerate((a0, a1, a2, a3)):
        total = total + dot_nn(a_ref[...], wo_ref[rel * shard : (rel + 1) * shard, :])
    keep_ref[...] = total
    for rel, m_ref in enumerate((m0, m1, m2, m3)):
        here = columns(proj ^ rel, shard)
        keep_ref[:, here] += ADAPTER_SCALE * dot_nn(rank, m_ref[1])
    residual = keep_ref[...]
    norm_ref[...] = (normalize(residual) * gain_ref[2:3, :]).astype(BF)
    mine = columns(ybit_of(meta), BLOCK // 2)
    res_ref[...] = keep_ref[mine, :]
    keep_ref[:, 0 : rank.shape[1]] = rank.astype(F32)
    rank_ref[...] = keep_ref[mine, 0 : rank.shape[1]].astype(BF)


def mix(meta, unit, x, gains, f_own, f_far, att, maps, keep, after=()):
    rows, width = x.shape
    shard = att[0].shape[1]
    rank = maps[0].shape[1]
    return kernel_call(
        mix_body,
        f"mix_{unit}",
        (1,),
        [
            pl.BlockSpec((BLOCK, width), lambda i, m: (2 * unit + core_of(m), 0)),
            whole(gains.shape),
            whole((BLOCK, width)),
            whole((BLOCK, width)),
        ]
        + [whole(one.shape) for one in att]
        + [whole((2, rank, shard))] * 4,
        [whole((BLOCK, width)), whole((BLOCK // 2, width)), whole((BLOCK // 2, rank))],
        [sds((BLOCK, width), BF), sds((BLOCK // 2, width), F32), sds((BLOCK // 2, rank), BF)],
        [pltpu.VMEM((BLOCK, width), F32)],
        after=after,
        keep=keep,
        use_keep=True,
    )(meta, x, gains, f_own, f_far, *att, *maps)


def local_columns(unit, meta, vocab, target_ref, out_ref):
    for group in range(4):
        half = core_of(meta) ^ (group >> 1)
        ids = target_ref[pl.ds((unit * 2 + half) * 2 + (group & 1), 1), :] - meta[PROJ] * vocab
        ids = jnp.where((ids >= 0) & (ids < vocab), ids, -1)
        square = jnp.transpose(jnp.broadcast_to(ids.astype(F32), (128, 128)))
        out_ref[group * 128 : (group + 1) * 128, :] = square.astype(jnp.int32)


def vocab_stats_body(unit, meta, _wo, _u, _p, _wo_out, u_ref, p_ref, *refs):
    vocab = u_ref.shape[0]
    chunks = vocab_chunks(vocab)
    if unit == 0:
        mine_ref, sib_ref, target_ref, table_ref, top_ref, st_ref, col_ref, acc_ref, sem = refs
        loads = table_loads(table_ref, u_ref, sem, sum(FIRST_GROUPS), SECOND_GROUPS)
    else:
        mine_ref, sib_ref, target_ref, top_ref, st_ref, col_ref, acc_ref = refs
        loads = {}
    for load in loads.values():
        load.start()
    acc_ref[...] = jnp.zeros_like(acc_ref)
    local_columns(unit, meta, vocab, target_ref, col_ref)
    lane = lax.broadcasted_iota(jnp.int32, (BLOCK, 128), 1)

    def chunk(place, start, size):
        col = lax.broadcasted_iota(jnp.int32, (BLOCK, size), 1)
        for half, rows_ref in enumerate((mine_ref, sib_ref)):
            here = slice(half * BLOCK, (half + 1) * BLOCK)
            logits = dot_nt(rows_ref[...], u_ref[pl.ds(start, size), :])
            top = jnp.max(logits, axis=1, keepdims=True)
            prob = jnp.exp(logits - top)
            total = jnp.sum(prob, axis=1, keepdims=True)
            hit = col == col_ref[here, 0:1] - start
            picked = jnp.sum(jnp.where(hit, logits, 0.0), axis=1, keepdims=True)
            p_ref[place, here, 0:size] = prob.astype(BF)
            acc = acc_ref[here, :]
            acc = jnp.where(lane == place, top, acc)
            acc = jnp.where(lane == place + 32, total, acc)
            acc_ref[here, :] = jnp.where(lane == 64, acc + picked, acc)

    if unit == 0:
        for_chunks(vocab, 0, sum(FIRST_GROUPS), TOGETHER_V, chunk)
        for load in loads.values():
            load.wait()
        for_chunks(vocab, sum(FIRST_GROUPS), len(chunks), TOGETHER_V, chunk)
    else:
        for_chunks(vocab, 0, len(chunks), len(chunks), chunk)
    acc = acc_ref[...]
    lane = lax.broadcasted_iota(jnp.int32, acc.shape, 1)
    top_ref[...] = acc
    tops = jnp.where(lane < len(chunks), acc, -1e30)
    best = jnp.max(tops, axis=1, keepdims=True)
    totals = pltpu.roll(acc, 128 - 32, 1)
    total = jnp.sum(
        jnp.where(lane < len(chunks), totals * jnp.exp(tops - best), 0.0), axis=1, keepdims=True
    )
    picked = jnp.sum(jnp.where(lane == 64, acc, 0.0), axis=1, keepdims=True)
    pair = jnp.where(lane == 0, best + jnp.log(total), jnp.where(lane == 1, picked, 0.0))
    st_ref[...] = jnp.transpose(pair)[0:8, :]


def vocab_stats(meta, unit, mine, sib, targets, table, keep, after=()):
    rows = 2 * BLOCK
    first = unit == 0
    return kernel_call(
        partial(vocab_stats_body, unit),
        f"vocab_stats_{unit}",
        (),
        [IN_VMEM] * 3 + [pl.BlockSpec(memory_space=pl.ANY)] * first,
        [IN_VMEM] * 3,
        [sds((rows, 128), F32), sds((8, rows), F32), sds((rows, 128), jnp.int32)],
        [pltpu.VMEM((rows, 128), F32)]
        + [pltpu.SemaphoreType.DMA((len(SECOND_GROUPS),))] * first,
        after=after,
        keep=keep,
        use_keep=True,
    )(meta, mine, sib, targets, *((table,) * first))


def swap_halves(pair):
    return jnp.concatenate([pair[:, BLOCK:], pair[:, :BLOCK]], axis=1)


def vocab_back_body(
    unit, meta, _wo, u_ref, p_ref, _wo_out, _u, _p, lens_ref, col_ref, top_ref, s0, s1, s2, s3,
    *refs,
):
    *outs, loss_ref, scale_ref, acc_ref = refs
    vocab = u_ref.shape[0]
    chunks = vocab_chunks(vocab)
    rows = 2 * BLOCK
    acc_ref[...] = jnp.zeros_like(acc_ref)
    parts = [s0[...], swap_halves(s1[...]), s2[...], swap_halves(s3[...])]
    lses = [part[0:1, :] for part in parts]
    best = jnp.maximum(jnp.maximum(lses[0], lses[1]), jnp.maximum(lses[2], lses[3]))
    total = sum(jnp.exp(one - best) for one in lses)
    log_norm = best + jnp.log(total)
    picked = sum(part[1:2, :] for part in parts)
    place = lax.broadcasted_iota(jnp.int32, (1, rows), 1)
    core = core_of(meta)
    offset = jnp.where(place < BLOCK, core * BLOCK, (1 - core) * BLOCK - BLOCK)
    valid = (unit * UNIT + place + offset < lens_ref[meta[SEQ]]).astype(F32)
    loss_ref[...] = jnp.broadcast_to(
        jnp.sum((log_norm - picked) * valid, axis=1, keepdims=True), (8, 128)
    )
    weight = valid / token_count(lens_ref)
    row = lax.broadcasted_iota(jnp.int32, (128, rows), 0)
    lines = jnp.where(row == 0, log_norm, 0.0)
    lines = jnp.where(row == 1, weight, lines)
    lines = jnp.where(row == 2, (jnp.exp(picked - log_norm) - 1.0) * weight, lines)
    cols = jnp.transpose(lines)
    lane = lax.broadcasted_iota(jnp.int32, (rows, 128), 1)
    take = lambda k: jnp.sum(jnp.where(lane == k, cols, 0.0), axis=1, keepdims=True)
    tops = jnp.where(lane < len(chunks), top_ref[...], -1e30)
    scales = jnp.exp(tops - take(0)) * take(1)
    scale_ref[...] = jnp.where(lane == 64, take(2), scales)

    lane = lax.broadcasted_iota(jnp.int32, (BLOCK, 128), 1)
    for place, (start, size) in enumerate(chunks):
        col = lax.broadcasted_iota(jnp.int32, (BLOCK, size), 1)
        for half in range(2):
            here = slice(half * BLOCK, (half + 1) * BLOCK)
            scales = scale_ref[here, :]
            at_hit = jnp.sum(jnp.where(lane == 64, scales, 0.0), axis=1, keepdims=True)
            scale = jnp.sum(jnp.where(lane == place, scales, 0.0), axis=1, keepdims=True)
            hit = col == col_ref[here, 0:1] - start
            grad = jnp.where(hit, at_hit, p_ref[place, here, 0:size].astype(F32) * scale)
            acc_ref[here, :] += dot_nn(grad.astype(BF), u_ref[start : start + size, :])

    if unit == 1:
        outs[0][...] = acc_ref[0:BLOCK, :].astype(BF)
        outs[1][...] = acc_ref[BLOCK:, :].astype(BF)
        return
    quarter = BLOCK // 2
    for rel, out_ref in enumerate(outs):
        place = (rel & 1) * 2 + (ybit_of(meta) ^ (rel >> 1))
        out_ref[...] = acc_ref[columns(place, quarter), :].astype(BF)


def vocab_back(meta, unit, lens, cols, tops, stats, keep, after=()):
    width = keep[1].shape[1]
    rows = 2 * BLOCK
    outs = [sds((BLOCK, width), BF)] * 2 if unit else [sds((BLOCK // 2, width), BF)] * 4
    return kernel_call(
        partial(vocab_back_body, unit),
        f"vocab_back_{unit}",
        (),
        [SCALARS] + [IN_VMEM] * 6,
        [IN_VMEM] * (len(outs) + 1),
        outs + [sds((8, 128), F32)],
        [
            pltpu.VMEM((rows, 128), F32),
            pltpu.VMEM((rows, width), F32),
        ],
        after=after,
        keep=keep,
        use_keep=True,
    )(meta, lens, cols, tops, *stats)


def split_body(meta, own_ref, got_ref, keep_ref, send_ref, sum_ref):
    sum_ref[...] = own_ref[...].astype(F32) + got_ref[...].astype(F32)
    ybit = ybit_of(meta)
    keep_ref[...] = sum_ref[columns(ybit, BLOCK // 2), :]
    send_ref[...] = sum_ref[columns(1 - ybit, BLOCK // 2), :].astype(BF)


def split_sum(meta, own, got, keep):
    rows, width = own.shape
    quarter = (rows // 2, width)
    return kernel_call(
        split_body, "split_sum", (1,),
        [whole(own.shape), whole(got.shape)],
        [whole(quarter)] * 2,
        [sds(quarter, F32), sds(quarter, BF)],
        [pltpu.VMEM((rows, width), F32)],
        keep=keep,
    )(meta, own, got)


def norm_back_body(last, meta, wo_ref, *refs):
    refs = refs[1:] if last else refs[5:]
    count = 2 if last else 4
    parts, refs = refs[:count], refs[count:]
    (res_ref, gain_ref, rank_ref), atts, maps = refs[:3], refs[3:7], refs[7:11]
    if last:
        before_ref, *outs, keep_ref, send_ref, hold_ref = refs[11:]
    else:
        *outs, sum_ref, hold_ref = refs[11:]
    proj = meta[PROJ]
    shard = atts[0].shape[1]
    dnormed = sum(part[...].astype(F32) for part in parts)
    residual = res_ref[...]
    center = residual - jnp.mean(residual, axis=-1, keepdims=True)
    spread = jnp.mean(center * center, axis=-1, keepdims=True)
    inv = lax.rsqrt(spread + EPS_NORM)
    hat = center * inv
    dhat = dnormed * gain_ref[2:3, :]
    dres = inv * (
        dhat
        - jnp.mean(dhat, axis=-1, keepdims=True)
        - hat * jnp.mean(dhat * hat, axis=-1, keepdims=True)
    )
    hold_ref[...] = dres.astype(BF)
    dbranch = hold_ref[...]
    drank = None
    for rel, m_ref in enumerate(maps):
        part = dot_nt(hold_ref[:, columns(proj ^ rel, shard)], m_ref[1])
        drank = part if drank is None else drank + part
    drank = (ADAPTER_SCALE * drank).astype(BF)
    for rel in range(4):
        w_piece = wo_ref[rel * shard : (rel + 1) * shard, :]
        datt = dot_nt(dbranch, w_piece) + dot_nn(drank, maps[rel][0])
        outs[rel][...] = datt.astype(BF)
        g_down = dot_tn(drank, atts[rel][...])
        g_up = ADAPTER_SCALE * dot_tn(rank_ref[...], hold_ref[:, columns(proj ^ rel, shard)])
        if last:
            dest = (keep_ref, send_ref)[rel & 1]
            dest[rel >> 1, 0] = (before_ref[rel, 0] + g_down).astype(BF)
            dest[rel >> 1, 1] = (before_ref[rel, 1] + g_up).astype(BF)
        else:
            sum_ref[rel, 0] = g_down
            sum_ref[rel, 1] = g_up


def norm_back(
    meta, unit, last, parts, residual, gains, rank_out, att, maps, before, keep, after=()
):
    quarter, width = residual.shape
    shard = att[0].shape[1]
    rank = rank_out.shape[1]
    piece = (quarter, shard)
    if last:
        more = [sds((2, 2, rank, shard), BF)] * 2
    else:
        more = [sds((4, 2, rank, shard), F32)]
    return kernel_call(
        partial(norm_back_body, last),
        f"norm_back_{unit}",
        (1,),
        [whole(one.shape) for one in parts]
        + [whole(residual.shape), whole(gains.shape), whole(rank_out.shape)]
        + [pl.BlockSpec(piece, lambda i, m: (ybit_of(m), 0))] * 4
        + [whole((2, rank, shard))] * 4
        + [whole(one.shape) for one in before],
        [whole(piece)] * 4 + [whole(one.shape) for one in more],
        [sds(piece, BF)] * 4 + more,
        [pltpu.VMEM((quarter, width), BF)],
        after=after,
        keep=keep,
        use_keep=True,
    )(meta, *parts, residual, gains, rank_out, *att, *maps, *before)


def signs(row_ids, col_ids, seed):
    hashed = row_ids * 1640531527 + col_ids * 747796405 + seed * 277803737
    hashed = hashed ^ hashed >> 15 & 131071
    hashed = hashed * 2024237689
    hashed = hashed ^ hashed >> 13 & 524287
    return 1.0 - 2.0 * (hashed >> 17 & 1).astype(F32)


def sketch_one(meta, seed, grad, sketch):
    rank, shard = grad.shape
    left_rows = lax.broadcasted_iota(jnp.int32, (sketch, shard), 1) + meta[PROJ] * shard
    left_cols = lax.broadcasted_iota(jnp.int32, (sketch, shard), 0)
    right_rows = lax.broadcasted_iota(jnp.int32, (rank, sketch), 0)
    right_cols = lax.broadcasted_iota(jnp.int32, (rank, sketch), 1)
    left = signs(left_rows, left_cols, 2 * seed).astype(BF)
    right = signs(right_rows, right_cols, 2 * seed + 1)
    return jnp.dot(dot_nt(left, grad), right, precision=lax.Precision.HIGHEST)


def local_sketch_body(meta, seeds_ref, lens_ref, own_ref, far_ref, up_ref, block_ref, full_ref):
    size = block_ref.shape[2]
    count = token_count(lens_ref)
    out = own_ref[...] + far_ref[...].astype(F32)
    for place, grad in enumerate((out[0], up_ref[0], up_ref[1], up_ref[2], out[1])):
        for dest in range(block_ref.shape[0]):
            block_ref[dest, place] = grad[dest * size : (dest + 1) * size].astype(BF)
        full_ref[place] = count * sketch_one(
            meta, seeds_ref[3 + place], grad.astype(BF), full_ref.shape[1]
        )


def local_sketch(meta, seeds, lens, own, far, ups, sketch_width):
    _, rank, shard = own.shape
    count = lens.shape[0]
    blocks = (count, 5, rank // count, shard)
    full = (5, sketch_width, sketch_width)
    return kernel_call(
        local_sketch_body, "local_sketch", (1,),
        [SCALARS, SCALARS, whole(own.shape), whole(far.shape), whole(ups.shape)],
        [whole(blocks), whole(full)],
        [sds(blocks, BF), sds(full, F32)],
        flops=10 * rank * shard * sketch_width,
        moved=16 * own.size,
    )(meta, seeds, lens, own, far, ups)


def gather_body(meta, keep_ref, got_ref, far_ref, five_ref, block_ref, grad_ref):
    size = block_ref.shape[2]
    total = keep_ref[0].astype(F32) + got_ref[0].astype(F32) + far_ref[...].astype(F32)
    grad_ref[...] = total.astype(BF)
    for dest in range(block_ref.shape[0]):
        for mat in range(3):
            block_ref[dest, mat] = total[mat, dest * size : (dest + 1) * size].astype(BF)
        block_ref[dest, 3:8] = five_ref[dest]


def gather_blocks(meta, keep, got, far, five):
    count, _, size, shard = five.shape
    blocks = (count, 8, size, shard)
    pair = pl.BlockSpec((1, *keep.shape[1:]), lambda i, m: (0, 0, 0, 0))
    return kernel_call(
        gather_body, "gather_blocks", (1,),
        [pair, pair, whole(far.shape), whole(five.shape)],
        [whole(blocks), whole(far.shape)],
        [sds(blocks, BF), sds(far.shape, BF)],
    )(meta, keep, got, far, five)


def sketch_body(meta, seeds_ref, lens_ref, grad_ref, five_ref, f0, f1, f2, f3, full_ref):
    count = token_count(lens_ref)
    sketch = full_ref.shape[1]
    full_ref[3:8] = five_ref[...]
    for mat in range(3):
        full_ref[mat] = count * sketch_one(meta, seeds_ref[mat], grad_ref[mat], sketch)
    size = sketch // 4
    for rel, out_ref in enumerate((f0, f1, f2, f3)):
        out_ref[...] = full_ref[:, columns(meta[PROJ] ^ rel, size), :]


def sketch(meta, seeds, lens, grads, five):
    sketch_width = five.shape[1]
    piece = (8, sketch_width // 4, sketch_width)
    return kernel_call(
        sketch_body, "sketch", (1,),
        [SCALARS, SCALARS, whole(grads.shape), whole(five.shape)],
        [whole(piece)] * 4,
        [sds(piece, F32)] * 4,
        [pltpu.VMEM((8, sketch_width, sketch_width), F32)],
        flops=2 * grads.size * sketch_width,
        moved=2 * grads.size,
    )(meta, seeds, lens, grads, five)


def lane_value(row, lane, place):
    return jnp.sum(jnp.where(lane == place, row, 0.0), axis=1, keepdims=True)


def tally_body(
    units, meta, got_ref, target_ref, f0, f1, f2, f3, *refs
):
    losses, (total_ref, line_ref) = refs[:units], refs[units:]
    total = jnp.sum(got_ref[...].astype(F32), axis=0)
    total_ref[...] = total
    features = f0[...] + f1[...] + f2[...] + f3[...]
    squares = jnp.sum(total * total)
    own = jnp.sum(features * features)
    loss = sum(jnp.sum(one[0:1, 0:1]) for one in losses)
    loss = jnp.where(meta[PROJ] == 0, loss, 0.0)
    lane = lax.broadcasted_iota(jnp.int32, (1, 128), 1)
    line = jnp.where(lane == 0, squares, 0.0)
    line = jnp.where(lane == 1, loss, line)
    line = jnp.where(lane == 2, own, line)
    checkpoints = target_ref.shape[0]
    for c in range(checkpoints):
        theirs = target_ref[c]
        line = jnp.where(lane == 3 + c, jnp.sum(features * theirs), line)
        line = jnp.where(lane == 3 + checkpoints + c, jnp.sum(theirs * theirs), line)
    line_ref[...] = jnp.broadcast_to(line, line_ref.shape)


def tally(meta, devices, got, targets, pieces, losses):
    _, mats, slice_rank, shard = got.shape
    args = (got, targets, *pieces, *losses)
    return kernel_call(
        partial(tally_body, len(losses)),
        "tally",
        (1,),
        [whole(one.shape) for one in args],
        [whole((mats, slice_rank, shard)), whole((devices, 128))],
        [sds((mats, slice_rank, shard), F32), sds((devices, 128), F32)],
    )(meta, *args)


def optimizer_step(weight, grad_in, first_in, second_in, clipping_scale):
    grad_clip = grad_in * clipping_scale
    first_new = BETA_ONE * first_in + (1.0 - BETA_ONE) * grad_clip
    second_new = BETA_TWO * second_in + (1.0 - BETA_TWO) * grad_clip * grad_clip
    first_hat = first_new / (1.0 - BETA_ONE**STEP)
    second_hat = second_new / (1.0 - BETA_TWO**STEP)
    new_weight = weight - LEARN_RATE * (
        first_hat / (jnp.sqrt(second_hat) + ADAM_EPS) + WEIGHT_DECAY * weight
    )
    return (new_weight, first_new, second_new)


def finish_body(
    proj_count, checkpoints, meta, lens_ref, lines_ref, total_ref,
    dw, uw, dm, um, ds, us,
    loss_out, norm_out, influence_out, dw_out, uw_out, dm_out, um_out, ds_out, us_out,
):
    lines = lines_ref[...]
    everyone = jnp.sum(lines, axis=0, keepdims=True)
    row = lax.broadcasted_iota(jnp.int32, lines.shape, 0)
    ours = jnp.sum(
        jnp.where(row // proj_count == meta[SEQ], lines, 0.0), axis=0, keepdims=True
    )
    lane = lax.broadcasted_iota(jnp.int32, (1, 128), 1)
    grad_norm = jnp.sqrt(lane_value(everyone, lane, 0))
    own = lane_value(ours, lane, 2)
    influence = jnp.zeros((1, 1), F32)
    for c in range(checkpoints):
        dot = lane_value(ours, lane, 3 + c)
        theirs = lane_value(ours, lane, 3 + checkpoints + c)
        influence += (1.0 - c / checkpoints) * dot * lax.rsqrt(own * theirs + 1e-12)
    loss_out[0] = jnp.sum(lane_value(everyone, lane, 1))
    loss_out[1] = token_count(lens_ref)
    norm_out[0] = jnp.sum(grad_norm)
    influence_out[0] = jnp.sum(influence)
    clip = jnp.minimum(1.0, CLIP_NORM / (grad_norm + 1e-06))
    half = total_ref.shape[0] // 2
    for base, ins, outs in (
        (0, (dw, dm, ds), (dw_out, dm_out, ds_out)),
        (half, (uw, um, us), (uw_out, um_out, us_out)),
    ):
        for k in range(half):
            new = optimizer_step(
                ins[0][k], total_ref[base + k], ins[1][k], ins[2][k], clip
            )
            for out, value in zip(outs, new):
                out[k] = value


def finish(meta, proj_count, checkpoints, lens, lines, total, params):
    block = whole(params[0].shape)
    return kernel_call(
        partial(finish_body, proj_count, checkpoints),
        "finish",
        (1,),
        [SCALARS, whole(lines.shape), whole(total.shape)] + [block] * 6,
        [SCALARS] * 3 + [block] * 6,
        [sds((2,), F32), sds((1,), F32), sds((1,), F32)] + [sds(params[0].shape, F32)] * 6,
        flops=20 * total.size,
        moved=28 * total.size,
    )(meta, lens, lines, total, *params)


def to_partner(array, axis, size, offset):
    return lax.ppermute(array, axis, [(i, i ^ offset) for i in range(size)])


def on_device(
    seq_count,
    proj_count,
    inputs,
    targets,
    lengths,
    norm_gain_vectors,
    query_key_value_weight,
    attention_output_weight,
    feedforward_input_weight,
    feedforward_output_weight,
    unembed,
    adapter_down_maps,
    adapter_up_maps,
    down_first_moment,
    up_first_moment,
    down_second_moment,
    up_second_moment,
    target_gradient_sketches,
    seeds,
):
    rows, width = inputs.shape
    shard = attention_output_weight.shape[0]
    vocab_local = unembed.shape[1]
    slice_rank = adapter_up_maps.shape[1]
    rank = slice_rank * seq_count
    sketch_width = target_gradient_sketches.shape[3]
    proj = lax.axis_index("proj")
    seq = lax.axis_index("dp")

    over_proj = lambda array, rel: to_partner(array, "proj", proj_count, rel)
    over_seq = lambda array, rel: to_partner(array, "dp", seq_count, rel)

    meta = jnp.stack([proj, seq]).astype(jnp.int32)
    targets = targets.reshape(rows // 128, 128)
    table = jnp.transpose(unembed)
    tables = rotary_tables(rows, shard)
    transposed = lambda array: jnp.transpose(array, (0, 2, 1))

    def from_all(array):
        y = over_proj(array, 2)
        return (array, over_proj(array, 1), y, over_proj(y, 1))

    def exchange(*pieces):
        return [pieces[0]] + [over_proj(pieces[rel], rel) for rel in (1, 2, 3)]

    packed = pack_maps(meta, seq_count, transposed(adapter_down_maps), adapter_up_maps)
    arrived = lax.all_to_all(packed, "dp", split_axis=0, concat_axis=0, tiled=True)
    wo = from_all(attention_output_weight)

    w_ffn = (feedforward_input_weight, feedforward_output_weight)
    f0_mine, f0_sib = ffn(meta, 0, inputs, norm_gain_vectors, *w_ffn)
    low, qkv = frozen_qkv(
        meta, inputs, norm_gain_vectors, jnp.transpose(query_key_value_weight, (1, 0, 2)),
        (f0_mine,),
    )
    maps, ups = unpack_maps(meta, arrived, (low,))
    maps = from_all(maps)
    f1_mine, f1_sib, f0_chip = ffn(
        meta, 1, inputs, norm_gain_vectors, *w_ffn, (f0_mine, over_proj(f0_sib, 1)), (maps[0],)
    )
    q0, k0, v0, rank_in0, mine, sib, lse0, f1_chip, *keep = attend(
        meta, 0, low, qkv, tables, maps, ups, table, (f1_mine, over_proj(f1_sib, 1)), wo
    )
    att0 = exchange(mine, sib, mine, sib)
    q1, k1, v1, rank_in1, mine, sib, lse1, *keep = attend(
        meta, 1, low, qkv, tables, maps, ups, table, past=(k0, v0), keep=keep
    )
    att1 = exchange(mine, sib, mine, sib)
    f_chip = (f0_chip, f1_chip)
    f_far = [over_proj(one, 2) for one in f_chip]

    def mix_unit(unit, att, keep, after):
        normed, residual, rank_out, *keep = mix(
            meta, unit, inputs, norm_gain_vectors, f_chip[unit], f_far[unit], att, maps, keep, after
        )
        return (normed, over_proj(normed, 1)), residual, rank_out, keep

    def stats_unit(unit, normed, keep, after=()):
        top, stat, cols, *keep = vocab_stats(meta, unit, *normed, targets, table, keep, after)
        return (cols, top), exchange(stat, stat, stat, stat), keep

    def back_unit(unit, top, stats, keep, after):
        results = vocab_back(meta, unit, lengths, *top, stats, keep, after)
        return results[:-4], results[-4], results[-3:]

    def norm_unit(unit, parts, residual, rank_out, att, before, keep, after):
        d0, d1, d2, d3, *more = norm_back(
            meta, unit, unit == 1, parts, residual, norm_gain_vectors,
            rank_out, att, maps, before, keep, after,
        )
        grads = more[: 1 + unit]
        return exchange(d0, d1, d2, d3), grads, more[1 + unit :]

    normed0, residual0, rank0, keep = mix_unit(0, att0, keep, (lse1,))
    top0, stats0, keep = stats_unit(0, normed0, keep)
    normed1, residual1, rank1, keep = mix_unit(1, att1, keep, (stats0[0],))
    dnormed0, loss0, keep = back_unit(0, top0, stats0, keep, (rank1,))
    dnormed0 = exchange(*dnormed0)
    top1, stats1, keep = stats_unit(1, normed1, keep, (loss0,))
    datt0, out_grads, keep = norm_unit(
        0, dnormed0, residual0, rank0, att0, (), keep, (stats1[0],)
    )
    (d_mine, d_sib), loss1, keep = back_unit(1, top1, stats1, keep, (datt0[0],))
    d_keep, d_send, *keep = split_sum(meta, d_mine, over_proj(d_sib, 1), keep[:1])
    dnormed1 = (d_keep, over_proj(d_send, 2))
    dq0, dk, dv, *keep = attend_back_first(
        meta, rows, datt0, q0, lse0, tables, (k0, v0), (d_keep,), keep
    )
    datt1, (out_keep, out_send), _ = norm_unit(
        1, dnormed1, residual1, rank1, att1, out_grads, keep, (dq0,)
    )
    out_own, out_far, in_keep, in_send, up_grads = attend_back_second(
        meta, datt1, q1, lse1, tables, (k0, v0, k1, v1), (dk, dv),
        (out_keep, over_proj(out_send, 1)), dq0, (rank_in0, rank_in1), ups, low,
    )
    out_far = over_proj(out_far, 2)
    in_got = over_proj(in_send, 1)
    in_far = over_proj((in_keep[1].astype(F32) + in_got[1].astype(F32)).astype(BF), 2)
    blocks, five = local_sketch(meta, seeds, lengths, out_own, out_far, up_grads, sketch_width)
    blocks, in_grads = gather_blocks(meta, in_keep, in_got, in_far, blocks)
    arrived = lax.all_to_all(blocks, "dp", split_axis=0, concat_axis=0, tiled=True)
    pieces = exchange(*sketch(meta, seeds, lengths, in_grads, five))

    device_count = seq_count * proj_count
    total, lines = tally(
        meta, device_count, arrived, target_gradient_sketches, pieces, (loss0, loss1)
    )
    lines = lax.all_to_all(lines, ("dp", "proj"), split_axis=0, concat_axis=0, tiled=True)
    params = (
        transposed(adapter_down_maps),
        adapter_up_maps,
        transposed(down_first_moment),
        up_first_moment,
        transposed(down_second_moment),
        up_second_moment,
    )
    loss_parts, grad_norm, influence, dw, uw, dm, um, ds, us = finish(
        meta, proj_count, target_gradient_sketches.shape[0], lengths, lines, total, params
    )
    return (
        loss_parts,
        grad_norm,
        influence,
        transposed(dw),
        uw,
        transposed(dm),
        um,
        transposed(ds),
        us,
    )


def solution(mesh):
    in_specs = (
        P("dp", None),
        P("dp"),
        P(),
        P(),
        P(None, None, "proj"),
        P("proj", None),
        P(None, "proj"),
        P("proj", None),
        P(None, "proj"),
        P(None, "proj", "dp"),
        P(None, "dp", "proj"),
        P(None, "proj", "dp"),
        P(None, "dp", "proj"),
        P(None, "proj", "dp"),
        P(None, "dp", "proj"),
        P(None, None, "proj", None),
        P(),
    )
    out_specs = (
        P(),
        P(),
        P("dp"),
        P(None, "proj", "dp"),
        P(None, "dp", "proj"),
        P(None, "proj", "dp"),
        P(None, "dp", "proj"),
        P(None, "proj", "dp"),
        P(None, "dp", "proj"),
    )
    return jax.shard_map(
        partial(on_device, mesh.shape["dp"], mesh.shape["proj"]),
        mesh=mesh,
        in_specs=in_specs,
        out_specs=out_specs,
        check_vma=False,
    )
```

```python
from functools import partial
import math

import jax
import jax.numpy as jnp
import numpy as np
from jax import lax
from jax.experimental import pallas as pl
from jax.experimental.pallas import tpu as pltpu
from jax.sharding import PartitionSpec as P

HEAD = 64
ROT = 16
STEP = 10

EPS_NORM = 1e-05
ADAPTER_SCALE = 0.25
CLIP_NORM = 0.05
LEARN_RATE = 0.05
BETA_ONE = 0.9
BETA_TWO = 0.99
ADAM_EPS = 1e-08
WEIGHT_DECAY = 0.01

BF = jnp.bfloat16
F32 = jnp.float32
BLOCK = 256
UNIT = 512
FIRST_GROUPS = (4, 4, 4, 3)
SECOND_GROUPS = (5, 5)
TOGETHER_V = 5
CHUNK_V = 512
MIB = 2**20

PROJ, SEQ = range(2)


def core_of(meta):
    return meta[PROJ] & 1


def ybit_of(meta):
    return meta[PROJ] >> 1


def token_count(lens_ref):
    return sum(lens_ref[i] for i in range(lens_ref.shape[0])).astype(F32)


def dot_nn(lhs, rhs):
    return lax.dot_general(lhs, rhs, (((1,), (0,)), ((), ())), preferred_element_type=F32)


def dot_nt(lhs, rhs):
    return lax.dot_general(lhs, rhs, (((1,), (1,)), ((), ())), preferred_element_type=F32)


def dot_tn(lhs, rhs):
    return lax.dot_general(lhs, rhs, (((0,), (0,)), ((), ())), preferred_element_type=F32)


def kernel_call(
    body, name, grid, in_specs, out_specs, out_shape, scratch=(), flops=0, moved=0, after=(),
    vmem=20, keep=(), use_keep=False,
):
    single = not isinstance(out_shape, (list, tuple))
    if single:
        out_specs, out_shape = [out_specs], [out_shape]
    first_keep = 1 + len(in_specs) + len(after)
    first_out = first_keep + len(keep)
    first_kept = first_out + len(out_shape)
    first_scratch = first_kept + len(keep)

    def run(*refs):
        kept = refs[first_keep:first_out] + refs[first_kept:first_scratch]
        body(
            refs[0],
            *(kept if use_keep else ()),
            *refs[1 : 1 + len(in_specs)],
            *refs[first_out:first_kept],
            *refs[first_scratch:],
        )

    anywhere = pl.BlockSpec(memory_space=pl.ANY)
    keep_spec = IN_VMEM if use_keep else anywhere
    call = pl.pallas_call(
        run,
        grid_spec=pltpu.PrefetchScalarGridSpec(
            num_scalar_prefetch=1,
            grid=grid,
            in_specs=list(in_specs) + [anywhere] * len(after) + [keep_spec] * len(keep),
            out_specs=list(out_specs) + [keep_spec] * len(keep),
            scratch_shapes=list(scratch),
        ),
        out_shape=list(out_shape) + [pltpu.VMEM(one.shape, one.dtype) for one in keep],
        input_output_aliases={
            first_keep + i: len(out_shape) + i for i in range(len(keep))
        },
        compiler_params=pltpu.CompilerParams(vmem_limit_bytes=vmem * MIB),
        cost_estimate=pl.CostEstimate(flops=10**12, bytes_accessed=1000, transcendentals=0),
        name=name,
    )

    def apply(*args):
        results = call(*args, *after, *[held(one) for one in keep])
        return results[0] if single else results

    return apply


def whole(shape):
    zeros = (0,) * len(shape)
    return pl.BlockSpec(shape, lambda *_: zeros)


SCALARS = pl.BlockSpec(memory_space=pltpu.SMEM)
IN_VMEM = pl.BlockSpec(memory_space=pltpu.VMEM)


def held(array):
    return pltpu.with_memory_space_constraint(array, pltpu.VMEM)


def sds(shape, dtype):
    return jax.ShapeDtypeStruct(shape, dtype)


def normalize(rows):
    center = rows - jnp.mean(rows, axis=-1, keepdims=True)
    spread = jnp.mean(center * center, axis=-1, keepdims=True)
    return center * lax.rsqrt(spread + EPS_NORM)


def columns(index, size):
    return pl.ds(pl.multiple_of(index * size, size), size)


def pack_body(meta, down_ref, up_ref, out_ref):
    mats = down_ref.shape[0]
    down, up = down_ref[...].astype(BF), up_ref[...].astype(BF)
    for dest in range(out_ref.shape[0]):
        out_ref[dest, 0] = down[mats - 1]
        out_ref[dest, 1] = up[mats - 1]
        out_ref[dest, 2 : mats + 1] = down[: mats - 1]
        out_ref[dest, mats + 1 :] = up[: mats - 1]


def pack_maps(meta, seq_count, down, up):
    shape = (seq_count, 2 * down.shape[0], *down.shape[1:])
    return kernel_call(
        pack_body, "pack_maps", (1,),
        [whole(down.shape), whole(up.shape)], whole(shape), sds(shape, BF),
        vmem=58,
    )(meta, down, up)


def unpack_body(meta, got_ref, out_ref, up_ref):
    count, _, size, _ = got_ref.shape
    for block in range(count):
        here = slice(block * size, (block + 1) * size)
        out_ref[:, here, :] = got_ref[block, 0:5]
        up_ref[:, here, :] = got_ref[block, 5:8]


def unpack_maps(meta, got, after):
    count, mats, size, shard = got.shape
    rank = count * size
    if size % 16:
        maps = jnp.transpose(got, (1, 0, 2, 3)).reshape(mats, rank, shard)
        return maps[:5], maps[5:]
    return kernel_call(
        unpack_body, "unpack_maps", (1,),
        [whole(got.shape)], [whole((5, rank, shard)), whole((3, rank, shard))],
        [sds((5, rank, shard), BF), sds((3, rank, shard), BF)],
        vmem=58,
        after=after,
    )(meta, got)


def side_sum(refs):
    one_ref, two_ref, out_ref = refs
    out_ref[...] = (one_ref[...].astype(F32) + two_ref[...].astype(F32)).astype(BF)


def ffn_chunk(low, up_ref, down_ref):
    hidden = dot_nn(low, up_ref[...])
    hidden = 0.5 * hidden * (1.0 + lax.erf(hidden * (0.5**0.5)))
    return dot_nn(hidden.astype(BF), down_ref[...])


def store_halves(meta, part_ref, mine_ref, sib_ref):
    core = core_of(meta)
    mine_ref[...] = part_ref[columns(core, BLOCK), :].astype(BF)
    sib_ref[...] = part_ref[columns(1 - core, BLOCK), :].astype(BF)


def front_body(
    chunks, meta, x_ref, gain_ref, up_ref, down_ref, w_ref,
    mine_ref, sib_ref, low_ref, out_ref, mlp_ref, part_ref,
):
    step = pl.program_id(0)

    @pl.when(step == 0)
    def _():
        mlp_ref[...] = (normalize(x_ref[...].astype(F32)) * gain_ref[1:2, :]).astype(BF)
        part_ref[...] = jnp.zeros_like(part_ref)

    @pl.when(step < chunks)
    def _():
        part_ref[...] += ffn_chunk(mlp_ref[...], up_ref, down_ref)

    @pl.when(step == chunks - 1)
    def _():
        store_halves(meta, part_ref, mine_ref, sib_ref)

    @pl.when(step >= chunks)
    def _():
        low = (normalize(x_ref[...].astype(F32)) * gain_ref[0:1, :]).astype(BF)
        low_ref[...] = low
        shard = w_ref.shape[2]
        for k in range(3):
            out_ref[:, k * shard : (k + 1) * shard] = dot_nn(low, w_ref[k])


def front(meta, x, gains, w_up, w_down, w_qkv):
    rows, width = x.shape
    out = 3 * w_qkv.shape[2]
    chunk = 512
    chunks = w_up.shape[1] // chunk
    units = rows // UNIT
    late = lambda i: jnp.maximum(i - chunks, 0)
    early = lambda i: jnp.minimum(i, chunks - 1)
    half = sds((BLOCK, width), BF)
    return kernel_call(
        partial(front_body, chunks),
        "front",
        (chunks + units,),
        [
            pl.BlockSpec((UNIT, width), lambda i, m: (late(i), 0)),
            whole(gains.shape),
            pl.BlockSpec((width, chunk), lambda i, m: (0, early(i))),
            pl.BlockSpec((chunk, width), lambda i, m: (early(i), 0)),
            whole(w_qkv.shape),
        ],
        [whole((BLOCK, width))] * 2
        + [
            pl.BlockSpec((UNIT, width), lambda i, m: (late(i), 0)),
            pl.BlockSpec((UNIT, out), lambda i, m: (late(i), 0)),
        ],
        [half, half, sds((rows, width), BF), sds((rows, out), F32)],
        [pltpu.VMEM((UNIT, width), BF), pltpu.VMEM((UNIT, width), F32)],
        vmem=58,
    )(meta, x, gains, w_up, w_down, w_qkv)


def ffn_body(
    meta, x_ref, gain_ref, up_ref, down_ref, one_ref, two_ref,
    mine_ref, sib_ref, sum_ref, low_ref, part_ref,
):
    step = pl.program_id(0)

    @pl.when(step == 0)
    def _():
        low_ref[...] = (normalize(x_ref[...].astype(F32)) * gain_ref[1:2, :]).astype(BF)
        part_ref[...] = jnp.zeros_like(part_ref)
        side_sum((one_ref, two_ref, sum_ref))

    part_ref[...] += ffn_chunk(low_ref[...], up_ref, down_ref)

    @pl.when(step == pl.num_programs(0) - 1)
    def _():
        store_halves(meta, part_ref, mine_ref, sib_ref)


def ffn(meta, unit, x, gains, w_up, w_down, sums, after=()):
    width = x.shape[1]
    chunk = 512
    half = sds((BLOCK, width), BF)
    return kernel_call(
        ffn_body,
        f"ffn_{unit}",
        (w_up.shape[1] // chunk,),
        [
            pl.BlockSpec((UNIT, width), lambda i, m: (unit, 0)),
            whole(gains.shape),
            pl.BlockSpec((width, chunk), lambda i, m: (0, i)),
            pl.BlockSpec((chunk, width), lambda i, m: (i, 0)),
        ]
        + [whole((BLOCK, width))] * len(sums),
        [whole((BLOCK, width))] * 3,
        [half] * 3,
        [pltpu.VMEM((UNIT, width), BF), pltpu.VMEM((UNIT, width), F32)],
        vmem=58,
        after=after,
    )(meta, x, gains, w_up, w_down, *sums)


def rotary_tables(rows, shard):
    half = ROT // 2
    freq = np.exp(np.arange(half) * (-2.0 * math.log(10000.0) / ROT))
    angles = np.arange(rows)[:, None] * freq[None, :]
    cos, sin = np.cos(angles), np.sin(angles)
    one = np.ones((rows, HEAD))
    one[:, :half] = cos
    one[:, half:ROT] = cos
    up = np.zeros((rows, HEAD))
    up[:, half:ROT] = sin
    down = np.zeros((rows, HEAD))
    down[:, :half] = sin
    heads = min(shard, 128) // HEAD
    return [jnp.asarray(np.tile(table, (1, heads)), F32) for table in (one, up, down)]


def across(table, width):
    return jnp.concatenate([table] * (width // table.shape[1]), axis=1)


def turn(rows, cos, up, down, sign):
    half = ROT // 2
    width = rows.shape[1]
    from_low = pltpu.roll(rows, half, 1)
    from_high = pltpu.roll(rows, width - half, 1)
    cos, up, down = (across(table, width) for table in (cos, up, down))
    return rows * cos + sign * (from_low * up - from_high * down)


def project_unit(
    meta, low_ref, qkv_ref, cos_ref, up_ref, down_ref, maps, ups, q_ref, k_ref, v_ref, rank_ref
):
    proj = meta[PROJ]
    shard = q_ref.shape[1]
    rank = ups.shape[1]
    total = None
    for rel, piece in enumerate(maps):
        low = low_ref[:, columns(proj ^ rel, shard)]
        part = dot_nt(low, piece[2:5].reshape(3 * rank, shard))
        total = part if total is None else total + part
    rank_in = total.astype(BF)
    rank_ref[...] = rank_in
    pre = [
        qkv_ref[:, k * shard : (k + 1) * shard]
        + ADAPTER_SCALE * dot_nn(rank_in[:, k * rank : (k + 1) * rank], ups[k])
        for k in range(3)
    ]
    tables = (cos_ref[...], up_ref[...], down_ref[...])
    q_ref[...] = turn(pre[0], *tables, 1.0).astype(BF)
    k_ref[...] = turn(pre[1], *tables, 1.0).astype(BF)
    v_ref[...] = pre[2].astype(BF)


def vocab_chunks(vocab):
    return [(start, min(CHUNK_V, vocab - start)) for start in range(0, vocab, CHUNK_V)]


def for_chunks(vocab, first, last, together, run):
    whole_chunks = min(last, vocab // CHUNK_V)
    steps = (whole_chunks - first) // together

    def several(step, carry):
        for k in range(together):
            place = first + step * together + k
            run(place, pl.multiple_of(place * CHUNK_V, CHUNK_V), CHUNK_V)
        return carry

    if steps > 1:
        lax.fori_loop(0, steps, several, 0)
        first += steps * together
    for place in range(first, last):
        run(place, place * CHUNK_V, min(CHUNK_V, vocab - place * CHUNK_V))


def table_loads(table_ref, dest_ref, sem, first, groups):
    loads = {}
    for index, group in enumerate(groups):
        start = first * CHUNK_V
        stop = min(start + group * CHUNK_V, table_ref.shape[0])
        here = pl.ds(start, stop - start)
        loads[start] = pltpu.make_async_copy(table_ref.at[here], dest_ref.at[here], sem.at[index])
        first += group
    return loads


def vocab_buffers(vocab, width):
    return [
        pltpu.VMEM((vocab, width), BF),
        pltpu.VMEM((len(vocab_chunks(vocab)), UNIT, CHUNK_V), BF),
    ]


def head_mask(shard, head):
    return lax.broadcasted_iota(jnp.int32, (1, shard), 1) // HEAD == head


def diagonal():
    rows = lax.broadcasted_iota(jnp.int32, (BLOCK, BLOCK), 0)
    cols = lax.broadcasted_iota(jnp.int32, (BLOCK, BLOCK), 1)
    return rows >= cols


def block_scores(query, k_ref, prev, causal):
    scale = HEAD**-0.5
    diag = dot_nt(query, k_ref[prev : prev + BLOCK, :]) * scale
    diag = jnp.where(causal, diag, -1e30)
    if prev == 0:
        return diag
    return jnp.concatenate([dot_nt(query, k_ref[0:prev, :]) * scale, diag], axis=1)


def attend_unit(unit, meta, q_ref, k_ref, v_ref, mine_ref, sib_ref, lse_ref):
    shard = q_ref.shape[1]
    causal = diagonal()
    lane = lax.broadcasted_iota(jnp.int32, (BLOCK, 128), 1)
    for half in range(UNIT // BLOCK):
        prev = unit * UNIT + half * BLOCK
        query = q_ref[half * BLOCK : (half + 1) * BLOCK, :]
        out = jnp.zeros((BLOCK, shard), F32)
        lse = jnp.zeros((BLOCK, 128), F32)
        for head in range(shard // HEAD):
            mask = head_mask(shard, head)
            scores = block_scores(jnp.where(mask, query, 0), k_ref, prev, causal)
            top = jnp.max(scores, axis=1, keepdims=True)
            prob = jnp.exp(scores - top)
            total = jnp.sum(prob, axis=1, keepdims=True)
            got = dot_nn(prob.astype(BF), v_ref[0 : prev + BLOCK, :]) / total
            out = jnp.where(mask, got, out)
            lse = jnp.where(lane == head, top + jnp.log(total), lse)
        lse_ref[half * BLOCK : (half + 1) * BLOCK, :] = lse
        low = out.astype(BF)

        @pl.when(core_of(meta) == half)
        def _():
            mine_ref[...] = low

        @pl.when(core_of(meta) != half)
        def _():
            sib_ref[...] = low


def attend_first_body(
    meta, low_ref, qkv_ref, cos_ref, up_ref, down_ref, m0, m1, m2, m3, ups, one_ref, two_ref,
    w0, w1, w2, w3,
    q_ref, k_ref, v_ref, rank_ref, mine_ref, sib_ref, lse_ref, sum_ref, wo_ref, _u, _p, sem,
):
    shard = w0.shape[0]
    loads = [
        pltpu.make_async_copy(piece, wo_ref.at[pl.ds(rel * shard, shard)], sem.at[rel])
        for rel, piece in enumerate((w0, w1, w2, w3))
    ]
    for load in loads:
        load.start()
    side_sum((one_ref, two_ref, sum_ref))
    project_unit(
        meta, low_ref, qkv_ref, cos_ref, up_ref, down_ref, (m0, m1, m2, m3), ups,
        q_ref, k_ref, v_ref, rank_ref,
    )
    attend_unit(0, meta, q_ref, k_ref, v_ref, mine_ref, sib_ref, lse_ref)
    for load in loads:
        load.wait()


def attend_second_body(
    meta, _wo, _u, _p, _wo_out, held_ref, _p_out,
    low_ref, qkv_ref, cos_ref, up_ref, down_ref, m0, m1, m2, m3, ups, k_past, v_past, table_ref,
    q_ref, k_ref, v_ref, rank_ref, mine_ref, sib_ref, lse_ref, keys_ref, values_ref, sem,
):
    loads = list(table_loads(table_ref, held_ref, sem, 0, FIRST_GROUPS).values())
    for load in loads:
        load.start()
    project_unit(
        meta, low_ref, qkv_ref, cos_ref, up_ref, down_ref, (m0, m1, m2, m3), ups,
        q_ref, k_ref, v_ref, rank_ref,
    )
    for past, new, every in ((k_past, k_ref, keys_ref), (v_past, v_ref, values_ref)):
        every[0:UNIT, :] = past[...]
        every[UNIT:, :] = new[...]
    attend_unit(1, meta, q_ref, keys_ref, values_ref, mine_ref, sib_ref, lse_ref)
    for load in loads:
        load.wait()


def attend(meta, unit, low, qkv, tables, maps, ups, table, sums=(), wo=(), past=(), keep=()):
    rows, width = low.shape
    shard = qkv.shape[1] // 3
    rank = ups.shape[1]
    anywhere = pl.BlockSpec(memory_space=pl.ANY)
    block = lambda cols: pl.BlockSpec((UNIT, cols), lambda i, m: (unit, 0))
    in_specs = (
        [block(width), block(3 * shard)]
        + [block(tables[0].shape[1])] * 3
        + [whole(one.shape) for one in (*maps, ups)]
    )
    out_specs = [whole((UNIT, shard))] * 3 + [whole((UNIT, 3 * rank))]
    out_specs += [whole((BLOCK, shard))] * 2 + [whole((UNIT, 128))]
    out_shape = [sds((UNIT, shard), BF)] * 3 + [sds((UNIT, 3 * rank), BF)]
    out_shape += [sds((BLOCK, shard), BF)] * 2 + [sds((UNIT, 128), F32)]
    if unit == 0:
        body = attend_first_body
        args = (*sums, *wo)
        in_specs += [whole(one.shape) for one in sums] + [anywhere] * 4
        out_specs += [whole((BLOCK, width))] + [anywhere] * 3
        out_shape += [sds((BLOCK, width), BF), pltpu.VMEM((4 * shard, width), BF)]
        out_shape += vocab_buffers(*table.shape)
        scratch = [pltpu.SemaphoreType.DMA((4,))]
    else:
        body = attend_second_body
        args = (*past, table)
        in_specs += [whole((UNIT, shard))] * 2 + [anywhere]
        scratch = [pltpu.VMEM((rows, shard), BF)] * 2
        scratch += [pltpu.SemaphoreType.DMA((len(FIRST_GROUPS),))]
    return kernel_call(
        body, f"attend_{unit}", (1,), in_specs, out_specs, out_shape, scratch,
        keep=keep, use_keep=unit == 1,
    )(meta, low, qkv, *tables, *maps, ups, *args)


def place_grads(meta, pieces, grad_ref):
    core, ybit = core_of(meta), ybit_of(meta)
    for rel, piece in enumerate(pieces):
        place = (core ^ (rel & 1)) * 2 + (ybit ^ (rel >> 1))
        grad_ref[columns(place, BLOCK // 2), :] = piece[...]


def attend_back_unit(unit, grad_ref, q_ref, k_ref, v_ref, lse_ref, tables, dk_ref, dv_ref):
    shard = q_ref.shape[1]
    causal = diagonal()
    lane = lax.broadcasted_iota(jnp.int32, (BLOCK, 128), 1)
    scale = HEAD**-0.5
    dqs = []
    for half in range(UNIT // BLOCK):
        prev = unit * UNIT + half * BLOCK
        known = prev + BLOCK
        here = slice(half * BLOCK, (half + 1) * BLOCK)
        query = q_ref[here, :]
        grad = grad_ref[here, :]
        lse = lse_ref[here, :]
        dq = jnp.zeros((BLOCK, shard), F32)
        for head in range(shard // HEAD):
            mask = head_mask(shard, head)
            own_q = jnp.where(mask, query, 0)
            own_g = jnp.where(mask, grad, 0)
            own_lse = jnp.sum(jnp.where(lane == head, lse, 0.0), axis=1, keepdims=True)
            prob = jnp.exp(block_scores(own_q, k_ref, prev, causal) - own_lse)
            dweights = dot_nt(own_g, v_ref[0:known, :])
            delta = jnp.sum(prob * dweights, axis=1, keepdims=True)
            dscores = (prob * (dweights - delta)).astype(BF)
            dq = dq + jnp.where(mask, dot_nn(dscores, k_ref[0:known, :]), 0.0)
            dk_ref[0:known, :] += dot_tn(dscores, own_q) * scale
            dv_ref[0:known, :] += dot_tn(prob.astype(BF), own_g)
        rows = slice(prev, known)
        dq = turn(dq * scale, *(one[rows, :] for one in tables), -1.0)
        dqs.append(dq.astype(BF))
    return dqs


def attend_back_first_body(
    meta, g0, g1, g2, g3, q_ref, lse_ref, cos_ref, up_ref, down_ref, k_ref, v_ref,
    dq_ref, dk_ref, dv_ref, grad_ref,
):
    dk_ref[...] = jnp.zeros_like(dk_ref)
    dv_ref[...] = jnp.zeros_like(dv_ref)
    place_grads(meta, (g0, g1, g2, g3), grad_ref)
    dqs = attend_back_unit(
        0, grad_ref, q_ref, k_ref, v_ref, lse_ref, (cos_ref, up_ref, down_ref), dk_ref, dv_ref
    )
    dq_ref[...] = jnp.concatenate(dqs, axis=0)


def attend_back_first(meta, rows, grads, query, lse, tables, known, after, keep):
    shard = query.shape[1]
    args = (*grads, query, lse, *tables, *known)
    sums = (rows, shard)
    return kernel_call(
        attend_back_first_body, "attend_back_0", (1,),
        [whole(one.shape) for one in args],
        [whole((UNIT, shard)), whole(sums), whole(sums)],
        [sds((UNIT, shard), BF), sds(sums, F32), sds(sums, F32)],
        [pltpu.VMEM((UNIT, shard), BF)],
        after=after,
        keep=keep,
    )(meta, *args)


def attend_back_second_body(
    meta, g0, g1, g2, g3, q_ref, lse_ref, cos_ref, up_ref, down_ref, k0, v0, k1, v1,
    dk_in, dv_in, pair_ref, got_ref, dq0, rank0, rank1, ups, low_ref,
    own_ref, far_ref, keep_ref, send_ref, up_grad_ref,
    grad_ref, k_ref, v_ref, dk_ref, dv_ref, drank_ref,
):
    own_ref[...] = pair_ref[0].astype(F32) + got_ref[0].astype(F32)
    far_ref[...] = (pair_ref[1].astype(F32) + got_ref[1].astype(F32)).astype(BF)
    for first, second, every in ((k0, k1, k_ref), (v0, v1, v_ref)):
        every[0:UNIT, :] = first[...]
        every[UNIT:, :] = second[...]
    dk_ref[...] = dk_in[...]
    dv_ref[...] = dv_in[...]
    place_grads(meta, (g0, g1, g2, g3), grad_ref)
    tables = (cos_ref, up_ref, down_ref)
    dqs = attend_back_unit(1, grad_ref, q_ref, k_ref, v_ref, lse_ref, tables, dk_ref, dv_ref)
    proj = meta[PROJ]
    rank, shard = ups.shape[1:]
    dk = turn(dk_ref[...], *(one[...] for one in tables), -1.0).astype(BF)
    dpre = [jnp.concatenate([dq0[...], *dqs], axis=0), dk, dv_ref[...].astype(BF)]
    rank_in = jnp.concatenate([rank0[...], rank1[...]], axis=0)
    for k in range(3):
        here = slice(k * rank, (k + 1) * rank)
        up_grad_ref[k] = ADAPTER_SCALE * dot_tn(rank_in[:, here], dpre[k])
        drank_ref[:, here] = (ADAPTER_SCALE * dot_nt(dpre[k], ups[k])).astype(BF)
    drank = drank_ref[...]
    for rel in range(4):
        grad = dot_tn(drank, low_ref[:, columns(proj ^ rel, shard)])
        dest = (keep_ref, send_ref)[rel & 1]
        dest[rel >> 1] = grad.reshape(3, rank, shard).astype(BF)


def attend_back_second(meta, grads, query, lse, tables, known, sums, pair, dq0, rank_in, ups, low):
    rows, shard = sums[0].shape
    rank = ups.shape[1]
    args = (*grads, query, lse, *tables, *known, *sums, *pair, dq0, *rank_in, ups, low)
    out_shape = [
        sds((2, rank, shard), F32), sds((2, rank, shard), BF),
        sds((2, 3, rank, shard), BF), sds((2, 3, rank, shard), BF), sds((3, rank, shard), F32),
    ]
    return kernel_call(
        attend_back_second_body, "attend_back_1", (1,),
        [whole(one.shape) for one in args],
        [whole(one.shape) for one in out_shape],
        out_shape,
        [pltpu.VMEM((UNIT, shard), BF)]
        + [pltpu.VMEM((rows, shard), BF)] * 2
        + [pltpu.VMEM((rows, shard), F32)] * 2
        + [pltpu.VMEM((rows, 3 * rank), BF)],
        vmem=40,
    )(meta, *args)


def mix_body(
    meta, wo_ref, _u, _p, _wo, _u_out, _p_out, x_ref, gain_ref, f_own, f_far, a0, a1, a2, a3,
    m0, m1, m2, m3, norm_ref, res_ref, rank_ref, keep_ref,
):
    proj = meta[PROJ]
    shard = a0.shape[1]
    rank = None
    for a_ref, m_ref in ((a0, m0), (a1, m1), (a2, m2), (a3, m3)):
        part = dot_nt(a_ref[...], m_ref[0])
        rank = part if rank is None else rank + part
    rank = rank.astype(BF)
    total = x_ref[...].astype(F32) + f_own[...].astype(F32) + f_far[...].astype(F32)
    for rel, a_ref in enumerate((a0, a1, a2, a3)):
        total = total + dot_nn(a_ref[...], wo_ref[rel * shard : (rel + 1) * shard, :])
    keep_ref[...] = total
    for rel, m_ref in enumerate((m0, m1, m2, m3)):
        here = columns(proj ^ rel, shard)
        keep_ref[:, here] += ADAPTER_SCALE * dot_nn(rank, m_ref[1])
    residual = keep_ref[...]
    norm_ref[...] = (normalize(residual) * gain_ref[2:3, :]).astype(BF)
    mine = columns(ybit_of(meta), BLOCK // 2)
    res_ref[...] = keep_ref[mine, :]
    keep_ref[:, 0 : rank.shape[1]] = rank.astype(F32)
    rank_ref[...] = keep_ref[mine, 0 : rank.shape[1]].astype(BF)


def mix(meta, unit, x, gains, f_own, f_far, att, maps, keep, after=()):
    rows, width = x.shape
    shard = att[0].shape[1]
    rank = maps[0].shape[1]
    return kernel_call(
        mix_body,
        f"mix_{unit}",
        (1,),
        [
            pl.BlockSpec((BLOCK, width), lambda i, m: (2 * unit + core_of(m), 0)),
            whole(gains.shape),
            whole((BLOCK, width)),
            whole((BLOCK, width)),
        ]
        + [whole(one.shape) for one in att]
        + [whole((2, rank, shard))] * 4,
        [whole((BLOCK, width)), whole((BLOCK // 2, width)), whole((BLOCK // 2, rank))],
        [sds((BLOCK, width), BF), sds((BLOCK // 2, width), F32), sds((BLOCK // 2, rank), BF)],
        [pltpu.VMEM((BLOCK, width), F32)],
        after=after,
        keep=keep,
        use_keep=True,
    )(meta, x, gains, f_own, f_far, *att, *maps)


def local_columns(unit, meta, vocab, target_ref, out_ref):
    for group in range(4):
        half = core_of(meta) ^ (group >> 1)
        ids = target_ref[pl.ds((unit * 2 + half) * 2 + (group & 1), 1), :] - meta[PROJ] * vocab
        ids = jnp.where((ids >= 0) & (ids < vocab), ids, -1)
        square = jnp.transpose(jnp.broadcast_to(ids.astype(F32), (128, 128)))
        out_ref[group * 128 : (group + 1) * 128, :] = square.astype(jnp.int32)


def vocab_stats_body(unit, meta, _wo, _u, _p, _wo_out, u_ref, p_ref, *refs):
    vocab = u_ref.shape[0]
    chunks = vocab_chunks(vocab)
    if unit == 0:
        mine_ref, sib_ref, target_ref, table_ref, top_ref, st_ref, col_ref, acc_ref, sem = refs
        loads = table_loads(table_ref, u_ref, sem, sum(FIRST_GROUPS), SECOND_GROUPS)
    else:
        mine_ref, sib_ref, target_ref, top_ref, st_ref, col_ref, acc_ref = refs
        loads = {}
    for load in loads.values():
        load.start()
    acc_ref[...] = jnp.zeros_like(acc_ref)
    local_columns(unit, meta, vocab, target_ref, col_ref)
    lane = lax.broadcasted_iota(jnp.int32, (BLOCK, 128), 1)

    def chunk(place, start, size):
        col = lax.broadcasted_iota(jnp.int32, (BLOCK, size), 1)
        for half, rows_ref in enumerate((mine_ref, sib_ref)):
            here = slice(half * BLOCK, (half + 1) * BLOCK)
            logits = dot_nt(rows_ref[...], u_ref[pl.ds(start, size), :])
            top = jnp.max(logits, axis=1, keepdims=True)
            prob = jnp.exp(logits - top)
            total = jnp.sum(prob, axis=1, keepdims=True)
            hit = col == col_ref[here, 0:1] - start
            picked = jnp.sum(jnp.where(hit, logits, 0.0), axis=1, keepdims=True)
            p_ref[place, here, 0:size] = prob.astype(BF)
            acc = acc_ref[here, :]
            acc = jnp.where(lane == place, top, acc)
            acc = jnp.where(lane == place + 32, total, acc)
            acc_ref[here, :] = jnp.where(lane == 64, acc + picked, acc)

    if unit == 0:
        for_chunks(vocab, 0, sum(FIRST_GROUPS), TOGETHER_V, chunk)
        for load in loads.values():
            load.wait()
        for_chunks(vocab, sum(FIRST_GROUPS), len(chunks), TOGETHER_V, chunk)
    else:
        for_chunks(vocab, 0, len(chunks), len(chunks), chunk)
    acc = acc_ref[...]
    lane = lax.broadcasted_iota(jnp.int32, acc.shape, 1)
    top_ref[...] = acc
    tops = jnp.where(lane < len(chunks), acc, -1e30)
    best = jnp.max(tops, axis=1, keepdims=True)
    totals = pltpu.roll(acc, 128 - 32, 1)
    total = jnp.sum(
        jnp.where(lane < len(chunks), totals * jnp.exp(tops - best), 0.0), axis=1, keepdims=True
    )
    picked = jnp.sum(jnp.where(lane == 64, acc, 0.0), axis=1, keepdims=True)
    pair = jnp.where(lane == 0, best + jnp.log(total), jnp.where(lane == 1, picked, 0.0))
    st_ref[...] = jnp.transpose(pair)[0:8, :]


def vocab_stats(meta, unit, mine, sib, targets, table, keep, after=()):
    rows = 2 * BLOCK
    first = unit == 0
    return kernel_call(
        partial(vocab_stats_body, unit),
        f"vocab_stats_{unit}",
        (),
        [IN_VMEM] * 3 + [pl.BlockSpec(memory_space=pl.ANY)] * first,
        [IN_VMEM] * 3,
        [sds((rows, 128), F32), sds((8, rows), F32), sds((rows, 128), jnp.int32)],
        [pltpu.VMEM((rows, 128), F32)]
        + [pltpu.SemaphoreType.DMA((len(SECOND_GROUPS),))] * first,
        after=after,
        keep=keep,
        use_keep=True,
    )(meta, mine, held(sib), targets, *((table,) * first))


def swap_halves(pair):
    return jnp.concatenate([pair[:, BLOCK:], pair[:, :BLOCK]], axis=1)


def vocab_back_body(
    unit, meta, _wo, u_ref, p_ref, _wo_out, _u, _p, lens_ref, col_ref, top_ref, s0, s1, s2, s3,
    *refs,
):
    *outs, loss_ref, scale_ref, acc_ref = refs
    vocab = u_ref.shape[0]
    chunks = vocab_chunks(vocab)
    rows = 2 * BLOCK
    acc_ref[...] = jnp.zeros_like(acc_ref)
    parts = [s0[...], swap_halves(s1[...]), s2[...], swap_halves(s3[...])]
    lses = [part[0:1, :] for part in parts]
    best = jnp.maximum(jnp.maximum(lses[0], lses[1]), jnp.maximum(lses[2], lses[3]))
    total = sum(jnp.exp(one - best) for one in lses)
    log_norm = best + jnp.log(total)
    picked = sum(part[1:2, :] for part in parts)
    place = lax.broadcasted_iota(jnp.int32, (1, rows), 1)
    core = core_of(meta)
    offset = jnp.where(place < BLOCK, core * BLOCK, (1 - core) * BLOCK - BLOCK)
    valid = (unit * UNIT + place + offset < lens_ref[meta[SEQ]]).astype(F32)
    loss_ref[...] = jnp.broadcast_to(
        jnp.sum((log_norm - picked) * valid, axis=1, keepdims=True), (8, 128)
    )
    weight = valid / token_count(lens_ref)
    row = lax.broadcasted_iota(jnp.int32, (128, rows), 0)
    lines = jnp.where(row == 0, log_norm, 0.0)
    lines = jnp.where(row == 1, weight, lines)
    lines = jnp.where(row == 2, (jnp.exp(picked - log_norm) - 1.0) * weight, lines)
    cols = jnp.transpose(lines)
    lane = lax.broadcasted_iota(jnp.int32, (rows, 128), 1)
    take = lambda k: jnp.sum(jnp.where(lane == k, cols, 0.0), axis=1, keepdims=True)
    tops = jnp.where(lane < len(chunks), top_ref[...], -1e30)
    scales = jnp.exp(tops - take(0)) * take(1)
    scale_ref[...] = jnp.where(lane == 64, take(2), scales)

    lane = lax.broadcasted_iota(jnp.int32, (BLOCK, 128), 1)
    for place, (start, size) in enumerate(chunks):
        col = lax.broadcasted_iota(jnp.int32, (BLOCK, size), 1)
        for half in range(2):
            here = slice(half * BLOCK, (half + 1) * BLOCK)
            scales = scale_ref[here, :]
            at_hit = jnp.sum(jnp.where(lane == 64, scales, 0.0), axis=1, keepdims=True)
            scale = jnp.sum(jnp.where(lane == place, scales, 0.0), axis=1, keepdims=True)
            hit = col == col_ref[here, 0:1] - start
            grad = jnp.where(hit, at_hit, p_ref[place, here, 0:size].astype(F32) * scale)
            acc_ref[here, :] += dot_nn(grad.astype(BF), u_ref[start : start + size, :])

    if unit == 1:
        outs[0][...] = acc_ref[0:BLOCK, :].astype(BF)
        outs[1][...] = acc_ref[BLOCK:, :].astype(BF)
        return
    quarter = BLOCK // 2
    for rel, out_ref in enumerate(outs):
        place = (rel & 1) * 2 + (ybit_of(meta) ^ (rel >> 1))
        out_ref[...] = acc_ref[columns(place, quarter), :].astype(BF)


def vocab_back(meta, unit, lens, cols, tops, stats, keep, after=()):
    width = keep[1].shape[1]
    rows = 2 * BLOCK
    outs = [sds((BLOCK, width), BF)] * 2 if unit else [sds((BLOCK // 2, width), BF)] * 4
    return kernel_call(
        partial(vocab_back_body, unit),
        f"vocab_back_{unit}",
        (),
        [SCALARS] + [IN_VMEM] * 6,
        [IN_VMEM] * (len(outs) + 1),
        outs + [sds((8, 128), F32)],
        [
            pltpu.VMEM((rows, 128), F32),
            pltpu.VMEM((rows, width), F32),
        ],
        after=after,
        keep=keep,
        use_keep=True,
    )(meta, lens, cols, tops, *stats)


def split_body(meta, own_ref, got_ref, keep_ref, send_ref, sum_ref):
    sum_ref[...] = own_ref[...].astype(F32) + got_ref[...].astype(F32)
    ybit = ybit_of(meta)
    keep_ref[...] = sum_ref[columns(ybit, BLOCK // 2), :]
    send_ref[...] = sum_ref[columns(1 - ybit, BLOCK // 2), :].astype(BF)


def split_sum(meta, own, got, keep):
    rows, width = own.shape
    quarter = (rows // 2, width)
    return kernel_call(
        split_body, "split_sum", (1,),
        [whole(own.shape), IN_VMEM],
        [whole(quarter)] * 2,
        [sds(quarter, F32), sds(quarter, BF)],
        [pltpu.VMEM((rows, width), F32)],
        keep=keep,
    )(meta, own, held(got))


def norm_back_body(last, meta, wo_ref, *refs):
    refs = refs[1:] if last else refs[5:]
    count = 2 if last else 4
    parts, refs = refs[:count], refs[count:]
    (res_ref, gain_ref, rank_ref), atts, maps = refs[:3], refs[3:7], refs[7:11]
    if last:
        before_ref, *outs, keep_ref, send_ref, hold_ref = refs[11:]
    else:
        *outs, sum_ref, hold_ref = refs[11:]
    proj = meta[PROJ]
    shard = atts[0].shape[1]
    dnormed = sum(part[...].astype(F32) for part in parts)
    residual = res_ref[...]
    center = residual - jnp.mean(residual, axis=-1, keepdims=True)
    spread = jnp.mean(center * center, axis=-1, keepdims=True)
    inv = lax.rsqrt(spread + EPS_NORM)
    hat = center * inv
    dhat = dnormed * gain_ref[2:3, :]
    dres = inv * (
        dhat
        - jnp.mean(dhat, axis=-1, keepdims=True)
        - hat * jnp.mean(dhat * hat, axis=-1, keepdims=True)
    )
    hold_ref[...] = dres.astype(BF)
    dbranch = hold_ref[...]
    drank = None
    for rel, m_ref in enumerate(maps):
        part = dot_nt(hold_ref[:, columns(proj ^ rel, shard)], m_ref[1])
        drank = part if drank is None else drank + part
    drank = (ADAPTER_SCALE * drank).astype(BF)
    for rel in range(4):
        w_piece = wo_ref[rel * shard : (rel + 1) * shard, :]
        datt = dot_nt(dbranch, w_piece) + dot_nn(drank, maps[rel][0])
        outs[rel][...] = datt.astype(BF)
        g_down = dot_tn(drank, atts[rel][...])
        g_up = ADAPTER_SCALE * dot_tn(rank_ref[...], hold_ref[:, columns(proj ^ rel, shard)])
        if last:
            dest = (keep_ref, send_ref)[rel & 1]
            dest[rel >> 1, 0] = (before_ref[rel, 0] + g_down).astype(BF)
            dest[rel >> 1, 1] = (before_ref[rel, 1] + g_up).astype(BF)
        else:
            sum_ref[rel, 0] = g_down
            sum_ref[rel, 1] = g_up


def norm_back(
    meta, unit, last, parts, residual, gains, rank_out, att, maps, before, keep, after=()
):
    quarter, width = residual.shape
    shard = att[0].shape[1]
    rank = rank_out.shape[1]
    piece = (quarter, shard)
    if last:
        more = [sds((2, 2, rank, shard), BF)] * 2
    else:
        more = [sds((4, 2, rank, shard), F32)]
    return kernel_call(
        partial(norm_back_body, last),
        f"norm_back_{unit}",
        (1,),
        [whole(one.shape) for one in parts]
        + [whole(residual.shape), whole(gains.shape), whole(rank_out.shape)]
        + [pl.BlockSpec(piece, lambda i, m: (ybit_of(m), 0))] * 4
        + [whole((2, rank, shard))] * 4
        + [whole(one.shape) for one in before],
        [whole(piece)] * 4 + [whole(one.shape) for one in more],
        [sds(piece, BF)] * 4 + more,
        [pltpu.VMEM((quarter, width), BF)],
        after=after,
        keep=keep,
        use_keep=True,
    )(meta, *parts, residual, gains, rank_out, *att, *maps, *before)


def signs(row_ids, col_ids, seed):
    hashed = row_ids * 1640531527 + col_ids * 747796405 + seed * 277803737
    hashed = hashed ^ hashed >> 15 & 131071
    hashed = hashed * 2024237689
    hashed = hashed ^ hashed >> 13 & 524287
    return 1.0 - 2.0 * (hashed >> 17 & 1).astype(F32)


def sketch_one(meta, seed, grad, sketch):
    rank, shard = grad.shape
    left_rows = lax.broadcasted_iota(jnp.int32, (sketch, shard), 1) + meta[PROJ] * shard
    left_cols = lax.broadcasted_iota(jnp.int32, (sketch, shard), 0)
    right_rows = lax.broadcasted_iota(jnp.int32, (rank, sketch), 0)
    right_cols = lax.broadcasted_iota(jnp.int32, (rank, sketch), 1)
    left = signs(left_rows, left_cols, 2 * seed).astype(BF)
    right = signs(right_rows, right_cols, 2 * seed + 1)
    return jnp.dot(dot_nt(left, grad), right, precision=lax.Precision.HIGHEST)


def local_sketch_body(meta, seeds_ref, lens_ref, own_ref, far_ref, up_ref, block_ref, full_ref):
    size = block_ref.shape[2]
    count = token_count(lens_ref)
    out = own_ref[...] + far_ref[...].astype(F32)
    for place, grad in enumerate((out[0], up_ref[0], up_ref[1], up_ref[2], out[1])):
        for dest in range(block_ref.shape[0]):
            block_ref[dest, place] = grad[dest * size : (dest + 1) * size].astype(BF)
        full_ref[place] = count * sketch_one(
            meta, seeds_ref[3 + place], grad.astype(BF), full_ref.shape[1]
        )


def local_sketch(meta, seeds, lens, own, far, ups, sketch_width):
    _, rank, shard = own.shape
    count = lens.shape[0]
    blocks = (count, 5, rank // count, shard)
    full = (5, sketch_width, sketch_width)
    return kernel_call(
        local_sketch_body, "local_sketch", (1,),
        [SCALARS, SCALARS, whole(own.shape), whole(far.shape), whole(ups.shape)],
        [whole(blocks), whole(full)],
        [sds(blocks, BF), sds(full, F32)],
        flops=10 * rank * shard * sketch_width,
        moved=16 * own.size,
    )(meta, seeds, lens, own, far, ups)


def gather_body(meta, keep_ref, got_ref, far_ref, five_ref, block_ref, grad_ref):
    size = block_ref.shape[2]
    total = keep_ref[0].astype(F32) + got_ref[0].astype(F32) + far_ref[...].astype(F32)
    grad_ref[...] = total.astype(BF)
    for dest in range(block_ref.shape[0]):
        for mat in range(3):
            block_ref[dest, mat] = total[mat, dest * size : (dest + 1) * size].astype(BF)
        block_ref[dest, 3:8] = five_ref[dest]


def gather_blocks(meta, keep, got, far, five):
    count, _, size, shard = five.shape
    blocks = (count, 8, size, shard)
    pair = pl.BlockSpec((1, *keep.shape[1:]), lambda i, m: (0, 0, 0, 0))
    return kernel_call(
        gather_body, "gather_blocks", (1,),
        [pair, pair, whole(far.shape), whole(five.shape)],
        [whole(blocks), whole(far.shape)],
        [sds(blocks, BF), sds(far.shape, BF)],
    )(meta, keep, got, far, five)


def sketch_body(meta, seeds_ref, lens_ref, grad_ref, five_ref, f0, f1, f2, f3, full_ref):
    count = token_count(lens_ref)
    sketch = full_ref.shape[1]
    full_ref[3:8] = five_ref[...]
    for mat in range(3):
        full_ref[mat] = count * sketch_one(meta, seeds_ref[mat], grad_ref[mat], sketch)
    size = sketch // 4
    for rel, out_ref in enumerate((f0, f1, f2, f3)):
        out_ref[...] = full_ref[:, columns(meta[PROJ] ^ rel, size), :]


def sketch(meta, seeds, lens, grads, five):
    sketch_width = five.shape[1]
    piece = (8, sketch_width // 4, sketch_width)
    return kernel_call(
        sketch_body, "sketch", (1,),
        [SCALARS, SCALARS, whole(grads.shape), whole(five.shape)],
        [whole(piece)] * 4,
        [sds(piece, F32)] * 4,
        [pltpu.VMEM((8, sketch_width, sketch_width), F32)],
        flops=2 * grads.size * sketch_width,
        moved=2 * grads.size,
    )(meta, seeds, lens, grads, five)


def lane_value(row, lane, place):
    return jnp.sum(jnp.where(lane == place, row, 0.0), axis=1, keepdims=True)


def tally_body(
    units, meta, got_ref, target_ref, f0, f1, f2, f3, *refs
):
    losses, (total_ref, line_ref) = refs[:units], refs[units:]
    total = jnp.sum(got_ref[...].astype(F32), axis=0)
    total_ref[...] = total
    features = f0[...] + f1[...] + f2[...] + f3[...]
    squares = jnp.sum(total * total)
    own = jnp.sum(features * features)
    loss = sum(jnp.sum(one[0:1, 0:1]) for one in losses)
    loss = jnp.where(meta[PROJ] == 0, loss, 0.0)
    lane = lax.broadcasted_iota(jnp.int32, (1, 128), 1)
    line = jnp.where(lane == 0, squares, 0.0)
    line = jnp.where(lane == 1, loss, line)
    line = jnp.where(lane == 2, own, line)
    checkpoints = target_ref.shape[0]
    for c in range(checkpoints):
        theirs = target_ref[c]
        line = jnp.where(lane == 3 + c, jnp.sum(features * theirs), line)
        line = jnp.where(lane == 3 + checkpoints + c, jnp.sum(theirs * theirs), line)
    line_ref[...] = jnp.broadcast_to(line, line_ref.shape)


def tally(meta, devices, got, targets, pieces, losses):
    _, mats, slice_rank, shard = got.shape
    args = (got, targets, *pieces, *losses)
    return kernel_call(
        partial(tally_body, len(losses)),
        "tally",
        (1,),
        [whole(one.shape) for one in args],
        [whole((mats, slice_rank, shard)), whole((devices, 128))],
        [sds((mats, slice_rank, shard), F32), sds((devices, 128), F32)],
    )(meta, *args)


def optimizer_step(weight, grad_in, first_in, second_in, clipping_scale):
    grad_clip = grad_in * clipping_scale
    first_new = BETA_ONE * first_in + (1.0 - BETA_ONE) * grad_clip
    second_new = BETA_TWO * second_in + (1.0 - BETA_TWO) * grad_clip * grad_clip
    first_hat = first_new / (1.0 - BETA_ONE**STEP)
    second_hat = second_new / (1.0 - BETA_TWO**STEP)
    new_weight = weight - LEARN_RATE * (
        first_hat / (jnp.sqrt(second_hat) + ADAM_EPS) + WEIGHT_DECAY * weight
    )
    return (new_weight, first_new, second_new)


def finish_body(
    proj_count, checkpoints, meta, lens_ref, lines_ref, total_ref,
    dw, uw, dm, um, ds, us,
    loss_out, norm_out, influence_out, dw_out, uw_out, dm_out, um_out, ds_out, us_out,
):
    lines = lines_ref[...]
    everyone = jnp.sum(lines, axis=0, keepdims=True)
    row = lax.broadcasted_iota(jnp.int32, lines.shape, 0)
    ours = jnp.sum(
        jnp.where(row // proj_count == meta[SEQ], lines, 0.0), axis=0, keepdims=True
    )
    lane = lax.broadcasted_iota(jnp.int32, (1, 128), 1)
    grad_norm = jnp.sqrt(lane_value(everyone, lane, 0))
    own = lane_value(ours, lane, 2)
    influence = jnp.zeros((1, 1), F32)
    for c in range(checkpoints):
        dot = lane_value(ours, lane, 3 + c)
        theirs = lane_value(ours, lane, 3 + checkpoints + c)
        influence += (1.0 - c / checkpoints) * dot * lax.rsqrt(own * theirs + 1e-12)
    loss_out[0] = jnp.sum(lane_value(everyone, lane, 1))
    loss_out[1] = token_count(lens_ref)
    norm_out[0] = jnp.sum(grad_norm)
    influence_out[0] = jnp.sum(influence)
    clip = jnp.minimum(1.0, CLIP_NORM / (grad_norm + 1e-06))
    half = total_ref.shape[0] // 2
    for base, ins, outs in (
        (0, (dw, dm, ds), (dw_out, dm_out, ds_out)),
        (half, (uw, um, us), (uw_out, um_out, us_out)),
    ):
        for k in range(half):
            new = optimizer_step(
                ins[0][k], total_ref[base + k], ins[1][k], ins[2][k], clip
            )
            for out, value in zip(outs, new):
                out[k] = value


def finish(meta, proj_count, checkpoints, lens, lines, total, params):
    block = whole(params[0].shape)
    return kernel_call(
        partial(finish_body, proj_count, checkpoints),
        "finish",
        (1,),
        [SCALARS, whole(lines.shape), whole(total.shape)] + [block] * 6,
        [SCALARS] * 3 + [block] * 6,
        [sds((2,), F32), sds((1,), F32), sds((1,), F32)] + [sds(params[0].shape, F32)] * 6,
        flops=20 * total.size,
        moved=28 * total.size,
    )(meta, lens, lines, total, *params)


def to_partner(array, axis, size, offset):
    return lax.ppermute(array, axis, [(i, i ^ offset) for i in range(size)])


def on_device(
    seq_count,
    proj_count,
    inputs,
    targets,
    lengths,
    norm_gain_vectors,
    query_key_value_weight,
    attention_output_weight,
    feedforward_input_weight,
    feedforward_output_weight,
    unembed,
    adapter_down_maps,
    adapter_up_maps,
    down_first_moment,
    up_first_moment,
    down_second_moment,
    up_second_moment,
    target_gradient_sketches,
    seeds,
):
    rows, width = inputs.shape
    shard = attention_output_weight.shape[0]
    vocab_local = unembed.shape[1]
    slice_rank = adapter_up_maps.shape[1]
    rank = slice_rank * seq_count
    sketch_width = target_gradient_sketches.shape[3]
    proj = lax.axis_index("proj")
    seq = lax.axis_index("dp")

    over_proj = lambda array, rel: to_partner(array, "proj", proj_count, rel)
    over_seq = lambda array, rel: to_partner(array, "dp", seq_count, rel)

    meta = jnp.stack([proj, seq]).astype(jnp.int32)
    targets = targets.reshape(rows // 128, 128)
    table = jnp.transpose(unembed)
    tables = rotary_tables(rows, shard)
    transposed = lambda array: jnp.transpose(array, (0, 2, 1))

    def from_all(array):
        y = over_proj(array, 2)
        return (array, over_proj(array, 1), y, over_proj(y, 1))

    def exchange(*pieces):
        return [pieces[0]] + [over_proj(pieces[rel], rel) for rel in (1, 2, 3)]

    packed = pack_maps(meta, seq_count, transposed(adapter_down_maps), adapter_up_maps)
    arrived = lax.all_to_all(packed, "dp", split_axis=0, concat_axis=0, tiled=True)
    later, _ = lax.optimization_barrier((attention_output_weight, packed))
    wo = (attention_output_weight, *from_all(later)[1:])

    w_ffn = (feedforward_input_weight, feedforward_output_weight)
    f0_mine, f0_sib, low, qkv = front(
        meta, inputs, norm_gain_vectors, *w_ffn, jnp.transpose(query_key_value_weight, (1, 0, 2))
    )
    maps, ups = unpack_maps(meta, arrived, (low,))
    maps = from_all(maps)
    f1_mine, f1_sib, f0_chip = ffn(
        meta, 1, inputs, norm_gain_vectors, *w_ffn, (f0_mine, over_proj(f0_sib, 1)), (maps[0],)
    )
    q0, k0, v0, rank_in0, mine, sib, lse0, f1_chip, *keep = attend(
        meta, 0, low, qkv, tables, maps, ups, table, (f1_mine, over_proj(f1_sib, 1)), wo
    )
    att0 = exchange(mine, sib, mine, sib)
    q1, k1, v1, rank_in1, mine, sib, lse1, *keep = attend(
        meta, 1, low, qkv, tables, maps, ups, table, past=(k0, v0), keep=keep
    )
    att1 = exchange(mine, sib, mine, sib)
    f_chip = (f0_chip, f1_chip)
    f_far = [over_proj(one, 2) for one in f_chip]

    def mix_unit(unit, att, keep, after):
        normed, residual, rank_out, *keep = mix(
            meta, unit, inputs, norm_gain_vectors, f_chip[unit], f_far[unit], att, maps, keep, after
        )
        return (normed, over_proj(normed, 1)), residual, rank_out, keep

    def stats_unit(unit, normed, keep, after=()):
        top, stat, cols, *keep = vocab_stats(meta, unit, *normed, targets, table, keep, after)
        return (cols, top), exchange(stat, stat, stat, stat), keep

    def back_unit(unit, top, stats, keep, after):
        results = vocab_back(meta, unit, lengths, *top, stats, keep, after)
        return results[:-4], results[-4], results[-3:]

    def norm_unit(unit, parts, residual, rank_out, att, before, keep, after):
        d0, d1, d2, d3, *more = norm_back(
            meta, unit, unit == 1, parts, residual, norm_gain_vectors,
            rank_out, att, maps, before, keep, after,
        )
        grads = more[: 1 + unit]
        return exchange(d0, d1, d2, d3), grads, more[1 + unit :]

    normed0, residual0, rank0, keep = mix_unit(0, att0, keep, (lse1,))
    top0, stats0, keep = stats_unit(0, normed0, keep)
    normed1, residual1, rank1, keep = mix_unit(1, att1, keep, (stats0[0],))
    dnormed0, loss0, keep = back_unit(0, top0, stats0, keep, (rank1,))
    dnormed0 = exchange(*dnormed0)
    top1, stats1, keep = stats_unit(1, normed1, keep, (loss0,))
    datt0, out_grads, keep = norm_unit(
        0, dnormed0, residual0, rank0, att0, (), keep, (stats1[0],)
    )
    (d_mine, d_sib), loss1, keep = back_unit(1, top1, stats1, keep, (datt0[0],))
    d_keep, d_send, *keep = split_sum(meta, d_mine, over_proj(d_sib, 1), keep[:1])
    dnormed1 = (d_keep, over_proj(d_send, 2))
    dq0, dk, dv, *keep = attend_back_first(
        meta, rows, datt0, q0, lse0, tables, (k0, v0), (d_keep,), keep
    )
    datt1, (out_keep, out_send), _ = norm_unit(
        1, dnormed1, residual1, rank1, att1, out_grads, keep, (dq0,)
    )
    out_own, out_far, in_keep, in_send, up_grads = attend_back_second(
        meta, datt1, q1, lse1, tables, (k0, v0, k1, v1), (dk, dv),
        (out_keep, over_proj(out_send, 1)), dq0, (rank_in0, rank_in1), ups, low,
    )
    out_far = over_proj(out_far, 2)
    in_got = over_proj(in_send, 1)
    in_far = over_proj((in_keep[1].astype(F32) + in_got[1].astype(F32)).astype(BF), 2)
    blocks, five = local_sketch(meta, seeds, lengths, out_own, out_far, up_grads, sketch_width)
    blocks, in_grads = gather_blocks(meta, in_keep, in_got, in_far, blocks)
    arrived = lax.all_to_all(blocks, "dp", split_axis=0, concat_axis=0, tiled=True)
    pieces = exchange(*sketch(meta, seeds, lengths, in_grads, five))

    device_count = seq_count * proj_count
    total, lines = tally(
        meta, device_count, arrived, target_gradient_sketches, pieces, (loss0, loss1)
    )
    lines = lax.all_to_all(lines, ("dp", "proj"), split_axis=0, concat_axis=0, tiled=True)
    params = (
        transposed(adapter_down_maps),
        adapter_up_maps,
        transposed(down_first_moment),
        up_first_moment,
        transposed(down_second_moment),
        up_second_moment,
    )
    loss_parts, grad_norm, influence, dw, uw, dm, um, ds, us = finish(
        meta, proj_count, target_gradient_sketches.shape[0], lengths, lines, total, params
    )
    return (
        loss_parts,
        grad_norm,
        influence,
        transposed(dw),
        uw,
        transposed(dm),
        um,
        transposed(ds),
        us,
    )


def solution(mesh):
    in_specs = (
        P("dp", None),
        P("dp"),
        P(),
        P(),
        P(None, None, "proj"),
        P("proj", None),
        P(None, "proj"),
        P("proj", None),
        P(None, "proj"),
        P(None, "proj", "dp"),
        P(None, "dp", "proj"),
        P(None, "proj", "dp"),
        P(None, "dp", "proj"),
        P(None, "proj", "dp"),
        P(None, "dp", "proj"),
        P(None, None, "proj", None),
        P(),
    )
    out_specs = (
        P(),
        P(),
        P("dp"),
        P(None, "proj", "dp"),
        P(None, "dp", "proj"),
        P(None, "proj", "dp"),
        P(None, "dp", "proj"),
        P(None, "proj", "dp"),
        P(None, "dp", "proj"),
    )
    return jax.shard_map(
        partial(on_device, mesh.shape["dp"], mesh.shape["proj"]),
        mesh=mesh,
        in_specs=in_specs,
        out_specs=out_specs,
        check_vma=False,
    )
```

```python
from functools import partial
import math

import jax
import jax.numpy as jnp
import numpy as np
from jax import lax
from jax.experimental import pallas as pl
from jax.experimental.pallas import tpu as pltpu
from jax.sharding import PartitionSpec as P

HEAD = 64
ROT = 16
STEP = 10

EPS_NORM = 1e-05
ADAPTER_SCALE = 0.25
CLIP_NORM = 0.05
LEARN_RATE = 0.05
BETA_ONE = 0.9
BETA_TWO = 0.99
ADAM_EPS = 1e-08
WEIGHT_DECAY = 0.01

BF = jnp.bfloat16
F32 = jnp.float32
BLOCK = 256
UNIT = 512
EARLY_GROUPS = (4, 4)
FIRST_GROUPS = (4, 4)
SECOND_GROUPS = (5, 4)
TOGETHER_V = 8
CHUNK_V = 512
MIB = 2**20

PROJ, SEQ = range(2)


def core_of(meta):
    return meta[PROJ] & 1


def ybit_of(meta):
    return meta[PROJ] >> 1


def token_count(lens_ref):
    return sum(lens_ref[i] for i in range(lens_ref.shape[0])).astype(F32)


def dot_nn(lhs, rhs):
    return lax.dot_general(lhs, rhs, (((1,), (0,)), ((), ())), preferred_element_type=F32)


def dot_nt(lhs, rhs):
    return lax.dot_general(lhs, rhs, (((1,), (1,)), ((), ())), preferred_element_type=F32)


def dot_tn(lhs, rhs):
    return lax.dot_general(lhs, rhs, (((0,), (0,)), ((), ())), preferred_element_type=F32)


def kernel_call(
    body, name, grid, in_specs, out_specs, out_shape, scratch=(), flops=0, moved=0, after=(),
    vmem=20, keep=(), use_keep=False,
):
    single = not isinstance(out_shape, (list, tuple))
    if single:
        out_specs, out_shape = [out_specs], [out_shape]
    first_keep = 1 + len(in_specs) + len(after)
    first_out = first_keep + len(keep)
    first_kept = first_out + len(out_shape)
    first_scratch = first_kept + len(keep)

    def run(*refs):
        kept = refs[first_keep:first_out] + refs[first_kept:first_scratch]
        body(
            refs[0],
            *(kept if use_keep else ()),
            *refs[1 : 1 + len(in_specs)],
            *refs[first_out:first_kept],
            *refs[first_scratch:],
        )

    anywhere = pl.BlockSpec(memory_space=pl.ANY)
    keep_spec = IN_VMEM if use_keep else anywhere
    call = pl.pallas_call(
        run,
        grid_spec=pltpu.PrefetchScalarGridSpec(
            num_scalar_prefetch=1,
            grid=grid,
            in_specs=list(in_specs) + [anywhere] * len(after) + [keep_spec] * len(keep),
            out_specs=list(out_specs) + [keep_spec] * len(keep),
            scratch_shapes=list(scratch),
        ),
        out_shape=list(out_shape) + [pltpu.VMEM(one.shape, one.dtype) for one in keep],
        input_output_aliases={
            first_keep + i: len(out_shape) + i for i in range(len(keep))
        },
        compiler_params=pltpu.CompilerParams(vmem_limit_bytes=vmem * MIB),
        cost_estimate=pl.CostEstimate(flops=10**12, bytes_accessed=1000, transcendentals=0),
        name=name,
    )

    def apply(*args):
        results = call(*args, *after, *[held(one) for one in keep])
        return results[0] if single else results

    return apply


def whole(shape):
    zeros = (0,) * len(shape)
    return pl.BlockSpec(shape, lambda *_: zeros)


SCALARS = pl.BlockSpec(memory_space=pltpu.SMEM)
IN_VMEM = pl.BlockSpec(memory_space=pltpu.VMEM)


def held(array):
    return pltpu.with_memory_space_constraint(array, pltpu.VMEM)


def sds(shape, dtype):
    return jax.ShapeDtypeStruct(shape, dtype)


def normalize(rows):
    center = rows - jnp.mean(rows, axis=-1, keepdims=True)
    spread = jnp.mean(center * center, axis=-1, keepdims=True)
    return center * lax.rsqrt(spread + EPS_NORM)


def columns(index, size):
    return pl.ds(pl.multiple_of(index * size, size), size)


def pack_body(meta, down_ref, up_ref, out_ref):
    mats = down_ref.shape[0]
    down, up = down_ref[...].astype(BF), up_ref[...].astype(BF)
    for dest in range(out_ref.shape[0]):
        out_ref[dest, 0] = down[mats - 1]
        out_ref[dest, 1] = up[mats - 1]
        out_ref[dest, 2 : mats + 1] = down[: mats - 1]
        out_ref[dest, mats + 1 :] = up[: mats - 1]


def pack_maps(meta, seq_count, down, up):
    shape = (seq_count, 2 * down.shape[0], *down.shape[1:])
    return kernel_call(
        pack_body, "pack_maps", (1,),
        [whole(down.shape), whole(up.shape)], whole(shape), sds(shape, BF),
        vmem=58,
    )(meta, down, up)


def unpack_body(meta, got_ref, out_ref, up_ref):
    count, _, size, _ = got_ref.shape
    for block in range(count):
        here = slice(block * size, (block + 1) * size)
        out_ref[:, here, :] = got_ref[block, 0:5]
        up_ref[:, here, :] = got_ref[block, 5:8]


def unpack_maps(meta, got, after):
    count, mats, size, shard = got.shape
    rank = count * size
    if size % 16:
        maps = jnp.transpose(got, (1, 0, 2, 3)).reshape(mats, rank, shard)
        return maps[:5], maps[5:]
    return kernel_call(
        unpack_body, "unpack_maps", (1,),
        [whole(got.shape)], [whole((5, rank, shard)), whole((3, rank, shard))],
        [sds((5, rank, shard), BF), sds((3, rank, shard), BF)],
        vmem=58,
        after=after,
    )(meta, got)


def side_sum(refs):
    one_ref, two_ref, out_ref = refs
    out_ref[...] = (one_ref[...].astype(F32) + two_ref[...].astype(F32)).astype(BF)


def ffn_chunk(low, up_ref, down_ref):
    hidden = dot_nn(low, up_ref[...])
    hidden = 0.5 * hidden * (1.0 + lax.erf(hidden * (0.5**0.5)))
    return dot_nn(hidden.astype(BF), down_ref[...])


def store_halves(meta, part_ref, mine_ref, sib_ref):
    core = core_of(meta)
    mine_ref[...] = part_ref[columns(core, BLOCK), :].astype(BF)
    sib_ref[...] = part_ref[columns(1 - core, BLOCK), :].astype(BF)


def front_body(
    chunks, meta, x_ref, gain_ref, up_ref, down_ref, w_ref,
    mine_ref, sib_ref, low_ref, out_ref, mlp_ref, part_ref,
):
    step = pl.program_id(0)

    @pl.when(step == 0)
    def _():
        mlp_ref[...] = (normalize(x_ref[...].astype(F32)) * gain_ref[1:2, :]).astype(BF)
        part_ref[...] = jnp.zeros_like(part_ref)

    @pl.when(step < chunks)
    def _():
        part_ref[...] += ffn_chunk(mlp_ref[...], up_ref, down_ref)

    @pl.when(step == chunks - 1)
    def _():
        store_halves(meta, part_ref, mine_ref, sib_ref)

    @pl.when(step >= chunks)
    def _():
        low = (normalize(x_ref[...].astype(F32)) * gain_ref[0:1, :]).astype(BF)
        low_ref[...] = low
        shard = w_ref.shape[2]
        for k in range(3):
            out_ref[:, k * shard : (k + 1) * shard] = dot_nn(low, w_ref[k])


def front(meta, x, gains, w_up, w_down, w_qkv):
    rows, width = x.shape
    out = 3 * w_qkv.shape[2]
    chunk = 512
    chunks = w_up.shape[1] // chunk
    units = rows // UNIT
    late = lambda i: jnp.maximum(i - chunks, 0)
    early = lambda i: jnp.minimum(i, chunks - 1)
    half = sds((BLOCK, width), BF)
    return kernel_call(
        partial(front_body, chunks),
        "front",
        (chunks + units,),
        [
            pl.BlockSpec((UNIT, width), lambda i, m: (late(i), 0)),
            whole(gains.shape),
            pl.BlockSpec((width, chunk), lambda i, m: (0, early(i))),
            pl.BlockSpec((chunk, width), lambda i, m: (early(i), 0)),
            whole(w_qkv.shape),
        ],
        [whole((BLOCK, width))] * 2
        + [
            pl.BlockSpec((UNIT, width), lambda i, m: (late(i), 0)),
            pl.BlockSpec((UNIT, out), lambda i, m: (late(i), 0)),
        ],
        [half, half, sds((rows, width), BF), sds((rows, out), F32)],
        [pltpu.VMEM((UNIT, width), BF), pltpu.VMEM((UNIT, width), F32)],
        vmem=58,
    )(meta, x, gains, w_up, w_down, w_qkv)


def ffn_body(
    meta, x_ref, gain_ref, up_ref, down_ref, one_ref, two_ref, table_ref,
    mine_ref, sib_ref, sum_ref, held_ref, _p, low_ref, part_ref, sem,
):
    step = pl.program_id(0)
    loads = list(table_loads(table_ref, held_ref, sem, 0, EARLY_GROUPS).values())

    @pl.when(step == 0)
    def _():
        for load in loads:
            load.start()
        low_ref[...] = (normalize(x_ref[...].astype(F32)) * gain_ref[1:2, :]).astype(BF)
        part_ref[...] = jnp.zeros_like(part_ref)
        side_sum((one_ref, two_ref, sum_ref))

    part_ref[...] += ffn_chunk(low_ref[...], up_ref, down_ref)

    @pl.when(step == pl.num_programs(0) - 1)
    def _():
        store_halves(meta, part_ref, mine_ref, sib_ref)
        for load in loads:
            load.wait()


def ffn(meta, unit, x, gains, w_up, w_down, sums, table, after=()):
    width = x.shape[1]
    anywhere = pl.BlockSpec(memory_space=pl.ANY)
    chunk = 512
    half = sds((BLOCK, width), BF)
    return kernel_call(
        ffn_body,
        f"ffn_{unit}",
        (w_up.shape[1] // chunk,),
        [
            pl.BlockSpec((UNIT, width), lambda i, m: (unit, 0)),
            whole(gains.shape),
            pl.BlockSpec((width, chunk), lambda i, m: (0, i)),
            pl.BlockSpec((chunk, width), lambda i, m: (i, 0)),
        ]
        + [whole((BLOCK, width))] * len(sums)
        + [anywhere],
        [whole((BLOCK, width))] * 3 + [anywhere] * 2,
        [half] * 3 + vocab_buffers(*table.shape),
        [
            pltpu.VMEM((UNIT, width), BF),
            pltpu.VMEM((UNIT, width), F32),
            pltpu.SemaphoreType.DMA((len(EARLY_GROUPS),)),
        ],
        after=after,
    )(meta, x, gains, w_up, w_down, *sums, table)


def rotary_tables(rows, shard):
    half = ROT // 2
    freq = np.exp(np.arange(half) * (-2.0 * math.log(10000.0) / ROT))
    angles = np.arange(rows)[:, None] * freq[None, :]
    cos, sin = np.cos(angles), np.sin(angles)
    one = np.ones((rows, HEAD))
    one[:, :half] = cos
    one[:, half:ROT] = cos
    up = np.zeros((rows, HEAD))
    up[:, half:ROT] = sin
    down = np.zeros((rows, HEAD))
    down[:, :half] = sin
    heads = min(shard, 128) // HEAD
    return [jnp.asarray(np.tile(table, (1, heads)), F32) for table in (one, up, down)]


def across(table, width):
    return jnp.concatenate([table] * (width // table.shape[1]), axis=1)


def turn(rows, cos, up, down, sign):
    half = ROT // 2
    width = rows.shape[1]
    from_low = pltpu.roll(rows, half, 1)
    from_high = pltpu.roll(rows, width - half, 1)
    cos, up, down = (across(table, width) for table in (cos, up, down))
    return rows * cos + sign * (from_low * up - from_high * down)


def project_unit(
    meta, low_ref, qkv_ref, cos_ref, up_ref, down_ref, maps, ups, q_ref, k_ref, v_ref, rank_ref
):
    proj = meta[PROJ]
    shard = q_ref.shape[1]
    rank = ups.shape[1]
    total = None
    for rel, piece in enumerate(maps):
        low = low_ref[:, columns(proj ^ rel, shard)]
        part = dot_nt(low, piece[2:5].reshape(3 * rank, shard))
        total = part if total is None else total + part
    rank_in = total.astype(BF)
    rank_ref[...] = rank_in
    pre = [
        qkv_ref[:, k * shard : (k + 1) * shard]
        + ADAPTER_SCALE * dot_nn(rank_in[:, k * rank : (k + 1) * rank], ups[k])
        for k in range(3)
    ]
    tables = (cos_ref[...], up_ref[...], down_ref[...])
    q_ref[...] = turn(pre[0], *tables, 1.0).astype(BF)
    k_ref[...] = turn(pre[1], *tables, 1.0).astype(BF)
    v_ref[...] = pre[2].astype(BF)


def vocab_chunks(vocab):
    return [(start, min(CHUNK_V, vocab - start)) for start in range(0, vocab, CHUNK_V)]


def for_chunks(vocab, first, last, together, run):
    whole_chunks = min(last, vocab // CHUNK_V)
    steps = (whole_chunks - first) // together

    def several(step, carry):
        for k in range(together):
            place = first + step * together + k
            run(place, pl.multiple_of(place * CHUNK_V, CHUNK_V), CHUNK_V)
        return carry

    if steps > 1:
        lax.fori_loop(0, steps, several, 0)
        first += steps * together
    for place in range(first, last):
        run(place, place * CHUNK_V, min(CHUNK_V, vocab - place * CHUNK_V))


def table_loads(table_ref, dest_ref, sem, first, groups):
    loads = {}
    for index, group in enumerate(groups):
        start = first * CHUNK_V
        stop = min(start + group * CHUNK_V, table_ref.shape[0])
        here = pl.ds(start, stop - start)
        loads[start] = pltpu.make_async_copy(table_ref.at[here], dest_ref.at[here], sem.at[index])
        first += group
    return loads


def vocab_buffers(vocab, width):
    return [
        pltpu.VMEM((vocab, width), BF),
        pltpu.VMEM((len(vocab_chunks(vocab)), UNIT, CHUNK_V), BF),
    ]


def head_mask(shard, head):
    return lax.broadcasted_iota(jnp.int32, (1, shard), 1) // HEAD == head


def diagonal():
    rows = lax.broadcasted_iota(jnp.int32, (BLOCK, BLOCK), 0)
    cols = lax.broadcasted_iota(jnp.int32, (BLOCK, BLOCK), 1)
    return rows >= cols


def block_scores(query, k_ref, prev, causal):
    scale = HEAD**-0.5
    diag = dot_nt(query, k_ref[prev : prev + BLOCK, :]) * scale
    diag = jnp.where(causal, diag, -1e30)
    if prev == 0:
        return diag
    return jnp.concatenate([dot_nt(query, k_ref[0:prev, :]) * scale, diag], axis=1)


def attend_unit(unit, meta, q_ref, k_ref, v_ref, mine_ref, sib_ref, lse_ref):
    shard = q_ref.shape[1]
    causal = diagonal()
    lane = lax.broadcasted_iota(jnp.int32, (BLOCK, 128), 1)
    for half in range(UNIT // BLOCK):
        prev = unit * UNIT + half * BLOCK
        query = q_ref[half * BLOCK : (half + 1) * BLOCK, :]
        out = jnp.zeros((BLOCK, shard), F32)
        lse = jnp.zeros((BLOCK, 128), F32)
        for head in range(shard // HEAD):
            mask = head_mask(shard, head)
            scores = block_scores(jnp.where(mask, query, 0), k_ref, prev, causal)
            top = jnp.max(scores, axis=1, keepdims=True)
            prob = jnp.exp(scores - top)
            total = jnp.sum(prob, axis=1, keepdims=True)
            got = dot_nn(prob.astype(BF), v_ref[0 : prev + BLOCK, :]) / total
            out = jnp.where(mask, got, out)
            lse = jnp.where(lane == head, top + jnp.log(total), lse)
        lse_ref[half * BLOCK : (half + 1) * BLOCK, :] = lse
        low = out.astype(BF)

        @pl.when(core_of(meta) == half)
        def _():
            mine_ref[...] = low

        @pl.when(core_of(meta) != half)
        def _():
            sib_ref[...] = low


def attend_first_body(
    meta, low_ref, qkv_ref, cos_ref, up_ref, down_ref, m0, m1, m2, m3, ups, one_ref, two_ref,
    w0, w1, w2, w3,
    q_ref, k_ref, v_ref, rank_ref, mine_ref, sib_ref, lse_ref, sum_ref, wo_ref, sem,
):
    shard = w0.shape[0]
    loads = [
        pltpu.make_async_copy(piece, wo_ref.at[pl.ds(rel * shard, shard)], sem.at[rel])
        for rel, piece in enumerate((w0, w1, w2, w3))
    ]
    for load in loads:
        load.start()
    side_sum((one_ref, two_ref, sum_ref))
    project_unit(
        meta, low_ref, qkv_ref, cos_ref, up_ref, down_ref, (m0, m1, m2, m3), ups,
        q_ref, k_ref, v_ref, rank_ref,
    )
    attend_unit(0, meta, q_ref, k_ref, v_ref, mine_ref, sib_ref, lse_ref)
    for load in loads:
        load.wait()


def attend_second_body(
    meta, _wo, _u, _p, _wo_out, held_ref, _p_out,
    low_ref, qkv_ref, cos_ref, up_ref, down_ref, m0, m1, m2, m3, ups, k_past, v_past, table_ref,
    q_ref, k_ref, v_ref, rank_ref, mine_ref, sib_ref, lse_ref, keys_ref, values_ref, sem,
):
    loads = list(
        table_loads(table_ref, held_ref, sem, sum(EARLY_GROUPS), FIRST_GROUPS).values()
    )
    for load in loads:
        load.start()
    project_unit(
        meta, low_ref, qkv_ref, cos_ref, up_ref, down_ref, (m0, m1, m2, m3), ups,
        q_ref, k_ref, v_ref, rank_ref,
    )
    for past, new, every in ((k_past, k_ref, keys_ref), (v_past, v_ref, values_ref)):
        every[0:UNIT, :] = past[...]
        every[UNIT:, :] = new[...]
    attend_unit(1, meta, q_ref, keys_ref, values_ref, mine_ref, sib_ref, lse_ref)
    for load in loads:
        load.wait()


def attend(meta, unit, low, qkv, tables, maps, ups, table, sums=(), wo=(), past=(), keep=()):
    rows, width = low.shape
    shard = qkv.shape[1] // 3
    rank = ups.shape[1]
    anywhere = pl.BlockSpec(memory_space=pl.ANY)
    block = lambda cols: pl.BlockSpec((UNIT, cols), lambda i, m: (unit, 0))
    in_specs = (
        [block(width), block(3 * shard)]
        + [block(tables[0].shape[1])] * 3
        + [whole(one.shape) for one in (*maps, ups)]
    )
    out_specs = [whole((UNIT, shard))] * 3 + [whole((UNIT, 3 * rank))]
    out_specs += [whole((BLOCK, shard))] * 2 + [whole((UNIT, 128))]
    out_shape = [sds((UNIT, shard), BF)] * 3 + [sds((UNIT, 3 * rank), BF)]
    out_shape += [sds((BLOCK, shard), BF)] * 2 + [sds((UNIT, 128), F32)]
    if unit == 0:
        body = attend_first_body
        args = (*sums, *wo)
        in_specs += [whole(one.shape) for one in sums] + [anywhere] * 4
        out_specs += [whole((BLOCK, width)), anywhere]
        out_shape += [sds((BLOCK, width), BF), pltpu.VMEM((4 * shard, width), BF)]
        scratch = [pltpu.SemaphoreType.DMA((4,))]
    else:
        body = attend_second_body
        args = (*past, table)
        in_specs += [whole((UNIT, shard))] * 2 + [anywhere]
        scratch = [pltpu.VMEM((rows, shard), BF)] * 2
        scratch += [pltpu.SemaphoreType.DMA((len(FIRST_GROUPS),))]
    return kernel_call(
        body, f"attend_{unit}", (1,), in_specs, out_specs, out_shape, scratch,
        keep=keep, use_keep=unit == 1,
    )(meta, low, qkv, *tables, *maps, ups, *args)


def place_grads(meta, pieces, grad_ref):
    core, ybit = core_of(meta), ybit_of(meta)
    for rel, piece in enumerate(pieces):
        place = (core ^ (rel & 1)) * 2 + (ybit ^ (rel >> 1))
        grad_ref[columns(place, BLOCK // 2), :] = piece[...]


def attend_back_unit(unit, grad_ref, q_ref, k_ref, v_ref, lse_ref, tables, dk_ref, dv_ref):
    shard = q_ref.shape[1]
    causal = diagonal()
    lane = lax.broadcasted_iota(jnp.int32, (BLOCK, 128), 1)
    scale = HEAD**-0.5
    dqs = []
    for half in range(UNIT // BLOCK):
        prev = unit * UNIT + half * BLOCK
        known = prev + BLOCK
        here = slice(half * BLOCK, (half + 1) * BLOCK)
        query = q_ref[here, :]
        grad = grad_ref[here, :]
        lse = lse_ref[here, :]
        dq = jnp.zeros((BLOCK, shard), F32)
        for head in range(shard // HEAD):
            mask = head_mask(shard, head)
            own_q = jnp.where(mask, query, 0)
            own_g = jnp.where(mask, grad, 0)
            own_lse = jnp.sum(jnp.where(lane == head, lse, 0.0), axis=1, keepdims=True)
            prob = jnp.exp(block_scores(own_q, k_ref, prev, causal) - own_lse)
            dweights = dot_nt(own_g, v_ref[0:known, :])
            delta = jnp.sum(prob * dweights, axis=1, keepdims=True)
            dscores = (prob * (dweights - delta)).astype(BF)
            dq = dq + jnp.where(mask, dot_nn(dscores, k_ref[0:known, :]), 0.0)
            dk_ref[0:known, :] += dot_tn(dscores, own_q) * scale
            dv_ref[0:known, :] += dot_tn(prob.astype(BF), own_g)
        rows = slice(prev, known)
        dq = turn(dq * scale, *(one[rows, :] for one in tables), -1.0)
        dqs.append(dq.astype(BF))
    return dqs


def attend_back_first_body(
    meta, g0, g1, g2, g3, q_ref, lse_ref, cos_ref, up_ref, down_ref, k_ref, v_ref,
    dq_ref, dk_ref, dv_ref, grad_ref,
):
    dk_ref[...] = jnp.zeros_like(dk_ref)
    dv_ref[...] = jnp.zeros_like(dv_ref)
    place_grads(meta, (g0, g1, g2, g3), grad_ref)
    dqs = attend_back_unit(
        0, grad_ref, q_ref, k_ref, v_ref, lse_ref, (cos_ref, up_ref, down_ref), dk_ref, dv_ref
    )
    dq_ref[...] = jnp.concatenate(dqs, axis=0)


def attend_back_first(meta, rows, grads, query, lse, tables, known, after, keep):
    shard = query.shape[1]
    args = (*grads, query, lse, *tables, *known)
    sums = (rows, shard)
    return kernel_call(
        attend_back_first_body, "attend_back_0", (1,),
        [whole(one.shape) for one in args],
        [whole((UNIT, shard)), whole(sums), whole(sums)],
        [sds((UNIT, shard), BF), sds(sums, F32), sds(sums, F32)],
        [pltpu.VMEM((UNIT, shard), BF)],
        after=after,
        keep=keep,
    )(meta, *args)


def attend_back_second_body(
    meta, g0, g1, g2, g3, q_ref, lse_ref, cos_ref, up_ref, down_ref, k0, v0, k1, v1,
    dk_in, dv_in, pair_ref, got_ref, dq0, rank0, rank1, ups, low_ref,
    own_ref, far_ref, keep_ref, send_ref, up_grad_ref,
    grad_ref, k_ref, v_ref, dk_ref, dv_ref, drank_ref,
):
    own_ref[...] = pair_ref[0].astype(F32) + got_ref[0].astype(F32)
    far_ref[...] = (pair_ref[1].astype(F32) + got_ref[1].astype(F32)).astype(BF)
    for first, second, every in ((k0, k1, k_ref), (v0, v1, v_ref)):
        every[0:UNIT, :] = first[...]
        every[UNIT:, :] = second[...]
    dk_ref[...] = dk_in[...]
    dv_ref[...] = dv_in[...]
    place_grads(meta, (g0, g1, g2, g3), grad_ref)
    tables = (cos_ref, up_ref, down_ref)
    dqs = attend_back_unit(1, grad_ref, q_ref, k_ref, v_ref, lse_ref, tables, dk_ref, dv_ref)
    proj = meta[PROJ]
    rank, shard = ups.shape[1:]
    dk = turn(dk_ref[...], *(one[...] for one in tables), -1.0).astype(BF)
    dpre = [jnp.concatenate([dq0[...], *dqs], axis=0), dk, dv_ref[...].astype(BF)]
    rank_in = jnp.concatenate([rank0[...], rank1[...]], axis=0)
    for k in range(3):
        here = slice(k * rank, (k + 1) * rank)
        up_grad_ref[k] = ADAPTER_SCALE * dot_tn(rank_in[:, here], dpre[k])
        drank_ref[:, here] = (ADAPTER_SCALE * dot_nt(dpre[k], ups[k])).astype(BF)
    drank = drank_ref[...]
    for rel in range(4):
        grad = dot_tn(drank, low_ref[:, columns(proj ^ rel, shard)])
        dest = (keep_ref, send_ref)[rel & 1]
        dest[rel >> 1] = grad.reshape(3, rank, shard).astype(BF)


def attend_back_second(meta, grads, query, lse, tables, known, sums, pair, dq0, rank_in, ups, low):
    rows, shard = sums[0].shape
    rank = ups.shape[1]
    args = (*grads, query, lse, *tables, *known, *sums, *pair, dq0, *rank_in, ups, low)
    out_shape = [
        sds((2, rank, shard), F32), sds((2, rank, shard), BF),
        sds((2, 3, rank, shard), BF), sds((2, 3, rank, shard), BF), sds((3, rank, shard), F32),
    ]
    return kernel_call(
        attend_back_second_body, "attend_back_1", (1,),
        [whole(one.shape) for one in args],
        [whole(one.shape) for one in out_shape],
        out_shape,
        [pltpu.VMEM((UNIT, shard), BF)]
        + [pltpu.VMEM((rows, shard), BF)] * 2
        + [pltpu.VMEM((rows, shard), F32)] * 2
        + [pltpu.VMEM((rows, 3 * rank), BF)],
        vmem=40,
    )(meta, *args)


def mix_body(
    meta, wo_ref, _u, _p, _wo, _u_out, _p_out, x_ref, gain_ref, f_own, f_far, a0, a1, a2, a3,
    m0, m1, m2, m3, norm_ref, res_ref, rank_ref, keep_ref,
):
    proj = meta[PROJ]
    shard = a0.shape[1]
    rank = None
    for a_ref, m_ref in ((a0, m0), (a1, m1), (a2, m2), (a3, m3)):
        part = dot_nt(a_ref[...], m_ref[0])
        rank = part if rank is None else rank + part
    rank = rank.astype(BF)
    total = x_ref[...].astype(F32) + f_own[...].astype(F32) + f_far[...].astype(F32)
    for rel, a_ref in enumerate((a0, a1, a2, a3)):
        total = total + dot_nn(a_ref[...], wo_ref[rel * shard : (rel + 1) * shard, :])
    keep_ref[...] = total
    for rel, m_ref in enumerate((m0, m1, m2, m3)):
        here = columns(proj ^ rel, shard)
        keep_ref[:, here] += ADAPTER_SCALE * dot_nn(rank, m_ref[1])
    residual = keep_ref[...]
    norm_ref[...] = (normalize(residual) * gain_ref[2:3, :]).astype(BF)
    mine = columns(ybit_of(meta), BLOCK // 2)
    res_ref[...] = keep_ref[mine, :]
    keep_ref[:, 0 : rank.shape[1]] = rank.astype(F32)
    rank_ref[...] = keep_ref[mine, 0 : rank.shape[1]].astype(BF)


def mix(meta, unit, x, gains, f_own, f_far, att, maps, keep, after=()):
    rows, width = x.shape
    shard = att[0].shape[1]
    rank = maps[0].shape[1]
    return kernel_call(
        mix_body,
        f"mix_{unit}",
        (1,),
        [
            pl.BlockSpec((BLOCK, width), lambda i, m: (2 * unit + core_of(m), 0)),
            whole(gains.shape),
            whole((BLOCK, width)),
            whole((BLOCK, width)),
        ]
        + [whole(one.shape) for one in att]
        + [whole((2, rank, shard))] * 4,
        [whole((BLOCK, width)), whole((BLOCK // 2, width)), whole((BLOCK // 2, rank))],
        [sds((BLOCK, width), BF), sds((BLOCK // 2, width), F32), sds((BLOCK // 2, rank), BF)],
        [pltpu.VMEM((BLOCK, width), F32)],
        after=after,
        keep=keep,
        use_keep=True,
    )(meta, x, gains, f_own, f_far, *att, *maps)


def local_columns(unit, meta, vocab, target_ref, out_ref):
    for group in range(4):
        half = core_of(meta) ^ (group >> 1)
        ids = target_ref[pl.ds((unit * 2 + half) * 2 + (group & 1), 1), :] - meta[PROJ] * vocab
        ids = jnp.where((ids >= 0) & (ids < vocab), ids, -1)
        square = jnp.transpose(jnp.broadcast_to(ids.astype(F32), (128, 128)))
        out_ref[group * 128 : (group + 1) * 128, :] = square.astype(jnp.int32)


def vocab_stats_body(unit, meta, _wo, _u, _p, _wo_out, u_ref, p_ref, *refs):
    vocab = u_ref.shape[0]
    chunks = vocab_chunks(vocab)
    if unit == 0:
        mine_ref, sib_ref, target_ref, table_ref, top_ref, st_ref, col_ref, acc_ref, sem = refs
        loads = table_loads(
            table_ref, u_ref, sem, sum(EARLY_GROUPS + FIRST_GROUPS), SECOND_GROUPS
        )
    else:
        mine_ref, sib_ref, target_ref, top_ref, st_ref, col_ref, acc_ref = refs
        loads = {}
    for load in loads.values():
        load.start()
    acc_ref[...] = jnp.zeros_like(acc_ref)
    local_columns(unit, meta, vocab, target_ref, col_ref)
    lane = lax.broadcasted_iota(jnp.int32, (BLOCK, 128), 1)

    def chunk(place, start, size):
        col = lax.broadcasted_iota(jnp.int32, (BLOCK, size), 1)
        for half, rows_ref in enumerate((mine_ref, sib_ref)):
            here = slice(half * BLOCK, (half + 1) * BLOCK)
            logits = dot_nt(rows_ref[...], u_ref[pl.ds(start, size), :])
            top = jnp.max(logits, axis=1, keepdims=True)
            prob = jnp.exp(logits - top)
            total = jnp.sum(prob, axis=1, keepdims=True)
            hit = col == col_ref[here, 0:1] - start
            picked = jnp.sum(jnp.where(hit, logits, 0.0), axis=1, keepdims=True)
            p_ref[place, here, 0:size] = prob.astype(BF)
            acc = acc_ref[here, :]
            acc = jnp.where(lane == place, top, acc)
            acc = jnp.where(lane == place + 32, total, acc)
            acc_ref[here, :] = jnp.where(lane == 64, acc + picked, acc)

    if unit == 0:
        there = sum(EARLY_GROUPS + FIRST_GROUPS)
        for_chunks(vocab, 0, there, TOGETHER_V, chunk)
        for load in loads.values():
            load.wait()
        for_chunks(vocab, there, len(chunks), TOGETHER_V, chunk)
    else:
        for_chunks(vocab, 0, len(chunks), len(chunks), chunk)
    acc = acc_ref[...]
    lane = lax.broadcasted_iota(jnp.int32, acc.shape, 1)
    top_ref[...] = acc
    tops = jnp.where(lane < len(chunks), acc, -1e30)
    best = jnp.max(tops, axis=1, keepdims=True)
    totals = pltpu.roll(acc, 128 - 32, 1)
    total = jnp.sum(
        jnp.where(lane < len(chunks), totals * jnp.exp(tops - best), 0.0), axis=1, keepdims=True
    )
    picked = jnp.sum(jnp.where(lane == 64, acc, 0.0), axis=1, keepdims=True)
    pair = jnp.where(lane == 0, best + jnp.log(total), jnp.where(lane == 1, picked, 0.0))
    st_ref[...] = jnp.transpose(pair)[0:8, :]


def vocab_stats(meta, unit, mine, sib, targets, table, keep, after=()):
    rows = 2 * BLOCK
    first = unit == 0
    return kernel_call(
        partial(vocab_stats_body, unit),
        f"vocab_stats_{unit}",
        (),
        [IN_VMEM] * 3 + [pl.BlockSpec(memory_space=pl.ANY)] * first,
        [IN_VMEM] * 3,
        [sds((rows, 128), F32), sds((8, rows), F32), sds((rows, 128), jnp.int32)],
        [pltpu.VMEM((rows, 128), F32)]
        + [pltpu.SemaphoreType.DMA((len(SECOND_GROUPS),))] * first,
        after=after,
        keep=keep,
        use_keep=True,
    )(meta, mine, held(sib), targets, *((table,) * first))


def swap_halves(pair):
    return jnp.concatenate([pair[:, BLOCK:], pair[:, :BLOCK]], axis=1)


def vocab_back_body(
    unit, meta, _wo, u_ref, p_ref, _wo_out, _u, _p, lens_ref, col_ref, top_ref, s0, s1, s2, s3,
    *refs,
):
    *outs, loss_ref, scale_ref, acc_ref = refs
    vocab = u_ref.shape[0]
    chunks = vocab_chunks(vocab)
    rows = 2 * BLOCK
    acc_ref[...] = jnp.zeros_like(acc_ref)
    parts = [s0[...], swap_halves(s1[...]), s2[...], swap_halves(s3[...])]
    lses = [part[0:1, :] for part in parts]
    best = jnp.maximum(jnp.maximum(lses[0], lses[1]), jnp.maximum(lses[2], lses[3]))
    total = sum(jnp.exp(one - best) for one in lses)
    log_norm = best + jnp.log(total)
    picked = sum(part[1:2, :] for part in parts)
    place = lax.broadcasted_iota(jnp.int32, (1, rows), 1)
    core = core_of(meta)
    offset = jnp.where(place < BLOCK, core * BLOCK, (1 - core) * BLOCK - BLOCK)
    valid = (unit * UNIT + place + offset < lens_ref[meta[SEQ]]).astype(F32)
    loss_ref[...] = jnp.broadcast_to(
        jnp.sum((log_norm - picked) * valid, axis=1, keepdims=True), (8, 128)
    )
    weight = valid / token_count(lens_ref)
    row = lax.broadcasted_iota(jnp.int32, (128, rows), 0)
    lines = jnp.where(row == 0, log_norm, 0.0)
    lines = jnp.where(row == 1, weight, lines)
    lines = jnp.where(row == 2, (jnp.exp(picked - log_norm) - 1.0) * weight, lines)
    cols = jnp.transpose(lines)
    lane = lax.broadcasted_iota(jnp.int32, (rows, 128), 1)
    take = lambda k: jnp.sum(jnp.where(lane == k, cols, 0.0), axis=1, keepdims=True)
    tops = jnp.where(lane < len(chunks), top_ref[...], -1e30)
    scales = jnp.exp(tops - take(0)) * take(1)
    scale_ref[...] = jnp.where(lane == 64, take(2), scales)

    lane = lax.broadcasted_iota(jnp.int32, (BLOCK, 128), 1)
    for place, (start, size) in enumerate(chunks):
        col = lax.broadcasted_iota(jnp.int32, (BLOCK, size), 1)
        for half in range(2):
            here = slice(half * BLOCK, (half + 1) * BLOCK)
            scales = scale_ref[here, :]
            at_hit = jnp.sum(jnp.where(lane == 64, scales, 0.0), axis=1, keepdims=True)
            scale = jnp.sum(jnp.where(lane == place, scales, 0.0), axis=1, keepdims=True)
            hit = col == col_ref[here, 0:1] - start
            grad = jnp.where(hit, at_hit, p_ref[place, here, 0:size].astype(F32) * scale)
            acc_ref[here, :] += dot_nn(grad.astype(BF), u_ref[start : start + size, :])

    if unit == 1:
        outs[0][...] = acc_ref[0:BLOCK, :].astype(BF)
        outs[1][...] = acc_ref[BLOCK:, :].astype(BF)
        return
    quarter = BLOCK // 2
    for rel, out_ref in enumerate(outs):
        place = (rel & 1) * 2 + (ybit_of(meta) ^ (rel >> 1))
        out_ref[...] = acc_ref[columns(place, quarter), :].astype(BF)


def vocab_back(meta, unit, lens, cols, tops, stats, keep, after=()):
    width = keep[1].shape[1]
    rows = 2 * BLOCK
    outs = [sds((BLOCK, width), BF)] * 2 if unit else [sds((BLOCK // 2, width), BF)] * 4
    return kernel_call(
        partial(vocab_back_body, unit),
        f"vocab_back_{unit}",
        (),
        [SCALARS] + [IN_VMEM] * 6,
        [IN_VMEM] * (len(outs) + 1),
        outs + [sds((8, 128), F32)],
        [
            pltpu.VMEM((rows, 128), F32),
            pltpu.VMEM((rows, width), F32),
        ],
        after=after,
        keep=keep,
        use_keep=True,
    )(meta, lens, cols, tops, *stats)


def split_body(meta, own_ref, got_ref, keep_ref, send_ref, sum_ref):
    sum_ref[...] = own_ref[...].astype(F32) + got_ref[...].astype(F32)
    ybit = ybit_of(meta)
    keep_ref[...] = sum_ref[columns(ybit, BLOCK // 2), :]
    send_ref[...] = sum_ref[columns(1 - ybit, BLOCK // 2), :].astype(BF)


def split_sum(meta, own, got, keep):
    rows, width = own.shape
    quarter = (rows // 2, width)
    return kernel_call(
        split_body, "split_sum", (1,),
        [whole(own.shape), IN_VMEM],
        [whole(quarter)] * 2,
        [sds(quarter, F32), sds(quarter, BF)],
        [pltpu.VMEM((rows, width), F32)],
        keep=keep,
    )(meta, own, held(got))


def norm_back_body(last, meta, wo_ref, *refs):
    refs = refs[1:] if last else refs[5:]
    count = 2 if last else 4
    parts, refs = refs[:count], refs[count:]
    (res_ref, gain_ref, rank_ref), atts, maps = refs[:3], refs[3:7], refs[7:11]
    if last:
        before_ref, *outs, keep_ref, send_ref, hold_ref = refs[11:]
    else:
        *outs, sum_ref, hold_ref = refs[11:]
    proj = meta[PROJ]
    shard = atts[0].shape[1]
    dnormed = sum(part[...].astype(F32) for part in parts)
    residual = res_ref[...]
    center = residual - jnp.mean(residual, axis=-1, keepdims=True)
    spread = jnp.mean(center * center, axis=-1, keepdims=True)
    inv = lax.rsqrt(spread + EPS_NORM)
    hat = center * inv
    dhat = dnormed * gain_ref[2:3, :]
    dres = inv * (
        dhat
        - jnp.mean(dhat, axis=-1, keepdims=True)
        - hat * jnp.mean(dhat * hat, axis=-1, keepdims=True)
    )
    hold_ref[...] = dres.astype(BF)
    dbranch = hold_ref[...]
    drank = None
    for rel, m_ref in enumerate(maps):
        part = dot_nt(hold_ref[:, columns(proj ^ rel, shard)], m_ref[1])
        drank = part if drank is None else drank + part
    drank = (ADAPTER_SCALE * drank).astype(BF)
    for rel in range(4):
        w_piece = wo_ref[rel * shard : (rel + 1) * shard, :]
        datt = dot_nt(dbranch, w_piece) + dot_nn(drank, maps[rel][0])
        outs[rel][...] = datt.astype(BF)
        g_down = dot_tn(drank, atts[rel][...])
        g_up = ADAPTER_SCALE * dot_tn(rank_ref[...], hold_ref[:, columns(proj ^ rel, shard)])
        if last:
            dest = (keep_ref, send_ref)[rel & 1]
            dest[rel >> 1, 0] = (before_ref[rel, 0] + g_down).astype(BF)
            dest[rel >> 1, 1] = (before_ref[rel, 1] + g_up).astype(BF)
        else:
            sum_ref[rel, 0] = g_down
            sum_ref[rel, 1] = g_up


def norm_back(
    meta, unit, last, parts, residual, gains, rank_out, att, maps, before, keep, after=()
):
    quarter, width = residual.shape
    shard = att[0].shape[1]
    rank = rank_out.shape[1]
    piece = (quarter, shard)
    if last:
        more = [sds((2, 2, rank, shard), BF)] * 2
    else:
        more = [sds((4, 2, rank, shard), F32)]
    return kernel_call(
        partial(norm_back_body, last),
        f"norm_back_{unit}",
        (1,),
        [whole(one.shape) for one in parts]
        + [whole(residual.shape), whole(gains.shape), whole(rank_out.shape)]
        + [pl.BlockSpec(piece, lambda i, m: (ybit_of(m), 0))] * 4
        + [whole((2, rank, shard))] * 4
        + [whole(one.shape) for one in before],
        [whole(piece)] * 4 + [whole(one.shape) for one in more],
        [sds(piece, BF)] * 4 + more,
        [pltpu.VMEM((quarter, width), BF)],
        after=after,
        keep=keep,
        use_keep=True,
    )(meta, *parts, residual, gains, rank_out, *att, *maps, *before)


def signs(row_ids, col_ids, seed):
    hashed = row_ids * 1640531527 + col_ids * 747796405 + seed * 277803737
    hashed = hashed ^ hashed >> 15 & 131071
    hashed = hashed * 2024237689
    hashed = hashed ^ hashed >> 13 & 524287
    return 1.0 - 2.0 * (hashed >> 17 & 1).astype(F32)


def sketch_one(meta, seed, grad, sketch):
    rank, shard = grad.shape
    left_rows = lax.broadcasted_iota(jnp.int32, (sketch, shard), 1) + meta[PROJ] * shard
    left_cols = lax.broadcasted_iota(jnp.int32, (sketch, shard), 0)
    right_rows = lax.broadcasted_iota(jnp.int32, (rank, sketch), 0)
    right_cols = lax.broadcasted_iota(jnp.int32, (rank, sketch), 1)
    left = signs(left_rows, left_cols, 2 * seed).astype(BF)
    right = signs(right_rows, right_cols, 2 * seed + 1)
    return jnp.dot(dot_nt(left, grad), right, precision=lax.Precision.HIGHEST)


def local_sketch_body(meta, seeds_ref, lens_ref, own_ref, far_ref, up_ref, block_ref, full_ref):
    size = block_ref.shape[2]
    count = token_count(lens_ref)
    out = own_ref[...] + far_ref[...].astype(F32)
    for place, grad in enumerate((out[0], up_ref[0], up_ref[1], up_ref[2], out[1])):
        for dest in range(block_ref.shape[0]):
            block_ref[dest, place] = grad[dest * size : (dest + 1) * size].astype(BF)
        full_ref[place] = count * sketch_one(
            meta, seeds_ref[3 + place], grad.astype(BF), full_ref.shape[1]
        )


def local_sketch(meta, seeds, lens, own, far, ups, sketch_width):
    _, rank, shard = own.shape
    count = lens.shape[0]
    blocks = (count, 5, rank // count, shard)
    full = (5, sketch_width, sketch_width)
    return kernel_call(
        local_sketch_body, "local_sketch", (1,),
        [SCALARS, SCALARS, whole(own.shape), whole(far.shape), whole(ups.shape)],
        [whole(blocks), whole(full)],
        [sds(blocks, BF), sds(full, F32)],
        flops=10 * rank * shard * sketch_width,
        moved=16 * own.size,
    )(meta, seeds, lens, own, far, ups)


def gather_body(meta, keep_ref, got_ref, far_ref, five_ref, block_ref, grad_ref):
    size = block_ref.shape[2]
    total = keep_ref[0].astype(F32) + got_ref[0].astype(F32) + far_ref[...].astype(F32)
    grad_ref[...] = total.astype(BF)
    for dest in range(block_ref.shape[0]):
        for mat in range(3):
            block_ref[dest, mat] = total[mat, dest * size : (dest + 1) * size].astype(BF)
        block_ref[dest, 3:8] = five_ref[dest]


def gather_blocks(meta, keep, got, far, five):
    count, _, size, shard = five.shape
    blocks = (count, 8, size, shard)
    pair = pl.BlockSpec((1, *keep.shape[1:]), lambda i, m: (0, 0, 0, 0))
    return kernel_call(
        gather_body, "gather_blocks", (1,),
        [pair, pair, whole(far.shape), whole(five.shape)],
        [whole(blocks), whole(far.shape)],
        [sds(blocks, BF), sds(far.shape, BF)],
    )(meta, keep, got, far, five)


def sketch_body(meta, seeds_ref, lens_ref, grad_ref, five_ref, f0, f1, f2, f3, full_ref):
    count = token_count(lens_ref)
    sketch = full_ref.shape[1]
    full_ref[3:8] = five_ref[...]
    for mat in range(3):
        full_ref[mat] = count * sketch_one(meta, seeds_ref[mat], grad_ref[mat], sketch)
    size = sketch // 4
    for rel, out_ref in enumerate((f0, f1, f2, f3)):
        out_ref[...] = full_ref[:, columns(meta[PROJ] ^ rel, size), :]


def sketch(meta, seeds, lens, grads, five):
    sketch_width = five.shape[1]
    piece = (8, sketch_width // 4, sketch_width)
    return kernel_call(
        sketch_body, "sketch", (1,),
        [SCALARS, SCALARS, whole(grads.shape), whole(five.shape)],
        [whole(piece)] * 4,
        [sds(piece, F32)] * 4,
        [pltpu.VMEM((8, sketch_width, sketch_width), F32)],
        flops=2 * grads.size * sketch_width,
        moved=2 * grads.size,
    )(meta, seeds, lens, grads, five)


def lane_value(row, lane, place):
    return jnp.sum(jnp.where(lane == place, row, 0.0), axis=1, keepdims=True)


def tally_body(
    units, meta, got_ref, target_ref, f0, f1, f2, f3, *refs
):
    losses, (total_ref, line_ref) = refs[:units], refs[units:]
    total = jnp.sum(got_ref[...].astype(F32), axis=0)
    total_ref[...] = total
    features = f0[...] + f1[...] + f2[...] + f3[...]
    squares = jnp.sum(total * total)
    own = jnp.sum(features * features)
    loss = sum(jnp.sum(one[0:1, 0:1]) for one in losses)
    loss = jnp.where(meta[PROJ] == 0, loss, 0.0)
    lane = lax.broadcasted_iota(jnp.int32, (1, 128), 1)
    line = jnp.where(lane == 0, squares, 0.0)
    line = jnp.where(lane == 1, loss, line)
    line = jnp.where(lane == 2, own, line)
    checkpoints = target_ref.shape[0]
    for c in range(checkpoints):
        theirs = target_ref[c]
        line = jnp.where(lane == 3 + c, jnp.sum(features * theirs), line)
        line = jnp.where(lane == 3 + checkpoints + c, jnp.sum(theirs * theirs), line)
    line_ref[...] = jnp.broadcast_to(line, line_ref.shape)


def tally(meta, devices, got, targets, pieces, losses):
    _, mats, slice_rank, shard = got.shape
    args = (got, targets, *pieces, *losses)
    return kernel_call(
        partial(tally_body, len(losses)),
        "tally",
        (1,),
        [whole(one.shape) for one in args],
        [whole((mats, slice_rank, shard)), whole((devices, 128))],
        [sds((mats, slice_rank, shard), F32), sds((devices, 128), F32)],
    )(meta, *args)


def optimizer_step(weight, grad_in, first_in, second_in, clipping_scale):
    grad_clip = grad_in * clipping_scale
    first_new = BETA_ONE * first_in + (1.0 - BETA_ONE) * grad_clip
    second_new = BETA_TWO * second_in + (1.0 - BETA_TWO) * grad_clip * grad_clip
    first_hat = first_new / (1.0 - BETA_ONE**STEP)
    second_hat = second_new / (1.0 - BETA_TWO**STEP)
    new_weight = weight - LEARN_RATE * (
        first_hat / (jnp.sqrt(second_hat) + ADAM_EPS) + WEIGHT_DECAY * weight
    )
    return (new_weight, first_new, second_new)


def finish_body(
    proj_count, checkpoints, meta, lens_ref, lines_ref, total_ref,
    dw, uw, dm, um, ds, us,
    loss_out, norm_out, influence_out, dw_out, uw_out, dm_out, um_out, ds_out, us_out,
):
    lines = lines_ref[...]
    everyone = jnp.sum(lines, axis=0, keepdims=True)
    row = lax.broadcasted_iota(jnp.int32, lines.shape, 0)
    ours = jnp.sum(
        jnp.where(row // proj_count == meta[SEQ], lines, 0.0), axis=0, keepdims=True
    )
    lane = lax.broadcasted_iota(jnp.int32, (1, 128), 1)
    grad_norm = jnp.sqrt(lane_value(everyone, lane, 0))
    own = lane_value(ours, lane, 2)
    influence = jnp.zeros((1, 1), F32)
    for c in range(checkpoints):
        dot = lane_value(ours, lane, 3 + c)
        theirs = lane_value(ours, lane, 3 + checkpoints + c)
        influence += (1.0 - c / checkpoints) * dot * lax.rsqrt(own * theirs + 1e-12)
    loss_out[0] = jnp.sum(lane_value(everyone, lane, 1))
    loss_out[1] = token_count(lens_ref)
    norm_out[0] = jnp.sum(grad_norm)
    influence_out[0] = jnp.sum(influence)
    clip = jnp.minimum(1.0, CLIP_NORM / (grad_norm + 1e-06))
    half = total_ref.shape[0] // 2
    for base, ins, outs in (
        (0, (dw, dm, ds), (dw_out, dm_out, ds_out)),
        (half, (uw, um, us), (uw_out, um_out, us_out)),
    ):
        for k in range(half):
            new = optimizer_step(
                ins[0][k], total_ref[base + k], ins[1][k], ins[2][k], clip
            )
            for out, value in zip(outs, new):
                out[k] = value


def finish(meta, proj_count, checkpoints, lens, lines, total, params):
    block = whole(params[0].shape)
    return kernel_call(
        partial(finish_body, proj_count, checkpoints),
        "finish",
        (1,),
        [SCALARS, whole(lines.shape), whole(total.shape)] + [block] * 6,
        [SCALARS] * 3 + [block] * 6,
        [sds((2,), F32), sds((1,), F32), sds((1,), F32)] + [sds(params[0].shape, F32)] * 6,
        flops=20 * total.size,
        moved=28 * total.size,
    )(meta, lens, lines, total, *params)


def to_partner(array, axis, size, offset):
    return lax.ppermute(array, axis, [(i, i ^ offset) for i in range(size)])


def on_device(
    seq_count,
    proj_count,
    inputs,
    targets,
    lengths,
    norm_gain_vectors,
    query_key_value_weight,
    attention_output_weight,
    feedforward_input_weight,
    feedforward_output_weight,
    unembed,
    adapter_down_maps,
    adapter_up_maps,
    down_first_moment,
    up_first_moment,
    down_second_moment,
    up_second_moment,
    target_gradient_sketches,
    seeds,
):
    rows, width = inputs.shape
    shard = attention_output_weight.shape[0]
    vocab_local = unembed.shape[1]
    slice_rank = adapter_up_maps.shape[1]
    rank = slice_rank * seq_count
    sketch_width = target_gradient_sketches.shape[3]
    proj = lax.axis_index("proj")
    seq = lax.axis_index("dp")

    over_proj = lambda array, rel: to_partner(array, "proj", proj_count, rel)
    over_seq = lambda array, rel: to_partner(array, "dp", seq_count, rel)

    meta = jnp.stack([proj, seq]).astype(jnp.int32)
    targets = targets.reshape(rows // 128, 128)
    table = jnp.transpose(unembed)
    tables = rotary_tables(rows, shard)
    transposed = lambda array: jnp.transpose(array, (0, 2, 1))

    def from_all(array):
        y = over_proj(array, 2)
        return (array, over_proj(array, 1), y, over_proj(y, 1))

    def exchange(*pieces):
        return [pieces[0]] + [over_proj(pieces[rel], rel) for rel in (1, 2, 3)]

    packed = pack_maps(meta, seq_count, transposed(adapter_down_maps), adapter_up_maps)
    arrived = lax.all_to_all(packed, "dp", split_axis=0, concat_axis=0, tiled=True)
    later, _ = lax.optimization_barrier((attention_output_weight, packed))
    wo = (attention_output_weight, *from_all(later)[1:])

    w_ffn = (feedforward_input_weight, feedforward_output_weight)
    f0_mine, f0_sib, low, qkv = front(
        meta, inputs, norm_gain_vectors, *w_ffn, jnp.transpose(query_key_value_weight, (1, 0, 2))
    )
    maps, ups = unpack_maps(meta, arrived, (low,))
    maps = from_all(maps)
    f1_mine, f1_sib, f0_chip, *buffers = ffn(
        meta, 1, inputs, norm_gain_vectors, *w_ffn, (f0_mine, over_proj(f0_sib, 1)), table, (maps[0],)
    )
    q0, k0, v0, rank_in0, mine, sib, lse0, f1_chip, *keep = attend(
        meta, 0, low, qkv, tables, maps, ups, table, (f1_mine, over_proj(f1_sib, 1)), wo,
        keep=buffers,
    )
    att0 = exchange(mine, sib, mine, sib)
    q1, k1, v1, rank_in1, mine, sib, lse1, *keep = attend(
        meta, 1, low, qkv, tables, maps, ups, table, past=(k0, v0), keep=keep
    )
    att1 = exchange(mine, sib, mine, sib)
    f_chip = (f0_chip, f1_chip)
    f_far = [over_proj(one, 2) for one in f_chip]

    def mix_unit(unit, att, keep, after):
        normed, residual, rank_out, *keep = mix(
            meta, unit, inputs, norm_gain_vectors, f_chip[unit], f_far[unit], att, maps, keep, after
        )
        return (normed, over_proj(normed, 1)), residual, rank_out, keep

    def stats_unit(unit, normed, keep, after=()):
        top, stat, cols, *keep = vocab_stats(meta, unit, *normed, targets, table, keep, after)
        return (cols, top), exchange(stat, stat, stat, stat), keep

    def back_unit(unit, top, stats, keep, after):
        results = vocab_back(meta, unit, lengths, *top, stats, keep, after)
        return results[:-4], results[-4], results[-3:]

    def norm_unit(unit, parts, residual, rank_out, att, before, keep, after):
        d0, d1, d2, d3, *more = norm_back(
            meta, unit, unit == 1, parts, residual, norm_gain_vectors,
            rank_out, att, maps, before, keep, after,
        )
        grads = more[: 1 + unit]
        return exchange(d0, d1, d2, d3), grads, more[1 + unit :]

    normed0, residual0, rank0, keep = mix_unit(0, att0, keep, (lse1,))
    top0, stats0, keep = stats_unit(0, normed0, keep)
    normed1, residual1, rank1, keep = mix_unit(1, att1, keep, (stats0[0],))
    dnormed0, loss0, keep = back_unit(0, top0, stats0, keep, (rank1,))
    dnormed0 = exchange(*dnormed0)
    top1, stats1, keep = stats_unit(1, normed1, keep, (loss0,))
    datt0, out_grads, keep = norm_unit(
        0, dnormed0, residual0, rank0, att0, (), keep, (stats1[0],)
    )
    (d_mine, d_sib), loss1, keep = back_unit(1, top1, stats1, keep, (datt0[0],))
    d_keep, d_send, *keep = split_sum(meta, d_mine, over_proj(d_sib, 1), keep[:1])
    dnormed1 = (d_keep, over_proj(d_send, 2))
    dq0, dk, dv, *keep = attend_back_first(
        meta, rows, datt0, q0, lse0, tables, (k0, v0), (d_keep,), keep
    )
    datt1, (out_keep, out_send), _ = norm_unit(
        1, dnormed1, residual1, rank1, att1, out_grads, keep, (dq0,)
    )
    out_own, out_far, in_keep, in_send, up_grads = attend_back_second(
        meta, datt1, q1, lse1, tables, (k0, v0, k1, v1), (dk, dv),
        (out_keep, over_proj(out_send, 1)), dq0, (rank_in0, rank_in1), ups, low,
    )
    out_far = over_proj(out_far, 2)
    in_got = over_proj(in_send, 1)
    in_far = over_proj((in_keep[1].astype(F32) + in_got[1].astype(F32)).astype(BF), 2)
    blocks, five = local_sketch(meta, seeds, lengths, out_own, out_far, up_grads, sketch_width)
    blocks, in_grads = gather_blocks(meta, in_keep, in_got, in_far, blocks)
    arrived = lax.all_to_all(blocks, "dp", split_axis=0, concat_axis=0, tiled=True)
    pieces = exchange(*sketch(meta, seeds, lengths, in_grads, five))

    device_count = seq_count * proj_count
    total, lines = tally(
        meta, device_count, arrived, target_gradient_sketches, pieces, (loss0, loss1)
    )
    lines = lax.all_to_all(lines, ("dp", "proj"), split_axis=0, concat_axis=0, tiled=True)
    params = (
        transposed(adapter_down_maps),
        adapter_up_maps,
        transposed(down_first_moment),
        up_first_moment,
        transposed(down_second_moment),
        up_second_moment,
    )
    loss_parts, grad_norm, influence, dw, uw, dm, um, ds, us = finish(
        meta, proj_count, target_gradient_sketches.shape[0], lengths, lines, total, params
    )
    return (
        loss_parts,
        grad_norm,
        influence,
        transposed(dw),
        uw,
        transposed(dm),
        um,
        transposed(ds),
        us,
    )


def solution(mesh):
    in_specs = (
        P("dp", None),
        P("dp"),
        P(),
        P(),
        P(None, None, "proj"),
        P("proj", None),
        P(None, "proj"),
        P("proj", None),
        P(None, "proj"),
        P(None, "proj", "dp"),
        P(None, "dp", "proj"),
        P(None, "proj", "dp"),
        P(None, "dp", "proj"),
        P(None, "proj", "dp"),
        P(None, "dp", "proj"),
        P(None, None, "proj", None),
        P(),
    )
    out_specs = (
        P(),
        P(),
        P("dp"),
        P(None, "proj", "dp"),
        P(None, "dp", "proj"),
        P(None, "proj", "dp"),
        P(None, "dp", "proj"),
        P(None, "proj", "dp"),
        P(None, "dp", "proj"),
    )
    return jax.shard_map(
        partial(on_device, mesh.shape["dp"], mesh.shape["proj"]),
        mesh=mesh,
        in_specs=in_specs,
        out_specs=out_specs,
        check_vma=False,
    )
```
